128 devices in a mesh: slab: 32 (over x, y, core), sub: 4 (over z).
Axes of the slice: x: 4, y: 4, z: 4, core: 2. Of those that a mesh axis runs over, the one named last changes fastest.
Arguments:
- load_values: float32 [3, 128, 32, 256], P(None, 'slab', 'sub'), may hold values from -6 to 6
- load_mask: int32 [128, 32, 256], P('slab', 'sub'), may hold values 0 or 1
- fixed_mask: int32 [128, 32, 256], P('slab', 'sub'), may hold values 0 or 1
- frequencies: float32 [3, 128], replicated, may hold values from -24 to 24
- weight_in: bfloat16 [256, 512], replicated, may hold values from -0.375 to 0.375
- weight_mid: bfloat16 [512, 512], replicated, may hold values from -0.25 to 0.25
- weight_out: bfloat16 [512], replicated, may hold values from -0.25 to 0.25
Outputs:
- displacement: float32 [3, 128, 32, 256], P(None, 'slab', 'sub')
- density: float32 [128, 32, 256], P('slab', 'sub')
- grad_weight_in: float32 [256, 512], replicated
- grad_weight_mid: float32 [512, 512], replicated
- grad_weight_out: float32 [512], replicated
The draws below stay inside these ranges and needn't reach their ends.
All inputs are finite; a program needn't handle non-finite values. No bound on the sum of `load_mask` or of `fixed_mask` on one device may be relied on, other than what follows from the above.
Results may differ from the reference program's by a relative error of at most 0.00055.
Values sent between devices are 32-bit elements; how exact they have to be, the bound alone decides.
No kernel may reach another device: no remote copies, remote signals or barrier semaphores. Data moves between devices by JAX's collectives and lax.ppermute only.
A program may use at most 256 MiB of HBM per device.

```python
import math
import jax
import jax.numpy as jnp
import numpy as np
from jax import lax

NFREQ = 128
FEAT = 256
HID = 512
ITERS = 3
NX = 128
NY = 32
NZ = 256
NE = 1048576


def touch_ends(array, stream_key, smallest, largest):
    longest = array.shape.index(max(array.shape))
    spots = []
    for shift in (0, 1):
        where = [jax.random.randint(jax.random.fold_in(stream_key, axis), (), 0, length) for axis, length in enumerate(array.shape)]
        where[longest] = (where[longest] + shift) % array.shape[longest]
        spots.append(tuple(where))
    return array.at[spots[0]].set(smallest).at[spots[1]].set(largest)


def block_levels(own_key, extent, split, smallest, largest):
    def one(position, parts):
        draws = jax.random.uniform(jax.random.fold_in(jax.random.fold_in(own_key, 6), position), (parts,), jnp.float32, smallest / len(split), largest / len(split))
        return jnp.repeat(jnp.exp(draws), extent[position] // parts).reshape((-1,) + (1,) * (len(extent) - position - 1))

    loudness = one(*split[0])
    for cut in split[1:]:
        loudness = loudness * one(*cut)
    return loudness


def noise(key, shape, deviation, reach, cuts=(), kind=jnp.bfloat16):
    level = block_levels(key, shape, cuts, -0.22, 0.18) if cuts else 1.0
    array = jax.random.normal(key, shape, jnp.float32) * deviation * level
    return jnp.minimum(jnp.maximum(array, -reach), reach).astype(kind)


def setup_inputs(seed: int = 0) -> dict:
    keys = jax.random.split(jax.random.key(seed), 8)
    return {
        "load_values": noise(keys[0], (3, NX, NY, NZ), 1.0, 6.0, ((1, 32), (2, 4)), jnp.float32),
        "load_mask": touch_ends((jax.random.randint(keys[1], (NX, NY, NZ), 0, 4) < 1).astype(jnp.int32), jax.random.fold_in(keys[1], 1), 0, 1),
        "fixed_mask": touch_ends((jax.random.randint(keys[2], (NX, NY, NZ), 0, 8) < 1).astype(jnp.int32), jax.random.fold_in(keys[2], 1), 0, 1),
        "frequencies": noise(keys[3], (3, NFREQ), 6.0, 24.0, (), jnp.float32),
        "weight_in": noise(keys[4], (FEAT, HID), FEAT ** -0.5, 0.375),
        "weight_mid": noise(keys[5], (HID, HID), HID ** -0.5, 0.25),
        "weight_out": noise(keys[6], (HID,), HID ** -0.5, 0.25),
    }


two_pi = 2.0 * math.pi
emin = 0.001
penalty = 4.0
vol_target = 0.3
corner_list = [(0, 0, 0), (0, 0, 1), (0, 1, 0), (0, 1, 1), (1, 0, 0), (1, 0, 1), (1, 1, 0), (1, 1, 1)]

def hex_stiffness():
    poisson = 0.3
    lame_first = poisson / ((1.0 + poisson) * (1.0 - 2.0 * poisson))
    lame_second = 0.5 / (1.0 + poisson)
    elastic = np.zeros((6, 6))
    elastic[:3, :3] = lame_first
    for axis_number in range(3):
        elastic[axis_number, axis_number] += 2.0 * lame_second
        elastic[axis_number + 3, axis_number + 3] = lame_second
    gauss_points = [0.5 - 0.5 / math.sqrt(3.0), 0.5 + 0.5 / math.sqrt(3.0)]
    matrix = np.zeros((24, 24))
    for point_x in gauss_points:
        for point_y in gauss_points:
            for point_z in gauss_points:
                location = (point_x, point_y, point_z)
                strain = np.zeros((6, 24))
                for corner_number, corner in enumerate(corner_list):
                    factors = [location[axis_number] if corner[axis_number] == 1 else 1.0 - location[axis_number] for axis_number in range(3)]
                    slopes = [1.0 if corner[axis_number] == 1 else -1.0 for axis_number in range(3)]
                    derivative = [slopes[0] * factors[1] * factors[2], factors[0] * slopes[1] * factors[2], factors[0] * factors[1] * slopes[2]]
                    column = 3 * corner_number
                    for axis_number in range(3):
                        strain[axis_number, column + axis_number] = derivative[axis_number]
                    strain[3, column + 1] = derivative[2]
                    strain[3, column + 2] = derivative[1]
                    strain[4, column + 0] = derivative[2]
                    strain[4, column + 2] = derivative[0]
                    strain[5, column + 0] = derivative[1]
                    strain[5, column + 1] = derivative[0]
                matrix += strain.T @ elastic @ strain / 8.0
    return matrix.astype(np.float32)

def element_values(padded, counts):
    pieces = []
    for corner in corner_list:
        for component in range(3):
            pieces.append(padded[component, corner[0]:corner[0] + counts[0], corner[1]:corner[1] + counts[1], corner[2]:corner[2] + counts[2]])
    return jnp.stack(pieces)

def element_forces(values, stiffness, table):
    return jnp.einsum('ij,jxyz->ixyz', table, values, precision=lax.Precision.HIGHEST) * stiffness[None]

def element_energy(values, table):
    return lax.optimization_barrier(jnp.sum(values * jnp.einsum('ij,jxyz->ixyz', table, values, precision=lax.Precision.HIGHEST), axis=0))

def assemble(forces, counts, shape):
    total = jnp.zeros(shape, jnp.float32)
    number = 0
    for corner in corner_list:
        for component in range(3):
            total = total.at[component, corner[0]:corner[0] + counts[0], corner[1]:corner[1] + counts[1], corner[2]:corner[2] + counts[2]].add(forces[number])
            number = number + 1
    return total

def encode(plane_number, y_first, ycount, grid_cells, frequencies):
    x_centre = (plane_number.astype(jnp.float32) + 0.5) / grid_cells[0]
    y_centre = ((y_first + jnp.arange(ycount, dtype=jnp.int32)).astype(jnp.float32) + 0.5) / grid_cells[1]
    z_centre = (jnp.arange(grid_cells[2], dtype=jnp.int32).astype(jnp.float32) + 0.5) / grid_cells[2]
    phase = two_pi * (x_centre * frequencies[0][None, None, :] + y_centre[:, None, None] * frequencies[1][None, None, :] + z_centre[None, :, None] * frequencies[2][None, None, :])
    phase = phase.reshape(ycount * grid_cells[2], frequencies.shape[1])
    return jnp.concatenate([jnp.cos(phase), jnp.sin(phase)], axis=1).astype(jnp.bfloat16)

def layer_pass(features, weights):
    preact_in = jnp.dot(features, weights[0], preferred_element_type=jnp.float32)
    hidden_in = jax.nn.silu(preact_in).astype(jnp.bfloat16)
    preact_mid = jnp.dot(hidden_in, weights[1], preferred_element_type=jnp.float32)
    hidden_mid = jax.nn.silu(preact_mid).astype(jnp.bfloat16)
    logits = jnp.dot(hidden_mid, weights[2], preferred_element_type=jnp.float32)
    return (preact_in, hidden_in, preact_mid, hidden_mid, jax.nn.sigmoid(logits))

def plane_density(plane_number, y_first, ycount, grid_cells, frequencies, weights):
    return layer_pass(encode(plane_number, y_first, ycount, grid_cells, frequencies), weights)[4]

def silu_slope(value):
    gate = jax.nn.sigmoid(value)
    return gate * (1.0 + value * (1.0 - gate))

def gradient_sum(plane_numbers, sens_planes, y_first, ycount, grid_cells, frequencies, weights):

    def one_plane(totals, inputs):
        plane_number, sensitivity = inputs
        features = encode(plane_number, y_first, ycount, grid_cells, frequencies)
        preact_in, hidden_in, preact_mid, hidden_mid, density = layer_pass(features, weights)
        slope_logit = sensitivity * density * (1.0 - density)
        grad_out = jnp.dot(slope_logit, hidden_mid.astype(jnp.float32), precision=lax.Precision.HIGHEST)
        slope_mid = (slope_logit[:, None] * weights[2].astype(jnp.float32)[None, :] * silu_slope(preact_mid)).astype(jnp.bfloat16)
        grad_mid = jnp.dot(hidden_in.T, slope_mid, preferred_element_type=jnp.float32)
        back_in = jnp.dot(slope_mid, weights[1].T, preferred_element_type=jnp.float32)
        slope_in = (back_in * silu_slope(preact_in)).astype(jnp.bfloat16)
        grad_in = jnp.dot(features.T, slope_in, preferred_element_type=jnp.float32)
        return ((totals[0] + grad_in, totals[1] + grad_mid, totals[2] + grad_out), None)
    width_in, width_hid = weights[0].shape
    start_totals = (jnp.zeros((width_in, width_hid), jnp.float32), jnp.zeros((width_hid, width_hid), jnp.float32), jnp.zeros((width_hid,), jnp.float32))
    return lax.scan(one_plane, start_totals, (plane_numbers, sens_planes))[0]

def apply_operator(field, stiffness, free, table):
    grid_cells = stiffness.shape
    held = field * free
    padded = jnp.pad(held, ((0, 0), (0, 1), (0, 1), (0, 1)))
    forces = element_forces(element_values(padded, grid_cells), stiffness, table)
    total = assemble(forces, grid_cells, (3, grid_cells[0] + 1, grid_cells[1] + 1, grid_cells[2] + 1))
    return free * total[:, :grid_cells[0], :grid_cells[1], :grid_cells[2]] + (1.0 - free) * field

def reference(load_values, load_mask, fixed_mask, frequencies, weight_in, weight_mid, weight_out):
    table = jnp.asarray(hex_stiffness())
    weights = (weight_in, weight_mid, weight_out)
    grid_cells = (NX, NY, NZ)
    planes = jnp.arange(NX, dtype=jnp.int32)
    density = lax.map(lambda plane_number: plane_density(plane_number, 0, NY, grid_cells, frequencies, weights), planes).reshape(NX, NY, NZ)
    stiffness = emin + (1.0 - emin) * density ** 3
    free = (1 - fixed_mask).astype(jnp.float32)[None]
    force = free * load_mask.astype(jnp.float32)[None] * load_values
    solution = jnp.zeros_like(force)
    residual = force
    direction = force
    norm_now = jnp.sum(residual * residual)
    for iteration in range(ITERS):
        image = apply_operator(direction, stiffness, free, table)
        alpha = norm_now / jnp.sum(direction * image)
        solution = solution + alpha * direction
        if iteration + 1 < ITERS:
            residual = residual - alpha * image
            norm_next = jnp.sum(residual * residual)
            direction = residual + norm_next / norm_now * direction
            norm_now = norm_next
    values = element_values(jnp.pad(solution, ((0, 0), (0, 1), (0, 1), (0, 1))), grid_cells)
    energy = element_energy(values, table)
    compliance = jnp.sum(stiffness * energy)
    volume = jnp.sum(density)
    sensitivity = -3.0 * (1.0 - emin) * density ** 2 * energy / compliance + 2.0 * penalty * (volume / NE - vol_target) / NE
    grads = gradient_sum(planes, sensitivity.reshape(NX, NY * NZ), 0, NY, grid_cells, frequencies, weights)
    return (solution, density, grads[0], grads[1], grads[2])
```

```python
import math

import jax
import jax.numpy as jnp
import numpy as np
from jax import lax
from jax.sharding import Mesh
from jax.sharding import PartitionSpec as P

ITERS = 3
SLAB = ("x", "y", "c")
CHIPS = ("x", "y", "z")


two_pi = 2.0 * math.pi
emin = 0.001
penalty = 4.0
vol_target = 0.3
corner_list = [
    (0, 0, 0),
    (0, 0, 1),
    (0, 1, 0),
    (0, 1, 1),
    (1, 0, 0),
    (1, 0, 1),
    (1, 1, 0),
    (1, 1, 1),
]


def extended(array, sides, width):
    for axis, dim in sides:
        size, length = (lax.axis_size(axis), array.shape[dim])
        up = [(i, (i + 1) % size) for i in range(size - 1)]
        down = [(j, i) for i, j in up]
        last = lax.slice_in_dim(array, length - width, length, axis=dim)
        first = lax.slice_in_dim(array, 0, width, axis=dim)
        before = lax.ppermute(last, axis, up)
        after = lax.ppermute(first, axis, down)
        array = jnp.concatenate([before, array, after], axis=dim)
    return array


def from_behind(block, axis, distance):
    devices = range(lax.axis_size(axis))
    route = [(i - distance, i) for i in devices if i - distance in devices]
    return lax.ppermute(block, axis, route)


def hex_stiffness():
    poisson = 0.3
    lame_first = poisson / ((1.0 + poisson) * (1.0 - 2.0 * poisson))
    lame_second = 0.5 / (1.0 + poisson)
    elastic = np.zeros((6, 6))
    elastic[:3, :3] = lame_first
    for axis_number in range(3):
        elastic[axis_number, axis_number] += 2.0 * lame_second
        elastic[axis_number + 3, axis_number + 3] = lame_second
    gauss_points = [0.5 - 0.5 / math.sqrt(3.0), 0.5 + 0.5 / math.sqrt(3.0)]
    matrix = np.zeros((24, 24))
    for point_x in gauss_points:
        for point_y in gauss_points:
            for point_z in gauss_points:
                location = (point_x, point_y, point_z)
                strain = np.zeros((6, 24))
                for corner_number, corner in enumerate(corner_list):
                    factors = [
                        (
                            location[axis_number]
                            if corner[axis_number] == 1
                            else 1.0 - location[axis_number]
                        )
                        for axis_number in range(3)
                    ]
                    slopes = [1.0 if corner[axis_number] == 1 else -1.0 for axis_number in range(3)]
                    derivative = [
                        slopes[0] * factors[1] * factors[2],
                        factors[0] * slopes[1] * factors[2],
                        factors[0] * factors[1] * slopes[2],
                    ]
                    column = 3 * corner_number
                    for axis_number in range(3):
                        strain[axis_number, column + axis_number] = derivative[axis_number]
                    strain[3, column + 1] = derivative[2]
                    strain[3, column + 2] = derivative[1]
                    strain[4, column + 0] = derivative[2]
                    strain[4, column + 2] = derivative[0]
                    strain[5, column + 0] = derivative[1]
                    strain[5, column + 1] = derivative[0]
                matrix += strain.T @ elastic @ strain / 8.0
    return matrix.astype(np.float32)


def element_values(padded, counts):
    pieces = []
    for corner in corner_list:
        for component in range(3):
            pieces.append(
                padded[
                    component,
                    corner[0] : corner[0] + counts[0],
                    corner[1] : corner[1] + counts[1],
                    corner[2] : corner[2] + counts[2],
                ]
            )
    return jnp.stack(pieces)


def element_forces(values, stiffness, table):
    return (
        jnp.einsum("ij,jxyz->ixyz", table, values, precision=lax.Precision.HIGHEST)
        * stiffness[None]
    )


def element_energy(values, table):
    return jnp.sum(
        values * jnp.einsum("ij,jxyz->ixyz", table, values, precision=lax.Precision.HIGHEST), axis=0
    )


def assemble(forces, counts, shape):
    components = []
    for component in range(3):
        total = None
        for corner_number, corner in enumerate(corner_list):
            widths = tuple(
                (
                    (
                        corner[dim_number],
                        shape[dim_number + 1] - counts[dim_number] - corner[dim_number],
                    )
                    for dim_number in range(3)
                )
            )
            placed = jnp.pad(forces[3 * corner_number + component], widths)
            total = placed if total is None else total + placed
        components.append(total)
    return jnp.stack(components)


def encode(plane_number, y_first, ycount, grid_cells, frequencies):
    x_centre = (plane_number.astype(jnp.float32) + 0.5) / grid_cells[0]
    y_centre = (
        (y_first + jnp.arange(ycount, dtype=jnp.int32)).astype(jnp.float32) + 0.5
    ) / grid_cells[1]
    z_centre = (jnp.arange(grid_cells[2], dtype=jnp.int32).astype(jnp.float32) + 0.5) / grid_cells[
        2
    ]
    phase = two_pi * (
        x_centre * frequencies[0][None, None, :]
        + y_centre[:, None, None] * frequencies[1][None, None, :]
        + z_centre[None, :, None] * frequencies[2][None, None, :]
    )
    phase = phase.reshape(ycount * grid_cells[2], frequencies.shape[1])
    return jnp.concatenate([jnp.cos(phase), jnp.sin(phase)], axis=1).astype(jnp.bfloat16)


def encode_planes(plane_numbers, y_first, ycount, grid_cells, frequencies):
    stacked = lax.map(
        lambda plane_number: encode(plane_number, y_first, ycount, grid_cells, frequencies),
        plane_numbers,
    )
    return stacked.reshape(stacked.shape[0] * stacked.shape[1], stacked.shape[2])


def layer_pass(features, weights):
    preact_in = jnp.dot(features, weights[0], preferred_element_type=jnp.float32)
    hidden_in = jax.nn.silu(preact_in).astype(jnp.bfloat16)
    preact_mid = jnp.dot(hidden_in, weights[1], preferred_element_type=jnp.float32)
    hidden_mid = jax.nn.silu(preact_mid).astype(jnp.bfloat16)
    logits = jnp.dot(hidden_mid, weights[2], preferred_element_type=jnp.float32)
    return (preact_in, hidden_in, preact_mid, hidden_mid, jax.nn.sigmoid(logits))


def silu_slope(value):
    gate = jax.nn.sigmoid(value)
    return gate * (1.0 + value * (1.0 - gate))


def backward_rows(features, stored, sens_rows, weights):
    preact_in, hidden_in, preact_mid, hidden_mid, density_rows = stored
    slope_logit = sens_rows * density_rows * (1.0 - density_rows)
    grad_out = jnp.dot(slope_logit, hidden_mid.astype(jnp.float32), precision=lax.Precision.HIGHEST)
    slope_mid = (
        slope_logit[:, None] * weights[2].astype(jnp.float32)[None, :] * silu_slope(preact_mid)
    ).astype(jnp.bfloat16)
    grad_mid = jnp.dot(hidden_in.T, slope_mid, preferred_element_type=jnp.float32)
    back_in = jnp.dot(slope_mid, weights[1].T, preferred_element_type=jnp.float32)
    slope_in = (back_in * silu_slope(preact_in)).astype(jnp.bfloat16)
    grad_in = jnp.dot(features.T, slope_in, preferred_element_type=jnp.float32)
    return (grad_in, grad_mid, grad_out)


def extended_values(field):
    padded = extended(field, ((SLAB, 1), ("z", 2)), 1)
    padded = jnp.pad(padded, ((0, 0), (0, 0), (0, 0), (0, 1)))
    counts = (field.shape[1] + 1, field.shape[2] + 1, field.shape[3])
    return element_values(padded, counts)


def apply_operator(field, stiff_ext, free, table):
    cells_x, cells_y, cells_z = (field.shape[1], field.shape[2], field.shape[3])
    held = field * free
    forces = element_forces(extended_values(held), stiff_ext, table)
    total = assemble(forces, stiff_ext.shape, (3, cells_x + 2, cells_y + 2, cells_z + 1))
    return free * total[:, 1 : cells_x + 1, 1 : cells_y + 1, :cells_z] + (1.0 - free) * field


def summed_everywhere(row):
    count = lax.axis_size(("x", "y", "c", "z"))
    sent = jnp.broadcast_to(row[None], (count,) + row.shape)
    got = lax.all_to_all(sent, ("x", "y", "c", "z"), 0, 0)
    return jnp.sum(got, axis=0)


def summed_rows(rows):
    chips = lax.axis_size(CHIPS)
    core = lax.axis_index("c")
    halves = rows.reshape(2, chips, rows.shape[0] // (2 * chips), rows.shape[1])
    swap = [(0, 1), (1, 0)]
    mine = lax.dynamic_index_in_dim(halves, core, 0, keepdims=False)
    other = lax.dynamic_index_in_dim(halves, 1 - core, 0, keepdims=False)
    half = mine + lax.ppermute(other, "c", swap)
    share = jnp.sum(lax.all_to_all(half, CHIPS, 0, 0), axis=0)
    half = lax.all_to_all(jnp.broadcast_to(share[None], half.shape), CHIPS, 0, 0)
    away = lax.ppermute(half, "c", swap)
    first = jnp.where(core == 0, half, away)
    second = jnp.where(core == 0, away, half)
    return jnp.concatenate([first, second], axis=0).reshape(rows.shape)


def krylov_steps(moments):
    mean = moments[1] / moments[0]
    scaled = [moments[k] / moments[0] / mean**k for k in range(2 * ITERS)]

    def product(left, right, shift):
        return sum(
            left[i] * right[j] * scaled[i + j + shift]
            for i in range(len(left))
            for j in range(len(right))
        )

    solution = [0.0] * ITERS
    residual = [1.0]
    direction = [1.0]
    norm_now = scaled[0]
    work = 0.0
    for iteration in range(ITERS):
        alpha = norm_now / product(direction, direction, 1)
        work = work + alpha * norm_now
        solution = [
            solution[i] + (alpha * direction[i] if i < len(direction) else 0.0)
            for i in range(ITERS)
        ]
        if iteration + 1 < ITERS:
            image = [0.0] + direction
            residual = [
                (residual[i] if i < len(residual) else 0.0) - alpha * image[i]
                for i in range(len(image))
            ]
            norm_next = product(residual, residual, 0)
            beta = norm_next / norm_now
            direction = [
                residual[i] + (beta * direction[i] if i < len(direction) else 0.0)
                for i in range(len(residual))
            ]
            norm_now = norm_next
    factors = [solution[i] / mean ** (i + 1) for i in range(ITERS)]
    return factors, work * moments[0] / mean


def on_device(load_values, load_mask, fixed_mask, frequencies, weight_in, weight_mid, weight_out):
    table = jnp.asarray(hex_stiffness())
    weights = (weight_in, weight_mid, weight_out)
    cells_x, cells_y, cells_z = fixed_mask.shape
    grid_cells = (cells_x * lax.axis_size(SLAB), cells_y * lax.axis_size("z"), cells_z)
    elements_total = grid_cells[0] * grid_cells[1] * grid_cells[2]
    x_first = lax.axis_index(SLAB) * cells_x
    y_first = lax.axis_index("z") * cells_y
    own_planes = x_first + jnp.arange(cells_x, dtype=jnp.int32)
    features = encode_planes(own_planes, y_first, cells_y, grid_cells, frequencies)
    stored = layer_pass(features, weights)
    density = stored[4].reshape(cells_x, cells_y, cells_z)
    stiffness = emin + (1.0 - emin) * density**3
    lower_plane = from_behind(stiffness[-1:], SLAB, 1)
    widened = jnp.concatenate([lower_plane, stiffness], axis=0)
    lower_row = from_behind(widened[:, -1:], "z", 1)
    stiff_ext = jnp.concatenate([lower_row, widened], axis=1)
    free = (1 - fixed_mask).astype(jnp.float32)[None]
    force = free * load_mask.astype(jnp.float32)[None] * load_values
    basis = [force]
    for step in range(ITERS - 1):
        basis.append(apply_operator(basis[-1], stiff_ext, free, table))
    values = [extended_values(vector) for vector in basis]
    last_energy = element_energy(values[-1], table)[1:, 1:]
    local = [jnp.sum(basis[k // 2] * basis[(k + 1) // 2]) for k in range(2 * ITERS - 1)]
    local.append(jnp.sum(stiffness * last_energy))
    local.append(jnp.sum(density))
    row = jnp.stack(local + [jnp.zeros((), jnp.float32)])
    totals = summed_everywhere(jnp.broadcast_to(row[:, None], (8, 128)))[:, 0]
    factors, compliance = krylov_steps([totals[k] for k in range(2 * ITERS)])
    volume = totals[2 * ITERS]
    solution = sum(factors[k] * basis[k] for k in range(ITERS))
    energy = element_energy(sum(factors[k] * values[k] for k in range(ITERS)), table)[1:, 1:]
    sensitivity = (
        -3.0 * (1.0 - emin) * density**2 * energy / compliance
        + 2.0 * penalty * (volume / elements_total - vol_target) / elements_total
    )
    sens_rows = sensitivity.reshape(cells_x * cells_y * cells_z)
    local_grads = backward_rows(features, stored, sens_rows, weights)
    grad_in, grad_mid, grad_out = local_grads
    spare = jnp.zeros((1024 - 769, grad_mid.shape[1]), jnp.float32)
    grads = summed_rows(jnp.concatenate([grad_mid, grad_in, grad_out[None], spare], axis=0))
    return (solution, density, grads[512:768], grads[:512], grads[768])


def solution(mesh):
    slab, sub = mesh.devices.shape
    fine = Mesh(mesh.devices.reshape(4, 4, slab // 16, sub), ("x", "y", "c", "z"))
    placed = (
        P(None, SLAB, "z", None),
        P(SLAB, "z", None),
        P(SLAB, "z", None),
        P(),
        P(),
        P(),
        P(),
    )
    return jax.shard_map(
        on_device,
        mesh=fine,
        in_specs=placed,
        out_specs=(P(None, SLAB, "z", None), P(SLAB, "z", None), P(), P(), P()),
        check_vma=False,
    )
```

```python
import functools
import itertools
import math

import jax
import jax.numpy as jnp
import numpy as np
from jax import lax
from jax.experimental import pallas as pl
from jax.experimental.pallas import tpu as pltpu
from jax.sharding import Mesh
from jax.sharding import PartitionSpec as P

ITERS = 3
SLAB = ("x", "y", "c")
CHIPS = ("x", "y", "z")
ALL = ("x", "y", "c", "z")
BF = jnp.bfloat16
F32 = jnp.float32

two_pi = 2.0 * math.pi
emin = 0.001
penalty = 4.0
vol_target = 0.3
ROWS = 16
corner_list = list(itertools.product((0, 1), repeat=3))
LAST = (((1,), (1,)), ((), ()))


def hex_stiffness():
    poisson = 0.3
    lame_first = poisson / ((1.0 + poisson) * (1.0 - 2.0 * poisson))
    lame_second = 0.5 / (1.0 + poisson)
    elastic = np.zeros((6, 6))
    elastic[:3, :3] = lame_first
    for axis_number in range(3):
        elastic[axis_number, axis_number] += 2.0 * lame_second
        elastic[axis_number + 3, axis_number + 3] = lame_second
    gauss_points = [0.5 - 0.5 / math.sqrt(3.0), 0.5 + 0.5 / math.sqrt(3.0)]
    matrix = np.zeros((24, 24))
    for location in itertools.product(gauss_points, repeat=3):
        strain = np.zeros((6, 24))
        for corner_number, corner in enumerate(corner_list):
            factors = [
                location[axis] if corner[axis] == 1 else 1.0 - location[axis] for axis in range(3)
            ]
            slopes = [1.0 if corner[axis] == 1 else -1.0 for axis in range(3)]
            derivative = [
                slopes[0] * factors[1] * factors[2],
                factors[0] * slopes[1] * factors[2],
                factors[0] * factors[1] * slopes[2],
            ]
            column = 3 * corner_number
            for axis in range(3):
                strain[axis, column + axis] = derivative[axis]
            strain[3, column + 1] = derivative[2]
            strain[3, column + 2] = derivative[1]
            strain[4, column + 0] = derivative[2]
            strain[4, column + 2] = derivative[0]
            strain[5, column + 0] = derivative[1]
            strain[5, column + 1] = derivative[0]
        matrix += strain.T @ elastic @ strain / 8.0
    return matrix


def modal_stiffness():
    table = hex_stiffness()
    change = np.zeros((24, 24))
    for row, wave in enumerate(corner_list):
        for column, corner in enumerate(corner_list):
            sign = np.prod([1.0 if c == 1 else -1.0 for w, c in zip(wave, corner) if w == 1])
            for d in range(3):
                change[3 * row + d, 3 * column + d] = sign
    modal = change @ table @ change.T / 64.0
    blocks = []
    for parity in corner_list:
        waves = [tuple(parity[a] ^ (a == d) for a in range(3)) for d in range(3)]
        index = [3 * corner_list.index(wave) + d for d, wave in enumerate(waves)]
        block = modal[np.ix_(index, index)]
        blocks.append((waves, np.where(np.abs(block) < 1e-9, 0.0, block)))
    return blocks


BLOCKS = modal_stiffness()


def lane_mask(shape, lane):
    return lax.broadcasted_iota(jnp.int32, shape, len(shape) - 1) == lane


def plane_modes(plane, rows):
    size = plane.shape[-1]
    ahead = jnp.where(lane_mask(plane.shape, size - 1), 0.0, pltpu.roll(plane, size - 1, 1))
    modes = {}
    for wave_z, part in ((0, plane + ahead), (1, ahead - plane)):
        following = pltpu.roll(part, ROWS - 1, 0)
        modes[0, wave_z] = (part + following)[:rows]
        modes[1, wave_z] = (following - part)[:rows]
    return modes


def element_modes(lower, upper):
    found = []
    for low, high in zip(lower, upper):
        modes = {}
        for key in low:
            modes[(0,) + key] = low[key] + high[key]
            modes[(1,) + key] = high[key] - low[key]
        found.append(modes)
    return found


def modal_forces(modes):
    for waves, block in BLOCKS:
        values = [modes[d][waves[d]] for d in range(3)]
        for d in range(3):
            total = None
            for other in range(3):
                if block[d, other] != 0.0:
                    term = np.float32(block[d, other]) * values[other]
                    total = term if total is None else total + term
            if total is not None:
                yield d, waves[d], values[d], total


def energy_of(modes):
    total = None
    for _, _, value, force in modal_forces(modes):
        total = value * force if total is None else total + value * force
    return total


def node_plane(gathered):
    parts = []
    for wave_z in (0, 1):
        even, odd = gathered[0, wave_z], gathered[1, wave_z]
        parts.append((even - odd) + pltpu.roll(even + odd, 1, 0))
    behind = pltpu.roll(parts[0] + parts[1], 1, 1)
    return (parts[0] - parts[1]) + jnp.where(lane_mask(behind.shape, 0), 0.0, behind)


def operator_planes(planes, stiff, free):
    modes = [[plane_modes(component, ROWS) for component in plane] for plane in planes]
    gathered = [[{} for _ in range(3)] for _ in planes]
    for e in range(len(planes) - 1):
        forces = [{} for _ in range(3)]
        for d, wave, _, force in modal_forces(element_modes(modes[e], modes[e + 1])):
            forces[d][wave] = force * stiff[e]
        for d in range(3):
            for key in itertools.product((0, 1), repeat=2):
                even, odd = forces[d].get((0,) + key), forces[d].get((1,) + key)
                for node, sign in ((e, -1), (e + 1, 1)):
                    if even is None:
                        term = odd if sign == 1 else -odd
                    else:
                        term = even + odd if sign == 1 else even - odd
                    held = gathered[node][d]
                    held[key] = term if key not in held else held[key] + term
    return [
        [node_plane(gathered[n][d]) * free[n - 1] for d in range(3)]
        for n in range(1, len(planes) - 1)
    ]


def krylov_kernel(loads, stiff, density, first, second, sums):
    planes = loads.shape[1]
    cells = planes - 5
    stiff_planes = [stiff[e] for e in range(planes - 1)]
    force = [[loads[d, p] for d in range(3)] for p in range(planes)]
    free = [loads[3, p] for p in range(planes)]
    image = operator_planes(force, stiff_planes, free[1:-1])
    twice = operator_planes(image, stiff_planes[1:-1], free[2:-2])
    own = (force[2 : 2 + cells], image[1 : 1 + cells], twice[:cells])
    rows = density.shape[1]

    def dot(left, right):
        total = None
        for p in range(cells):
            for d in range(3):
                term = left[p][d][:rows] * right[p][d][:rows]
                total = term if total is None else total + term
        return total

    totals = [dot(own[k // 2], own[(k + 1) // 2]) for k in range(2 * ITERS - 1)]
    modes = [[plane_modes(component, rows) for component in plane] for plane in twice]
    last = None
    volume = None
    for e in range(cells):
        term = stiff_planes[2 + e][:rows] * energy_of(element_modes(modes[e], modes[e + 1]))
        last = term if last is None else last + term
        volume = density[e] if volume is None else volume + density[e]
    totals += [last, volume]
    row_number = lax.broadcasted_iota(jnp.int32, sums.shape[1:], 0)
    result = jnp.zeros(sums.shape[1:], F32)
    for k, total in enumerate(totals):
        scalar = jnp.sum(jnp.sum(total, axis=0, keepdims=True), axis=1, keepdims=True)
        result = jnp.where(row_number == k, scalar, result)
    sums[...] = jnp.broadcast_to(result[None], sums.shape)
    for p in range(cells + 1):
        for d in range(3):
            first[d, p] = image[1 + p][d]
            second[d, p] = twice[p][d]


def krylov_steps(moments):
    mean = moments[1] / moments[0]
    powers = [None, mean]
    for k in range(2, 2 * ITERS):
        powers.append(powers[-1] * mean)
    scaled = [moments[k] / moments[0] / powers[k] if k else 1.0 for k in range(2 * ITERS)]

    def product(left, right, shift):
        return sum(
            left[i] * right[j] * scaled[i + j + shift]
            for i in range(len(left))
            for j in range(len(right))
        )

    solution = [0.0] * ITERS
    residual = [1.0]
    direction = [1.0]
    norm_now = scaled[0]
    work = 0.0
    for iteration in range(ITERS):
        alpha = norm_now / product(direction, direction, 1)
        work = work + alpha * norm_now
        solution = [
            solution[i] + (alpha * direction[i] if i < len(direction) else 0.0)
            for i in range(ITERS)
        ]
        if iteration + 1 < ITERS:
            image = [0.0] + direction
            residual = [
                (residual[i] if i < len(residual) else 0.0) - alpha * image[i]
                for i in range(len(image))
            ]
            norm_next = product(residual, residual, 0)
            beta = norm_next / norm_now
            direction = [
                residual[i] + (beta * direction[i] if i < len(direction) else 0.0)
                for i in range(len(residual))
            ]
            norm_now = norm_next
    factors = [solution[i] / powers[i + 1] for i in range(ITERS)]
    return factors, work * moments[0] / mean


def energy_kernel(elements, parts, loads, first, second, density, solution, slope):
    totals = jnp.sum(parts[...], axis=0)
    rows_of = [totals[k : k + 1, :] for k in range(2 * ITERS + 1)]
    factors, compliance = krylov_steps(rows_of[: 2 * ITERS])
    volume = rows_of[2 * ITERS]
    constant = 2.0 * penalty * (volume / elements - vol_target) / elements
    scale = -3.0 * (1.0 - emin) / compliance
    wide = [jnp.concatenate([value, value], axis=1) for value in factors + [scale, constant]]
    cells, rows, _ = density.shape
    modes = []
    for p in range(cells + 1):
        plane = []
        for d in range(3):
            value = wide[0] * loads[d, 2 + p] + wide[1] * first[d, p] + wide[2] * second[d, p]
            if p < cells:
                solution[d, p] = value[:rows]
            plane.append(plane_modes(value, rows))
        modes.append(plane)
    for e in range(cells):
        energy = energy_of(element_modes(modes[e], modes[e + 1]))
        held = density[e]
        slope[e] = (wide[3] * held * held * energy + wide[4]) * held * (1.0 - held)


def gated(half):
    up = 1.0 + jnp.tanh(half)
    value = half * up
    return value, up + value * (2.0 - up)


def features_of(x_cos, x_sin, z_cos, z_sin, column):
    cos = x_cos[0, :, column : column + 1]
    sin = x_sin[0, :, column : column + 1]
    return jnp.concatenate([z_cos * cos - z_sin * sin, z_sin * cos + z_cos * sin], 0).astype(BF)


def forward_kernel(
    x_cos, x_sin, z_cos, z_sin, w_in, w_mid, w_out, w_row,
    density, stiff, hidden_in, slope_mid, slope_in, hidden_mid, *, width,
):
    columns, size = density.shape[1:]
    step = pl.program_id(0)
    for g in range(columns // width):
        picked = [
            features_of(x_cos, x_sin, z_cos[...], z_sin[...], g * width + q) for q in range(width)
        ]
        features = jnp.concatenate(picked, 1)
        span = width * size
        place = pl.ds(pl.multiple_of(step * (columns * size) + g * span, span), span)
        value, slope = gated(jnp.dot(w_in[...], features, preferred_element_type=F32))
        value = value.astype(BF)
        hidden_in[:, place] = value
        slope_in[:, place] = slope.astype(BF)
        value, slope = gated(jnp.dot(w_mid[...], value, preferred_element_type=F32))
        value = value.astype(BF)
        hidden_mid[:, place] = value
        slope_mid[:, place] = (w_out[...] * slope).astype(BF)
        logits = jnp.dot(w_row[...], value, preferred_element_type=F32)[:1]
        held = 0.5 * jnp.tanh(0.5 * logits) + 0.5
        for q in range(width):
            part = held[:, q * size : (q + 1) * size]
            density[0, g * width + q : g * width + q + 1, :] = part
            stiff[0, g * width + q : g * width + q + 1, :] = emin + (1.0 - emin) * (
                part * part * part
            )


def back_kernel(w_mid, slope_mid, slope_in, back, *, span):
    place = pl.ds(pl.multiple_of(pl.program_id(0) * span, span), span)
    product = jnp.dot(w_mid[...], slope_mid[:, place], preferred_element_type=F32)
    back[:, place] = (product * slope_in[:, place].astype(F32)).astype(BF)


def gradient_kernel(
    slope, x_cos, x_sin, z_cos, z_sin, hidden_in, slope_mid, back, hidden_mid,
    grads, grad_out, running, *, steps,
):
    step = pl.program_id(0)

    @pl.when(step == 0)
    def _():
        grads[...] = jnp.zeros_like(grads)
        running[...] = jnp.zeros_like(running)

    columns, size = slope.shape[1:]
    span = columns * size
    picked = []
    for q in range(columns):
        features = features_of(x_cos, x_sin, z_cos[...], z_sin[...], q).astype(F32)
        picked.append((features * slope[0, q : q + 1, :]).astype(BF))
    features = jnp.concatenate(picked, 1)
    place = pl.ds(pl.multiple_of(step * span, span), span)
    row = jnp.concatenate([slope[0, q : q + 1, :] for q in range(columns)], 1)
    hidden = (hidden_in[:, place].astype(F32) * row).astype(BF)
    mid = lax.dot_general(hidden, slope_mid[:, place], LAST, preferred_element_type=F32)
    first = lax.dot_general(features, back[:, place], LAST, preferred_element_type=F32)
    height = mid.shape[0]
    for k in range(grads.shape[0]):
        grads[k, :height, :] += mid[:, k * 128 : (k + 1) * 128]
        grads[k, height:, :] += first[:, k * 128 : (k + 1) * 128]
    product = hidden_mid[:, place].astype(F32) * row
    total = product[:, :128]
    for k in range(1, span // 128):
        total = total + product[:, k * 128 : (k + 1) * 128]
    running[...] += total

    @pl.when(step == steps - 1)
    def _():
        line = jnp.sum(running[...].T, axis=0, keepdims=True)
        for k in range(grad_out.shape[0]):
            grad_out[k : k + 1, :] = line[:, k * 128 : (k + 1) * 128]


WHOLE = pl.BlockSpec(memory_space=pltpu.VMEM)


def fixed(shape):
    return pl.BlockSpec(shape, lambda i: (0,) * len(shape))


def in_vmem(array):
    return pltpu.with_memory_space_constraint(array, pltpu.VMEM)


def params(mebibytes):
    return pltpu.CompilerParams(vmem_limit_bytes=mebibytes << 20)


def shifted(block, axis, distance):
    size = lax.axis_size(axis)
    route = [(i, (i + distance) % size) for i in range(size)]
    got = lax.ppermute(block, axis, route)
    at_end = lax.axis_index(axis) == (0 if distance == 1 else size - 1)
    return jnp.where(at_end, 0.0, got)


def with_rows(block, before, after):
    dim = block.ndim - 2
    size = block.shape[dim]
    behind = shifted(lax.slice_in_dim(block, size - before, size, axis=dim), "z", 1)
    ahead = shifted(lax.slice_in_dim(block, 0, after, axis=dim), "z", -1)
    space = block.shape[:dim] + (ROWS - size - before - after,) + block.shape[dim + 1 :]
    return jnp.concatenate([block, ahead, jnp.zeros(space, F32), behind], axis=dim)


def with_planes(block, before, after):
    dim = block.ndim - 3
    size = block.shape[dim]
    behind = shifted(lax.slice_in_dim(block, size - before, size, axis=dim), SLAB, 1)
    ahead = shifted(lax.slice_in_dim(block, 0, after, axis=dim), SLAB, -1)
    return jnp.concatenate([behind, block, ahead], axis=dim)


def summed_grads(grads, grad_out):
    chips = lax.axis_size(CHIPS)
    core = lax.axis_index("c")
    swap = [(0, 1), (1, 0)]
    halves = grads.reshape(2, chips, -1, 128)
    height = halves.shape[2]
    mine = lax.dynamic_index_in_dim(halves, core, 0, keepdims=False)
    other = lax.dynamic_index_in_dim(halves, 1 - core, 0, keepdims=False)
    half = mine + lax.ppermute(other, "c", swap)
    share = jnp.sum(lax.all_to_all(half, CHIPS, 0, 0), axis=0)
    share = jnp.concatenate([share, grad_out], axis=0)
    half = lax.all_to_all(jnp.broadcast_to(share[None], (chips,) + share.shape), CHIPS, 0, 0)
    out_half = jnp.sum(half[:, height:], axis=0)
    half = half[:, :height]
    away = lax.ppermute(half, "c", swap)
    out_away = lax.ppermute(out_half, "c", swap)
    first = jnp.where(core == 0, half, away)
    second = jnp.where(core == 0, away, half)
    return jnp.stack([first, second]).reshape(grads.shape), out_half + out_away


def on_device(load_values, load_mask, fixed_mask, frequencies, weight_in, weight_mid, weight_out):
    cells_x, cells_y, cells_z = fixed_mask.shape
    grid_cells = (cells_x * lax.axis_size(SLAB), cells_y * lax.axis_size("z"), cells_z)
    elements_total = grid_cells[0] * grid_cells[1] * grid_cells[2]
    x_first = lax.axis_index(SLAB) * cells_x
    y_first = lax.axis_index("z") * cells_y
    hidden = weight_mid.shape[0]
    rows = cells_x * cells_y * cells_z

    free = (1 - fixed_mask).astype(F32)[None]
    force = free * load_mask.astype(F32)[None] * load_values
    loads = with_planes(with_rows(jnp.concatenate([force, free], 0), 2, 3), 2, 3)

    def centre(first, count, total):
        return ((first + jnp.arange(count, dtype=jnp.int32)).astype(F32) + 0.5) / total

    x_phase = two_pi * (
        centre(x_first, cells_x, grid_cells[0])[:, None, None] * frequencies[0][None, :, None]
        + centre(y_first, cells_y, grid_cells[1])[None, None, :] * frequencies[1][None, :, None]
    )
    z_phase = two_pi * frequencies[2][:, None] * centre(0, cells_z, grid_cells[2])[None, :]
    tables = (jnp.cos(x_phase), jnp.sin(x_phase), jnp.cos(z_phase), jnp.sin(z_phase))
    half = jnp.asarray(0.5, BF)
    out_row = jnp.pad(weight_out[None], ((0, 15), (0, 0)))

    table_specs = [pl.BlockSpec((1,) + x_phase.shape[1:], lambda i: (i, 0, 0))] * 2
    table_specs += [fixed(z_phase.shape)] * 2
    plane_spec = pl.BlockSpec((1, cells_y, cells_z), lambda i: (i, 0, 0))
    plane_shape = jax.ShapeDtypeStruct((cells_x, cells_y, cells_z), F32)
    kept = pltpu.VMEM((hidden, rows), BF)
    density, stiff, hidden_in, slope_mid, slope_in, hidden_mid = pl.pallas_call(
        functools.partial(forward_kernel, width=4),
        name="forward",
        grid=(cells_x,),
        in_specs=table_specs
        + [fixed((hidden, weight_in.shape[0])), fixed((hidden, hidden))]
        + [fixed((hidden, 1)), fixed((16, hidden))],
        out_specs=[plane_spec, plane_spec, WHOLE, WHOLE, WHOLE, WHOLE],
        out_shape=[plane_shape, plane_shape, kept, kept, kept, kept],
        compiler_params=params(20),
    )(
        *tables,
        weight_in.T * half,
        weight_mid.T * half,
        0.5 * weight_out.astype(F32)[:, None],
        out_row,
    )
    stiff = with_planes(with_rows(stiff, 2, 2), 2, 2)

    span = 1024
    back = pl.pallas_call(
        functools.partial(back_kernel, span=span),
        name="back",
        grid=(rows // span,),
        in_specs=[fixed((hidden, hidden)), WHOLE, WHOLE],
        out_specs=WHOLE,
        out_shape=kept,
        input_output_aliases={2: 0},
        compiler_params=params(20),
        cost_estimate=pl.CostEstimate(
            flops=2 * hidden * hidden * rows, bytes_accessed=6 * hidden * rows, transcendentals=0
        ),
    )(weight_mid * half, in_vmem(slope_mid), in_vmem(slope_in))

    devices = lax.axis_size(ALL)
    held = jax.ShapeDtypeStruct((3, cells_x + 1, ROWS, cells_z), F32)
    first, second, sums = pl.pallas_call(
        krylov_kernel,
        name="krylov",
        out_shape=[held, held, jax.ShapeDtypeStruct((devices, 8, 128), F32)],
        compiler_params=params(20),
    )(loads, stiff, density)
    parts = lax.all_to_all(sums, ALL, 0, 0)
    solution, slope = pl.pallas_call(
        functools.partial(energy_kernel, elements_total),
        name="energy",
        out_shape=[jax.ShapeDtypeStruct((3, cells_x, cells_y, cells_z), F32), plane_shape],
        compiler_params=params(20),
    )(parts, loads, first, second, density)

    height = hidden + weight_in.shape[0]
    groups = hidden // 128
    grads, grad_out = pl.pallas_call(
        functools.partial(gradient_kernel, steps=cells_x),
        name="gradients",
        grid=(cells_x,),
        in_specs=[plane_spec] + table_specs + [WHOLE] * 4,
        out_specs=[fixed((groups, height, 128)), fixed((groups, 128))],
        out_shape=[
            jax.ShapeDtypeStruct((groups, height, 128), F32),
            jax.ShapeDtypeStruct((groups, 128), F32),
        ],
        scratch_shapes=[pltpu.VMEM((hidden, 128), F32)],
        compiler_params=params(20),
    )(slope, *tables, *[in_vmem(a) for a in (hidden_in, slope_mid, back, hidden_mid)])
    grads, grad_out = summed_grads(grads, grad_out)
    grads = grads.transpose(1, 0, 2).reshape(height, hidden)
    return (solution, density, grads[hidden:], grads[:hidden], grad_out.reshape(hidden))


def solution(mesh):
    slab, sub = mesh.devices.shape
    fine = Mesh(mesh.devices.reshape(4, 4, slab // 16, sub), ALL)
    field = P(SLAB, "z", None)
    vector = P(None, SLAB, "z", None)
    return jax.shard_map(
        on_device,
        mesh=fine,
        in_specs=(vector, field, field, P(), P(), P(), P()),
        out_specs=(vector, field, P(), P(), P()),
        check_vma=False,
    )
```

```python
import functools
import itertools
import math

import jax
import jax.numpy as jnp
import numpy as np
from jax import lax
from jax.experimental import pallas as pl
from jax.experimental.pallas import tpu as pltpu
from jax.sharding import Mesh
from jax.sharding import PartitionSpec as P

ITERS = 3
SLAB = ("x", "y", "c")
CHIPS = ("x", "y", "z")
ALL = ("x", "y", "c", "z")
BF = jnp.bfloat16
F32 = jnp.float32

two_pi = 2.0 * math.pi
emin = 0.001
penalty = 4.0
vol_target = 0.3
ROWS = 16
corner_list = list(itertools.product((0, 1), repeat=3))
LAST = (((1,), (1,)), ((), ()))


def hex_stiffness():
    poisson = 0.3
    lame_first = poisson / ((1.0 + poisson) * (1.0 - 2.0 * poisson))
    lame_second = 0.5 / (1.0 + poisson)
    elastic = np.zeros((6, 6))
    elastic[:3, :3] = lame_first
    for axis_number in range(3):
        elastic[axis_number, axis_number] += 2.0 * lame_second
        elastic[axis_number + 3, axis_number + 3] = lame_second
    gauss_points = [0.5 - 0.5 / math.sqrt(3.0), 0.5 + 0.5 / math.sqrt(3.0)]
    matrix = np.zeros((24, 24))
    for location in itertools.product(gauss_points, repeat=3):
        strain = np.zeros((6, 24))
        for corner_number, corner in enumerate(corner_list):
            factors = [
                location[axis] if corner[axis] == 1 else 1.0 - location[axis] for axis in range(3)
            ]
            slopes = [1.0 if corner[axis] == 1 else -1.0 for axis in range(3)]
            derivative = [
                slopes[0] * factors[1] * factors[2],
                factors[0] * slopes[1] * factors[2],
                factors[0] * factors[1] * slopes[2],
            ]
            column = 3 * corner_number
            for axis in range(3):
                strain[axis, column + axis] = derivative[axis]
            strain[3, column + 1] = derivative[2]
            strain[3, column + 2] = derivative[1]
            strain[4, column + 0] = derivative[2]
            strain[4, column + 2] = derivative[0]
            strain[5, column + 0] = derivative[1]
            strain[5, column + 1] = derivative[0]
        matrix += strain.T @ elastic @ strain / 8.0
    return matrix


def modal_stiffness():
    table = hex_stiffness()
    change = np.zeros((24, 24))
    for row, wave in enumerate(corner_list):
        for column, corner in enumerate(corner_list):
            sign = np.prod([1.0 if c == 1 else -1.0 for w, c in zip(wave, corner) if w == 1])
            for d in range(3):
                change[3 * row + d, 3 * column + d] = sign
    modal = change @ table @ change.T / 64.0
    blocks = []
    for parity in corner_list:
        waves = [tuple(parity[a] ^ (a == d) for a in range(3)) for d in range(3)]
        index = [3 * corner_list.index(wave) + d for d, wave in enumerate(waves)]
        block = modal[np.ix_(index, index)]
        blocks.append((waves, np.where(np.abs(block) < 1e-9, 0.0, block)))
    return blocks


BLOCKS = modal_stiffness()


def lane_mask(shape, lane):
    return lax.broadcasted_iota(jnp.int32, shape, len(shape) - 1) == lane


def plane_modes(plane, rows):
    size = plane.shape[-1]
    ahead = jnp.where(lane_mask(plane.shape, size - 1), 0.0, pltpu.roll(plane, size - 1, 1))
    modes = {}
    for wave_z, part in ((0, plane + ahead), (1, ahead - plane)):
        following = pltpu.roll(part, ROWS - 1, 0)
        modes[0, wave_z] = (part + following)[:rows]
        modes[1, wave_z] = (following - part)[:rows]
    return modes


def element_modes(lower, upper):
    found = []
    for low, high in zip(lower, upper):
        modes = {}
        for key in low:
            modes[(0,) + key] = low[key] + high[key]
            modes[(1,) + key] = high[key] - low[key]
        found.append(modes)
    return found


def modal_forces(modes):
    for waves, block in BLOCKS:
        values = [modes[d][waves[d]] for d in range(3)]
        for d in range(3):
            total = None
            for other in range(3):
                if block[d, other] != 0.0:
                    term = np.float32(block[d, other]) * values[other]
                    total = term if total is None else total + term
            if total is not None:
                yield d, waves[d], values[d], total


def energy_of(modes):
    total = None
    for _, _, value, force in modal_forces(modes):
        total = value * force if total is None else total + value * force
    return total


def node_plane(gathered):
    parts = []
    for wave_z in (0, 1):
        even, odd = gathered[0, wave_z], gathered[1, wave_z]
        parts.append((even - odd) + pltpu.roll(even + odd, 1, 0))
    behind = pltpu.roll(parts[0] + parts[1], 1, 1)
    return (parts[0] - parts[1]) + jnp.where(lane_mask(behind.shape, 0), 0.0, behind)


def operator_planes(planes, stiff, free):
    modes = [[plane_modes(component, ROWS) for component in plane] for plane in planes]
    gathered = [[{} for _ in range(3)] for _ in planes]
    for e in range(len(planes) - 1):
        forces = [{} for _ in range(3)]
        for d, wave, _, force in modal_forces(element_modes(modes[e], modes[e + 1])):
            forces[d][wave] = force * stiff[e]
        for d in range(3):
            for key in itertools.product((0, 1), repeat=2):
                even, odd = forces[d].get((0,) + key), forces[d].get((1,) + key)
                for node, sign in ((e, -1), (e + 1, 1)):
                    if even is None:
                        term = odd if sign == 1 else -odd
                    else:
                        term = even + odd if sign == 1 else even - odd
                    held = gathered[node][d]
                    held[key] = term if key not in held else held[key] + term
    return [
        [node_plane(gathered[n][d]) * free[n - 1] for d in range(3)]
        for n in range(1, len(planes) - 1)
    ]


def kept_if(flag):
    return jnp.where(flag == 0, 1.0, 0.0)


def krylov_kernel(place, loads, loads_behind, loads_ahead, stiff, stiff_behind, stiff_ahead, density,
                  first, second, sums):
    cells = loads.shape[1]
    low, high = kept_if(place[SLAB_FIRST]), kept_if(place[SLAB_LAST])

    def load_planes(d):
        planes = [loads_behind[d, p] * low for p in range(2)]
        planes += [loads[d, p] for p in range(cells)]
        return planes + [loads_ahead[d, p] * high for p in range(3)]

    stiff_planes = [stiff_behind[p] * low for p in range(2)]
    stiff_planes += [stiff[p] for p in range(cells)]
    stiff_planes += [stiff_ahead[p] * high for p in range(2)]
    force = [list(plane) for plane in zip(*[load_planes(d) for d in range(3)])]
    free = load_planes(3)
    image = operator_planes(force, stiff_planes, free[1:-1])
    twice = operator_planes(image, stiff_planes[1:-1], free[2:-2])
    own = (force[2 : 2 + cells], image[1 : 1 + cells], twice[:cells])
    rows = density.shape[1]

    def dot(left, right):
        total = None
        for p in range(cells):
            for d in range(3):
                term = left[p][d][:rows] * right[p][d][:rows]
                total = term if total is None else total + term
        return total

    totals = [dot(own[k // 2], own[(k + 1) // 2]) for k in range(2 * ITERS - 1)]
    modes = [[plane_modes(component, rows) for component in plane] for plane in twice]
    last = None
    volume = None
    for e in range(cells):
        term = stiff_planes[2 + e][:rows] * energy_of(element_modes(modes[e], modes[e + 1]))
        last = term if last is None else last + term
        volume = density[e] if volume is None else volume + density[e]
    totals += [last, volume]
    row_number = lax.broadcasted_iota(jnp.int32, sums.shape, 0)
    result = jnp.zeros(sums.shape, F32)
    for k, total in enumerate(totals):
        scalar = jnp.sum(jnp.sum(total, axis=0, keepdims=True), axis=1, keepdims=True)
        result = jnp.where(row_number == k, scalar, result)
    sums[...] = result
    for p in range(cells + 1):
        for d in range(3):
            first[d, p] = image[1 + p][d]
            second[d, p] = twice[p][d]


def krylov_steps(moments):
    mean = moments[1] / moments[0]
    powers = [None, mean]
    for k in range(2, 2 * ITERS):
        powers.append(powers[-1] * mean)
    scaled = [moments[k] / moments[0] / powers[k] if k else 1.0 for k in range(2 * ITERS)]

    def product(left, right, shift):
        return sum(
            left[i] * right[j] * scaled[i + j + shift]
            for i in range(len(left))
            for j in range(len(right))
        )

    solution = [0.0] * ITERS
    residual = [1.0]
    direction = [1.0]
    norm_now = scaled[0]
    work = 0.0
    for iteration in range(ITERS):
        alpha = norm_now / product(direction, direction, 1)
        work = work + alpha * norm_now
        solution = [
            solution[i] + (alpha * direction[i] if i < len(direction) else 0.0)
            for i in range(ITERS)
        ]
        if iteration + 1 < ITERS:
            image = [0.0] + direction
            residual = [
                (residual[i] if i < len(residual) else 0.0) - alpha * image[i]
                for i in range(len(image))
            ]
            norm_next = product(residual, residual, 0)
            beta = norm_next / norm_now
            direction = [
                residual[i] + (beta * direction[i] if i < len(direction) else 0.0)
                for i in range(len(residual))
            ]
            norm_now = norm_next
    factors = [solution[i] / powers[i + 1] for i in range(ITERS)]
    return factors, work * moments[0] / mean


def energy_kernel(elements, place, sums, loads, loads_ahead, first, second, density, solution, slope):
    rows_of = [sums[k : k + 1, :] for k in range(2 * ITERS + 1)]
    factors, compliance = krylov_steps(rows_of[: 2 * ITERS])
    volume = rows_of[2 * ITERS]
    constant = 2.0 * penalty * (volume / elements - vol_target) / elements
    scale = -3.0 * (1.0 - emin) / compliance
    wide = [jnp.concatenate([value, value], axis=1) for value in factors + [scale, constant]]
    high = kept_if(place[SLAB_LAST])
    cells, rows, _ = density.shape
    modes = []
    for p in range(cells + 1):
        plane = []
        for d in range(3):
            load = loads[d, p] if p < cells else loads_ahead[d, 0] * high
            value = wide[0] * load + wide[1] * first[d, p] + wide[2] * second[d, p]
            if p < cells:
                solution[d, p] = value[:rows]
            plane.append(plane_modes(value, rows))
        modes.append(plane)
    for e in range(cells):
        energy = energy_of(element_modes(modes[e], modes[e + 1]))
        held = density[e]
        slope[e] = (wide[3] * held * held * energy + wide[4]) * held * (1.0 - held)


def column_of(line):
    size = line.shape[1]
    shape = (size, size)
    same = lax.broadcasted_iota(jnp.int32, shape, 0) == lax.broadcasted_iota(jnp.int32, shape, 1)
    return jnp.sum(jnp.where(same, line, 0.0), axis=1, keepdims=True)


def prepare_kernel(
    grid_cells, place, load_values, load_mask, fixed_mask, frequencies, w_in, w_mid, w_out,
    loads, loads_first, loads_last, x_cos, x_sin, z_cos, z_sin, w_in_t, w_mid_t, w_mid_half,
    w_column, w_row,
):
    cells, rows, size = load_mask.shape
    free = (1 - fixed_mask[...]).astype(F32)
    held = free * load_mask[...].astype(F32)
    for d in range(4):
        field = free if d == 3 else held * load_values[d]
        loads[d] = field
        loads_first[d] = field[:, :3]
        loads_last[d] = field[:, rows - 2 :]
    columns = [column_of(frequencies[k : k + 1, :]) for k in range(3)]
    half = rows // 2
    lanes = 2 * cells * half
    number = lax.broadcasted_iota(jnp.int32, (1, lanes), 1)
    side = number // (cells * half)
    plane = (number // half) % cells
    inner = number % half
    row = jnp.where(side == 1, inner + 2, jnp.where(inner < 2, inner, inner + half))
    x_centre = ((place[X_FIRST] + plane).astype(F32) + 0.5) / grid_cells[0]
    y_centre = ((place[Y_FIRST] + row).astype(F32) + 0.5) / grid_cells[1]
    phase = two_pi * (x_centre * columns[0] + y_centre * columns[1])
    cos, sin = jnp.cos(phase), jnp.sin(phase)
    for k in range(2 * cells):
        x_cos[k] = cos[:, k * half : (k + 1) * half]
        x_sin[k] = sin[:, k * half : (k + 1) * half]
    z_number = lax.broadcasted_iota(jnp.int32, (1, size), 1)
    phase = two_pi * (((z_number.astype(F32) + 0.5) / grid_cells[2]) * columns[2])
    z_cos[...] = jnp.cos(phase)
    z_sin[...] = jnp.sin(phase)
    w_in_t[...] = (0.5 * w_in[...].astype(F32)).T.astype(BF)
    middle = 0.5 * w_mid[...].astype(F32)
    w_mid_half[...] = middle.astype(BF)
    w_mid_t[...] = middle.T.astype(BF)
    line = w_out[...].astype(F32)
    w_column[...] = 0.5 * column_of(line)
    w_row[...] = jnp.broadcast_to(line, w_row.shape).astype(BF)


def with_rows(stop, start, block, ahead, behind):
    space = ROWS - block.shape[0] - ahead.shape[0] - behind.shape[0]
    zeros = jnp.zeros((space, block.shape[1]), F32)
    return jnp.concatenate([block, ahead * stop, zeros, behind * start], axis=0)


def load_rows_kernel(place, loads, ahead, behind, joined, to_before, to_next):
    start, stop = kept_if(place[Z_FIRST]), kept_if(place[Z_LAST])
    cells = loads.shape[1]
    for d in range(loads.shape[0]):
        for p in range(cells):
            block = with_rows(stop, start, loads[d, p], ahead[d, p], behind[d, p])
            joined[d, p] = block
            if p < to_before.shape[1]:
                to_before[d, p] = block
            if p >= cells - to_next.shape[1]:
                to_next[d, p - (cells - to_next.shape[1])] = block


def stiff_rows_kernel(place, stiff, ahead, behind, joined, to_before, to_next):
    start, stop = kept_if(place[Z_FIRST]), kept_if(place[Z_LAST])
    cells = stiff.shape[0]
    for p in range(cells):
        block = with_rows(stop, start, stiff[p], ahead[p], behind[p])
        joined[p] = block
        if p < to_before.shape[0]:
            to_before[p] = block
        if p >= cells - to_next.shape[0]:
            to_next[p - (cells - to_next.shape[0])] = block


def gated(half):
    up = 1.0 + jnp.tanh(half)
    value = half * up
    return value, up + value * (2.0 - up)


def features_of(x_cos, x_sin, z_cos, z_sin, column):
    cos = x_cos[0, :, column : column + 1]
    sin = x_sin[0, :, column : column + 1]
    return jnp.concatenate([z_cos * cos - z_sin * sin, z_sin * cos + z_cos * sin], 0).astype(BF)


def forward_columns(tables, weights, kept, spans):
    x_cos, x_sin, z_cos, z_sin = tables
    w_in, w_mid, w_column, w_row = weights
    hidden_in, slope_mid, slope_in, hidden_mid = kept

    def keep(array, value):
        for start, first, count in spans:
            array[:, pl.ds(start, count)] = value[:, first : first + count]

    columns = x_cos.shape[2]
    picked = [features_of(x_cos, x_sin, z_cos[...], z_sin[...], q) for q in range(columns)]
    features = jnp.concatenate(picked, 1)
    value, slope = gated(jnp.dot(w_in[...], features, preferred_element_type=F32))
    value = value.astype(BF)
    keep(hidden_in, value)
    keep(slope_in, slope.astype(BF))
    value, slope = gated(jnp.dot(w_mid[...], value, preferred_element_type=F32))
    value = value.astype(BF)
    keep(hidden_mid, value)
    keep(slope_mid, (w_column[...] * slope).astype(BF))
    logits = jnp.dot(w_row[...], value, preferred_element_type=F32)[:1]
    return 0.5 * jnp.tanh(0.5 * logits) + 0.5


def stiffness_of(density):
    return emin + (1.0 - emin) * (density * density * density)


def outer_kernel(
    x_cos, x_sin, z_cos, z_sin, w_in, w_mid, w_column, w_row,
    density, stiff_first, stiff_last, *kept,
):
    size = density.shape[2]
    start = pl.multiple_of(pl.program_id(0) * (8 * size), 8 * size)
    spans = [(start, 0, 2 * size), (start + 6 * size, 2 * size, 2 * size)]
    tables, weights = (x_cos, x_sin, z_cos, z_sin), (w_in, w_mid, w_column, w_row)
    line = forward_columns(tables, weights, kept, spans)
    for q in range(4):
        part = line[:, q * size : (q + 1) * size]
        density[0, q : q + 1, :] = part
        (stiff_first if q < 2 else stiff_last)[0, q % 2 : q % 2 + 1, :] = stiffness_of(part)


def inner_kernel(
    x_cos, x_sin, z_cos, z_sin, w_in, w_mid, w_column, w_row, outer, *rest,
):
    density, stiff = rest[4:6]
    size = density.shape[2]
    start = pl.multiple_of(pl.program_id(0) * (8 * size), 8 * size)
    tables, weights = (x_cos, x_sin, z_cos, z_sin), (w_in, w_mid, w_column, w_row)
    line = forward_columns(tables, weights, rest[6:], [(start + 2 * size, 0, 4 * size)])
    for r in range(8):
        if 2 <= r < 6:
            part = line[:, (r - 2) * size : (r - 1) * size]
        else:
            q = r if r < 2 else r - 4
            part = outer[0, q : q + 1, :]
        density[0, r : r + 1, :] = part
        stiff[0, r : r + 1, :] = stiffness_of(part)


def back_kernel(w_mid, slope_mid, slope_in, back, *, first, span):
    place = pl.ds(pl.multiple_of(first + pl.program_id(0) * span, span), span)
    product = jnp.dot(w_mid[...], slope_mid[:, place], preferred_element_type=F32)
    back[:, place] = (product * slope_in[:, place].astype(F32)).astype(BF)


def in_three(value):
    high = value.astype(BF)
    rest = value - high.astype(F32)
    middle = rest.astype(BF)
    low = (rest - middle.astype(F32)).astype(BF)
    return jnp.concatenate([high, middle, low, jnp.zeros((13, value.shape[1]), BF)], axis=0)


def gradient_kernel(
    place, slope, x_cos, x_sin, z_cos, z_sin, hidden_in, slope_mid, back, hidden_mid,
    mine, other, grad_out, total, running, *, steps,
):
    step = pl.program_id(0)

    @pl.when(step == 0)
    def _():
        total[...] = jnp.zeros_like(total)
        running[...] = jnp.zeros_like(running)

    rows, size = slope.shape[1:]
    half = rows // 2
    mid = first = out = None
    for number, group in enumerate(((0, 1, 6, 7), (2, 3, 4, 5))):
        lines = [slope[0, r : r + 1, :] for r in group]
        picked = []
        for q in range(half):
            cos, sin = x_cos[number, 0, :, q : q + 1], x_sin[number, 0, :, q : q + 1]
            upper = (z_cos[...] * cos - z_sin[...] * sin) * lines[q]
            lower = (z_sin[...] * cos + z_cos[...] * sin) * lines[q]
            picked.append(jnp.concatenate([upper, lower], 0).astype(BF))
        features = jnp.concatenate(picked, 1)
        line = jnp.concatenate(lines, 1)

        def kept(array):
            pieces, q = [], 0
            while q < half:
                run = 1
                while q + run < half and group[q + run] == group[q] + run:
                    run += 1
                start = pl.multiple_of(step * (rows * size) + group[q] * size, size)
                pieces.append(array[:, pl.ds(start, run * size)])
                q += run
            return pieces[0] if len(pieces) == 1 else jnp.concatenate(pieces, 1)

        hidden = (kept(hidden_in).astype(F32) * line).astype(BF)
        terms = (
            lax.dot_general(hidden, kept(slope_mid), LAST, preferred_element_type=F32),
            lax.dot_general(features, kept(back), LAST, preferred_element_type=F32),
            lax.dot_general(kept(hidden_mid), in_three(line), LAST, preferred_element_type=F32),
        )
        if mid is None:
            mid, first, out = terms
        else:
            mid, first, out = mid + terms[0], first + terms[1], out + terms[2]
    height = mid.shape[0]
    for k in range(total.shape[0]):
        total[k, :height, :] += mid[:, k * 128 : (k + 1) * 128]
        total[k, height:, :] += first[:, k * 128 : (k + 1) * 128]
    running[:, : out.shape[1]] += out

    @pl.when(step == steps - 1)
    def _():
        core = place[CORE]
        for k in range(mine.shape[0]):
            mine[k] = total[2 * core + k]
            other[k] = total[2 * (1 - core) + k]
        line = jnp.sum(running[...].T, axis=0, keepdims=True)
        for k in range(grad_out.shape[0]):
            grad_out[k : k + 1, :] = line[:, k * 128 : (k + 1) * 128]


def finish_kernel(place, half, away, grad_in, grad_mid, grad_out):
    chips = half.shape[0]
    height = half.shape[1] - 2 * grad_out.shape[0]
    middle = grad_mid.shape[0]
    at_first = place[CORE] == 0
    for group in range(4):
        part = pl.ds((group % 2) * (chips // 2), chips // 2)
        own, far = half[part, :height, :], away[part, :height, :]
        picked = jnp.where(at_first, own, far) if group < 2 else jnp.where(at_first, far, own)
        picked = picked.reshape(-1, 128)
        lanes = slice(group * 128, (group + 1) * 128)
        grad_mid[:, lanes] = picked[:middle]
        grad_in[:, lanes] = picked[middle:]
    out = jnp.sum(half[:, height:, :], axis=0) + jnp.sum(away[:, height:, :], axis=0)
    grad_out[...] = out[: grad_out.shape[0]]


VM = pltpu.VMEM
WHOLE = pl.BlockSpec(memory_space=pltpu.VMEM)
SCALARS = pl.BlockSpec(memory_space=pltpu.SMEM)
X_FIRST, Y_FIRST, CORE, SLAB_FIRST, SLAB_LAST, Z_FIRST, Z_LAST = range(7)


def fixed(shape):
    return pl.BlockSpec(shape, lambda i: (0,) * len(shape))


def in_vmem(*arrays):
    return [pltpu.with_memory_space_constraint(array, pltpu.VMEM) for array in arrays]


def params(mebibytes=8):
    return pltpu.CompilerParams(vmem_limit_bytes=mebibytes << 20)


def shaped(*shape, dtype=F32):
    return jax.ShapeDtypeStruct(shape, dtype)


def simple(kernel, name, out_shape, place, *operands):
    return pl.pallas_call(
        kernel,
        name=name,
        in_specs=[SCALARS] + [WHOLE] * len(operands),
        out_specs=[WHOLE] * len(out_shape),
        out_shape=out_shape,
        compiler_params=params(),
    )(place, *operands)


def shifted(block, axis, distance):
    size = lax.axis_size(axis)
    return lax.ppermute(block, axis, [(i, (i + distance) % size) for i in range(size)])


def summed(values):
    values = values + lax.ppermute(values, "c", [(0, 1), (1, 0)])
    for axis in ("z", "y", "x"):
        others = [shifted(values, axis, k) for k in range(1, lax.axis_size(axis))]
        values = values + sum(others)
    return values


def on_device(load_values, load_mask, fixed_mask, frequencies, weight_in, weight_mid, weight_out):
    cells_x, cells_y, cells_z = fixed_mask.shape
    slab, sub = lax.axis_index(SLAB), lax.axis_index("z")
    slabs, subs = lax.axis_size(SLAB), lax.axis_size("z")
    grid_cells = (cells_x * slabs, cells_y * subs, cells_z)
    elements_total = grid_cells[0] * grid_cells[1] * grid_cells[2]
    place = jnp.stack(
        [slab * cells_x, sub * cells_y, lax.axis_index("c")]
        + [(slab == 0) * 1, (slab == slabs - 1) * 1, (sub == 0) * 1, (sub == subs - 1) * 1, slab * 0]
    ).astype(jnp.int32)
    inputs, hidden = weight_in.shape
    rows = cells_x * cells_y * cells_z
    half_rows = cells_y // 2
    field = (cells_x, cells_y, cells_z)
    table = shaped(2 * cells_x, inputs // 2, half_rows)
    (
        loads, loads_first, loads_last, x_cos, x_sin, z_cos, z_sin,
        w_in_t, w_mid_t, w_mid_half, w_column, w_row,
    ) = simple(
        functools.partial(prepare_kernel, grid_cells),
        "prepare",
        [
            shaped(4, *field),
            shaped(4, cells_x, 3, cells_z),
            shaped(4, cells_x, 2, cells_z),
            table,
            table,
            shaped(inputs // 2, cells_z),
            shaped(inputs // 2, cells_z),
            shaped(hidden, inputs, dtype=BF),
            shaped(hidden, hidden, dtype=BF),
            shaped(hidden, hidden, dtype=BF),
            shaped(hidden, 1),
            shaped(16, hidden, dtype=BF),
        ],
        place, load_values, load_mask, fixed_mask, frequencies, weight_in, weight_mid,
        weight_out[None],
    )

    loads_up = shifted(loads_first, "z", -1)
    loads_down = shifted(loads_last, "z", 1)
    weights = (w_in_t, w_mid_t, w_column, w_row)
    weight_specs = [fixed(array.shape) for array in weights]
    x_spec = (1, inputs // 2, half_rows)
    z_specs = [fixed(z_cos.shape)] * 2
    kept = [VM((hidden, rows), BF)] * 4

    def plane_spec(count):
        return pl.BlockSpec((1, count, cells_z), lambda i: (i, 0, 0))

    cost = pl.CostEstimate(
        flops=(inputs + hidden) * hidden * rows,
        bytes_accessed=4 * hidden * rows,
        transcendentals=hidden * rows,
    )
    outer, stiff_first, stiff_last, *stored = pl.pallas_call(
        outer_kernel,
        name="outer",
        grid=(cells_x,),
        in_specs=[pl.BlockSpec(x_spec, lambda i: (i, 0, 0))] * 2 + z_specs + weight_specs,
        out_specs=[plane_spec(half_rows), plane_spec(2), plane_spec(2)] + [WHOLE] * 4,
        out_shape=[
            shaped(cells_x, half_rows, cells_z),
            shaped(cells_x, 2, cells_z),
            shaped(cells_x, 2, cells_z),
        ]
        + kept,
        compiler_params=params(12),
        cost_estimate=cost,
    )(x_cos, x_sin, z_cos, z_sin, *weights)
    loads_16, loads_before, loads_next = simple(
        load_rows_kernel,
        "load_rows",
        [
            shaped(4, cells_x, ROWS, cells_z),
            shaped(4, 3, ROWS, cells_z),
            shaped(4, 2, ROWS, cells_z),
        ],
        place, loads, loads_up, loads_down,
    )
    loads_ahead = shifted(loads_before, SLAB, -1)
    loads_behind = shifted(loads_next, SLAB, 1)
    stiff_up = shifted(stiff_first, "z", -1)
    stiff_down = shifted(stiff_last, "z", 1)
    density, stiff, *stored = pl.pallas_call(
        inner_kernel,
        name="inner",
        grid=(cells_x,),
        in_specs=[pl.BlockSpec(x_spec, lambda i: (cells_x + i, 0, 0))] * 2
        + z_specs
        + weight_specs
        + [plane_spec(half_rows)]
        + [WHOLE] * 4,
        out_specs=[plane_spec(cells_y)] * 2 + [WHOLE] * 4,
        out_shape=[shaped(*field)] * 2 + kept,
        input_output_aliases={9 + k: 2 + k for k in range(4)},
        compiler_params=params(12),
        cost_estimate=cost,
    )(x_cos, x_sin, z_cos, z_sin, *weights, outer, *in_vmem(*stored))
    hidden_in, slope_mid, slope_in, hidden_mid = stored
    stiff_16, stiff_before, stiff_next = simple(
        stiff_rows_kernel,
        "stiff_rows",
        [shaped(cells_x, ROWS, cells_z), shaped(2, ROWS, cells_z), shaped(2, ROWS, cells_z)],
        place, stiff, stiff_up, stiff_down,
    )
    stiff_ahead = shifted(stiff_before, SLAB, -1)
    stiff_behind = shifted(stiff_next, SLAB, 1)

    span = 1024
    back = slope_in
    parts = 2
    for part in range(parts):
        back = pl.pallas_call(
            functools.partial(back_kernel, first=part * (rows // parts), span=span),
            name=f"back_{part}",
            grid=(rows // parts // span,),
            in_specs=[fixed((hidden, hidden)), WHOLE, WHOLE],
            out_specs=WHOLE,
            out_shape=kept[0],
            input_output_aliases={2: 0},
            compiler_params=params(),
            cost_estimate=pl.CostEstimate(
                flops=2 * hidden * hidden * rows // parts,
                bytes_accessed=6 * hidden * rows // parts,
                transcendentals=0,
            ),
        )(w_mid_half, *in_vmem(slope_mid, back))

    held = shaped(3, cells_x + 1, ROWS, cells_z)
    first, second, sums = simple(
        krylov_kernel,
        "krylov",
        [held, held, shaped(8, 128)],
        place, loads_16, loads_behind, loads_ahead, stiff_16, stiff_behind, stiff_ahead, density,
    )
    solution, slope = simple(
        functools.partial(energy_kernel, elements_total),
        "energy",
        [shaped(3, *field), shaped(*field)],
        place, summed(sums), loads_16, loads_ahead, first, second, density,
    )

    height = hidden + inputs
    groups = hidden // 128
    pair = pl.BlockSpec((2, 1) + x_spec[1:], lambda i: (0, i, 0, 0))
    tables = [array.reshape((2, cells_x) + x_spec[1:]) for array in (x_cos, x_sin)]
    mine, other, grad_out = pl.pallas_call(
        functools.partial(gradient_kernel, steps=cells_x),
        name="gradients",
        grid=(cells_x,),
        in_specs=[SCALARS, plane_spec(cells_y), pair, pair] + z_specs + [WHOLE] * 4,
        out_specs=[fixed((groups // 2, height, 128))] * 2 + [fixed((groups, 128))],
        out_shape=[shaped(groups // 2, height, 128)] * 2 + [shaped(groups, 128)],
        scratch_shapes=[VM((groups, height, 128), F32), VM((hidden, 128), F32)],
        compiler_params=params(20),
    )(place, slope, *tables, z_cos, z_sin, *in_vmem(hidden_in, slope_mid, back, hidden_mid))

    chips = lax.axis_size(CHIPS)
    swap = [(0, 1), (1, 0)]
    half = (mine + lax.ppermute(other, "c", swap)).reshape(chips, -1, 128)
    share = jnp.sum(lax.all_to_all(half, CHIPS, 0, 0), axis=0)
    share = jnp.concatenate([share, grad_out, jnp.zeros_like(grad_out)], axis=0)
    half = lax.all_to_all(jnp.broadcast_to(share[None], (chips,) + share.shape), CHIPS, 0, 0)
    away = lax.ppermute(half, "c", swap)
    grad_in, grad_mid, grad_out = simple(
        finish_kernel,
        "finish",
        [shaped(inputs, hidden), shaped(hidden, hidden), shaped(groups, 128)],
        place, half, away,
    )
    return solution, density, grad_in, grad_mid, grad_out.reshape(hidden)


def solution(mesh):
    slab, sub = mesh.devices.shape
    fine = Mesh(mesh.devices.reshape(4, 4, slab // 16, sub), ALL)
    field = P(SLAB, "z", None)
    vector = P(None, SLAB, "z", None)
    return jax.shard_map(
        on_device,
        mesh=fine,
        in_specs=(vector, field, field, P(), P(), P(), P()),
        out_specs=(vector, field, P(), P(), P()),
        check_vma=False,
    )
```

```python
import functools
import itertools
import math

import jax
import jax.numpy as jnp
import numpy as np
from jax import lax
from jax.experimental import pallas as pl
from jax.experimental.pallas import tpu as pltpu
from jax.sharding import Mesh
from jax.sharding import PartitionSpec as P

ITERS = 3
SLAB = ("x", "y", "c")
CHIPS = ("x", "y", "z")
ALL = ("x", "y", "c", "z")
BF = jnp.bfloat16
F32 = jnp.float32

two_pi = 2.0 * math.pi
emin = 0.001
penalty = 4.0
vol_target = 0.3
ROWS = 16
corner_list = list(itertools.product((0, 1), repeat=3))
LAST = (((1,), (1,)), ((), ()))


def hex_stiffness():
    poisson = 0.3
    lame_first = poisson / ((1.0 + poisson) * (1.0 - 2.0 * poisson))
    lame_second = 0.5 / (1.0 + poisson)
    elastic = np.zeros((6, 6))
    elastic[:3, :3] = lame_first
    for axis_number in range(3):
        elastic[axis_number, axis_number] += 2.0 * lame_second
        elastic[axis_number + 3, axis_number + 3] = lame_second
    gauss_points = [0.5 - 0.5 / math.sqrt(3.0), 0.5 + 0.5 / math.sqrt(3.0)]
    matrix = np.zeros((24, 24))
    for location in itertools.product(gauss_points, repeat=3):
        strain = np.zeros((6, 24))
        for corner_number, corner in enumerate(corner_list):
            factors = [
                location[axis] if corner[axis] == 1 else 1.0 - location[axis] for axis in range(3)
            ]
            slopes = [1.0 if corner[axis] == 1 else -1.0 for axis in range(3)]
            derivative = [
                slopes[0] * factors[1] * factors[2],
                factors[0] * slopes[1] * factors[2],
                factors[0] * factors[1] * slopes[2],
            ]
            column = 3 * corner_number
            for axis in range(3):
                strain[axis, column + axis] = derivative[axis]
            strain[3, column + 1] = derivative[2]
            strain[3, column + 2] = derivative[1]
            strain[4, column + 0] = derivative[2]
            strain[4, column + 2] = derivative[0]
            strain[5, column + 0] = derivative[1]
            strain[5, column + 1] = derivative[0]
        matrix += strain.T @ elastic @ strain / 8.0
    return matrix


def modal_stiffness():
    table = hex_stiffness()
    change = np.zeros((24, 24))
    for row, wave in enumerate(corner_list):
        for column, corner in enumerate(corner_list):
            sign = np.prod([1.0 if c == 1 else -1.0 for w, c in zip(wave, corner) if w == 1])
            for d in range(3):
                change[3 * row + d, 3 * column + d] = sign
    modal = change @ table @ change.T / 64.0
    blocks = []
    for parity in corner_list:
        waves = [tuple(parity[a] ^ (a == d) for a in range(3)) for d in range(3)]
        index = [3 * corner_list.index(wave) + d for d, wave in enumerate(waves)]
        block = modal[np.ix_(index, index)]
        blocks.append((waves, np.where(np.abs(block) < 1e-9, 0.0, block)))
    return blocks


BLOCKS = modal_stiffness()


def lane_mask(shape, lane):
    return lax.broadcasted_iota(jnp.int32, shape, len(shape) - 1) == lane


def plane_modes(plane, rows):
    size = plane.shape[-1]
    ahead = jnp.where(lane_mask(plane.shape, size - 1), 0.0, pltpu.roll(plane, size - 1, 1))
    modes = {}
    for wave_z, part in ((0, plane + ahead), (1, ahead - plane)):
        following = pltpu.roll(part, ROWS - 1, 0)
        modes[0, wave_z] = (part + following)[:rows]
        modes[1, wave_z] = (following - part)[:rows]
    return modes


def element_modes(lower, upper):
    found = []
    for low, high in zip(lower, upper):
        modes = {}
        for key in low:
            modes[(0,) + key] = low[key] + high[key]
            modes[(1,) + key] = high[key] - low[key]
        found.append(modes)
    return found


def modal_forces(modes):
    for waves, block in BLOCKS:
        values = [modes[d][waves[d]] for d in range(3)]
        for d in range(3):
            total = None
            for other in range(3):
                if block[d, other] != 0.0:
                    term = np.float32(block[d, other]) * values[other]
                    total = term if total is None else total + term
            if total is not None:
                yield d, waves[d], values[d], total


def energy_of(modes):
    total = None
    for _, _, value, force in modal_forces(modes):
        total = value * force if total is None else total + value * force
    return total


def node_plane(gathered):
    parts = []
    for wave_z in (0, 1):
        even, odd = gathered[0, wave_z], gathered[1, wave_z]
        parts.append((even - odd) + pltpu.roll(even + odd, 1, 0))
    behind = pltpu.roll(parts[0] + parts[1], 1, 1)
    return (parts[0] - parts[1]) + jnp.where(lane_mask(behind.shape, 0), 0.0, behind)


def operator_planes(planes, stiff, free):
    modes = [[plane_modes(component, ROWS) for component in plane] for plane in planes]
    gathered = [[{} for _ in range(3)] for _ in planes]
    for e in range(len(planes) - 1):
        forces = [{} for _ in range(3)]
        for d, wave, _, force in modal_forces(element_modes(modes[e], modes[e + 1])):
            forces[d][wave] = force * stiff[e]
        for d in range(3):
            for key in itertools.product((0, 1), repeat=2):
                even, odd = forces[d].get((0,) + key), forces[d].get((1,) + key)
                for node, sign in ((e, -1), (e + 1, 1)):
                    if even is None:
                        term = odd if sign == 1 else -odd
                    else:
                        term = even + odd if sign == 1 else even - odd
                    held = gathered[node][d]
                    held[key] = term if key not in held else held[key] + term
    return [
        [node_plane(gathered[n][d]) * free[n - 1] for d in range(3)]
        for n in range(1, len(planes) - 1)
    ]


def kept_if(flag):
    return jnp.where(flag == 0, 1.0, 0.0)


def with_rows(place, block, ahead, behind):
    start, stop = kept_if(place[Z_FIRST]), kept_if(place[Z_LAST])
    space = ROWS - block.shape[0] - ahead.shape[0] - behind.shape[0]
    zeros = jnp.zeros((space, block.shape[1]), F32)
    return jnp.concatenate([block, ahead * stop, zeros, behind * start], axis=0)


def load_plane(place, loads, ahead, behind, d, p):
    slot = d * loads.shape[1] + p
    return with_rows(place, loads[d, p], ahead[slot], behind[slot])


def krylov_kernel(place, loads, ahead, behind, stiff, stiff_ahead, stiff_behind, density,
                  first, second, sums):
    planes = loads.shape[1]
    cells = planes - 5
    low, high = kept_if(place[SLAB_FIRST]), kept_if(place[SLAB_LAST])
    stiff_planes = [stiff_behind[p] * low for p in range(2)]
    stiff_planes += [stiff[p] for p in range(cells)]
    stiff_planes += [stiff_ahead[p] * high for p in range(2)]
    loaded = [
        [load_plane(place, loads, ahead, behind, d, p) for d in range(4)] for p in range(planes)
    ]
    force = [plane[:3] for plane in loaded]
    free = [plane[3] for plane in loaded]
    image = operator_planes(force, stiff_planes, free[1:-1])
    twice = operator_planes(image, stiff_planes[1:-1], free[2:-2])
    own = (force[2 : 2 + cells], image[1 : 1 + cells], twice[:cells])
    rows = density.shape[1]

    def dot(left, right):
        total = None
        for p in range(cells):
            for d in range(3):
                term = left[p][d][:rows] * right[p][d][:rows]
                total = term if total is None else total + term
        return total

    totals = [dot(own[k // 2], own[(k + 1) // 2]) for k in range(2 * ITERS - 1)]
    modes = [[plane_modes(component, rows) for component in plane] for plane in twice]
    last = None
    volume = None
    for e in range(cells):
        term = stiff_planes[2 + e][:rows] * energy_of(element_modes(modes[e], modes[e + 1]))
        last = term if last is None else last + term
        volume = density[e] if volume is None else volume + density[e]
    totals += [last, volume]
    row_number = lax.broadcasted_iota(jnp.int32, sums.shape, 0)
    result = jnp.zeros(sums.shape, F32)
    for k, total in enumerate(totals):
        scalar = jnp.sum(jnp.sum(total, axis=0, keepdims=True), axis=1, keepdims=True)
        result = jnp.where(row_number == k, scalar, result)
    sums[...] = result
    for p in range(cells + 1):
        for d in range(3):
            first[d, p] = image[1 + p][d]
            second[d, p] = twice[p][d]


def krylov_steps(moments):
    mean = moments[1] / moments[0]
    powers = [None, mean]
    for k in range(2, 2 * ITERS):
        powers.append(powers[-1] * mean)
    scaled = [moments[k] / moments[0] / powers[k] if k else 1.0 for k in range(2 * ITERS)]

    def product(left, right, shift):
        return sum(
            left[i] * right[j] * scaled[i + j + shift]
            for i in range(len(left))
            for j in range(len(right))
        )

    solution = [0.0] * ITERS
    residual = [1.0]
    direction = [1.0]
    norm_now = scaled[0]
    work = 0.0
    for iteration in range(ITERS):
        alpha = norm_now / product(direction, direction, 1)
        work = work + alpha * norm_now
        solution = [
            solution[i] + (alpha * direction[i] if i < len(direction) else 0.0)
            for i in range(ITERS)
        ]
        if iteration + 1 < ITERS:
            image = [0.0] + direction
            residual = [
                (residual[i] if i < len(residual) else 0.0) - alpha * image[i]
                for i in range(len(image))
            ]
            norm_next = product(residual, residual, 0)
            beta = norm_next / norm_now
            direction = [
                residual[i] + (beta * direction[i] if i < len(direction) else 0.0)
                for i in range(len(residual))
            ]
            norm_now = norm_next
    factors = [solution[i] / powers[i + 1] for i in range(ITERS)]
    return factors, work * moments[0] / mean


def energy_kernel(
    elements, place, sums, loads, ahead, behind, first, second, density, solution, slope, out
):
    rows_of = [sums[k : k + 1, :] for k in range(2 * ITERS + 1)]
    factors, compliance = krylov_steps(rows_of[: 2 * ITERS])
    volume = rows_of[2 * ITERS]
    constant = 2.0 * penalty * (volume / elements - vol_target) / elements
    scale = -3.0 * (1.0 - emin) / compliance
    wide = [jnp.concatenate([value, value], axis=1) for value in factors + [scale, constant]]
    cells, rows, _ = density.shape
    modes = []
    for p in range(cells + 1):
        plane = []
        for d in range(3):
            load = load_plane(place, loads, ahead, behind, d, 2 + p)
            value = wide[0] * load + wide[1] * first[d, p] + wide[2] * second[d, p]
            if p < cells:
                solution[d, p] = value[:rows]
            plane.append(plane_modes(value, rows))
        modes.append(plane)
    for e in range(cells):
        energy = energy_of(element_modes(modes[e], modes[e + 1]))
        held = density[e]
        out[e] = held
        slope[e] = (wide[3] * held * held * energy + wide[4]) * held * (1.0 - held)


def column_of(line):
    size = line.shape[1]
    shape = (size, size)
    same = lax.broadcasted_iota(jnp.int32, shape, 0) == lax.broadcasted_iota(jnp.int32, shape, 1)
    return jnp.sum(jnp.where(same, line, 0.0), axis=1, keepdims=True)


def prepare_kernel(
    grid_cells, place, load_values, load_mask, fixed_mask, frequencies, w_in, w_mid, w_out,
    loads, loads_first, loads_last, x_cos, x_sin, z_cos, z_sin, w_in_t, w_mid_t, w_mid_half,
    w_column, w_row,
):
    cells, rows, size = load_mask.shape
    free = (1 - fixed_mask[...]).astype(F32)
    held = free * load_mask[...].astype(F32)
    for d in range(4):
        field = free if d == 3 else held * load_values[d]
        loads[d] = field
        loads_first[d] = field[:3]
        loads_last[d] = field[cells - 2 :]
    columns = [column_of(frequencies[k : k + 1, :]) for k in range(3)]
    half = rows // 2
    lanes = 2 * cells * half
    number = lax.broadcasted_iota(jnp.int32, (1, lanes), 1)
    side = number // (cells * half)
    plane = (number // half) % cells
    inner = number % half
    row = jnp.where(side == 1, inner + 2, jnp.where(inner < 2, inner, inner + half))
    x_centre = ((place[X_FIRST] + plane).astype(F32) + 0.5) / grid_cells[0]
    y_centre = ((place[Y_FIRST] + row).astype(F32) + 0.5) / grid_cells[1]
    phase = two_pi * (x_centre * columns[0] + y_centre * columns[1])
    cos, sin = jnp.cos(phase), jnp.sin(phase)
    for k in range(2 * cells):
        x_cos[k] = cos[:, k * half : (k + 1) * half]
        x_sin[k] = sin[:, k * half : (k + 1) * half]
    z_number = lax.broadcasted_iota(jnp.int32, (1, size), 1)
    phase = two_pi * (((z_number.astype(F32) + 0.5) / grid_cells[2]) * columns[2])
    z_cos[...] = jnp.cos(phase)
    z_sin[...] = jnp.sin(phase)
    w_in_t[...] = (0.5 * w_in[...].astype(F32)).T.astype(BF)
    middle = 0.5 * w_mid[...].astype(F32)
    w_mid_half[...] = middle.astype(BF)
    w_mid_t[...] = middle.T.astype(BF)
    line = w_out[...].astype(F32)[None, :]
    w_column[...] = 0.5 * column_of(line)
    w_row[...] = jnp.broadcast_to(line, w_row.shape).astype(BF)


def pack_kernel(place, loads, loads_ahead, loads_behind, stiff_first, stiff_last,
                planes, to_before, to_next):
    low, high = kept_if(place[SLAB_FIRST]), kept_if(place[SLAB_LAST])
    cells, rows = loads.shape[1:3]
    count = planes.shape[1]
    for d in range(4):
        for p in range(count):
            if p < 2:
                block = loads_behind[d, p] * low
            elif p < 2 + cells:
                block = loads[d, p - 2]
            else:
                block = loads_ahead[d, p - 2 - cells] * high
            planes[d, p] = block
            to_before[d * count + p] = block[:3]
            to_next[d * count + p] = block[rows - 2 :]
    for p in range(cells):
        to_before[4 * count + p, :2, :] = stiff_first[p]
        to_before[4 * count + p, 2:, :] = stiff_first[p, 1:]
        to_next[4 * count + p] = stiff_last[p]


def stiff_rows_kernel(place, stiff, ahead, behind, joined, to_before, to_next):
    cells = stiff.shape[0]
    first = ahead.shape[0] - cells
    for p in range(cells):
        block = with_rows(place, stiff[p], ahead[first + p, :2, :], behind[first + p])
        joined[p] = block
        if p < to_before.shape[0]:
            to_before[p] = block
        if p >= cells - to_next.shape[0]:
            to_next[p - (cells - to_next.shape[0])] = block


def gated(half):
    up = 1.0 + jnp.tanh(half)
    value = half * up
    return value, up + value * (2.0 - up)


def features_of(x_cos, x_sin, z_cos, z_sin, column):
    cos = x_cos[0, :, column : column + 1]
    sin = x_sin[0, :, column : column + 1]
    return jnp.concatenate([z_cos * cos - z_sin * sin, z_sin * cos + z_cos * sin], 0).astype(BF)


def forward_columns(tables, weights, kept, spans):
    x_cos, x_sin, z_cos, z_sin = tables
    w_in, w_mid, w_column, w_row = weights
    hidden_in, slope_mid, slope_in, hidden_mid = kept

    def keep(array, value):
        for start, first, count in spans:
            array[:, pl.ds(start, count)] = value[:, first : first + count]

    columns = x_cos.shape[2]
    picked = [features_of(x_cos, x_sin, z_cos[...], z_sin[...], q) for q in range(columns)]
    features = jnp.concatenate(picked, 1)
    value, slope = gated(jnp.dot(w_in[...], features, preferred_element_type=F32))
    value = value.astype(BF)
    keep(hidden_in, value)
    keep(slope_in, slope.astype(BF))
    value, slope = gated(jnp.dot(w_mid[...], value, preferred_element_type=F32))
    value = value.astype(BF)
    keep(hidden_mid, value)
    keep(slope_mid, (w_column[...] * slope).astype(BF))
    logits = jnp.dot(w_row[...], value, preferred_element_type=F32)[:1]
    return 0.5 * jnp.tanh(0.5 * logits) + 0.5


def stiffness_of(density):
    return emin + (1.0 - emin) * (density * density * density)


def outer_kernel(
    x_cos, x_sin, z_cos, z_sin, w_in, w_mid, w_column, w_row,
    density, stiff_first, stiff_last, *kept,
):
    size = density.shape[2]
    start = pl.multiple_of(pl.program_id(0) * (8 * size), 8 * size)
    spans = [(start, 0, 2 * size), (start + 6 * size, 2 * size, 2 * size)]
    tables, weights = (x_cos, x_sin, z_cos, z_sin), (w_in, w_mid, w_column, w_row)
    line = forward_columns(tables, weights, kept, spans)
    for q in range(4):
        part = line[:, q * size : (q + 1) * size]
        density[0, q : q + 1, :] = part
        (stiff_first if q < 2 else stiff_last)[0, q % 2 : q % 2 + 1, :] = stiffness_of(part)


def inner_kernel(
    x_cos, x_sin, z_cos, z_sin, w_in, w_mid, w_column, w_row, outer, *rest,
):
    density, stiff = rest[4:6]
    size = density.shape[2]
    plane = pl.program_id(0)
    start = pl.multiple_of(plane * (8 * size), 8 * size)
    tables, weights = (x_cos, x_sin, z_cos, z_sin), (w_in, w_mid, w_column, w_row)
    line = forward_columns(tables, weights, rest[6:], [(start + 2 * size, 0, 4 * size)])
    for r in range(8):
        if 2 <= r < 6:
            part = line[:, (r - 2) * size : (r - 1) * size]
        else:
            q = r if r < 2 else r - 4
            part = outer[0, q : q + 1, :]
        density[plane, r : r + 1, :] = part
        stiff[plane, r : r + 1, :] = stiffness_of(part)


def back_kernel(w_mid, slope_mid, slope_in, back, *, first, span):
    place = pl.ds(pl.multiple_of(first + pl.program_id(0) * span, span), span)
    product = jnp.dot(w_mid[...], slope_mid[:, place], preferred_element_type=F32)
    back[:, place] = (product * slope_in[:, place].astype(F32)).astype(BF)


def in_three(value):
    high = value.astype(BF)
    rest = value - high.astype(F32)
    middle = rest.astype(BF)
    low = (rest - middle.astype(F32)).astype(BF)
    return jnp.concatenate([high, middle, low, jnp.zeros((13, value.shape[1]), BF)], axis=0)


def gradient_kernel(
    place, slope, x_cos, x_sin, z_cos, z_sin, hidden_in, slope_mid, back, hidden_mid,
    mine, other, grad_out, total, running, *, steps,
):
    step = pl.program_id(0)

    @pl.when(step == 0)
    def _():
        total[...] = jnp.zeros_like(total)
        running[...] = jnp.zeros_like(running)

    rows, size = slope.shape[1:]
    half = rows // 2
    mid = first = out = None
    for number, group in enumerate(((0, 1, 6, 7), (2, 3, 4, 5))):
        lines = [slope[0, r : r + 1, :] for r in group]
        picked = []
        for q in range(half):
            cos, sin = x_cos[number, 0, :, q : q + 1], x_sin[number, 0, :, q : q + 1]
            upper = (z_cos[...] * cos - z_sin[...] * sin) * lines[q]
            lower = (z_sin[...] * cos + z_cos[...] * sin) * lines[q]
            picked.append(jnp.concatenate([upper, lower], 0).astype(BF))
        features = jnp.concatenate(picked, 1)
        line = jnp.concatenate(lines, 1)

        def kept(array):
            pieces, q = [], 0
            while q < half:
                run = 1
                while q + run < half and group[q + run] == group[q] + run:
                    run += 1
                start = pl.multiple_of(step * (rows * size) + group[q] * size, size)
                pieces.append(array[:, pl.ds(start, run * size)])
                q += run
            return pieces[0] if len(pieces) == 1 else jnp.concatenate(pieces, 1)

        hidden = (kept(hidden_in).astype(F32) * line).astype(BF)
        terms = (
            lax.dot_general(hidden, kept(slope_mid), LAST, preferred_element_type=F32),
            lax.dot_general(features, kept(back), LAST, preferred_element_type=F32),
            lax.dot_general(kept(hidden_mid), in_three(line), LAST, preferred_element_type=F32),
        )
        if mid is None:
            mid, first, out = terms
        else:
            mid, first, out = mid + terms[0], first + terms[1], out + terms[2]
    height = mid.shape[0]
    for k in range(total.shape[0]):
        total[k, :height, :] += mid[:, k * 128 : (k + 1) * 128]
        total[k, height:, :] += first[:, k * 128 : (k + 1) * 128]
    running[:, : out.shape[1]] += out

    @pl.when(step == steps - 1)
    def _():
        core = place[CORE]
        for k in range(mine.shape[0]):
            mine[k] = total[2 * core + k]
            other[k] = total[2 * (1 - core) + k]
        line = jnp.sum(running[...].T, axis=0, keepdims=True)
        for k in range(grad_out.shape[0]):
            grad_out[k : k + 1, :] = line[:, k * 128 : (k + 1) * 128]


def finish_kernel(place, half, away, grad_in, grad_mid, grad_out):
    chips = half.shape[0]
    height = half.shape[1] - 2 * grad_out.shape[0]
    middle = grad_mid.shape[0]
    at_first = place[CORE] == 0
    for group in range(4):
        part = pl.ds((group % 2) * (chips // 2), chips // 2)
        own, far = half[part, :height, :], away[part, :height, :]
        picked = jnp.where(at_first, own, far) if group < 2 else jnp.where(at_first, far, own)
        picked = picked.reshape(-1, 128)
        lanes = slice(group * 128, (group + 1) * 128)
        grad_mid[:, lanes] = picked[:middle]
        grad_in[:, lanes] = picked[middle:]
    out = jnp.sum(half[:, height:, :], axis=0) + jnp.sum(away[:, height:, :], axis=0)
    grad_out[...] = out[: grad_out.shape[0]]


VM = pltpu.VMEM
WHOLE = pl.BlockSpec(memory_space=pltpu.VMEM)
SCALARS = pl.BlockSpec(memory_space=pltpu.SMEM)
X_FIRST, Y_FIRST, CORE, SLAB_FIRST, SLAB_LAST, Z_FIRST, Z_LAST = range(7)


def fixed(shape):
    return pl.BlockSpec(shape, lambda i: (0,) * len(shape))


def in_vmem(*arrays):
    return [pltpu.with_memory_space_constraint(array, pltpu.VMEM) for array in arrays]


def params(mebibytes=8):
    return pltpu.CompilerParams(vmem_limit_bytes=mebibytes << 20)


def shaped(*shape, dtype=F32):
    return jax.ShapeDtypeStruct(shape, dtype)


def simple(kernel, name, out_shape, place, *operands, space=None):
    if space is not None:
        operands = [pltpu.with_memory_space_constraint(array, space) for array in operands]
    return pl.pallas_call(
        kernel,
        name=name,
        in_specs=[SCALARS] + [WHOLE] * len(operands),
        out_specs=[WHOLE] * len(out_shape),
        out_shape=out_shape,
        compiler_params=params(),
    )(place, *operands)


def shifted(block, axis, distance):
    size = lax.axis_size(axis)
    return lax.ppermute(block, axis, [(i, (i + distance) % size) for i in range(size)])


def summed(values):
    values = values + lax.ppermute(values, "c", [(0, 1), (1, 0)])
    for axis in ("z", "y", "x"):
        others = [shifted(values, axis, k) for k in range(1, lax.axis_size(axis))]
        values = values + sum(others)
    return values


def on_device(load_values, load_mask, fixed_mask, frequencies, weight_in, weight_mid, weight_out):
    cells_x, cells_y, cells_z = fixed_mask.shape
    slab, sub = lax.axis_index(SLAB), lax.axis_index("z")
    slabs, subs = lax.axis_size(SLAB), lax.axis_size("z")
    grid_cells = (cells_x * slabs, cells_y * subs, cells_z)
    elements_total = grid_cells[0] * grid_cells[1] * grid_cells[2]
    place = jnp.stack(
        [slab * cells_x, sub * cells_y, lax.axis_index("c")]
        + [(slab == 0) * 1, (slab == slabs - 1) * 1, (sub == 0) * 1, (sub == subs - 1) * 1, slab * 0]
    ).astype(jnp.int32)
    inputs, hidden = weight_in.shape
    rows = cells_x * cells_y * cells_z
    half_rows = cells_y // 2
    field = (cells_x, cells_y, cells_z)
    table = shaped(2 * cells_x, inputs // 2, half_rows)
    (
        loads, loads_first, loads_last, x_cos, x_sin, z_cos, z_sin,
        w_in_t, w_mid_t, w_mid_half, w_column, w_row,
    ) = simple(
        functools.partial(prepare_kernel, grid_cells),
        "prepare",
        [
            shaped(4, *field),
            shaped(4, 3, cells_y, cells_z),
            shaped(4, 2, cells_y, cells_z),
            table,
            table,
            shaped(inputs // 2, cells_z),
            shaped(inputs // 2, cells_z),
            shaped(hidden, inputs, dtype=BF),
            shaped(hidden, hidden, dtype=BF),
            shaped(hidden, hidden, dtype=BF),
            shaped(hidden, 1),
            shaped(16, hidden, dtype=BF),
        ],
        place, load_values, load_mask, fixed_mask, frequencies, weight_in, weight_mid,
        weight_out, space=pltpu.HBM,
    )

    loads_ahead = shifted(loads_first, SLAB, -1)
    loads_behind = shifted(loads_last, SLAB, 1)
    weights = (w_in_t, w_mid_t, w_column, w_row)
    weight_specs = [fixed(array.shape) for array in weights]
    x_spec = (1, inputs // 2, half_rows)
    z_specs = [fixed(z_cos.shape)] * 2
    kept = [VM((hidden, rows), BF)] * 4

    def plane_spec(count):
        return pl.BlockSpec((1, count, cells_z), lambda i: (i, 0, 0))

    cost = pl.CostEstimate(
        flops=(inputs + hidden) * hidden * rows,
        bytes_accessed=4 * hidden * rows,
        transcendentals=hidden * rows,
    )
    outer, stiff_first, stiff_last, *stored = pl.pallas_call(
        outer_kernel,
        name="outer",
        grid=(cells_x,),
        in_specs=[pl.BlockSpec(x_spec, lambda i: (i, 0, 0))] * 2 + z_specs + weight_specs,
        out_specs=[plane_spec(half_rows), plane_spec(2), plane_spec(2)] + [WHOLE] * 4,
        out_shape=[
            shaped(cells_x, half_rows, cells_z),
            shaped(cells_x, 2, cells_z),
            shaped(cells_x, 2, cells_z),
        ]
        + kept,
        compiler_params=params(12),
        cost_estimate=cost,
    )(x_cos, x_sin, z_cos, z_sin, *weights)
    planes = cells_x + 5
    slots = 4 * planes + cells_x
    loads, rows_first, rows_last = simple(
        pack_kernel,
        "pack",
        [shaped(4, planes, cells_y, cells_z), shaped(slots, 3, cells_z), shaped(slots, 2, cells_z)],
        place, loads, loads_ahead, loads_behind, stiff_first, stiff_last,
    )
    rows_ahead = shifted(rows_first, "z", -1)
    rows_behind = shifted(rows_last, "z", 1)
    density, stiff, *stored = pl.pallas_call(
        inner_kernel,
        name="inner",
        grid=(cells_x,),
        in_specs=[pl.BlockSpec(x_spec, lambda i: (cells_x + i, 0, 0))] * 2
        + z_specs
        + weight_specs
        + [plane_spec(half_rows)]
        + [WHOLE] * 4,
        out_specs=[WHOLE] * 2 + [WHOLE] * 4,
        out_shape=[VM(field, F32)] * 2 + kept,
        input_output_aliases={9 + k: 2 + k for k in range(4)},
        compiler_params=params(12),
        cost_estimate=cost,
    )(x_cos, x_sin, z_cos, z_sin, *weights, outer, *in_vmem(*stored))
    hidden_in, slope_mid, slope_in, hidden_mid = stored
    stiff_16, stiff_before, stiff_next = simple(
        stiff_rows_kernel,
        "stiff_rows",
        [shaped(cells_x, ROWS, cells_z), shaped(2, ROWS, cells_z), shaped(2, ROWS, cells_z)],
        place, stiff, rows_ahead, rows_behind,
    )
    stiff_ahead = shifted(stiff_before, SLAB, -1)
    stiff_behind = shifted(stiff_next, SLAB, 1)

    span = 1024
    back = slope_in
    parts = 2
    for part in range(parts):
        back = pl.pallas_call(
            functools.partial(back_kernel, first=part * (rows // parts), span=span),
            name=f"back_{part}",
            grid=(rows // parts // span,),
            in_specs=[fixed((hidden, hidden)), WHOLE, WHOLE],
            out_specs=WHOLE,
            out_shape=kept[0],
            input_output_aliases={2: 0},
            compiler_params=params(),
            cost_estimate=pl.CostEstimate(
                flops=2 * hidden * hidden * rows // parts,
                bytes_accessed=6 * hidden * rows // parts,
                transcendentals=0,
            ),
        )(w_mid_half, *in_vmem(slope_mid, back))

    held = shaped(3, cells_x + 1, ROWS, cells_z)
    first, second, sums = simple(
        krylov_kernel,
        "krylov",
        [held, held, shaped(8, 128)],
        place, loads, rows_ahead, rows_behind, stiff_16, stiff_ahead, stiff_behind, density,
    )
    solution, slope, density = simple(
        functools.partial(energy_kernel, elements_total),
        "energy",
        [shaped(3, *field), shaped(*field), shaped(*field)],
        place, summed(sums), loads, rows_ahead, rows_behind, first, second, density,
    )

    height = hidden + inputs
    groups = hidden // 128
    pair = pl.BlockSpec((2, 1) + x_spec[1:], lambda i: (0, i, 0, 0))
    tables = [array.reshape((2, cells_x) + x_spec[1:]) for array in (x_cos, x_sin)]
    mine, other, grad_out = pl.pallas_call(
        functools.partial(gradient_kernel, steps=cells_x),
        name="gradients",
        grid=(cells_x,),
        in_specs=[SCALARS, plane_spec(cells_y), pair, pair] + z_specs + [WHOLE] * 4,
        out_specs=[WHOLE] * 2 + [fixed((groups, 128))],
        out_shape=[VM((groups // 2, height, 128), F32)] * 2 + [shaped(groups, 128)],
        scratch_shapes=[VM((groups, height, 128), F32), VM((hidden, 128), F32)],
        compiler_params=params(20),
    )(place, slope, *tables, z_cos, z_sin, *in_vmem(hidden_in, slope_mid, back, hidden_mid))

    chips = lax.axis_size(CHIPS)
    swap = [(0, 1), (1, 0)]
    half = (mine + lax.ppermute(other, "c", swap)).reshape(chips, -1, 128)
    share = jnp.sum(lax.all_to_all(half, CHIPS, 0, 0), axis=0)
    share = jnp.concatenate([share, grad_out, jnp.zeros_like(grad_out)], axis=0)
    half = lax.all_to_all(jnp.broadcast_to(share[None], (chips,) + share.shape), CHIPS, 0, 0)
    away = lax.ppermute(half, "c", swap)
    grad_in, grad_mid, grad_out = simple(
        finish_kernel,
        "finish",
        [shaped(inputs, hidden), shaped(hidden, hidden), shaped(groups, 128)],
        place, half, away,
    )
    return solution, density, grad_in, grad_mid, grad_out.reshape(hidden)


def solution(mesh):
    slab, sub = mesh.devices.shape
    fine = Mesh(mesh.devices.reshape(4, 4, slab // 16, sub), ALL)
    field = P(SLAB, "z", None)
    vector = P(None, SLAB, "z", None)
    return jax.shard_map(
        on_device,
        mesh=fine,
        in_specs=(vector, field, field, P(), P(), P(), P()),
        out_specs=(vector, field, P(), P(), P()),
        check_vma=False,
    )
```

```python
import functools
import itertools
import math

import jax
import jax.numpy as jnp
import numpy as np
from jax import lax
from jax.experimental import pallas as pl
from jax.experimental.pallas import tpu as pltpu
from jax.sharding import Mesh
from jax.sharding import PartitionSpec as P

ITERS = 3
SLAB = ("x", "y", "c")
CHIPS = ("x", "y", "z")
ALL = ("x", "y", "c", "z")
BF = jnp.bfloat16
F32 = jnp.float32

two_pi = 2.0 * math.pi
emin = 0.001
penalty = 4.0
vol_target = 0.3
ROWS = 16
corner_list = list(itertools.product((0, 1), repeat=3))
LAST = (((1,), (1,)), ((), ()))


def hex_stiffness():
    poisson = 0.3
    lame_first = poisson / ((1.0 + poisson) * (1.0 - 2.0 * poisson))
    lame_second = 0.5 / (1.0 + poisson)
    elastic = np.zeros((6, 6))
    elastic[:3, :3] = lame_first
    for axis_number in range(3):
        elastic[axis_number, axis_number] += 2.0 * lame_second
        elastic[axis_number + 3, axis_number + 3] = lame_second
    gauss_points = [0.5 - 0.5 / math.sqrt(3.0), 0.5 + 0.5 / math.sqrt(3.0)]
    matrix = np.zeros((24, 24))
    for location in itertools.product(gauss_points, repeat=3):
        strain = np.zeros((6, 24))
        for corner_number, corner in enumerate(corner_list):
            factors = [
                location[axis] if corner[axis] == 1 else 1.0 - location[axis] for axis in range(3)
            ]
            slopes = [1.0 if corner[axis] == 1 else -1.0 for axis in range(3)]
            derivative = [
                slopes[0] * factors[1] * factors[2],
                factors[0] * slopes[1] * factors[2],
                factors[0] * factors[1] * slopes[2],
            ]
            column = 3 * corner_number
            for axis in range(3):
                strain[axis, column + axis] = derivative[axis]
            strain[3, column + 1] = derivative[2]
            strain[3, column + 2] = derivative[1]
            strain[4, column + 0] = derivative[2]
            strain[4, column + 2] = derivative[0]
            strain[5, column + 0] = derivative[1]
            strain[5, column + 1] = derivative[0]
        matrix += strain.T @ elastic @ strain / 8.0
    return matrix


def modal_stiffness():
    table = hex_stiffness()
    change = np.zeros((24, 24))
    for row, wave in enumerate(corner_list):
        for column, corner in enumerate(corner_list):
            sign = np.prod([1.0 if c == 1 else -1.0 for w, c in zip(wave, corner) if w == 1])
            for d in range(3):
                change[3 * row + d, 3 * column + d] = sign
    modal = change @ table @ change.T / 64.0
    blocks = []
    for parity in corner_list:
        waves = [tuple(parity[a] ^ (a == d) for a in range(3)) for d in range(3)]
        index = [3 * corner_list.index(wave) + d for d, wave in enumerate(waves)]
        block = modal[np.ix_(index, index)]
        blocks.append((waves, np.where(np.abs(block) < 1e-9, 0.0, block)))
    return blocks


BLOCKS = modal_stiffness()


def lane_mask(shape, lane):
    return lax.broadcasted_iota(jnp.int32, shape, len(shape) - 1) == lane


def plane_modes(plane, rows):
    size = plane.shape[-1]
    ahead = jnp.where(lane_mask(plane.shape, size - 1), 0.0, pltpu.roll(plane, size - 1, 1))
    modes = {}
    for wave_z, part in ((0, plane + ahead), (1, ahead - plane)):
        following = pltpu.roll(part, ROWS - 1, 0)
        modes[0, wave_z] = (part + following)[:rows]
        modes[1, wave_z] = (following - part)[:rows]
    return modes


def element_modes(lower, upper):
    found = []
    for low, high in zip(lower, upper):
        modes = {}
        for key in low:
            modes[(0,) + key] = low[key] + high[key]
            modes[(1,) + key] = high[key] - low[key]
        found.append(modes)
    return found


def modal_forces(modes):
    for waves, block in BLOCKS:
        values = [modes[d][waves[d]] for d in range(3)]
        for d in range(3):
            total = None
            for other in range(3):
                if block[d, other] != 0.0:
                    term = np.float32(block[d, other]) * values[other]
                    total = term if total is None else total + term
            if total is not None:
                yield d, waves[d], values[d], total


def energy_of(modes):
    total = None
    for _, _, value, force in modal_forces(modes):
        total = value * force if total is None else total + value * force
    return total


def node_plane(gathered):
    parts = []
    for wave_z in (0, 1):
        even, odd = gathered[0, wave_z], gathered[1, wave_z]
        parts.append((even - odd) + pltpu.roll(even + odd, 1, 0))
    behind = pltpu.roll(parts[0] + parts[1], 1, 1)
    return (parts[0] - parts[1]) + jnp.where(lane_mask(behind.shape, 0), 0.0, behind)


def operator_planes(planes, stiff, free):
    modes = [[plane_modes(component, ROWS) for component in plane] for plane in planes]
    gathered = [[{} for _ in range(3)] for _ in planes]
    for e in range(len(planes) - 1):
        forces = [{} for _ in range(3)]
        for d, wave, _, force in modal_forces(element_modes(modes[e], modes[e + 1])):
            forces[d][wave] = force * stiff[e]
        for d in range(3):
            for key in itertools.product((0, 1), repeat=2):
                even, odd = forces[d].get((0,) + key), forces[d].get((1,) + key)
                for node, sign in ((e, -1), (e + 1, 1)):
                    if even is None:
                        term = odd if sign == 1 else -odd
                    else:
                        term = even + odd if sign == 1 else even - odd
                    held = gathered[node][d]
                    held[key] = term if key not in held else held[key] + term
    return [
        [node_plane(gathered[n][d]) * free[n - 1] for d in range(3)]
        for n in range(1, len(planes) - 1)
    ]


def kept_if(flag):
    return jnp.where(flag == 0, 1.0, 0.0)


def with_rows(place, block, ahead, behind):
    start, stop = kept_if(place[Z_FIRST]), kept_if(place[Z_LAST])
    space = ROWS - block.shape[0] - ahead.shape[0] - behind.shape[0]
    zeros = jnp.zeros((space, block.shape[1]), F32)
    return jnp.concatenate([block, ahead * stop, zeros, behind * start], axis=0)


def load_plane(place, loads, ahead, behind, d, p):
    slot = d * loads.shape[1] + p
    return with_rows(place, loads[d, p], ahead[slot], behind[slot])


def krylov_kernel(place, loads, ahead, behind, stiff, stiff_ahead, stiff_behind, density,
                  first, second, sums):
    planes = loads.shape[1]
    cells = planes - 5
    low, high = kept_if(place[SLAB_FIRST]), kept_if(place[SLAB_LAST])
    stiff_planes = [stiff_behind[p] * low for p in range(2)]
    stiff_planes += [stiff[p] for p in range(cells)]
    stiff_planes += [stiff_ahead[p] * high for p in range(2)]
    loaded = [
        [load_plane(place, loads, ahead, behind, d, p) for d in range(4)] for p in range(planes)
    ]
    force = [plane[:3] for plane in loaded]
    free = [plane[3] for plane in loaded]
    image = operator_planes(force, stiff_planes, free[1:-1])
    twice = operator_planes(image, stiff_planes[1:-1], free[2:-2])
    own = (force[2 : 2 + cells], image[1 : 1 + cells], twice[:cells])
    rows = density.shape[1]

    def dot(left, right):
        total = None
        for p in range(cells):
            for d in range(3):
                term = left[p][d][:rows] * right[p][d][:rows]
                total = term if total is None else total + term
        return total

    totals = [dot(own[k // 2], own[(k + 1) // 2]) for k in range(2 * ITERS - 1)]
    modes = [[plane_modes(component, rows) for component in plane] for plane in twice]
    last = None
    volume = None
    for e in range(cells):
        term = stiff_planes[2 + e][:rows] * energy_of(element_modes(modes[e], modes[e + 1]))
        last = term if last is None else last + term
        volume = density[e] if volume is None else volume + density[e]
    totals += [last, volume]
    row_number = lax.broadcasted_iota(jnp.int32, sums.shape, 0)
    result = jnp.zeros(sums.shape, F32)
    for k, total in enumerate(totals):
        scalar = jnp.sum(jnp.sum(total, axis=0, keepdims=True), axis=1, keepdims=True)
        result = jnp.where(row_number == k, scalar, result)
    sums[...] = result
    for p in range(cells + 1):
        for d in range(3):
            first[d, p] = image[1 + p][d]
            second[d, p] = twice[p][d]


def krylov_steps(moments):
    mean = moments[1] / moments[0]
    powers = [None, mean]
    for k in range(2, 2 * ITERS):
        powers.append(powers[-1] * mean)
    scaled = [moments[k] / moments[0] / powers[k] if k else 1.0 for k in range(2 * ITERS)]

    def product(left, right, shift):
        return sum(
            left[i] * right[j] * scaled[i + j + shift]
            for i in range(len(left))
            for j in range(len(right))
        )

    solution = [0.0] * ITERS
    residual = [1.0]
    direction = [1.0]
    norm_now = scaled[0]
    work = 0.0
    for iteration in range(ITERS):
        alpha = norm_now / product(direction, direction, 1)
        work = work + alpha * norm_now
        solution = [
            solution[i] + (alpha * direction[i] if i < len(direction) else 0.0)
            for i in range(ITERS)
        ]
        if iteration + 1 < ITERS:
            image = [0.0] + direction
            residual = [
                (residual[i] if i < len(residual) else 0.0) - alpha * image[i]
                for i in range(len(image))
            ]
            norm_next = product(residual, residual, 0)
            beta = norm_next / norm_now
            direction = [
                residual[i] + (beta * direction[i] if i < len(direction) else 0.0)
                for i in range(len(residual))
            ]
            norm_now = norm_next
    factors = [solution[i] / powers[i + 1] for i in range(ITERS)]
    return factors, work * moments[0] / mean


def energy_kernel(
    elements, place, sums, loads, ahead, behind, first, second, density, solution, slope, out
):
    rows_of = [sums[k : k + 1, :] for k in range(2 * ITERS + 1)]
    factors, compliance = krylov_steps(rows_of[: 2 * ITERS])
    volume = rows_of[2 * ITERS]
    constant = 2.0 * penalty * (volume / elements - vol_target) / elements
    scale = -3.0 * (1.0 - emin) / compliance
    wide = [jnp.concatenate([value, value], axis=1) for value in factors + [scale, constant]]
    cells, rows, _ = density.shape
    modes = []
    for p in range(cells + 1):
        plane = []
        for d in range(3):
            load = load_plane(place, loads, ahead, behind, d, 2 + p)
            value = wide[0] * load + wide[1] * first[d, p] + wide[2] * second[d, p]
            if p < cells:
                solution[d, p] = value[:rows]
            plane.append(plane_modes(value, rows))
        modes.append(plane)
    for e in range(cells):
        energy = energy_of(element_modes(modes[e], modes[e + 1]))
        held = density[e]
        out[e] = held
        slope[e] = (wide[3] * held * held * energy + wide[4]) * held * (1.0 - held)


def column_of(line):
    size = line.shape[1]
    shape = (size, size)
    same = lax.broadcasted_iota(jnp.int32, shape, 0) == lax.broadcasted_iota(jnp.int32, shape, 1)
    return jnp.sum(jnp.where(same, line, 0.0), axis=1, keepdims=True)


def prepare_kernel(
    grid_cells, place, load_values, load_mask, fixed_mask, frequencies, w_in, w_mid, w_out,
    loads, loads_first, loads_last, x_cos, x_sin, z_cos, z_sin, w_in_t, w_mid_t, w_mid_half,
    w_column, w_row,
):
    cells, rows, size = load_mask.shape
    free = (1 - fixed_mask[...]).astype(F32)
    held = free * load_mask[...].astype(F32)
    for d in range(4):
        field = free if d == 3 else held * load_values[d]
        loads[d] = field
        loads_first[d] = field[:3]
        loads_last[d] = field[cells - 2 :]
    columns = [column_of(frequencies[k : k + 1, :]) for k in range(3)]
    half = rows // 2
    lanes = 2 * cells * half
    number = lax.broadcasted_iota(jnp.int32, (1, lanes), 1)
    side = number // (cells * half)
    plane = (number // half) % cells
    inner = number % half
    row = jnp.where(side == 1, inner + 2, jnp.where(inner < 2, inner, inner + half))
    x_centre = ((place[X_FIRST] + plane).astype(F32) + 0.5) / grid_cells[0]
    y_centre = ((place[Y_FIRST] + row).astype(F32) + 0.5) / grid_cells[1]
    phase = two_pi * (x_centre * columns[0] + y_centre * columns[1])
    cos, sin = jnp.cos(phase), jnp.sin(phase)
    for k in range(2 * cells):
        x_cos[k] = cos[:, k * half : (k + 1) * half]
        x_sin[k] = sin[:, k * half : (k + 1) * half]
    z_number = lax.broadcasted_iota(jnp.int32, (1, size), 1)
    phase = two_pi * (((z_number.astype(F32) + 0.5) / grid_cells[2]) * columns[2])
    z_cos[...] = jnp.cos(phase)
    z_sin[...] = jnp.sin(phase)
    w_in_t[...] = (0.5 * w_in[...].astype(F32)).T.astype(BF)
    middle = 0.5 * w_mid[...].astype(F32)
    w_mid_half[...] = middle.astype(BF)
    w_mid_t[...] = middle.T.astype(BF)
    line = w_out[...].astype(F32)[None, :]
    w_column[...] = 0.5 * column_of(line)
    w_row[...] = jnp.broadcast_to(line, w_row.shape).astype(BF)


def pack_kernel(place, loads, loads_ahead, loads_behind, stiff_first, stiff_last,
                planes, to_before, to_next):
    low, high = kept_if(place[SLAB_FIRST]), kept_if(place[SLAB_LAST])
    cells, rows = loads.shape[1:3]
    count = planes.shape[1]
    for d in range(4):
        for p in range(count):
            if p < 2:
                block = loads_behind[d, p] * low
            elif p < 2 + cells:
                block = loads[d, p - 2]
            else:
                block = loads_ahead[d, p - 2 - cells] * high
            planes[d, p] = block
            to_before[d * count + p] = block[:3]
            to_next[d * count + p] = block[rows - 2 :]
    for p in range(cells):
        to_before[4 * count + p, :2, :] = stiff_first[p]
        to_before[4 * count + p, 2:, :] = stiff_first[p, 1:]
        to_next[4 * count + p] = stiff_last[p]


def stiff_rows_kernel(place, stiff, ahead, behind, joined, to_before, to_next):
    cells = stiff.shape[0]
    first = ahead.shape[0] - cells
    for p in range(cells):
        block = with_rows(place, stiff[p], ahead[first + p, :2, :], behind[first + p])
        joined[p] = block
        if p < to_before.shape[0]:
            to_before[p] = block
        if p >= cells - to_next.shape[0]:
            to_next[p - (cells - to_next.shape[0])] = block


def gated(half):
    up = 1.0 + jnp.tanh(half)
    value = half * up
    return value, up + value * (2.0 - up)


def features_of(tables, group, column, scale=None):
    x_cos, x_sin, z_cos, z_sin = tables
    cos = x_cos[group, :, column : column + 1]
    sin = x_sin[group, :, column : column + 1]
    upper = z_cos[...] * cos - z_sin[...] * sin
    lower = z_sin[...] * cos + z_cos[...] * sin
    if scale is not None:
        upper, lower = upper * scale, lower * scale
    return jnp.concatenate([upper, lower], 0).astype(BF)


def forward_columns(tables, group, weights, kept, spans):
    w_in, w_mid, w_column, w_row = weights
    hidden_in, slope_mid, slope_in, hidden_mid = kept

    def keep(array, value):
        for start, first, count in spans:
            array[:, start : start + count] = value[:, first : first + count]

    columns = tables[0].shape[2]
    features = jnp.concatenate([features_of(tables, group, q) for q in range(columns)], 1)
    value, slope = gated(jnp.dot(w_in[...], features, preferred_element_type=F32))
    value = value.astype(BF)
    keep(hidden_in, value)
    keep(slope_in, slope.astype(BF))
    value, slope = gated(jnp.dot(w_mid[...], value, preferred_element_type=F32))
    value = value.astype(BF)
    keep(hidden_mid, value)
    keep(slope_mid, (w_column[...] * slope).astype(BF))
    logits = jnp.dot(w_row[...], value, preferred_element_type=F32)[:1]
    return 0.5 * jnp.tanh(0.5 * logits) + 0.5


def stiffness_of(density):
    return emin + (1.0 - emin) * (density * density * density)


def outer_kernel(
    x_cos, x_sin, z_cos, z_sin, w_in, w_mid, w_column, w_row,
    density, stiff_first, stiff_last, *kept,
):
    tables, weights = (x_cos, x_sin, z_cos, z_sin), (w_in, w_mid, w_column, w_row)
    cells, _, size = density.shape
    for p in range(cells):
        start = p * 8 * size
        spans = [(start, 0, 2 * size), (start + 6 * size, 2 * size, 2 * size)]
        line = forward_columns(tables, p, weights, kept, spans)
        for q in range(4):
            part = line[:, q * size : (q + 1) * size]
            density[p, q : q + 1, :] = part
            (stiff_first if q < 2 else stiff_last)[p, q % 2 : q % 2 + 1, :] = stiffness_of(part)


def inner_kernel(
    x_cos, x_sin, z_cos, z_sin, w_in, w_mid, w_column, w_row, outer, *rest,
):
    tables, weights = (x_cos, x_sin, z_cos, z_sin), (w_in, w_mid, w_column, w_row)
    density, stiff = rest[4:6]
    cells, rows, size = density.shape
    for p in range(cells):
        spans = [((p * 8 + 2) * size, 0, 4 * size)]
        line = forward_columns(tables, cells + p, weights, rest[6:], spans)
        for r in range(rows):
            if 2 <= r < 6:
                part = line[:, (r - 2) * size : (r - 1) * size]
            else:
                q = r if r < 2 else r - 4
                part = outer[p, q : q + 1, :]
            density[p, r : r + 1, :] = part
            stiff[p, r : r + 1, :] = stiffness_of(part)


def back_kernel(w_mid, slope_mid, slope_in, back, *, first, count, span):
    for start in range(first, first + count, span):
        place = slice(start, start + span)
        product = jnp.dot(w_mid[...], slope_mid[:, place], preferred_element_type=F32)
        back[:, place] = (product * slope_in[:, place].astype(F32)).astype(BF)


def gradient_kernel(
    place, slope, x_cos, x_sin, z_cos, z_sin, hidden_in, slope_mid, back, hidden_mid,
    mine, other, grad_out, mid, first, running,
):
    tables = (x_cos, x_sin, z_cos, z_sin)
    cells, rows, size = slope.shape
    half = rows // 2
    group_of = [(0, r) if r < 2 else (0, r - half) if r >= rows - 2 else (1, r - 2) for r in range(rows)]
    for p in range(cells):
        lines = [slope[p, r : r + 1, :] for r in range(rows)]
        picked = [
            features_of(tables, side * cells + p, q, line) for (side, q), line in zip(group_of, lines)
        ]
        features = jnp.concatenate(picked, 1)
        line = jnp.concatenate(lines, 1)
        span = slice(p * rows * size, (p + 1) * rows * size)
        hidden = (hidden_in[:, span].astype(F32) * line).astype(BF)
        product = hidden_mid[:, span].astype(F32) * line
        total = product[:, :128]
        for k in range(1, rows * size // 128):
            total = total + product[:, k * 128 : (k + 1) * 128]
        terms = (
            lax.dot_general(hidden, slope_mid[:, span], LAST, preferred_element_type=F32),
            lax.dot_general(back[:, span], features, LAST, preferred_element_type=F32),
            total,
        )
        for held, term in zip((mid, first, running), terms):
            if p == 0:
                held[...] = term
            else:
                held[...] += term
    core = place[CORE]
    height = mid.shape[0]
    first_t = first[...].T
    for k in range(2):
        for owner in range(2):
            lanes = slice((2 * owner + k) * 128, (2 * owner + k + 1) * 128)

            @pl.when(core == owner)
            def _():
                mine[k, :height, :] = mid[:, lanes]
                mine[k, height:, :] = first_t[:, lanes]

            @pl.when(core != owner)
            def _():
                other[k, :height, :] = mid[:, lanes]
                other[k, height:, :] = first_t[:, lanes]

    line = jnp.sum(running[...].T, axis=0, keepdims=True)
    for k in range(grad_out.shape[0]):
        grad_out[k : k + 1, :] = line[:, k * 128 : (k + 1) * 128]


def finish_kernel(place, half, away, grad_in, grad_mid, grad_out):
    chips = half.shape[0]
    height = half.shape[1] - 2 * grad_out.shape[0]
    middle = grad_mid.shape[0]
    at_first = place[CORE] == 0
    for group in range(4):
        part = pl.ds((group % 2) * (chips // 2), chips // 2)
        own, far = half[part, :height, :], away[part, :height, :]
        picked = jnp.where(at_first, own, far) if group < 2 else jnp.where(at_first, far, own)
        picked = picked.reshape(-1, 128)
        lanes = slice(group * 128, (group + 1) * 128)
        grad_mid[:, lanes] = picked[:middle]
        grad_in[:, lanes] = picked[middle:]
    out = jnp.sum(half[:, height:, :], axis=0) + jnp.sum(away[:, height:, :], axis=0)
    grad_out[...] = out[: grad_out.shape[0]]


VM = pltpu.VMEM
WHOLE = pl.BlockSpec(memory_space=pltpu.VMEM)
SCALARS = pl.BlockSpec(memory_space=pltpu.SMEM)
X_FIRST, Y_FIRST, CORE, SLAB_FIRST, SLAB_LAST, Z_FIRST, Z_LAST = range(7)


def params(mebibytes=8):
    return pltpu.CompilerParams(vmem_limit_bytes=mebibytes << 20)


def shaped(*shape, dtype=F32):
    return jax.ShapeDtypeStruct(shape, dtype)


def held(*shape, dtype=F32):
    return VM(shape, dtype)


def run(kernel, name, out_shape, *operands, scalars=1, space=pltpu.VMEM, scratch=(), limit=8, **more):
    arrays = [pltpu.with_memory_space_constraint(array, space) for array in operands[scalars:]]
    return pl.pallas_call(
        kernel,
        name=name,
        in_specs=[SCALARS] * scalars + [WHOLE] * len(arrays),
        out_specs=[WHOLE] * len(out_shape),
        out_shape=out_shape,
        scratch_shapes=list(scratch),
        compiler_params=params(limit),
        **more,
    )(*operands[:scalars], *arrays)


def shifted(block, axis, distance):
    size = lax.axis_size(axis)
    return lax.ppermute(block, axis, [(i, (i + distance) % size) for i in range(size)])


def summed(values):
    values = values + lax.ppermute(values, "c", [(0, 1), (1, 0)])
    for axis in ("z", "y", "x"):
        others = [shifted(values, axis, k) for k in range(1, lax.axis_size(axis))]
        values = values + sum(others)
    return values


def on_device(load_values, load_mask, fixed_mask, frequencies, weight_in, weight_mid, weight_out):
    cells_x, cells_y, cells_z = fixed_mask.shape
    slab, sub = lax.axis_index(SLAB), lax.axis_index("z")
    slabs, subs = lax.axis_size(SLAB), lax.axis_size("z")
    grid_cells = (cells_x * slabs, cells_y * subs, cells_z)
    elements_total = grid_cells[0] * grid_cells[1] * grid_cells[2]
    place = jnp.stack(
        [slab * cells_x, sub * cells_y, lax.axis_index("c")]
        + [(slab == 0) * 1, (slab == slabs - 1) * 1, (sub == 0) * 1, (sub == subs - 1) * 1, slab * 0]
    ).astype(jnp.int32)
    inputs, hidden = weight_in.shape
    rows = cells_x * cells_y * cells_z
    half_rows = cells_y // 2
    field = (cells_x, cells_y, cells_z)
    table = held(2 * cells_x, inputs // 2, half_rows)
    line = held(inputs // 2, cells_z)
    (
        loads, loads_first, loads_last, x_cos, x_sin, z_cos, z_sin,
        w_in_t, w_mid_t, w_mid_half, w_column, w_row,
    ) = run(
        functools.partial(prepare_kernel, grid_cells),
        "prepare",
        [
            held(4, *field),
            held(4, 3, cells_y, cells_z),
            held(4, 2, cells_y, cells_z),
            table,
            table,
            line,
            line,
            held(hidden, inputs, dtype=BF),
            held(hidden, hidden, dtype=BF),
            held(hidden, hidden, dtype=BF),
            held(hidden, 1),
            held(16, hidden, dtype=BF),
        ],
        place, load_values, load_mask, fixed_mask, frequencies, weight_in, weight_mid,
        weight_out, space=pltpu.HBM,
    )

    loads_ahead = shifted(loads_first, SLAB, -1)
    loads_behind = shifted(loads_last, SLAB, 1)
    network = (x_cos, x_sin, z_cos, z_sin, w_in_t, w_mid_t, w_column, w_row)
    kept = [held(hidden, rows, dtype=BF)] * 4
    cost = pl.CostEstimate(
        flops=(inputs + hidden) * hidden * rows,
        bytes_accessed=4 * hidden * rows,
        transcendentals=hidden * rows,
    )
    outer, stiff_first, stiff_last, *stored = run(
        outer_kernel,
        "outer",
        [held(cells_x, half_rows, cells_z)] + [held(cells_x, 2, cells_z)] * 2 + kept,
        *network,
        scalars=0,
        limit=12,
        cost_estimate=cost,
    )
    planes = cells_x + 5
    slots = 4 * planes + cells_x
    loads, rows_first, rows_last = run(
        pack_kernel,
        "pack",
        [held(4, planes, cells_y, cells_z), held(slots, 3, cells_z), held(slots, 2, cells_z)],
        place, loads, loads_ahead, loads_behind, stiff_first, stiff_last,
    )
    rows_ahead = shifted(rows_first, "z", -1)
    rows_behind = shifted(rows_last, "z", 1)
    density, stiff, *stored = run(
        inner_kernel,
        "inner",
        [held(*field)] * 2 + kept,
        *network,
        outer,
        *stored,
        scalars=0,
        limit=12,
        input_output_aliases={9 + k: 2 + k for k in range(4)},
        cost_estimate=cost,
    )
    hidden_in, slope_mid, slope_in, hidden_mid = stored
    stiff_16, stiff_before, stiff_next = run(
        stiff_rows_kernel,
        "stiff_rows",
        [held(cells_x, ROWS, cells_z), held(2, ROWS, cells_z), held(2, ROWS, cells_z)],
        place, stiff, rows_ahead, rows_behind,
    )
    stiff_ahead = shifted(stiff_before, SLAB, -1)
    stiff_behind = shifted(stiff_next, SLAB, 1)

    back = slope_in
    parts = 2
    for part in range(parts):
        count = rows // parts
        (back,) = run(
            functools.partial(back_kernel, first=part * count, count=count, span=1024),
            f"back_{part}",
            kept[:1],
            w_mid_half,
            slope_mid,
            back,
            scalars=0,
            limit=10,
            input_output_aliases={2: 0},
            cost_estimate=pl.CostEstimate(
                flops=2 * hidden * hidden * count,
                bytes_accessed=6 * hidden * count,
                transcendentals=0,
            ),
        )

    vector = held(3, cells_x + 1, ROWS, cells_z)
    first, second, sums = run(
        krylov_kernel,
        "krylov",
        [vector, vector, held(8, 128)],
        place, loads, rows_ahead, rows_behind, stiff_16, stiff_ahead, stiff_behind, density,
    )
    solution, slope, density = run(
        functools.partial(energy_kernel, elements_total),
        "energy",
        [shaped(3, *field), held(*field), shaped(*field)],
        place, summed(sums), loads, rows_ahead, rows_behind, first, second, density,
    )

    height = hidden + inputs
    groups = hidden // 128
    mine, other, grad_out = run(
        gradient_kernel,
        "gradients",
        [held(groups // 2, height, 128)] * 2 + [held(groups, 128)],
        place, slope, x_cos, x_sin, z_cos, z_sin, hidden_in, slope_mid, back, hidden_mid,
        limit=20,
        scratch=[VM((hidden, hidden), F32), VM((hidden, inputs), F32), VM((hidden, 128), F32)],
    )

    chips = lax.axis_size(CHIPS)
    swap = [(0, 1), (1, 0)]
    half = (mine + lax.ppermute(other, "c", swap)).reshape(chips, -1, 128)
    share = jnp.sum(lax.all_to_all(half, CHIPS, 0, 0), axis=0)
    share = jnp.concatenate([share, grad_out, jnp.zeros_like(grad_out)], axis=0)
    half = lax.all_to_all(jnp.broadcast_to(share[None], (chips,) + share.shape), CHIPS, 0, 0)
    away = lax.ppermute(half, "c", swap)
    grad_in, grad_mid, grad_out = run(
        finish_kernel,
        "finish",
        [shaped(inputs, hidden), shaped(hidden, hidden), shaped(groups, 128)],
        place, half, away,
    )
    return solution, density, grad_in, grad_mid, grad_out.reshape(hidden)


def solution(mesh):
    slab, sub = mesh.devices.shape
    fine = Mesh(mesh.devices.reshape(4, 4, slab // 16, sub), ALL)
    field = P(SLAB, "z", None)
    vector = P(None, SLAB, "z", None)
    return jax.shard_map(
        on_device,
        mesh=fine,
        in_specs=(vector, field, field, P(), P(), P(), P()),
        out_specs=(vector, field, P(), P(), P()),
        check_vma=False,
    )
```

```python
import functools
import itertools
import math

import jax
import jax.numpy as jnp
import numpy as np
from jax import lax
from jax.experimental import pallas as pl
from jax.experimental.pallas import tpu as pltpu
from jax.sharding import Mesh
from jax.sharding import PartitionSpec as P

ITERS = 3
SLAB = ("x", "y", "c")
CHIPS = ("x", "y", "z")
ALL = ("x", "y", "c", "z")
BF = jnp.bfloat16
F32 = jnp.float32

two_pi = 2.0 * math.pi
emin = 0.001
penalty = 4.0
vol_target = 0.3
ROWS = 16
corner_list = list(itertools.product((0, 1), repeat=3))
LAST = (((1,), (1,)), ((), ()))


def hex_stiffness():
    poisson = 0.3
    lame_first = poisson / ((1.0 + poisson) * (1.0 - 2.0 * poisson))
    lame_second = 0.5 / (1.0 + poisson)
    elastic = np.zeros((6, 6))
    elastic[:3, :3] = lame_first
    for axis_number in range(3):
        elastic[axis_number, axis_number] += 2.0 * lame_second
        elastic[axis_number + 3, axis_number + 3] = lame_second
    gauss_points = [0.5 - 0.5 / math.sqrt(3.0), 0.5 + 0.5 / math.sqrt(3.0)]
    matrix = np.zeros((24, 24))
    for location in itertools.product(gauss_points, repeat=3):
        strain = np.zeros((6, 24))
        for corner_number, corner in enumerate(corner_list):
            factors = [
                location[axis] if corner[axis] == 1 else 1.0 - location[axis] for axis in range(3)
            ]
            slopes = [1.0 if corner[axis] == 1 else -1.0 for axis in range(3)]
            derivative = [
                slopes[0] * factors[1] * factors[2],
                factors[0] * slopes[1] * factors[2],
                factors[0] * factors[1] * slopes[2],
            ]
            column = 3 * corner_number
            for axis in range(3):
                strain[axis, column + axis] = derivative[axis]
            strain[3, column + 1] = derivative[2]
            strain[3, column + 2] = derivative[1]
            strain[4, column + 0] = derivative[2]
            strain[4, column + 2] = derivative[0]
            strain[5, column + 0] = derivative[1]
            strain[5, column + 1] = derivative[0]
        matrix += strain.T @ elastic @ strain / 8.0
    return matrix


def modal_stiffness():
    table = hex_stiffness()
    change = np.zeros((24, 24))
    for row, wave in enumerate(corner_list):
        for column, corner in enumerate(corner_list):
            sign = np.prod([1.0 if c == 1 else -1.0 for w, c in zip(wave, corner) if w == 1])
            for d in range(3):
                change[3 * row + d, 3 * column + d] = sign
    modal = change @ table @ change.T / 64.0
    blocks = []
    for parity in corner_list:
        waves = [tuple(parity[a] ^ (a == d) for a in range(3)) for d in range(3)]
        index = [3 * corner_list.index(wave) + d for d, wave in enumerate(waves)]
        block = modal[np.ix_(index, index)]
        blocks.append((waves, np.where(np.abs(block) < 1e-9, 0.0, block)))
    return blocks


BLOCKS = modal_stiffness()


def lane_mask(shape, lane):
    return lax.broadcasted_iota(jnp.int32, shape, len(shape) - 1) == lane


def plane_modes(plane, rows):
    size = plane.shape[-1]
    ahead = jnp.where(lane_mask(plane.shape, size - 1), 0.0, pltpu.roll(plane, size - 1, 1))
    modes = {}
    for wave_z, part in ((0, plane + ahead), (1, ahead - plane)):
        following = pltpu.roll(part, ROWS - 1, 0)
        modes[0, wave_z] = (part + following)[:rows]
        modes[1, wave_z] = (following - part)[:rows]
    return modes


def element_modes(lower, upper):
    found = []
    for low, high in zip(lower, upper):
        modes = {}
        for key in low:
            modes[(0,) + key] = low[key] + high[key]
            modes[(1,) + key] = high[key] - low[key]
        found.append(modes)
    return found


def modal_forces(modes):
    for waves, block in BLOCKS:
        values = [modes[d][waves[d]] for d in range(3)]
        for d in range(3):
            total = None
            for other in range(3):
                if block[d, other] != 0.0:
                    term = np.float32(block[d, other]) * values[other]
                    total = term if total is None else total + term
            if total is not None:
                yield d, waves[d], values[d], total


def energy_of(modes):
    total = None
    for _, _, value, force in modal_forces(modes):
        total = value * force if total is None else total + value * force
    return total


def node_plane(gathered):
    parts = []
    for wave_z in (0, 1):
        even, odd = gathered[0, wave_z], gathered[1, wave_z]
        parts.append((even - odd) + pltpu.roll(even + odd, 1, 0))
    behind = pltpu.roll(parts[0] + parts[1], 1, 1)
    return (parts[0] - parts[1]) + jnp.where(lane_mask(behind.shape, 0), 0.0, behind)


def operator_planes(planes, stiff, free):
    modes = [[plane_modes(component, ROWS) for component in plane] for plane in planes]
    gathered = [[{} for _ in range(3)] for _ in planes]
    for e in range(len(planes) - 1):
        forces = [{} for _ in range(3)]
        for d, wave, _, force in modal_forces(element_modes(modes[e], modes[e + 1])):
            forces[d][wave] = force * stiff[e]
        for d in range(3):
            for key in itertools.product((0, 1), repeat=2):
                even, odd = forces[d].get((0,) + key), forces[d].get((1,) + key)
                for node, sign in ((e, -1), (e + 1, 1)):
                    if even is None:
                        term = odd if sign == 1 else -odd
                    else:
                        term = even + odd if sign == 1 else even - odd
                    held = gathered[node][d]
                    held[key] = term if key not in held else held[key] + term
    return [
        [node_plane(gathered[n][d]) * free[n - 1] for d in range(3)]
        for n in range(1, len(planes) - 1)
    ]


def kept_if(flag):
    return jnp.where(flag == 0, 1.0, 0.0)


def with_rows(place, block, ahead, behind):
    start, stop = kept_if(place[Z_FIRST]), kept_if(place[Z_LAST])
    space = ROWS - block.shape[0] - ahead.shape[0] - behind.shape[0]
    zeros = jnp.zeros((space, block.shape[1]), F32)
    return jnp.concatenate([block, ahead * stop, zeros, behind * start], axis=0)


def load_plane(place, loads, ahead, behind, d, p):
    slot = d * loads.shape[1] + p
    return with_rows(place, loads[d, p], ahead[slot], behind[slot])


def krylov_kernel(place, loads, ahead, behind, stiff, stiff_ahead, stiff_behind, density,
                  first, second, sums):
    planes = loads.shape[1]
    cells = planes - 5
    low, high = kept_if(place[SLAB_FIRST]), kept_if(place[SLAB_LAST])
    stiff_planes = [stiff_behind[p] * low for p in range(2)]
    stiff_planes += [stiff[p] for p in range(cells)]
    stiff_planes += [stiff_ahead[p] * high for p in range(2)]
    loaded = [
        [load_plane(place, loads, ahead, behind, d, p) for d in range(4)] for p in range(planes)
    ]
    force = [plane[:3] for plane in loaded]
    free = [plane[3] for plane in loaded]
    image = operator_planes(force, stiff_planes, free[1:-1])
    twice = operator_planes(image, stiff_planes[1:-1], free[2:-2])
    own = (force[2 : 2 + cells], image[1 : 1 + cells], twice[:cells])
    rows = density.shape[1]

    def dot(left, right):
        total = None
        for p in range(cells):
            for d in range(3):
                term = left[p][d][:rows] * right[p][d][:rows]
                total = term if total is None else total + term
        return total

    totals = [dot(own[k // 2], own[(k + 1) // 2]) for k in range(2 * ITERS - 1)]
    modes = [[plane_modes(component, rows) for component in plane] for plane in twice]
    last = None
    volume = None
    for e in range(cells):
        term = stiff_planes[2 + e][:rows] * energy_of(element_modes(modes[e], modes[e + 1]))
        last = term if last is None else last + term
        volume = density[e] if volume is None else volume + density[e]
    totals += [last, volume]
    row_number = lax.broadcasted_iota(jnp.int32, sums.shape, 0)
    result = jnp.zeros(sums.shape, F32)
    for k, total in enumerate(totals):
        scalar = jnp.sum(jnp.sum(total, axis=0, keepdims=True), axis=1, keepdims=True)
        result = jnp.where(row_number == k, scalar, result)
    sums[...] = result
    for p in range(cells + 1):
        for d in range(3):
            first[d, p] = image[1 + p][d]
            second[d, p] = twice[p][d]


def krylov_steps(moments):
    mean = moments[1] / moments[0]
    powers = [None, mean]
    for k in range(2, 2 * ITERS):
        powers.append(powers[-1] * mean)
    scaled = [moments[k] / moments[0] / powers[k] if k else 1.0 for k in range(2 * ITERS)]

    def product(left, right, shift):
        return sum(
            left[i] * right[j] * scaled[i + j + shift]
            for i in range(len(left))
            for j in range(len(right))
        )

    solution = [0.0] * ITERS
    residual = [1.0]
    direction = [1.0]
    norm_now = scaled[0]
    work = 0.0
    for iteration in range(ITERS):
        alpha = norm_now / product(direction, direction, 1)
        work = work + alpha * norm_now
        solution = [
            solution[i] + (alpha * direction[i] if i < len(direction) else 0.0)
            for i in range(ITERS)
        ]
        if iteration + 1 < ITERS:
            image = [0.0] + direction
            residual = [
                (residual[i] if i < len(residual) else 0.0) - alpha * image[i]
                for i in range(len(image))
            ]
            norm_next = product(residual, residual, 0)
            beta = norm_next / norm_now
            direction = [
                residual[i] + (beta * direction[i] if i < len(direction) else 0.0)
                for i in range(len(residual))
            ]
            norm_now = norm_next
    factors = [solution[i] / powers[i + 1] for i in range(ITERS)]
    return factors, work * moments[0] / mean


def energy_kernel(
    elements, place, sums, loads, ahead, behind, first, second, density, solution, slope, out
):
    rows_of = [sums[k : k + 1, :] for k in range(2 * ITERS + 1)]
    factors, compliance = krylov_steps(rows_of[: 2 * ITERS])
    volume = rows_of[2 * ITERS]
    constant = 2.0 * penalty * (volume / elements - vol_target) / elements
    scale = -3.0 * (1.0 - emin) / compliance
    wide = [jnp.concatenate([value, value], axis=1) for value in factors + [scale, constant]]
    cells, rows, _ = density.shape
    modes = []
    for p in range(cells + 1):
        plane = []
        for d in range(3):
            load = load_plane(place, loads, ahead, behind, d, 2 + p)
            value = wide[0] * load + wide[1] * first[d, p] + wide[2] * second[d, p]
            if p < cells:
                solution[d, p] = value[:rows]
            plane.append(plane_modes(value, rows))
        modes.append(plane)
    for e in range(cells):
        energy = energy_of(element_modes(modes[e], modes[e + 1]))
        held = density[e]
        out[e] = held
        slope[e] = (wide[3] * held * held * energy + wide[4]) * held * (1.0 - held)


def column_of(line):
    size = line.shape[1]
    shape = (size, size)
    same = lax.broadcasted_iota(jnp.int32, shape, 0) == lax.broadcasted_iota(jnp.int32, shape, 1)
    return jnp.sum(jnp.where(same, line, 0.0), axis=1, keepdims=True)


def prepare_kernel(
    grid_cells, place, load_values, load_mask, fixed_mask, frequencies, w_in, w_mid, w_out,
    loads, loads_first, loads_last, x_cos, x_sin, z_cos, z_sin, w_in_t, w_mid_t, w_mid_half,
    w_column, w_row,
):
    cells, rows, size = load_mask.shape
    free = (1 - fixed_mask[...]).astype(F32)
    held = free * load_mask[...].astype(F32)
    for d in range(4):
        field = free if d == 3 else held * load_values[d]
        loads[d] = field
        loads_first[d] = field[:3]
        loads_last[d] = field[cells - 2 :]
    columns = [column_of(frequencies[k : k + 1, :]) for k in range(3)]
    half = rows // 2
    lanes = 2 * cells * half
    number = lax.broadcasted_iota(jnp.int32, (1, lanes), 1)
    side = number // (cells * half)
    plane = (number // half) % cells
    inner = number % half
    row = jnp.where(side == 1, inner + 2, jnp.where(inner < 2, inner, inner + half))
    x_centre = ((place[X_FIRST] + plane).astype(F32) + 0.5) / grid_cells[0]
    y_centre = ((place[Y_FIRST] + row).astype(F32) + 0.5) / grid_cells[1]
    phase = two_pi * (x_centre * columns[0] + y_centre * columns[1])
    cos, sin = jnp.cos(phase), jnp.sin(phase)
    for k in range(2 * cells):
        x_cos[k] = cos[:, k * half : (k + 1) * half]
        x_sin[k] = sin[:, k * half : (k + 1) * half]
    z_number = lax.broadcasted_iota(jnp.int32, (1, size), 1)
    phase = two_pi * (((z_number.astype(F32) + 0.5) / grid_cells[2]) * columns[2])
    z_cos[...] = jnp.cos(phase)
    z_sin[...] = jnp.sin(phase)
    w_in_t[...] = (0.5 * w_in[...].astype(F32)).T.astype(BF)
    middle = 0.5 * w_mid[...].astype(F32)
    w_mid_half[...] = middle.astype(BF)
    w_mid_t[...] = middle.T.astype(BF)
    line = w_out[...].astype(F32)[None, :]
    w_column[...] = 0.5 * column_of(line)
    w_row[...] = jnp.broadcast_to(line, w_row.shape).astype(BF)


def pack_kernel(place, loads, loads_ahead, loads_behind, stiff_first, stiff_last,
                planes, to_before, to_next):
    low, high = kept_if(place[SLAB_FIRST]), kept_if(place[SLAB_LAST])
    cells, rows = loads.shape[1:3]
    count = planes.shape[1]
    for d in range(4):
        for p in range(count):
            if p < 2:
                block = loads_behind[d, p] * low
            elif p < 2 + cells:
                block = loads[d, p - 2]
            else:
                block = loads_ahead[d, p - 2 - cells] * high
            planes[d, p] = block
            to_before[d * count + p] = block[:3]
            to_next[d * count + p] = block[rows - 2 :]
    for p in range(cells):
        to_before[4 * count + p, :2, :] = stiff_first[p]
        to_before[4 * count + p, 2:, :] = stiff_first[p, 1:]
        to_next[4 * count + p] = stiff_last[p]


def stiff_rows_kernel(place, stiff, ahead, behind, joined, to_before, to_next):
    cells = stiff.shape[0]
    first = ahead.shape[0] - cells
    for p in range(cells):
        block = with_rows(place, stiff[p], ahead[first + p, :2, :], behind[first + p])
        joined[p] = block
        if p < to_before.shape[0]:
            to_before[p] = block
        if p >= cells - to_next.shape[0]:
            to_next[p - (cells - to_next.shape[0])] = block


def gated(half):
    up = 1.0 + jnp.tanh(half)
    value = half * up
    return value, up + value * (2.0 - up)


def features_of(tables, group, column, scale=None):
    x_cos, x_sin, z_cos, z_sin = tables
    cos = x_cos[group, :, column : column + 1]
    sin = x_sin[group, :, column : column + 1]
    upper = z_cos[...] * cos - z_sin[...] * sin
    lower = z_sin[...] * cos + z_cos[...] * sin
    if scale is not None:
        upper, lower = upper * scale, lower * scale
    return jnp.concatenate([upper, lower], 0).astype(BF)


def forward_columns(tables, group, weights, kept, spans):
    w_in, w_mid, w_column, w_row = weights
    hidden_in, slope_mid, slope_in, hidden_mid = kept

    def keep(array, value):
        for start, first, count in spans:
            array[:, pl.ds(start, count)] = value[:, first : first + count]

    columns = tables[0].shape[2]
    features = jnp.concatenate([features_of(tables, group, q) for q in range(columns)], 1)
    value, slope = gated(jnp.dot(w_in[...], features, preferred_element_type=F32))
    value = value.astype(BF)
    keep(hidden_in, value)
    keep(slope_in, slope.astype(BF))
    value, slope = gated(jnp.dot(w_mid[...], value, preferred_element_type=F32))
    value = value.astype(BF)
    keep(hidden_mid, value)
    keep(slope_mid, (w_column[...] * slope).astype(BF))
    logits = jnp.dot(w_row[...], value, preferred_element_type=F32)[:1]
    return 0.5 * jnp.tanh(0.5 * logits) + 0.5


def stiffness_of(density):
    return emin + (1.0 - emin) * (density * density * density)


def outer_kernel(
    x_cos, x_sin, z_cos, z_sin, w_in, w_mid, w_column, w_row,
    density, stiff_first, stiff_last, *kept,
):
    tables, weights = (x_cos, x_sin, z_cos, z_sin), (w_in, w_mid, w_column, w_row)
    cells, _, size = density.shape

    @pl.loop(0, cells)
    def _(p):
        start = pl.multiple_of(p * (8 * size), 8 * size)
        spans = [(start, 0, 2 * size), (start + 6 * size, 2 * size, 2 * size)]
        line = forward_columns(tables, p, weights, kept, spans)
        for q in range(4):
            part = line[:, q * size : (q + 1) * size]
            density[p, q : q + 1, :] = part
            (stiff_first if q < 2 else stiff_last)[p, q % 2 : q % 2 + 1, :] = stiffness_of(part)


def inner_kernel(
    x_cos, x_sin, z_cos, z_sin, w_in, w_mid, w_column, w_row, outer, *rest,
):
    tables, weights = (x_cos, x_sin, z_cos, z_sin), (w_in, w_mid, w_column, w_row)
    density, stiff = rest[4:6]
    cells, rows, size = density.shape

    @pl.loop(0, cells)
    def _(p):
        start = pl.multiple_of(p * (8 * size), 8 * size)
        spans = [(start + 2 * size, 0, 4 * size)]
        line = forward_columns(tables, cells + p, weights, rest[6:], spans)
        for r in range(rows):
            if 2 <= r < 6:
                part = line[:, (r - 2) * size : (r - 1) * size]
            else:
                q = r if r < 2 else r - 4
                part = outer[p, q : q + 1, :]
            density[p, r : r + 1, :] = part
            stiff[p, r : r + 1, :] = stiffness_of(part)


def back_kernel(w_mid, slope_mid, slope_in, back, *, first, count, span):
    for start in range(first, first + count, span):
        place = slice(start, start + span)
        product = jnp.dot(w_mid[...], slope_mid[:, place], preferred_element_type=F32)
        back[:, place] = (product * slope_in[:, place].astype(F32)).astype(BF)


def gradient_kernel(
    place, slope, x_cos, x_sin, z_cos, z_sin, hidden_in, slope_mid, back, hidden_mid,
    mine, other, grad_out, mid, first, running,
):
    tables = (x_cos, x_sin, z_cos, z_sin)
    cells, rows, size = slope.shape
    half = rows // 2
    group_of = [(0, r) if r < 2 else (0, r - half) if r >= rows - 2 else (1, r - 2) for r in range(rows)]
    for p in range(cells):
        lines = [slope[p, r : r + 1, :] for r in range(rows)]
        picked = [
            features_of(tables, side * cells + p, q, line) for (side, q), line in zip(group_of, lines)
        ]
        features = jnp.concatenate(picked, 1)
        line = jnp.concatenate(lines, 1)
        span = slice(p * rows * size, (p + 1) * rows * size)
        hidden = (hidden_in[:, span].astype(F32) * line).astype(BF)
        product = hidden_mid[:, span].astype(F32) * line
        total = product[:, :128]
        for k in range(1, rows * size // 128):
            total = total + product[:, k * 128 : (k + 1) * 128]
        terms = (
            lax.dot_general(hidden, slope_mid[:, span], LAST, preferred_element_type=F32),
            lax.dot_general(back[:, span], features, LAST, preferred_element_type=F32),
            total,
        )
        for held, term in zip((mid, first, running), terms):
            if p == 0:
                held[...] = term
            else:
                held[...] += term
    core = place[CORE]
    height = mid.shape[0]
    first_t = first[...].T
    for k in range(2):
        for owner in range(2):
            lanes = slice((2 * owner + k) * 128, (2 * owner + k + 1) * 128)

            @pl.when(core == owner)
            def _():
                mine[k, :height, :] = mid[:, lanes]
                mine[k, height:, :] = first_t[:, lanes]

            @pl.when(core != owner)
            def _():
                other[k, :height, :] = mid[:, lanes]
                other[k, height:, :] = first_t[:, lanes]

    line = jnp.sum(running[...].T, axis=0, keepdims=True)
    for k in range(grad_out.shape[0]):
        grad_out[k : k + 1, :] = line[:, k * 128 : (k + 1) * 128]


def finish_kernel(place, half, away, grad_in, grad_mid, grad_out):
    chips = half.shape[0]
    height = half.shape[1] - 2 * grad_out.shape[0]
    middle = grad_mid.shape[0]
    at_first = place[CORE] == 0
    for group in range(4):
        part = pl.ds((group % 2) * (chips // 2), chips // 2)
        own, far = half[part, :height, :], away[part, :height, :]
        picked = jnp.where(at_first, own, far) if group < 2 else jnp.where(at_first, far, own)
        picked = picked.reshape(-1, 128)
        lanes = slice(group * 128, (group + 1) * 128)
        grad_mid[:, lanes] = picked[:middle]
        grad_in[:, lanes] = picked[middle:]
    out = jnp.sum(half[:, height:, :], axis=0) + jnp.sum(away[:, height:, :], axis=0)
    grad_out[...] = out[: grad_out.shape[0]]


VM = pltpu.VMEM
WHOLE = pl.BlockSpec(memory_space=pltpu.VMEM)
SCALARS = pl.BlockSpec(memory_space=pltpu.SMEM)
X_FIRST, Y_FIRST, CORE, SLAB_FIRST, SLAB_LAST, Z_FIRST, Z_LAST = range(7)


def params(mebibytes=8):
    return pltpu.CompilerParams(vmem_limit_bytes=mebibytes << 20)


def shaped(*shape, dtype=F32):
    return jax.ShapeDtypeStruct(shape, dtype)


def held(*shape, dtype=F32):
    return VM(shape, dtype)


def run(kernel, name, out_shape, *operands, scalars=1, space=pltpu.VMEM, scratch=(), limit=8, **more):
    arrays = [pltpu.with_memory_space_constraint(array, space) for array in operands[scalars:]]
    return pl.pallas_call(
        kernel,
        name=name,
        in_specs=[SCALARS] * scalars + [WHOLE] * len(arrays),
        out_specs=[WHOLE] * len(out_shape),
        out_shape=out_shape,
        scratch_shapes=list(scratch),
        compiler_params=params(limit),
        **more,
    )(*operands[:scalars], *arrays)


def shifted(block, axis, distance):
    size = lax.axis_size(axis)
    return lax.ppermute(block, axis, [(i, (i + distance) % size) for i in range(size)])


def summed(values):
    values = values + lax.ppermute(values, "c", [(0, 1), (1, 0)])
    for axis in ("z", "y", "x"):
        others = [shifted(values, axis, k) for k in range(1, lax.axis_size(axis))]
        values = values + sum(others)
    return values


def on_device(load_values, load_mask, fixed_mask, frequencies, weight_in, weight_mid, weight_out):
    cells_x, cells_y, cells_z = fixed_mask.shape
    slab, sub = lax.axis_index(SLAB), lax.axis_index("z")
    slabs, subs = lax.axis_size(SLAB), lax.axis_size("z")
    grid_cells = (cells_x * slabs, cells_y * subs, cells_z)
    elements_total = grid_cells[0] * grid_cells[1] * grid_cells[2]
    place = jnp.stack(
        [slab * cells_x, sub * cells_y, lax.axis_index("c")]
        + [(slab == 0) * 1, (slab == slabs - 1) * 1, (sub == 0) * 1, (sub == subs - 1) * 1, slab * 0]
    ).astype(jnp.int32)
    inputs, hidden = weight_in.shape
    rows = cells_x * cells_y * cells_z
    half_rows = cells_y // 2
    field = (cells_x, cells_y, cells_z)
    table = held(2 * cells_x, inputs // 2, half_rows)
    line = held(inputs // 2, cells_z)
    (
        loads, loads_first, loads_last, x_cos, x_sin, z_cos, z_sin,
        w_in_t, w_mid_t, w_mid_half, w_column, w_row,
    ) = run(
        functools.partial(prepare_kernel, grid_cells),
        "prepare",
        [
            held(4, *field),
            held(4, 3, cells_y, cells_z),
            held(4, 2, cells_y, cells_z),
            table,
            table,
            line,
            line,
            held(hidden, inputs, dtype=BF),
            held(hidden, hidden, dtype=BF),
            held(hidden, hidden, dtype=BF),
            held(hidden, 1),
            held(16, hidden, dtype=BF),
        ],
        place, load_values, load_mask, fixed_mask, frequencies, weight_in, weight_mid,
        weight_out, space=pltpu.HBM,
    )

    loads_ahead = shifted(loads_first, SLAB, -1)
    loads_behind = shifted(loads_last, SLAB, 1)
    network = (x_cos, x_sin, z_cos, z_sin, w_in_t, w_mid_t, w_column, w_row)
    kept = [held(hidden, rows, dtype=BF)] * 4
    cost = pl.CostEstimate(
        flops=(inputs + hidden) * hidden * rows,
        bytes_accessed=4 * hidden * rows,
        transcendentals=hidden * rows,
    )
    outer, stiff_first, stiff_last, *stored = run(
        outer_kernel,
        "outer",
        [held(cells_x, half_rows, cells_z)] + [held(cells_x, 2, cells_z)] * 2 + kept,
        *network,
        scalars=0,
        limit=12,
        cost_estimate=cost,
    )
    planes = cells_x + 5
    slots = 4 * planes + cells_x
    loads, rows_first, rows_last = run(
        pack_kernel,
        "pack",
        [held(4, planes, cells_y, cells_z), held(slots, 3, cells_z), held(slots, 2, cells_z)],
        place, loads, loads_ahead, loads_behind, stiff_first, stiff_last,
    )
    rows_ahead = shifted(rows_first, "z", -1)
    rows_behind = shifted(rows_last, "z", 1)
    density, stiff, *stored = run(
        inner_kernel,
        "inner",
        [held(*field)] * 2 + kept,
        *network,
        outer,
        *stored,
        scalars=0,
        limit=12,
        input_output_aliases={9 + k: 2 + k for k in range(4)},
        cost_estimate=cost,
    )
    hidden_in, slope_mid, slope_in, hidden_mid = stored
    stiff_16, stiff_before, stiff_next = run(
        stiff_rows_kernel,
        "stiff_rows",
        [held(cells_x, ROWS, cells_z), held(2, ROWS, cells_z), held(2, ROWS, cells_z)],
        place, stiff, rows_ahead, rows_behind,
    )
    stiff_ahead = shifted(stiff_before, SLAB, -1)
    stiff_behind = shifted(stiff_next, SLAB, 1)

    back = slope_in
    parts = 2
    for part in range(parts):
        count = rows // parts
        (back,) = run(
            functools.partial(back_kernel, first=part * count, count=count, span=1024),
            f"back_{part}",
            kept[:1],
            w_mid_half,
            slope_mid,
            back,
            scalars=0,
            limit=10,
            input_output_aliases={2: 0},
            cost_estimate=pl.CostEstimate(
                flops=2 * hidden * hidden * count,
                bytes_accessed=6 * hidden * count,
                transcendentals=0,
            ),
        )

    vector = held(3, cells_x + 1, ROWS, cells_z)
    first, second, sums = run(
        krylov_kernel,
        "krylov",
        [vector, vector, held(8, 128)],
        place, loads, rows_ahead, rows_behind, stiff_16, stiff_ahead, stiff_behind, density,
    )
    solution, slope, density = run(
        functools.partial(energy_kernel, elements_total),
        "energy",
        [shaped(3, *field), held(*field), shaped(*field)],
        place, summed(sums), loads, rows_ahead, rows_behind, first, second, density,
    )

    height = hidden + inputs
    groups = hidden // 128
    mine, other, grad_out = run(
        gradient_kernel,
        "gradients",
        [held(groups // 2, height, 128)] * 2 + [held(groups, 128)],
        place, slope, x_cos, x_sin, z_cos, z_sin, hidden_in, slope_mid, back, hidden_mid,
        limit=20,
        scratch=[VM((hidden, hidden), F32), VM((hidden, inputs), F32), VM((hidden, 128), F32)],
    )

    chips = lax.axis_size(CHIPS)
    swap = [(0, 1), (1, 0)]
    half = (mine + lax.ppermute(other, "c", swap)).reshape(chips, -1, 128)
    share = jnp.sum(lax.all_to_all(half, CHIPS, 0, 0), axis=0)
    share = jnp.concatenate([share, grad_out, jnp.zeros_like(grad_out)], axis=0)
    half = lax.all_to_all(jnp.broadcast_to(share[None], (chips,) + share.shape), CHIPS, 0, 0)
    away = lax.ppermute(half, "c", swap)
    grad_in, grad_mid, grad_out = run(
        finish_kernel,
        "finish",
        [shaped(inputs, hidden), shaped(hidden, hidden), shaped(groups, 128)],
        place, half, away,
    )
    return solution, density, grad_in, grad_mid, grad_out.reshape(hidden)


def solution(mesh):
    slab, sub = mesh.devices.shape
    fine = Mesh(mesh.devices.reshape(4, 4, slab // 16, sub), ALL)
    field = P(SLAB, "z", None)
    vector = P(None, SLAB, "z", None)
    return jax.shard_map(
        on_device,
        mesh=fine,
        in_specs=(vector, field, field, P(), P(), P(), P()),
        out_specs=(vector, field, P(), P(), P()),
        check_vma=False,
    )
```

```python
import functools
import itertools
import math

import jax
import jax.numpy as jnp
import numpy as np
from jax import lax
from jax.experimental import pallas as pl
from jax.experimental.pallas import tpu as pltpu
from jax.sharding import Mesh
from jax.sharding import PartitionSpec as P

ITERS = 3
SLAB = ("x", "y", "c")
CHIPS = ("x", "y", "z")
ALL = ("x", "y", "c", "z")
BF = jnp.bfloat16
F32 = jnp.float32

two_pi = 2.0 * math.pi
emin = 0.001
penalty = 4.0
vol_target = 0.3
ROWS = 16
corner_list = list(itertools.product((0, 1), repeat=3))
LAST = (((1,), (1,)), ((), ()))


def hex_stiffness():
    poisson = 0.3
    lame_first = poisson / ((1.0 + poisson) * (1.0 - 2.0 * poisson))
    lame_second = 0.5 / (1.0 + poisson)
    elastic = np.zeros((6, 6))
    elastic[:3, :3] = lame_first
    for axis_number in range(3):
        elastic[axis_number, axis_number] += 2.0 * lame_second
        elastic[axis_number + 3, axis_number + 3] = lame_second
    gauss_points = [0.5 - 0.5 / math.sqrt(3.0), 0.5 + 0.5 / math.sqrt(3.0)]
    matrix = np.zeros((24, 24))
    for location in itertools.product(gauss_points, repeat=3):
        strain = np.zeros((6, 24))
        for corner_number, corner in enumerate(corner_list):
            factors = [
                location[axis] if corner[axis] == 1 else 1.0 - location[axis] for axis in range(3)
            ]
            slopes = [1.0 if corner[axis] == 1 else -1.0 for axis in range(3)]
            derivative = [
                slopes[0] * factors[1] * factors[2],
                factors[0] * slopes[1] * factors[2],
                factors[0] * factors[1] * slopes[2],
            ]
            column = 3 * corner_number
            for axis in range(3):
                strain[axis, column + axis] = derivative[axis]
            strain[3, column + 1] = derivative[2]
            strain[3, column + 2] = derivative[1]
            strain[4, column + 0] = derivative[2]
            strain[4, column + 2] = derivative[0]
            strain[5, column + 0] = derivative[1]
            strain[5, column + 1] = derivative[0]
        matrix += strain.T @ elastic @ strain / 8.0
    return matrix


def modal_stiffness():
    table = hex_stiffness()
    change = np.zeros((24, 24))
    for row, wave in enumerate(corner_list):
        for column, corner in enumerate(corner_list):
            sign = np.prod([1.0 if c == 1 else -1.0 for w, c in zip(wave, corner) if w == 1])
            for d in range(3):
                change[3 * row + d, 3 * column + d] = sign
    modal = change @ table @ change.T / 64.0
    blocks = []
    for parity in corner_list:
        waves = [tuple(parity[a] ^ (a == d) for a in range(3)) for d in range(3)]
        index = [3 * corner_list.index(wave) + d for d, wave in enumerate(waves)]
        block = modal[np.ix_(index, index)]
        blocks.append((waves, np.where(np.abs(block) < 1e-9, 0.0, block)))
    return blocks


BLOCKS = modal_stiffness()


def lane_mask(shape, lane):
    return lax.broadcasted_iota(jnp.int32, shape, len(shape) - 1) == lane


def plane_modes(plane, rows):
    size = plane.shape[-1]
    ahead = jnp.where(lane_mask(plane.shape, size - 1), 0.0, pltpu.roll(plane, size - 1, 1))
    modes = {}
    for wave_z, part in ((0, plane + ahead), (1, ahead - plane)):
        following = pltpu.roll(part, ROWS - 1, 0)
        modes[0, wave_z] = (part + following)[:rows]
        modes[1, wave_z] = (following - part)[:rows]
    return modes


def element_modes(lower, upper):
    found = []
    for low, high in zip(lower, upper):
        modes = {}
        for key in low:
            modes[(0,) + key] = low[key] + high[key]
            modes[(1,) + key] = high[key] - low[key]
        found.append(modes)
    return found


def modal_forces(modes):
    for waves, block in BLOCKS:
        values = [modes[d][waves[d]] for d in range(3)]
        for d in range(3):
            total = None
            for other in range(3):
                if block[d, other] != 0.0:
                    term = np.float32(block[d, other]) * values[other]
                    total = term if total is None else total + term
            if total is not None:
                yield d, waves[d], values[d], total


def energy_of(modes):
    total = None
    for _, _, value, force in modal_forces(modes):
        total = value * force if total is None else total + value * force
    return total


def node_plane(gathered):
    parts = []
    for wave_z in (0, 1):
        even, odd = gathered[0, wave_z], gathered[1, wave_z]
        parts.append((even - odd) + pltpu.roll(even + odd, 1, 0))
    behind = pltpu.roll(parts[0] + parts[1], 1, 1)
    return (parts[0] - parts[1]) + jnp.where(lane_mask(behind.shape, 0), 0.0, behind)


def operator_planes(planes, stiff, free):
    modes = [[plane_modes(component, ROWS) for component in plane] for plane in planes]
    gathered = [[{} for _ in range(3)] for _ in planes]
    for e in range(len(planes) - 1):
        forces = [{} for _ in range(3)]
        for d, wave, _, force in modal_forces(element_modes(modes[e], modes[e + 1])):
            forces[d][wave] = force * stiff[e]
        for d in range(3):
            for key in itertools.product((0, 1), repeat=2):
                even, odd = forces[d].get((0,) + key), forces[d].get((1,) + key)
                for node, sign in ((e, -1), (e + 1, 1)):
                    if even is None:
                        term = odd if sign == 1 else -odd
                    else:
                        term = even + odd if sign == 1 else even - odd
                    held = gathered[node][d]
                    held[key] = term if key not in held else held[key] + term
    return [
        [node_plane(gathered[n][d]) * free[n - 1] for d in range(3)]
        for n in range(1, len(planes) - 1)
    ]


def kept_if(flag):
    return jnp.where(flag == 0, 1.0, 0.0)


def with_rows(place, block, ahead, behind):
    start, stop = kept_if(place[Z_FIRST]), kept_if(place[Z_LAST])
    space = ROWS - block.shape[0] - ahead.shape[0] - behind.shape[0]
    zeros = jnp.zeros((space, block.shape[1]), F32)
    return jnp.concatenate([block, ahead * stop, zeros, behind * start], axis=0)


def load_plane(place, loads, ahead, behind, d, p):
    slot = d * loads.shape[1] + p
    return with_rows(place, loads[d, p], ahead[slot], behind[slot])


def krylov_kernel(place, loads, ahead, behind, stiff, stiff_ahead, stiff_behind, density,
                  ready, first, second, sums):
    planes = loads.shape[1]
    cells = planes - 5
    low, high = kept_if(place[SLAB_FIRST]), kept_if(place[SLAB_LAST])
    stiff_planes = [stiff_behind[p] * low for p in range(2)]
    stiff_planes += [stiff[p] for p in range(cells)]
    stiff_planes += [stiff_ahead[p] * high for p in range(2)]
    loaded = [
        [load_plane(place, loads, ahead, behind, d, p) for d in range(4)] for p in range(planes)
    ]
    force = [plane[:3] for plane in loaded]
    free = [plane[3] for plane in loaded]
    image = operator_planes(force, stiff_planes, free[1:-1])
    twice = operator_planes(image, stiff_planes[1:-1], free[2:-2])
    own = (force[2 : 2 + cells], image[1 : 1 + cells], twice[:cells])
    rows = density.shape[1]

    def dot(left, right):
        total = None
        for p in range(cells):
            for d in range(3):
                term = left[p][d][:rows] * right[p][d][:rows]
                total = term if total is None else total + term
        return total

    totals = [dot(own[k // 2], own[(k + 1) // 2]) for k in range(2 * ITERS - 1)]
    modes = [[plane_modes(component, rows) for component in plane] for plane in twice]
    last = None
    volume = None
    for e in range(cells):
        term = stiff_planes[2 + e][:rows] * energy_of(element_modes(modes[e], modes[e + 1]))
        last = term if last is None else last + term
        volume = density[e] if volume is None else volume + density[e]
    totals += [last, volume]
    row_number = lax.broadcasted_iota(jnp.int32, sums.shape, 0)
    result = jnp.zeros(sums.shape, F32)
    for k, total in enumerate(totals):
        scalar = jnp.sum(jnp.sum(total, axis=0, keepdims=True), axis=1, keepdims=True)
        result = jnp.where(row_number == k, scalar, result)
    sums[...] = result
    for p in range(cells + 1):
        for d in range(3):
            first[d, p] = image[1 + p][d]
            second[d, p] = twice[p][d]


def krylov_steps(moments):
    mean = moments[1] / moments[0]
    powers = [None, mean]
    for k in range(2, 2 * ITERS):
        powers.append(powers[-1] * mean)
    scaled = [moments[k] / moments[0] / powers[k] if k else 1.0 for k in range(2 * ITERS)]

    def product(left, right, shift):
        return sum(
            left[i] * right[j] * scaled[i + j + shift]
            for i in range(len(left))
            for j in range(len(right))
        )

    solution = [0.0] * ITERS
    residual = [1.0]
    direction = [1.0]
    norm_now = scaled[0]
    work = 0.0
    for iteration in range(ITERS):
        alpha = norm_now / product(direction, direction, 1)
        work = work + alpha * norm_now
        solution = [
            solution[i] + (alpha * direction[i] if i < len(direction) else 0.0)
            for i in range(ITERS)
        ]
        if iteration + 1 < ITERS:
            image = [0.0] + direction
            residual = [
                (residual[i] if i < len(residual) else 0.0) - alpha * image[i]
                for i in range(len(image))
            ]
            norm_next = product(residual, residual, 0)
            beta = norm_next / norm_now
            direction = [
                residual[i] + (beta * direction[i] if i < len(direction) else 0.0)
                for i in range(len(residual))
            ]
            norm_now = norm_next
    factors = [solution[i] / powers[i + 1] for i in range(ITERS)]
    return factors, work * moments[0] / mean


def energy_kernel(
    elements, place, sums, loads, ahead, behind, first, second, density, solution, slope, out
):
    rows_of = [sums[k : k + 1, :] for k in range(2 * ITERS + 1)]
    factors, compliance = krylov_steps(rows_of[: 2 * ITERS])
    volume = rows_of[2 * ITERS]
    constant = 2.0 * penalty * (volume / elements - vol_target) / elements
    scale = -3.0 * (1.0 - emin) / compliance
    wide = [jnp.concatenate([value, value], axis=1) for value in factors + [scale, constant]]
    cells, rows, _ = density.shape
    modes = []
    for p in range(cells + 1):
        plane = []
        for d in range(3):
            load = load_plane(place, loads, ahead, behind, d, 2 + p)
            value = wide[0] * load + wide[1] * first[d, p] + wide[2] * second[d, p]
            if p < cells:
                solution[d, p] = value[:rows]
            plane.append(plane_modes(value, rows))
        modes.append(plane)
    for e in range(cells):
        energy = energy_of(element_modes(modes[e], modes[e + 1]))
        held = density[e]
        out[e] = held
        slope[e] = (wide[3] * held * held * energy + wide[4]) * held * (1.0 - held)


def column_of(line):
    size = line.shape[1]
    shape = (size, size)
    same = lax.broadcasted_iota(jnp.int32, shape, 0) == lax.broadcasted_iota(jnp.int32, shape, 1)
    return jnp.sum(jnp.where(same, line, 0.0), axis=1, keepdims=True)


def prepare_kernel(
    grid_cells, place, load_values, load_mask, fixed_mask, frequencies, w_in, w_mid, w_out,
    loads, loads_first, loads_last, x_cos, x_sin, z_cos, z_sin, w_in_t, w_mid_t, w_mid_half,
    w_column, w_row,
):
    cells, rows, size = load_mask.shape
    free = (1 - fixed_mask[...]).astype(F32)
    held = free * load_mask[...].astype(F32)
    for d in range(4):
        field = free if d == 3 else held * load_values[d]
        loads[d] = field
        loads_first[d] = field[:3]
        loads_last[d] = field[cells - 2 :]
    columns = [column_of(frequencies[k : k + 1, :]) for k in range(3)]
    half = rows // 2
    lanes = 2 * cells * half
    number = lax.broadcasted_iota(jnp.int32, (1, lanes), 1)
    side = number // (cells * half)
    plane = (number // half) % cells
    inner = number % half
    row = jnp.where(side == 1, inner + 2, jnp.where(inner < 2, inner, inner + half))
    x_centre = ((place[X_FIRST] + plane).astype(F32) + 0.5) / grid_cells[0]
    y_centre = ((place[Y_FIRST] + row).astype(F32) + 0.5) / grid_cells[1]
    phase = two_pi * (x_centre * columns[0] + y_centre * columns[1])
    cos, sin = jnp.cos(phase), jnp.sin(phase)
    for k in range(2 * cells):
        x_cos[k] = cos[:, k * half : (k + 1) * half]
        x_sin[k] = sin[:, k * half : (k + 1) * half]
    z_number = lax.broadcasted_iota(jnp.int32, (1, size), 1)
    phase = two_pi * (((z_number.astype(F32) + 0.5) / grid_cells[2]) * columns[2])
    z_cos[...] = jnp.cos(phase)
    z_sin[...] = jnp.sin(phase)
    w_in_t[...] = (0.5 * w_in[...].astype(F32)).T.astype(BF)
    middle = 0.5 * w_mid[...].astype(F32)
    w_mid_half[...] = middle.astype(BF)
    w_mid_t[...] = middle.T.astype(BF)
    line = w_out[...].astype(F32)[None, :]
    w_column[...] = 0.5 * column_of(line)
    w_row[...] = jnp.broadcast_to(line, w_row.shape).astype(BF)


def pack_kernel(place, loads, loads_ahead, loads_behind, stiff_first, stiff_last,
                planes, to_before, to_next):
    low, high = kept_if(place[SLAB_FIRST]), kept_if(place[SLAB_LAST])
    cells, rows = loads.shape[1:3]
    count = planes.shape[1]
    for d in range(4):
        for p in range(count):
            if p < 2:
                block = loads_behind[d, p] * low
            elif p < 2 + cells:
                block = loads[d, p - 2]
            else:
                block = loads_ahead[d, p - 2 - cells] * high
            planes[d, p] = block
            to_before[d * count + p] = block[:3]
            to_next[d * count + p] = block[rows - 2 :]
    for p in range(cells):
        to_before[4 * count + p, :2, :] = stiff_first[p]
        to_before[4 * count + p, 2:, :] = stiff_first[p, 1:]
        to_next[4 * count + p] = stiff_last[p]


def stiff_rows_kernel(place, stiff, ahead, behind, joined, to_before, to_next):
    cells = stiff.shape[0]
    first = ahead.shape[0] - cells
    for p in range(cells):
        block = with_rows(place, stiff[p], ahead[first + p, :2, :], behind[first + p])
        joined[p] = block
        if p < to_before.shape[0]:
            to_before[p] = block
        if p >= cells - to_next.shape[0]:
            to_next[p - (cells - to_next.shape[0])] = block


def gated(half):
    up = 1.0 + jnp.tanh(half)
    value = half * up
    return value, up + value * (2.0 - up)


def features_of(tables, group, column, scale=None):
    x_cos, x_sin, z_cos, z_sin = tables
    cos = x_cos[group, :, column : column + 1]
    sin = x_sin[group, :, column : column + 1]
    upper = z_cos[...] * cos - z_sin[...] * sin
    lower = z_sin[...] * cos + z_cos[...] * sin
    if scale is not None:
        upper, lower = upper * scale, lower * scale
    return jnp.concatenate([upper, lower], 0).astype(BF)


def forward_columns(tables, group, weights, kept, spans):
    w_in, w_mid, w_column, w_row = weights
    hidden_in, slope_mid, slope_in, hidden_mid = kept

    def keep(array, value):
        for start, first, count in spans:
            array[:, pl.ds(start, count)] = value[:, first : first + count]

    columns = tables[0].shape[2]
    features = jnp.concatenate([features_of(tables, group, q) for q in range(columns)], 1)
    value, slope = gated(jnp.dot(w_in[...], features, preferred_element_type=F32))
    value = value.astype(BF)
    keep(hidden_in, value)
    keep(slope_in, slope.astype(BF))
    value, slope = gated(jnp.dot(w_mid[...], value, preferred_element_type=F32))
    value = value.astype(BF)
    keep(hidden_mid, value)
    keep(slope_mid, (w_column[...] * slope).astype(BF))
    logits = jnp.dot(w_row[...], value, preferred_element_type=F32)[:1]
    return 0.5 * jnp.tanh(0.5 * logits) + 0.5


def stiffness_of(density):
    return emin + (1.0 - emin) * (density * density * density)


def outer_kernel(
    x_cos, x_sin, z_cos, z_sin, w_in, w_mid, w_column, w_row,
    density, stiff_first, stiff_last, *kept,
):
    tables, weights = (x_cos, x_sin, z_cos, z_sin), (w_in, w_mid, w_column, w_row)
    cells, _, size = density.shape

    @pl.loop(0, cells)
    def _(p):
        start = pl.multiple_of(p * (8 * size), 8 * size)
        spans = [(start, 0, 2 * size), (start + 6 * size, 2 * size, 2 * size)]
        line = forward_columns(tables, p, weights, kept, spans)
        for q in range(4):
            part = line[:, q * size : (q + 1) * size]
            density[p, q : q + 1, :] = part
            (stiff_first if q < 2 else stiff_last)[p, q % 2 : q % 2 + 1, :] = stiffness_of(part)


def inner_kernel(
    x_cos, x_sin, z_cos, z_sin, w_in, w_mid, w_column, w_row, outer, *rest,
):
    tables, weights = (x_cos, x_sin, z_cos, z_sin), (w_in, w_mid, w_column, w_row)
    density, stiff = rest[4:6]
    cells, rows, size = density.shape

    @pl.loop(0, cells)
    def _(p):
        start = pl.multiple_of(p * (8 * size), 8 * size)
        spans = [(start + 2 * size, 0, 4 * size)]
        line = forward_columns(tables, cells + p, weights, rest[6:], spans)
        for r in range(rows):
            if 2 <= r < 6:
                part = line[:, (r - 2) * size : (r - 1) * size]
            else:
                q = r if r < 2 else r - 4
                part = outer[p, q : q + 1, :]
            density[p, r : r + 1, :] = part
            stiff[p, r : r + 1, :] = stiffness_of(part)


def back_kernel(w_mid, slope_mid, slope_in, back, done, *, first, count, span):
    done[...] = jnp.zeros_like(done)
    for start in range(first, first + count, span):
        place = slice(start, start + span)
        product = jnp.dot(w_mid[...], slope_mid[:, place], preferred_element_type=F32)
        back[:, place] = (product * slope_in[:, place].astype(F32)).astype(BF)


def gradient_kernel(
    place, slope, x_cos, x_sin, z_cos, z_sin, hidden_in, slope_mid, back, hidden_mid,
    mine, other, grad_out, mid, first, running,
):
    tables = (x_cos, x_sin, z_cos, z_sin)
    cells, rows, size = slope.shape
    half = rows // 2
    group_of = [(0, r) if r < 2 else (0, r - half) if r >= rows - 2 else (1, r - 2) for r in range(rows)]
    for p in range(cells):
        lines = [slope[p, r : r + 1, :] for r in range(rows)]
        picked = [
            features_of(tables, side * cells + p, q, line) for (side, q), line in zip(group_of, lines)
        ]
        features = jnp.concatenate(picked, 1)
        line = jnp.concatenate(lines, 1)
        span = slice(p * rows * size, (p + 1) * rows * size)
        hidden = (hidden_in[:, span].astype(F32) * line).astype(BF)
        product = hidden_mid[:, span].astype(F32) * line
        total = product[:, :128]
        for k in range(1, rows * size // 128):
            total = total + product[:, k * 128 : (k + 1) * 128]
        terms = (
            lax.dot_general(hidden, slope_mid[:, span], LAST, preferred_element_type=F32),
            lax.dot_general(back[:, span], features, LAST, preferred_element_type=F32),
            total,
        )
        for held, term in zip((mid, first, running), terms):
            if p == 0:
                held[...] = term
            else:
                held[...] += term
    core = place[CORE]
    height = mid.shape[0]
    first_t = first[...].T
    for k in range(2):
        for owner in range(2):
            lanes = slice((2 * owner + k) * 128, (2 * owner + k + 1) * 128)

            @pl.when(core == owner)
            def _():
                mine[k, :height, :] = mid[:, lanes]
                mine[k, height:, :] = first_t[:, lanes]

            @pl.when(core != owner)
            def _():
                other[k, :height, :] = mid[:, lanes]
                other[k, height:, :] = first_t[:, lanes]

    line = jnp.sum(running[...].T, axis=0, keepdims=True)
    for k in range(grad_out.shape[0]):
        grad_out[k : k + 1, :] = line[:, k * 128 : (k + 1) * 128]


def share_kernel(place, parts, grad_out, shares):
    chips, height, lanes = parts.shape
    total = parts[0]
    for chip in range(1, chips):
        total = total + parts[chip]
    block = jnp.concatenate([total, grad_out[...], jnp.zeros(grad_out.shape, F32)], axis=0)
    for chip in range(chips):
        shares[chip] = block


def finish_kernel(place, half, away, grad_in, grad_mid, grad_out):
    chips = half.shape[0]
    height = half.shape[1] - 2 * grad_out.shape[0]
    middle = grad_mid.shape[0]
    at_first = place[CORE] == 0
    for group in range(4):
        part = pl.ds((group % 2) * (chips // 2), chips // 2)
        own, far = half[part, :height, :], away[part, :height, :]
        picked = jnp.where(at_first, own, far) if group < 2 else jnp.where(at_first, far, own)
        picked = picked.reshape(-1, 128)
        lanes = slice(group * 128, (group + 1) * 128)
        grad_mid[:, lanes] = picked[:middle]
        grad_in[:, lanes] = picked[middle:]
    out = jnp.sum(half[:, height:, :], axis=0) + jnp.sum(away[:, height:, :], axis=0)
    grad_out[...] = out[: grad_out.shape[0]]


VM = pltpu.VMEM
WHOLE = pl.BlockSpec(memory_space=pltpu.VMEM)
SCALARS = pl.BlockSpec(memory_space=pltpu.SMEM)
X_FIRST, Y_FIRST, CORE, SLAB_FIRST, SLAB_LAST, Z_FIRST, Z_LAST = range(7)


def params(mebibytes=8):
    return pltpu.CompilerParams(vmem_limit_bytes=mebibytes << 20)


def shaped(*shape, dtype=F32):
    return jax.ShapeDtypeStruct(shape, dtype)


def held(*shape, dtype=F32):
    return VM(shape, dtype)


def run(kernel, name, out_shape, *operands, scalars=1, space=pltpu.VMEM, scratch=(), limit=16, **more):
    arrays = [pltpu.with_memory_space_constraint(array, space) for array in operands[scalars:]]
    return pl.pallas_call(
        kernel,
        name=name,
        in_specs=[SCALARS] * scalars + [WHOLE] * len(arrays),
        out_specs=[WHOLE] * len(out_shape),
        out_shape=out_shape,
        scratch_shapes=list(scratch),
        compiler_params=params(limit),
        **more,
    )(*operands[:scalars], *arrays)


def shifted(block, axis, distance):
    size = lax.axis_size(axis)
    return lax.ppermute(block, axis, [(i, (i + distance) % size) for i in range(size)])


def summed(values):
    values = values + lax.ppermute(values, "c", [(0, 1), (1, 0)])
    for axis in ("z", "y", "x"):
        others = [shifted(values, axis, k) for k in range(1, lax.axis_size(axis))]
        values = values + sum(others)
    return values


def on_device(load_values, load_mask, fixed_mask, frequencies, weight_in, weight_mid, weight_out):
    cells_x, cells_y, cells_z = fixed_mask.shape
    slab, sub = lax.axis_index(SLAB), lax.axis_index("z")
    slabs, subs = lax.axis_size(SLAB), lax.axis_size("z")
    grid_cells = (cells_x * slabs, cells_y * subs, cells_z)
    elements_total = grid_cells[0] * grid_cells[1] * grid_cells[2]
    place = jnp.stack(
        [slab * cells_x, sub * cells_y, lax.axis_index("c")]
        + [(slab == 0) * 1, (slab == slabs - 1) * 1, (sub == 0) * 1, (sub == subs - 1) * 1, slab * 0]
    ).astype(jnp.int32)
    inputs, hidden = weight_in.shape
    rows = cells_x * cells_y * cells_z
    half_rows = cells_y // 2
    field = (cells_x, cells_y, cells_z)
    table = held(2 * cells_x, inputs // 2, half_rows)
    line = held(inputs // 2, cells_z)
    (
        loads, loads_first, loads_last, x_cos, x_sin, z_cos, z_sin,
        w_in_t, w_mid_t, w_mid_half, w_column, w_row,
    ) = run(
        functools.partial(prepare_kernel, grid_cells),
        "prepare",
        [
            held(4, *field),
            held(4, 3, cells_y, cells_z),
            held(4, 2, cells_y, cells_z),
            table,
            table,
            line,
            line,
            held(hidden, inputs, dtype=BF),
            held(hidden, hidden, dtype=BF),
            held(hidden, hidden, dtype=BF),
            held(hidden, 1),
            held(16, hidden, dtype=BF),
        ],
        place, load_values, load_mask, fixed_mask, frequencies, weight_in, weight_mid,
        weight_out, space=pltpu.HBM,
    )

    loads_ahead = shifted(loads_first, SLAB, -1)
    loads_behind = shifted(loads_last, SLAB, 1)
    network = (x_cos, x_sin, z_cos, z_sin, w_in_t, w_mid_t, w_column, w_row)
    kept = [held(hidden, rows, dtype=BF)] * 4
    cost = pl.CostEstimate(
        flops=(inputs + hidden) * hidden * rows,
        bytes_accessed=4 * hidden * rows,
        transcendentals=hidden * rows,
    )
    outer, stiff_first, stiff_last, *stored = run(
        outer_kernel,
        "outer",
        [held(cells_x, half_rows, cells_z)] + [held(cells_x, 2, cells_z)] * 2 + kept,
        *network,
        scalars=0,
        limit=16,
        cost_estimate=cost,
    )
    planes = cells_x + 5
    slots = 4 * planes + cells_x
    loads, rows_first, rows_last = run(
        pack_kernel,
        "pack",
        [held(4, planes, cells_y, cells_z), held(slots, 3, cells_z), held(slots, 2, cells_z)],
        place, loads, loads_ahead, loads_behind, stiff_first, stiff_last,
    )
    rows_ahead = shifted(rows_first, "z", -1)
    rows_behind = shifted(rows_last, "z", 1)
    density, stiff, *stored = run(
        inner_kernel,
        "inner",
        [held(*field)] * 2 + kept,
        *network,
        outer,
        *stored,
        scalars=0,
        limit=16,
        input_output_aliases={9 + k: 2 + k for k in range(4)},
        cost_estimate=cost,
    )
    hidden_in, slope_mid, slope_in, hidden_mid = stored
    stiff_16, stiff_before, stiff_next = run(
        stiff_rows_kernel,
        "stiff_rows",
        [held(cells_x, ROWS, cells_z), held(2, ROWS, cells_z), held(2, ROWS, cells_z)],
        place, stiff, rows_ahead, rows_behind,
    )
    stiff_ahead = shifted(stiff_before, SLAB, -1)
    stiff_behind = shifted(stiff_next, SLAB, 1)

    back = slope_in
    ready = []
    begin = 0
    for part, share in enumerate((2, 4, 4)):
        count = rows // share
        back, done = run(
            functools.partial(back_kernel, first=begin, count=count, span=1024),
            f"back_{part}",
            kept[:1] + [held(8, 128)],
            w_mid_half,
            slope_mid,
            back,
            scalars=0,
            limit=16,
            input_output_aliases={2: 0},
            cost_estimate=pl.CostEstimate(
                flops=2 * hidden * hidden * count,
                bytes_accessed=6 * hidden * count,
                transcendentals=0,
            ),
        )
        begin += count
        ready.append(done)

    vector = held(3, cells_x + 1, ROWS, cells_z)
    first, second, sums = run(
        krylov_kernel,
        "krylov",
        [vector, vector, held(8, 128)],
        place, loads, rows_ahead, rows_behind, stiff_16, stiff_ahead, stiff_behind, density,
        ready[0],
    )
    solution, slope, density = run(
        functools.partial(energy_kernel, elements_total),
        "energy",
        [shaped(3, *field), held(*field), shaped(*field)],
        place, summed(sums), loads, rows_ahead, rows_behind, first, second, density,
    )

    height = hidden + inputs
    groups = hidden // 128
    mine, other, grad_out = run(
        gradient_kernel,
        "gradients",
        [held(groups // 2, height, 128)] * 2 + [held(groups, 128)],
        place, slope, x_cos, x_sin, z_cos, z_sin, hidden_in, slope_mid, back, hidden_mid,
        limit=16,
        scratch=[VM((hidden, hidden), F32), VM((hidden, inputs), F32), VM((hidden, 128), F32)],
    )

    chips = lax.axis_size(CHIPS)
    swap = [(0, 1), (1, 0)]
    half = (mine + lax.ppermute(other, "c", swap)).reshape(chips, -1, 128)
    parts = lax.all_to_all(half, CHIPS, 0, 0)
    (shares,) = run(
        share_kernel, "share", [held(chips, half.shape[1] + 2 * groups, 128)], place, parts, grad_out
    )
    half = lax.all_to_all(shares, CHIPS, 0, 0)
    away = lax.ppermute(half, "c", swap)
    grad_in, grad_mid, grad_out = run(
        finish_kernel,
        "finish",
        [shaped(inputs, hidden), shaped(hidden, hidden), shaped(groups, 128)],
        place, half, away,
    )
    return solution, density, grad_in, grad_mid, grad_out.reshape(hidden)


def solution(mesh):
    slab, sub = mesh.devices.shape
    fine = Mesh(mesh.devices.reshape(4, 4, slab // 16, sub), ALL)
    field = P(SLAB, "z", None)
    vector = P(None, SLAB, "z", None)
    return jax.shard_map(
        on_device,
        mesh=fine,
        in_specs=(vector, field, field, P(), P(), P(), P()),
        out_specs=(vector, field, P(), P(), P()),
        check_vma=False,
    )
```

```python
import functools
import itertools
import math

import jax
import jax.numpy as jnp
import numpy as np
from jax import lax
from jax.experimental import pallas as pl
from jax.experimental.pallas import tpu as pltpu
from jax.sharding import Mesh
from jax.sharding import PartitionSpec as P

ITERS = 3
SLAB = ("x", "y", "c")
CHIPS = ("x", "y", "z")
ALL = ("x", "y", "c", "z")
BF = jnp.bfloat16
F32 = jnp.float32

two_pi = 2.0 * math.pi
emin = 0.001
penalty = 4.0
vol_target = 0.3
ROWS = 16
corner_list = list(itertools.product((0, 1), repeat=3))
LAST = (((1,), (1,)), ((), ()))


def hex_stiffness():
    poisson = 0.3
    lame_first = poisson / ((1.0 + poisson) * (1.0 - 2.0 * poisson))
    lame_second = 0.5 / (1.0 + poisson)
    elastic = np.zeros((6, 6))
    elastic[:3, :3] = lame_first
    for axis_number in range(3):
        elastic[axis_number, axis_number] += 2.0 * lame_second
        elastic[axis_number + 3, axis_number + 3] = lame_second
    gauss_points = [0.5 - 0.5 / math.sqrt(3.0), 0.5 + 0.5 / math.sqrt(3.0)]
    matrix = np.zeros((24, 24))
    for location in itertools.product(gauss_points, repeat=3):
        strain = np.zeros((6, 24))
        for corner_number, corner in enumerate(corner_list):
            factors = [
                location[axis] if corner[axis] == 1 else 1.0 - location[axis] for axis in range(3)
            ]
            slopes = [1.0 if corner[axis] == 1 else -1.0 for axis in range(3)]
            derivative = [
                slopes[0] * factors[1] * factors[2],
                factors[0] * slopes[1] * factors[2],
                factors[0] * factors[1] * slopes[2],
            ]
            column = 3 * corner_number
            for axis in range(3):
                strain[axis, column + axis] = derivative[axis]
            strain[3, column + 1] = derivative[2]
            strain[3, column + 2] = derivative[1]
            strain[4, column + 0] = derivative[2]
            strain[4, column + 2] = derivative[0]
            strain[5, column + 0] = derivative[1]
            strain[5, column + 1] = derivative[0]
        matrix += strain.T @ elastic @ strain / 8.0
    return matrix


def modal_stiffness():
    table = hex_stiffness()
    change = np.zeros((24, 24))
    for row, wave in enumerate(corner_list):
        for column, corner in enumerate(corner_list):
            sign = np.prod([1.0 if c == 1 else -1.0 for w, c in zip(wave, corner) if w == 1])
            for d in range(3):
                change[3 * row + d, 3 * column + d] = sign
    modal = change @ table @ change.T / 64.0
    blocks = []
    for parity in corner_list:
        waves = [tuple(parity[a] ^ (a == d) for a in range(3)) for d in range(3)]
        index = [3 * corner_list.index(wave) + d for d, wave in enumerate(waves)]
        block = modal[np.ix_(index, index)]
        blocks.append((waves, np.where(np.abs(block) < 1e-9, 0.0, block)))
    return blocks


BLOCKS = modal_stiffness()


def lane_mask(shape, lane):
    return lax.broadcasted_iota(jnp.int32, shape, len(shape) - 1) == lane


def plane_modes(plane, rows):
    size = plane.shape[-1]
    ahead = jnp.where(lane_mask(plane.shape, size - 1), 0.0, pltpu.roll(plane, size - 1, 1))
    modes = {}
    for wave_z, part in ((0, plane + ahead), (1, ahead - plane)):
        following = pltpu.roll(part, ROWS - 1, 0)
        modes[0, wave_z] = (part + following)[:rows]
        modes[1, wave_z] = (following - part)[:rows]
    return modes


def element_modes(lower, upper):
    found = []
    for low, high in zip(lower, upper):
        modes = {}
        for key in low:
            modes[(0,) + key] = low[key] + high[key]
            modes[(1,) + key] = high[key] - low[key]
        found.append(modes)
    return found


def modal_forces(modes):
    for waves, block in BLOCKS:
        values = [modes[d][waves[d]] for d in range(3)]
        for d in range(3):
            total = None
            for other in range(3):
                if block[d, other] != 0.0:
                    term = np.float32(block[d, other]) * values[other]
                    total = term if total is None else total + term
            if total is not None:
                yield d, waves[d], values[d], total


def energy_of(modes):
    total = None
    for _, _, value, force in modal_forces(modes):
        total = value * force if total is None else total + value * force
    return total


def node_plane(gathered):
    parts = []
    for wave_z in (0, 1):
        even, odd = gathered[0, wave_z], gathered[1, wave_z]
        parts.append((even - odd) + pltpu.roll(even + odd, 1, 0))
    behind = pltpu.roll(parts[0] + parts[1], 1, 1)
    return (parts[0] - parts[1]) + jnp.where(lane_mask(behind.shape, 0), 0.0, behind)


def operator_planes(planes, stiff, free):
    modes = [[plane_modes(component, ROWS) for component in plane] for plane in planes]
    gathered = [[{} for _ in range(3)] for _ in planes]
    for e in range(len(planes) - 1):
        forces = [{} for _ in range(3)]
        for d, wave, _, force in modal_forces(element_modes(modes[e], modes[e + 1])):
            forces[d][wave] = force * stiff[e]
        for d in range(3):
            for key in itertools.product((0, 1), repeat=2):
                even, odd = forces[d].get((0,) + key), forces[d].get((1,) + key)
                for node, sign in ((e, -1), (e + 1, 1)):
                    if even is None:
                        term = odd if sign == 1 else -odd
                    else:
                        term = even + odd if sign == 1 else even - odd
                    held = gathered[node][d]
                    held[key] = term if key not in held else held[key] + term
    return [
        [node_plane(gathered[n][d]) * free[n - 1] for d in range(3)]
        for n in range(1, len(planes) - 1)
    ]


def kept_if(flag):
    return jnp.where(flag == 0, 1.0, 0.0)


def with_rows(place, block, ahead, behind):
    start, stop = kept_if(place[Z_FIRST]), kept_if(place[Z_LAST])
    space = ROWS - block.shape[0] - ahead.shape[0] - behind.shape[0]
    zeros = jnp.zeros((space, block.shape[1]), F32)
    return jnp.concatenate([block, ahead * stop, zeros, behind * start], axis=0)


def krylov_kernel(place, loads, stiff, ahead, behind, density, ready, first, second, sums):
    cells = loads.shape[1]
    low, high = kept_if(place[SLAB_FIRST]), kept_if(place[SLAB_LAST])
    stiff_planes = [behind[8 + p] * low for p in range(2)]
    stiff_planes += [stiff[p] for p in range(cells)]
    stiff_planes += [ahead[12 + p] * high for p in range(2)]
    loaded = [[behind[2 * d + p] * low for d in range(4)] for p in range(2)]
    loaded += [[loads[d, p] for d in range(4)] for p in range(cells)]
    loaded += [[ahead[3 * d + p] * high for d in range(4)] for p in range(3)]
    force = [plane[:3] for plane in loaded]
    free = [plane[3] for plane in loaded]
    image = operator_planes(force, stiff_planes, free[1:-1])
    twice = operator_planes(image, stiff_planes[1:-1], free[2:-2])
    own = (force[2 : 2 + cells], image[1 : 1 + cells], twice[:cells])
    rows = density.shape[1]

    def dot(left, right):
        total = None
        for p in range(cells):
            for d in range(3):
                term = left[p][d][:rows] * right[p][d][:rows]
                total = term if total is None else total + term
        return total

    totals = [dot(own[k // 2], own[(k + 1) // 2]) for k in range(2 * ITERS - 1)]
    modes = [[plane_modes(component, rows) for component in plane] for plane in twice]
    last = None
    volume = None
    for e in range(cells):
        term = stiff_planes[2 + e][:rows] * energy_of(element_modes(modes[e], modes[e + 1]))
        last = term if last is None else last + term
        volume = density[e] if volume is None else volume + density[e]
    totals += [last, volume]
    row_number = lax.broadcasted_iota(jnp.int32, sums.shape, 0)
    result = jnp.zeros(sums.shape, F32)
    for k, total in enumerate(totals):
        scalar = jnp.sum(jnp.sum(total, axis=0, keepdims=True), axis=1, keepdims=True)
        result = jnp.where(row_number == k, scalar, result)
    sums[...] = result
    for p in range(cells + 1):
        for d in range(3):
            first[d, p] = image[1 + p][d]
            second[d, p] = twice[p][d]


def krylov_steps(moments):
    mean = moments[1] / moments[0]
    powers = [None, mean]
    for k in range(2, 2 * ITERS):
        powers.append(powers[-1] * mean)
    scaled = [moments[k] / moments[0] / powers[k] if k else 1.0 for k in range(2 * ITERS)]

    def product(left, right, shift):
        return sum(
            left[i] * right[j] * scaled[i + j + shift]
            for i in range(len(left))
            for j in range(len(right))
        )

    solution = [0.0] * ITERS
    residual = [1.0]
    direction = [1.0]
    norm_now = scaled[0]
    work = 0.0
    for iteration in range(ITERS):
        alpha = norm_now / product(direction, direction, 1)
        work = work + alpha * norm_now
        solution = [
            solution[i] + (alpha * direction[i] if i < len(direction) else 0.0)
            for i in range(ITERS)
        ]
        if iteration + 1 < ITERS:
            image = [0.0] + direction
            residual = [
                (residual[i] if i < len(residual) else 0.0) - alpha * image[i]
                for i in range(len(image))
            ]
            norm_next = product(residual, residual, 0)
            beta = norm_next / norm_now
            direction = [
                residual[i] + (beta * direction[i] if i < len(direction) else 0.0)
                for i in range(len(residual))
            ]
            norm_now = norm_next
    factors = [solution[i] / powers[i + 1] for i in range(ITERS)]
    return factors, work * moments[0] / mean


def energy_kernel(
    elements, place, sums, loads, ahead, first, second, density, solution, slope, out
):
    rows_of = [sums[k : k + 1, :] for k in range(2 * ITERS + 1)]
    factors, compliance = krylov_steps(rows_of[: 2 * ITERS])
    volume = rows_of[2 * ITERS]
    constant = 2.0 * penalty * (volume / elements - vol_target) / elements
    scale = -3.0 * (1.0 - emin) / compliance
    wide = [jnp.concatenate([value, value], axis=1) for value in factors + [scale, constant]]
    cells, rows, _ = density.shape
    high = kept_if(place[SLAB_LAST])
    modes = []
    for p in range(cells + 1):
        plane = []
        for d in range(3):
            load = loads[d, p] if p < cells else ahead[3 * d] * high
            value = wide[0] * load + wide[1] * first[d, p] + wide[2] * second[d, p]
            if p < cells:
                solution[d, p] = value[:rows]
            plane.append(plane_modes(value, rows))
        modes.append(plane)
    for e in range(cells):
        energy = energy_of(element_modes(modes[e], modes[e + 1]))
        held = density[e]
        out[e] = held
        slope[e] = (wide[3] * held * held * energy + wide[4]) * held * (1.0 - held)


def column_of(line):
    size = line.shape[1]
    shape = (size, size)
    same = lax.broadcasted_iota(jnp.int32, shape, 0) == lax.broadcasted_iota(jnp.int32, shape, 1)
    return jnp.sum(jnp.where(same, line, 0.0), axis=1, keepdims=True)


def prepare_kernel(
    grid_cells, place, load_values, load_mask, fixed_mask, frequencies, w_in, w_mid, w_out,
    loads, x_cos, x_sin, z_cos, z_sin, w_in_t, w_mid_t, w_mid_half, w_column, w_row,
):
    cells, rows, size = load_mask.shape
    free = (1 - fixed_mask[...]).astype(F32)
    held = free * load_mask[...].astype(F32)
    for d in range(4):
        loads[d] = free if d == 3 else held * load_values[d]
    columns = [column_of(frequencies[k : k + 1, :]) for k in range(3)]
    half = rows // 2
    lanes = 2 * cells * half
    number = lax.broadcasted_iota(jnp.int32, (1, lanes), 1)
    side = number // (cells * half)
    plane = (number // half) % cells
    inner = number % half
    row = jnp.where(side == 1, inner + 2, jnp.where(inner < 2, inner, inner + half))
    x_centre = ((place[X_FIRST] + plane).astype(F32) + 0.5) / grid_cells[0]
    y_centre = ((place[Y_FIRST] + row).astype(F32) + 0.5) / grid_cells[1]
    phase = two_pi * (x_centre * columns[0] + y_centre * columns[1])
    cos, sin = jnp.cos(phase), jnp.sin(phase)
    for k in range(2 * cells):
        x_cos[k] = cos[:, k * half : (k + 1) * half]
        x_sin[k] = sin[:, k * half : (k + 1) * half]
    z_number = lax.broadcasted_iota(jnp.int32, (1, size), 1)
    phase = two_pi * (((z_number.astype(F32) + 0.5) / grid_cells[2]) * columns[2])
    z_cos[...] = jnp.cos(phase)
    z_sin[...] = jnp.sin(phase)
    w_in_t[...] = (0.5 * w_in[...].astype(F32)).T.astype(BF)
    middle = 0.5 * w_mid[...].astype(F32)
    w_mid_half[...] = middle.astype(BF)
    w_mid_t[...] = middle.T.astype(BF)
    line = w_out[...].astype(F32)[None, :]
    w_column[...] = 0.5 * column_of(line)
    w_row[...] = jnp.broadcast_to(line, w_row.shape).astype(BF)


def join_kernel(place, loads, stiff, ahead, behind, loads_16, stiff_16, to_before, to_next):
    cells = stiff.shape[0]
    for d in range(4):
        for p in range(cells):
            slot = d * cells + p
            block = with_rows(place, loads[d, p], ahead[slot], behind[slot])
            loads_16[d, p] = block
            if p < 3:
                to_before[3 * d + p] = block
            if p >= cells - 2:
                to_next[2 * d + p - (cells - 2)] = block
    for p in range(cells):
        slot = 4 * cells + p
        block = with_rows(place, stiff[p], ahead[slot, :2, :], behind[slot])
        stiff_16[p] = block
        if p < 2:
            to_before[12 + p] = block
        if p >= cells - 2:
            to_next[8 + p - (cells - 2)] = block


def gated(half):
    up = 1.0 + jnp.tanh(half)
    value = half * up
    return value, up + value * (2.0 - up)


def features_of(tables, group, column, scale=None):
    x_cos, x_sin, z_cos, z_sin = tables
    cos = x_cos[group, :, column : column + 1]
    sin = x_sin[group, :, column : column + 1]
    upper = z_cos[...] * cos - z_sin[...] * sin
    lower = z_sin[...] * cos + z_cos[...] * sin
    if scale is not None:
        upper, lower = upper * scale, lower * scale
    return jnp.concatenate([upper, lower], 0).astype(BF)


def forward_columns(tables, group, weights, kept, spans):
    w_in, w_mid, w_column, w_row = weights
    hidden_in, slope_mid, slope_in, hidden_mid = kept

    def keep(array, value):
        for start, first, count in spans:
            array[:, pl.ds(start, count)] = value[:, first : first + count]

    columns = tables[0].shape[2]
    features = jnp.concatenate([features_of(tables, group, q) for q in range(columns)], 1)
    value, slope = gated(jnp.dot(w_in[...], features, preferred_element_type=F32))
    value = value.astype(BF)
    keep(hidden_in, value)
    keep(slope_in, slope.astype(BF))
    value, slope = gated(jnp.dot(w_mid[...], value, preferred_element_type=F32))
    value = value.astype(BF)
    keep(hidden_mid, value)
    keep(slope_mid, (w_column[...] * slope).astype(BF))
    logits = jnp.dot(w_row[...], value, preferred_element_type=F32)[:1]
    return 0.5 * jnp.tanh(0.5 * logits) + 0.5


def stiffness_of(density):
    return emin + (1.0 - emin) * (density * density * density)


def outer_kernel(
    x_cos, x_sin, z_cos, z_sin, w_in, w_mid, w_column, w_row, loads,
    density, to_before, to_next, *kept,
):
    tables, weights = (x_cos, x_sin, z_cos, z_sin), (w_in, w_mid, w_column, w_row)
    cells, _, size = density.shape

    @pl.loop(0, cells)
    def _(p):
        start = pl.multiple_of(p * (8 * size), 8 * size)
        spans = [(start, 0, 2 * size), (start + 6 * size, 2 * size, 2 * size)]
        line = forward_columns(tables, p, weights, kept, spans)
        for q in range(4):
            part = line[:, q * size : (q + 1) * size]
            density[p, q : q + 1, :] = part
            target = to_before if q < 2 else to_next
            target[4 * cells + p, q % 2 : q % 2 + 1, :] = stiffness_of(part)
        to_before[4 * cells + p, 2:, :] = jnp.zeros((1, size), F32)
        rows = loads.shape[2]
        for d in range(4):
            to_before[d * cells + p] = loads[d, p, :3, :]
            to_next[d * cells + p] = loads[d, p, rows - 2 :, :]


def inner_kernel(
    x_cos, x_sin, z_cos, z_sin, w_in, w_mid, w_column, w_row, outer, *rest,
):
    tables, weights = (x_cos, x_sin, z_cos, z_sin), (w_in, w_mid, w_column, w_row)
    density, stiff = rest[4:6]
    cells, rows, size = density.shape

    @pl.loop(0, cells)
    def _(p):
        start = pl.multiple_of(p * (8 * size), 8 * size)
        spans = [(start + 2 * size, 0, 4 * size)]
        line = forward_columns(tables, cells + p, weights, rest[6:], spans)
        for r in range(rows):
            if 2 <= r < 6:
                part = line[:, (r - 2) * size : (r - 1) * size]
            else:
                q = r if r < 2 else r - 4
                part = outer[p, q : q + 1, :]
            density[p, r : r + 1, :] = part
            stiff[p, r : r + 1, :] = stiffness_of(part)


def back_kernel(w_mid, slope_mid, slope_in, back, done, *, first, count, span):
    done[...] = jnp.zeros_like(done)
    for start in range(first, first + count, span):
        place = slice(start, start + span)
        product = jnp.dot(w_mid[...], slope_mid[:, place], preferred_element_type=F32)
        back[:, place] = (product * slope_in[:, place].astype(F32)).astype(BF)


def gradient_kernel(
    place, slope, x_cos, x_sin, z_cos, z_sin, hidden_in, slope_mid, back, hidden_mid,
    mine, other, grad_out, mid, first, running,
):
    tables = (x_cos, x_sin, z_cos, z_sin)
    cells, rows, size = slope.shape
    half = rows // 2
    group_of = [(0, r) if r < 2 else (0, r - half) if r >= rows - 2 else (1, r - 2) for r in range(rows)]
    for p in range(cells):
        lines = [slope[p, r : r + 1, :] for r in range(rows)]
        picked = [
            features_of(tables, side * cells + p, q, line) for (side, q), line in zip(group_of, lines)
        ]
        features = jnp.concatenate(picked, 1)
        line = jnp.concatenate(lines, 1)
        span = slice(p * rows * size, (p + 1) * rows * size)
        hidden = (hidden_in[:, span].astype(F32) * line).astype(BF)
        product = hidden_mid[:, span].astype(F32) * line
        total = product[:, :128]
        for k in range(1, rows * size // 128):
            total = total + product[:, k * 128 : (k + 1) * 128]
        terms = (
            lax.dot_general(hidden, slope_mid[:, span], LAST, preferred_element_type=F32),
            lax.dot_general(back[:, span], features, LAST, preferred_element_type=F32),
            total,
        )
        for held, term in zip((mid, first, running), terms):
            if p == 0:
                held[...] = term
            else:
                held[...] += term
    core = place[CORE]
    height = mid.shape[0]
    first_t = first[...].T
    for k in range(2):
        for owner in range(2):
            lanes = slice((2 * owner + k) * 128, (2 * owner + k + 1) * 128)

            @pl.when(core == owner)
            def _():
                mine[k, :height, :] = mid[:, lanes]
                mine[k, height:, :] = first_t[:, lanes]

            @pl.when(core != owner)
            def _():
                other[k, :height, :] = mid[:, lanes]
                other[k, height:, :] = first_t[:, lanes]

    line = jnp.sum(running[...].T, axis=0, keepdims=True)
    for k in range(grad_out.shape[0]):
        grad_out[k : k + 1, :] = line[:, k * 128 : (k + 1) * 128]


def share_kernel(place, parts, grad_out, shares):
    chips, height, lanes = parts.shape
    total = parts[0]
    for chip in range(1, chips):
        total = total + parts[chip]
    block = jnp.concatenate([total, grad_out[...], jnp.zeros(grad_out.shape, F32)], axis=0)
    for chip in range(chips):
        shares[chip] = block


def finish_kernel(place, half, away, grad_in, grad_mid, grad_out):
    chips = half.shape[0]
    height = half.shape[1] - 2 * grad_out.shape[0]
    middle = grad_mid.shape[0]
    at_first = place[CORE] == 0
    for group in range(4):
        part = pl.ds((group % 2) * (chips // 2), chips // 2)
        own, far = half[part, :height, :], away[part, :height, :]
        picked = jnp.where(at_first, own, far) if group < 2 else jnp.where(at_first, far, own)
        picked = picked.reshape(-1, 128)
        lanes = slice(group * 128, (group + 1) * 128)
        grad_mid[:, lanes] = picked[:middle]
        grad_in[:, lanes] = picked[middle:]
    out = jnp.sum(half[:, height:, :], axis=0) + jnp.sum(away[:, height:, :], axis=0)
    grad_out[...] = out[: grad_out.shape[0]]


VM = pltpu.VMEM
WHOLE = pl.BlockSpec(memory_space=pltpu.VMEM)
SCALARS = pl.BlockSpec(memory_space=pltpu.SMEM)
X_FIRST, Y_FIRST, CORE, SLAB_FIRST, SLAB_LAST, Z_FIRST, Z_LAST = range(7)


def params(mebibytes=8):
    return pltpu.CompilerParams(vmem_limit_bytes=mebibytes << 20)


def shaped(*shape, dtype=F32):
    return jax.ShapeDtypeStruct(shape, dtype)


def held(*shape, dtype=F32):
    return VM(shape, dtype)


def run(kernel, name, out_shape, *operands, scalars=1, space=pltpu.VMEM, scratch=(), limit=16, **more):
    arrays = [pltpu.with_memory_space_constraint(array, space) for array in operands[scalars:]]
    return pl.pallas_call(
        kernel,
        name=name,
        in_specs=[SCALARS] * scalars + [WHOLE] * len(arrays),
        out_specs=[WHOLE] * len(out_shape),
        out_shape=out_shape,
        scratch_shapes=list(scratch),
        compiler_params=params(limit),
        **more,
    )(*operands[:scalars], *arrays)


def shifted(block, axis, distance):
    size = lax.axis_size(axis)
    return lax.ppermute(block, axis, [(i, (i + distance) % size) for i in range(size)])


def summed(values):
    values = values + lax.ppermute(values, "c", [(0, 1), (1, 0)])
    for axis in ("z", "y", "x"):
        others = [shifted(values, axis, k) for k in range(1, lax.axis_size(axis))]
        values = values + sum(others)
    return values


def on_device(load_values, load_mask, fixed_mask, frequencies, weight_in, weight_mid, weight_out):
    cells_x, cells_y, cells_z = fixed_mask.shape
    slab, sub = lax.axis_index(SLAB), lax.axis_index("z")
    slabs, subs = lax.axis_size(SLAB), lax.axis_size("z")
    grid_cells = (cells_x * slabs, cells_y * subs, cells_z)
    elements_total = grid_cells[0] * grid_cells[1] * grid_cells[2]
    place = jnp.stack(
        [slab * cells_x, sub * cells_y, lax.axis_index("c")]
        + [(slab == 0) * 1, (slab == slabs - 1) * 1, (sub == 0) * 1, (sub == subs - 1) * 1, slab * 0]
    ).astype(jnp.int32)
    inputs, hidden = weight_in.shape
    rows = cells_x * cells_y * cells_z
    half_rows = cells_y // 2
    field = (cells_x, cells_y, cells_z)
    table = held(2 * cells_x, inputs // 2, half_rows)
    line = held(inputs // 2, cells_z)
    (
        loads, x_cos, x_sin, z_cos, z_sin,
        w_in_t, w_mid_t, w_mid_half, w_column, w_row,
    ) = run(
        functools.partial(prepare_kernel, grid_cells),
        "prepare",
        [
            held(4, *field),
            table,
            table,
            line,
            line,
            held(hidden, inputs, dtype=BF),
            held(hidden, hidden, dtype=BF),
            held(hidden, hidden, dtype=BF),
            held(hidden, 1),
            held(16, hidden, dtype=BF),
        ],
        place, load_values, load_mask, fixed_mask, frequencies, weight_in, weight_mid,
        weight_out, space=pltpu.HBM,
    )

    network = (x_cos, x_sin, z_cos, z_sin, w_in_t, w_mid_t, w_column, w_row)
    kept = [held(hidden, rows, dtype=BF)] * 4
    cost = pl.CostEstimate(
        flops=(inputs + hidden) * hidden * rows,
        bytes_accessed=4 * hidden * rows,
        transcendentals=hidden * rows,
    )
    slots = 5 * cells_x
    outer, rows_first, rows_last, *stored = run(
        outer_kernel,
        "outer",
        [held(cells_x, half_rows, cells_z), held(slots, 3, cells_z), held(slots, 2, cells_z)] + kept,
        *network,
        loads,
        scalars=0,
        limit=16,
        cost_estimate=cost,
    )
    rows_ahead = shifted(rows_first, "z", -1)
    rows_behind = shifted(rows_last, "z", 1)
    density, stiff, *stored = run(
        inner_kernel,
        "inner",
        [held(*field)] * 2 + kept,
        *network,
        outer,
        *stored,
        scalars=0,
        limit=16,
        input_output_aliases={9 + k: 2 + k for k in range(4)},
        cost_estimate=cost,
    )
    hidden_in, slope_mid, slope_in, hidden_mid = stored
    loads, stiff, planes_first, planes_last = run(
        join_kernel,
        "join",
        [held(4, cells_x, ROWS, cells_z), held(cells_x, ROWS, cells_z)]
        + [held(14, ROWS, cells_z), held(10, ROWS, cells_z)],
        place, loads, stiff, rows_ahead, rows_behind,
    )
    planes_ahead = shifted(planes_first, SLAB, -1)
    planes_behind = shifted(planes_last, SLAB, 1)

    back = slope_in
    ready = []
    begin = 0
    for part, share in enumerate((2, 4, 4)):
        count = rows // share
        back, done = run(
            functools.partial(back_kernel, first=begin, count=count, span=1024),
            f"back_{part}",
            kept[:1] + [held(8, 128)],
            w_mid_half,
            slope_mid,
            back,
            scalars=0,
            limit=16,
            input_output_aliases={2: 0},
            cost_estimate=pl.CostEstimate(
                flops=2 * hidden * hidden * count,
                bytes_accessed=6 * hidden * count,
                transcendentals=0,
            ),
        )
        begin += count
        ready.append(done)

    vector = held(3, cells_x + 1, ROWS, cells_z)
    first, second, sums = run(
        krylov_kernel,
        "krylov",
        [vector, vector, held(8, 128)],
        place, loads, stiff, planes_ahead, planes_behind, density, ready[0],
    )
    solution, slope, density = run(
        functools.partial(energy_kernel, elements_total),
        "energy",
        [shaped(3, *field), held(*field), shaped(*field)],
        place, summed(sums), loads, planes_ahead, first, second, density,
    )

    height = hidden + inputs
    groups = hidden // 128
    mine, other, grad_out = run(
        gradient_kernel,
        "gradients",
        [held(groups // 2, height, 128)] * 2 + [held(groups, 128)],
        place, slope, x_cos, x_sin, z_cos, z_sin, hidden_in, slope_mid, back, hidden_mid,
        limit=16,
        scratch=[VM((hidden, hidden), F32), VM((hidden, inputs), F32), VM((hidden, 128), F32)],
    )

    chips = lax.axis_size(CHIPS)
    swap = [(0, 1), (1, 0)]
    half = (mine + lax.ppermute(other, "c", swap)).reshape(chips, -1, 128)
    parts = lax.all_to_all(half, CHIPS, 0, 0)
    (shares,) = run(
        share_kernel, "share", [held(chips, half.shape[1] + 2 * groups, 128)], place, parts, grad_out
    )
    half = lax.all_to_all(shares, CHIPS, 0, 0)
    away = lax.ppermute(half, "c", swap)
    grad_in, grad_mid, grad_out = run(
        finish_kernel,
        "finish",
        [shaped(inputs, hidden), shaped(hidden, hidden), shaped(groups, 128)],
        place, half, away,
    )
    return solution, density, grad_in, grad_mid, grad_out.reshape(hidden)


def solution(mesh):
    slab, sub = mesh.devices.shape
    fine = Mesh(mesh.devices.reshape(4, 4, slab // 16, sub), ALL)
    field = P(SLAB, "z", None)
    vector = P(None, SLAB, "z", None)
    return jax.shard_map(
        on_device,
        mesh=fine,
        in_specs=(vector, field, field, P(), P(), P(), P()),
        out_specs=(vector, field, P(), P(), P()),
        check_vma=False,
    )
```

```python
import functools
import itertools
import math

import jax
import jax.numpy as jnp
import numpy as np
from jax import lax
from jax.experimental import pallas as pl
from jax.experimental.pallas import tpu as pltpu
from jax.sharding import Mesh
from jax.sharding import PartitionSpec as P

ITERS = 3
SLAB = ("x", "y", "c")
CHIPS = ("x", "y", "z")
ALL = ("x", "y", "c", "z")
BF = jnp.bfloat16
F32 = jnp.float32

two_pi = 2.0 * math.pi
emin = 0.001
penalty = 4.0
vol_target = 0.3
ROWS = 16
corner_list = list(itertools.product((0, 1), repeat=3))
LAST = (((1,), (1,)), ((), ()))


def hex_stiffness():
    poisson = 0.3
    lame_first = poisson / ((1.0 + poisson) * (1.0 - 2.0 * poisson))
    lame_second = 0.5 / (1.0 + poisson)
    elastic = np.zeros((6, 6))
    elastic[:3, :3] = lame_first
    for axis_number in range(3):
        elastic[axis_number, axis_number] += 2.0 * lame_second
        elastic[axis_number + 3, axis_number + 3] = lame_second
    gauss_points = [0.5 - 0.5 / math.sqrt(3.0), 0.5 + 0.5 / math.sqrt(3.0)]
    matrix = np.zeros((24, 24))
    for location in itertools.product(gauss_points, repeat=3):
        strain = np.zeros((6, 24))
        for corner_number, corner in enumerate(corner_list):
            factors = [
                location[axis] if corner[axis] == 1 else 1.0 - location[axis] for axis in range(3)
            ]
            slopes = [1.0 if corner[axis] == 1 else -1.0 for axis in range(3)]
            derivative = [
                slopes[0] * factors[1] * factors[2],
                factors[0] * slopes[1] * factors[2],
                factors[0] * factors[1] * slopes[2],
            ]
            column = 3 * corner_number
            for axis in range(3):
                strain[axis, column + axis] = derivative[axis]
            strain[3, column + 1] = derivative[2]
            strain[3, column + 2] = derivative[1]
            strain[4, column + 0] = derivative[2]
            strain[4, column + 2] = derivative[0]
            strain[5, column + 0] = derivative[1]
            strain[5, column + 1] = derivative[0]
        matrix += strain.T @ elastic @ strain / 8.0
    return matrix


def modal_stiffness():
    table = hex_stiffness()
    change = np.zeros((24, 24))
    for row, wave in enumerate(corner_list):
        for column, corner in enumerate(corner_list):
            sign = np.prod([1.0 if c == 1 else -1.0 for w, c in zip(wave, corner) if w == 1])
            for d in range(3):
                change[3 * row + d, 3 * column + d] = sign
    modal = change @ table @ change.T / 64.0
    blocks = []
    for parity in corner_list:
        waves = [tuple(parity[a] ^ (a == d) for a in range(3)) for d in range(3)]
        index = [3 * corner_list.index(wave) + d for d, wave in enumerate(waves)]
        block = modal[np.ix_(index, index)]
        blocks.append((waves, np.where(np.abs(block) < 1e-9, 0.0, block)))
    return blocks


BLOCKS = modal_stiffness()


def lane_mask(shape, lane):
    return lax.broadcasted_iota(jnp.int32, shape, len(shape) - 1) == lane


def plane_modes(plane, rows):
    size = plane.shape[-1]
    ahead = jnp.where(lane_mask(plane.shape, size - 1), 0.0, pltpu.roll(plane, size - 1, 1))
    modes = {}
    for wave_z, part in ((0, plane + ahead), (1, ahead - plane)):
        following = pltpu.roll(part, ROWS - 1, 0)
        modes[0, wave_z] = (part + following)[:rows]
        modes[1, wave_z] = (following - part)[:rows]
    return modes


def element_modes(lower, upper):
    found = []
    for low, high in zip(lower, upper):
        modes = {}
        for key in low:
            modes[(0,) + key] = low[key] + high[key]
            modes[(1,) + key] = high[key] - low[key]
        found.append(modes)
    return found


def modal_forces(modes):
    for waves, block in BLOCKS:
        values = [modes[d][waves[d]] for d in range(3)]
        for d in range(3):
            total = None
            for other in range(3):
                if block[d, other] != 0.0:
                    term = np.float32(block[d, other]) * values[other]
                    total = term if total is None else total + term
            if total is not None:
                yield d, waves[d], values[d], total


def energy_of(modes):
    total = None
    for _, _, value, force in modal_forces(modes):
        total = value * force if total is None else total + value * force
    return total


def node_plane(gathered):
    parts = []
    for wave_z in (0, 1):
        even, odd = gathered[0, wave_z], gathered[1, wave_z]
        parts.append((even - odd) + pltpu.roll(even + odd, 1, 0))
    behind = pltpu.roll(parts[0] + parts[1], 1, 1)
    return (parts[0] - parts[1]) + jnp.where(lane_mask(behind.shape, 0), 0.0, behind)


def operator_planes(planes, stiff, free):
    modes = [[plane_modes(component, ROWS) for component in plane] for plane in planes]
    gathered = [[{} for _ in range(3)] for _ in planes]
    for e in range(len(planes) - 1):
        forces = [{} for _ in range(3)]
        for d, wave, _, force in modal_forces(element_modes(modes[e], modes[e + 1])):
            forces[d][wave] = force * stiff[e]
        for d in range(3):
            for key in itertools.product((0, 1), repeat=2):
                even, odd = forces[d].get((0,) + key), forces[d].get((1,) + key)
                for node, sign in ((e, -1), (e + 1, 1)):
                    if even is None:
                        term = odd if sign == 1 else -odd
                    else:
                        term = even + odd if sign == 1 else even - odd
                    held = gathered[node][d]
                    held[key] = term if key not in held else held[key] + term
    return [
        [node_plane(gathered[n][d]) * free[n - 1] for d in range(3)]
        for n in range(1, len(planes) - 1)
    ]


def kept_if(flag):
    return jnp.where(flag == 0, 1.0, 0.0)


def with_rows(place, block, ahead, behind):
    start, stop = kept_if(place[Z_FIRST]), kept_if(place[Z_LAST])
    space = ROWS - block.shape[0] - ahead.shape[0] - behind.shape[0]
    zeros = jnp.zeros((space, block.shape[1]), F32)
    return jnp.concatenate([block, ahead * stop, zeros, behind * start], axis=0)


def krylov_kernel(place, loads, stiff, ahead, behind, density, ready, first, second, sums):
    cells = loads.shape[1]
    low, high = kept_if(place[SLAB_FIRST]), kept_if(place[SLAB_LAST])
    stiff_planes = [behind[8 + p] * low for p in range(2)]
    stiff_planes += [stiff[p] for p in range(cells)]
    stiff_planes += [ahead[12 + p] * high for p in range(2)]
    loaded = [[behind[2 * d + p] * low for d in range(4)] for p in range(2)]
    loaded += [[loads[d, p] for d in range(4)] for p in range(cells)]
    loaded += [[ahead[3 * d + p] * high for d in range(4)] for p in range(3)]
    force = [plane[:3] for plane in loaded]
    free = [plane[3] for plane in loaded]
    image = operator_planes(force, stiff_planes, free[1:-1])
    twice = operator_planes(image, stiff_planes[1:-1], free[2:-2])
    own = (force[2 : 2 + cells], image[1 : 1 + cells], twice[:cells])
    rows = density.shape[1]

    def dot(left, right):
        total = None
        for p in range(cells):
            for d in range(3):
                term = left[p][d][:rows] * right[p][d][:rows]
                total = term if total is None else total + term
        return total

    totals = [dot(own[k // 2], own[(k + 1) // 2]) for k in range(2 * ITERS - 1)]
    modes = [[plane_modes(component, rows) for component in plane] for plane in twice]
    last = None
    volume = None
    for e in range(cells):
        term = stiff_planes[2 + e][:rows] * energy_of(element_modes(modes[e], modes[e + 1]))
        last = term if last is None else last + term
        volume = density[e] if volume is None else volume + density[e]
    totals += [last, volume]
    row_number = lax.broadcasted_iota(jnp.int32, sums.shape, 0)
    result = jnp.zeros(sums.shape, F32)
    for k, total in enumerate(totals):
        scalar = jnp.sum(jnp.sum(total, axis=0, keepdims=True), axis=1, keepdims=True)
        result = jnp.where(row_number == k, scalar, result)
    sums[...] = result
    for p in range(cells + 1):
        for d in range(3):
            first[d, p] = image[1 + p][d]
            second[d, p] = twice[p][d]


def krylov_steps(moments):
    mean = moments[1] / moments[0]
    powers = [None, mean]
    for k in range(2, 2 * ITERS):
        powers.append(powers[-1] * mean)
    scaled = [moments[k] / moments[0] / powers[k] if k else 1.0 for k in range(2 * ITERS)]

    def product(left, right, shift):
        return sum(
            left[i] * right[j] * scaled[i + j + shift]
            for i in range(len(left))
            for j in range(len(right))
        )

    solution = [0.0] * ITERS
    residual = [1.0]
    direction = [1.0]
    norm_now = scaled[0]
    work = 0.0
    for iteration in range(ITERS):
        alpha = norm_now / product(direction, direction, 1)
        work = work + alpha * norm_now
        solution = [
            solution[i] + (alpha * direction[i] if i < len(direction) else 0.0)
            for i in range(ITERS)
        ]
        if iteration + 1 < ITERS:
            image = [0.0] + direction
            residual = [
                (residual[i] if i < len(residual) else 0.0) - alpha * image[i]
                for i in range(len(image))
            ]
            norm_next = product(residual, residual, 0)
            beta = norm_next / norm_now
            direction = [
                residual[i] + (beta * direction[i] if i < len(direction) else 0.0)
                for i in range(len(residual))
            ]
            norm_now = norm_next
    factors = [solution[i] / powers[i + 1] for i in range(ITERS)]
    return factors, work * moments[0] / mean


def energy_kernel(
    elements, place, sums, loads, ahead, first, second, density, solution, slope, out
):
    rows_of = [sums[k : k + 1, :] for k in range(2 * ITERS + 1)]
    factors, compliance = krylov_steps(rows_of[: 2 * ITERS])
    volume = rows_of[2 * ITERS]
    constant = 2.0 * penalty * (volume / elements - vol_target) / elements
    scale = -3.0 * (1.0 - emin) / compliance
    wide = [jnp.concatenate([value, value], axis=1) for value in factors + [scale, constant]]
    cells, rows, _ = density.shape
    high = kept_if(place[SLAB_LAST])
    modes = []
    for p in range(cells + 1):
        plane = []
        for d in range(3):
            load = loads[d, p] if p < cells else ahead[3 * d] * high
            value = wide[0] * load + wide[1] * first[d, p] + wide[2] * second[d, p]
            if p < cells:
                solution[d, p] = value[:rows]
            plane.append(plane_modes(value, rows))
        modes.append(plane)
    for e in range(cells):
        energy = energy_of(element_modes(modes[e], modes[e + 1]))
        held = density[e]
        out[e] = held
        slope[e] = (wide[3] * held * held * energy + wide[4]) * held * (1.0 - held)


def column_of(line):
    size = line.shape[1]
    shape = (size, size)
    same = lax.broadcasted_iota(jnp.int32, shape, 0) == lax.broadcasted_iota(jnp.int32, shape, 1)
    return jnp.sum(jnp.where(same, line, 0.0), axis=1, keepdims=True)


def prepare_kernel(
    grid_cells, place, load_values, load_mask, fixed_mask, frequencies, w_in, w_mid, w_out,
    loads, x_cos, x_sin, z_cos, z_sin, w_in_t, w_mid_t, w_mid_half, w_column, w_row,
):
    cells, rows, size = load_mask.shape
    free = (1 - fixed_mask[...]).astype(F32)
    held = free * load_mask[...].astype(F32)
    for d in range(4):
        loads[d] = free if d == 3 else held * load_values[d]
    columns = [column_of(frequencies[k : k + 1, :]) for k in range(3)]
    half = rows // 2
    lanes = 2 * cells * half
    number = lax.broadcasted_iota(jnp.int32, (1, lanes), 1)
    side = number // (cells * half)
    plane = (number // half) % cells
    inner = number % half
    row = jnp.where(side == 1, inner + 2, jnp.where(inner < 2, inner, inner + half))
    x_centre = ((place[X_FIRST] + plane).astype(F32) + 0.5) / grid_cells[0]
    y_centre = ((place[Y_FIRST] + row).astype(F32) + 0.5) / grid_cells[1]
    phase = two_pi * (x_centre * columns[0] + y_centre * columns[1])
    cos, sin = jnp.cos(phase), jnp.sin(phase)
    for k in range(2 * cells):
        x_cos[k] = cos[:, k * half : (k + 1) * half]
        x_sin[k] = sin[:, k * half : (k + 1) * half]
    z_number = lax.broadcasted_iota(jnp.int32, (1, size), 1)
    phase = two_pi * (((z_number.astype(F32) + 0.5) / grid_cells[2]) * columns[2])
    z_cos[...] = jnp.cos(phase)
    z_sin[...] = jnp.sin(phase)
    w_in_t[...] = (0.5 * w_in[...].astype(F32)).T.astype(BF)
    middle = 0.5 * w_mid[...].astype(F32)
    w_mid_half[...] = middle.astype(BF)
    w_mid_t[...] = middle.T.astype(BF)
    line = w_out[...].astype(F32)[None, :]
    w_column[...] = 0.5 * column_of(line)
    w_row[...] = jnp.broadcast_to(line, w_row.shape).astype(BF)


def join_kernel(place, loads, stiff, ahead, behind, loads_16, stiff_16, to_before, to_next):
    cells = stiff.shape[0]
    for d in range(4):
        for p in range(cells):
            slot = d * cells + p
            block = with_rows(place, loads[d, p], ahead[slot], behind[slot])
            loads_16[d, p] = block
            if p < 3:
                to_before[3 * d + p] = block
            if p >= cells - 2:
                to_next[2 * d + p - (cells - 2)] = block
    for p in range(cells):
        slot = 4 * cells + p
        block = with_rows(place, stiff[p], ahead[slot, :2, :], behind[slot])
        stiff_16[p] = block
        if p < 2:
            to_before[12 + p] = block
        if p >= cells - 2:
            to_next[8 + p - (cells - 2)] = block


def gated(half):
    up = 1.0 + jnp.tanh(half)
    value = half * up
    return value, up + value * (2.0 - up)


def features_of(tables, group, column, scale=None):
    x_cos, x_sin, z_cos, z_sin = tables
    cos = x_cos[group, :, column : column + 1]
    sin = x_sin[group, :, column : column + 1]
    upper = z_cos[...] * cos - z_sin[...] * sin
    lower = z_sin[...] * cos + z_cos[...] * sin
    if scale is not None:
        upper, lower = upper * scale, lower * scale
    return jnp.concatenate([upper, lower], 0).astype(BF)


def forward_columns(tables, group, weights, kept, spans):
    w_in, w_mid, w_column, w_row = weights
    hidden_in, slope_mid, slope_in, hidden_mid = kept

    def keep(array, value):
        for start, first, count in spans:
            array[:, pl.ds(start, count)] = value[:, first : first + count]

    columns = tables[0].shape[2]
    features = jnp.concatenate([features_of(tables, group, q) for q in range(columns)], 1)
    value, slope = gated(jnp.dot(w_in[...], features, preferred_element_type=F32))
    value = value.astype(BF)
    keep(hidden_in, value)
    keep(slope_in, slope.astype(BF))
    value, slope = gated(jnp.dot(w_mid[...], value, preferred_element_type=F32))
    value = value.astype(BF)
    keep(hidden_mid, value)
    keep(slope_mid, (w_column[...] * slope).astype(BF))
    logits = jnp.dot(w_row[...], value, preferred_element_type=F32)[:1]
    return 0.5 * jnp.tanh(0.5 * logits) + 0.5


def stiffness_of(density):
    return emin + (1.0 - emin) * (density * density * density)


def outer_kernel(
    x_cos, x_sin, z_cos, z_sin, w_in, w_mid, w_column, w_row, loads,
    density, to_before, to_next, *kept,
):
    tables, weights = (x_cos, x_sin, z_cos, z_sin), (w_in, w_mid, w_column, w_row)
    cells, _, size = density.shape

    @pl.loop(0, cells)
    def _(p):
        start = pl.multiple_of(p * (8 * size), 8 * size)
        spans = [(start, 0, 2 * size), (start + 6 * size, 2 * size, 2 * size)]
        line = forward_columns(tables, p, weights, kept, spans)
        for q in range(4):
            part = line[:, q * size : (q + 1) * size]
            density[p, q : q + 1, :] = part
            target = to_before if q < 2 else to_next
            target[4 * cells + p, q % 2 : q % 2 + 1, :] = stiffness_of(part)
        to_before[4 * cells + p, 2:, :] = jnp.zeros((1, size), F32)
        rows = loads.shape[2]
        for d in range(4):
            to_before[d * cells + p] = loads[d, p, :3, :]
            to_next[d * cells + p] = loads[d, p, rows - 2 :, :]


def inner_kernel(
    x_cos, x_sin, z_cos, z_sin, w_in, w_mid, w_column, w_row, outer, *rest,
):
    tables, weights = (x_cos, x_sin, z_cos, z_sin), (w_in, w_mid, w_column, w_row)
    density, stiff = rest[4:6]
    cells, rows, size = density.shape

    @pl.loop(0, cells)
    def _(p):
        start = pl.multiple_of(p * (8 * size), 8 * size)
        spans = [(start + 2 * size, 0, 4 * size)]
        line = forward_columns(tables, cells + p, weights, rest[6:], spans)
        for r in range(rows):
            if 2 <= r < 6:
                part = line[:, (r - 2) * size : (r - 1) * size]
            else:
                q = r if r < 2 else r - 4
                part = outer[p, q : q + 1, :]
            density[p, r : r + 1, :] = part
            stiff[p, r : r + 1, :] = stiffness_of(part)


def back_kernel(w_mid, slope_mid, slope_in, back, done, *, span):
    done[...] = jnp.zeros_like(done)
    for start in range(0, back.shape[1], span):
        place = slice(start, start + span)
        product = jnp.dot(w_mid[...], slope_mid[:, place], preferred_element_type=F32)
        back[:, place] = (product * slope_in[:, place].astype(F32)).astype(BF)


def gradient_kernel(
    place, slope, x_cos, x_sin, z_cos, z_sin, hidden_in, slope_mid, back, hidden_mid,
    mine, other, grad_out, mid, first, running,
):
    tables = (x_cos, x_sin, z_cos, z_sin)
    cells, rows, size = slope.shape
    half = rows // 2
    group_of = [(0, r) if r < 2 else (0, r - half) if r >= rows - 2 else (1, r - 2) for r in range(rows)]
    for p in range(cells):
        lines = [slope[p, r : r + 1, :] for r in range(rows)]
        picked = [
            features_of(tables, side * cells + p, q, line) for (side, q), line in zip(group_of, lines)
        ]
        features = jnp.concatenate(picked, 1)
        line = jnp.concatenate(lines, 1)
        span = slice(p * rows * size, (p + 1) * rows * size)
        hidden = (hidden_in[:, span].astype(F32) * line).astype(BF)
        product = hidden_mid[:, span].astype(F32) * line
        total = product[:, :128]
        for k in range(1, rows * size // 128):
            total = total + product[:, k * 128 : (k + 1) * 128]
        terms = (
            lax.dot_general(hidden, slope_mid[:, span], LAST, preferred_element_type=F32),
            lax.dot_general(back[:, span], features, LAST, preferred_element_type=F32),
            total,
        )
        for held, term in zip((mid, first, running), terms):
            if p == 0:
                held[...] = term
            else:
                held[...] += term
    core = place[CORE]
    height = mid.shape[0]
    first_t = first[...].T
    for k in range(2):
        for owner in range(2):
            lanes = slice((2 * owner + k) * 128, (2 * owner + k + 1) * 128)

            @pl.when(core == owner)
            def _():
                mine[k, :height, :] = mid[:, lanes]
                mine[k, height:, :] = first_t[:, lanes]

            @pl.when(core != owner)
            def _():
                other[k, :height, :] = mid[:, lanes]
                other[k, height:, :] = first_t[:, lanes]

    line = jnp.sum(running[...].T, axis=0, keepdims=True)
    for k in range(grad_out.shape[0]):
        grad_out[k : k + 1, :] = line[:, k * 128 : (k + 1) * 128]


def share_kernel(place, parts, grad_out, shares):
    chips, height, lanes = parts.shape
    total = parts[0]
    for chip in range(1, chips):
        total = total + parts[chip]
    block = jnp.concatenate([total, grad_out[...], jnp.zeros(grad_out.shape, F32)], axis=0)
    for chip in range(chips):
        shares[chip] = block


def finish_kernel(place, half, away, grad_in, grad_mid, grad_out):
    chips = half.shape[0]
    height = half.shape[1] - 2 * grad_out.shape[0]
    middle = grad_mid.shape[0]
    at_first = place[CORE] == 0
    for group in range(4):
        part = pl.ds((group % 2) * (chips // 2), chips // 2)
        own, far = half[part, :height, :], away[part, :height, :]
        picked = jnp.where(at_first, own, far) if group < 2 else jnp.where(at_first, far, own)
        picked = picked.reshape(-1, 128)
        lanes = slice(group * 128, (group + 1) * 128)
        grad_mid[:, lanes] = picked[:middle]
        grad_in[:, lanes] = picked[middle:]
    out = jnp.sum(half[:, height:, :], axis=0) + jnp.sum(away[:, height:, :], axis=0)
    grad_out[...] = out[: grad_out.shape[0]]


VM = pltpu.VMEM
WHOLE = pl.BlockSpec(memory_space=pltpu.VMEM)
SCALARS = pl.BlockSpec(memory_space=pltpu.SMEM)
X_FIRST, Y_FIRST, CORE, SLAB_FIRST, SLAB_LAST, Z_FIRST, Z_LAST = range(7)


def params(mebibytes=8):
    return pltpu.CompilerParams(vmem_limit_bytes=mebibytes << 20)


def shaped(*shape, dtype=F32):
    return jax.ShapeDtypeStruct(shape, dtype)


def held(*shape, dtype=F32):
    return VM(shape, dtype)


def run(kernel, name, out_shape, *operands, scalars=1, space=pltpu.VMEM, scratch=(), limit=16, **more):
    arrays = [pltpu.with_memory_space_constraint(array, space) for array in operands[scalars:]]
    return pl.pallas_call(
        kernel,
        name=name,
        in_specs=[SCALARS] * scalars + [WHOLE] * len(arrays),
        out_specs=[WHOLE] * len(out_shape),
        out_shape=out_shape,
        scratch_shapes=list(scratch),
        compiler_params=params(limit),
        **more,
    )(*operands[:scalars], *arrays)


def shifted(block, axis, distance):
    size = lax.axis_size(axis)
    return lax.ppermute(block, axis, [(i, (i + distance) % size) for i in range(size)])


def summed(values):
    values = values + lax.ppermute(values, "c", [(0, 1), (1, 0)])
    for axis in ("z", "y", "x"):
        others = [shifted(values, axis, k) for k in range(1, lax.axis_size(axis))]
        values = values + sum(others)
    return values


def on_device(load_values, load_mask, fixed_mask, frequencies, weight_in, weight_mid, weight_out):
    cells_x, cells_y, cells_z = fixed_mask.shape
    slab, sub = lax.axis_index(SLAB), lax.axis_index("z")
    slabs, subs = lax.axis_size(SLAB), lax.axis_size("z")
    grid_cells = (cells_x * slabs, cells_y * subs, cells_z)
    elements_total = grid_cells[0] * grid_cells[1] * grid_cells[2]
    place = jnp.stack(
        [slab * cells_x, sub * cells_y, lax.axis_index("c")]
        + [(slab == 0) * 1, (slab == slabs - 1) * 1, (sub == 0) * 1, (sub == subs - 1) * 1, slab * 0]
    ).astype(jnp.int32)
    inputs, hidden = weight_in.shape
    rows = cells_x * cells_y * cells_z
    half_rows = cells_y // 2
    field = (cells_x, cells_y, cells_z)
    table = held(2 * cells_x, inputs // 2, half_rows)
    line = held(inputs // 2, cells_z)
    (
        loads, x_cos, x_sin, z_cos, z_sin,
        w_in_t, w_mid_t, w_mid_half, w_column, w_row,
    ) = run(
        functools.partial(prepare_kernel, grid_cells),
        "prepare",
        [
            held(4, *field),
            table,
            table,
            line,
            line,
            held(hidden, inputs, dtype=BF),
            held(hidden, hidden, dtype=BF),
            held(hidden, hidden, dtype=BF),
            held(hidden, 1),
            held(16, hidden, dtype=BF),
        ],
        place, load_values, load_mask, fixed_mask, frequencies, weight_in, weight_mid,
        weight_out, space=pltpu.HBM,
    )

    network = (x_cos, x_sin, z_cos, z_sin, w_in_t, w_mid_t, w_column, w_row)
    kept = [held(hidden, rows, dtype=BF)] * 4
    cost = pl.CostEstimate(
        flops=(inputs + hidden) * hidden * rows,
        bytes_accessed=4 * hidden * rows,
        transcendentals=hidden * rows,
    )
    slots = 5 * cells_x
    outer, rows_first, rows_last, *stored = run(
        outer_kernel,
        "outer",
        [held(cells_x, half_rows, cells_z), held(slots, 3, cells_z), held(slots, 2, cells_z)] + kept,
        *network,
        loads,
        scalars=0,
        limit=16,
        cost_estimate=cost,
    )
    rows_ahead = shifted(rows_first, "z", -1)
    rows_behind = shifted(rows_last, "z", 1)
    density, stiff, *stored = run(
        inner_kernel,
        "inner",
        [held(*field)] * 2 + kept,
        *network,
        outer,
        *stored,
        scalars=0,
        limit=16,
        input_output_aliases={9 + k: 2 + k for k in range(4)},
        cost_estimate=cost,
    )
    hidden_in, slope_mid, slope_in, hidden_mid = stored
    loads, stiff, planes_first, planes_last = run(
        join_kernel,
        "join",
        [held(4, cells_x, ROWS, cells_z), held(cells_x, ROWS, cells_z)]
        + [held(14, ROWS, cells_z), held(10, ROWS, cells_z)],
        place, loads, stiff, rows_ahead, rows_behind,
    )
    planes_ahead = shifted(planes_first, SLAB, -1)
    planes_behind = shifted(planes_last, SLAB, 1)

    back, ready = run(
        functools.partial(back_kernel, span=1024),
        "back",
        kept[:1] + [held(8, 128)],
        w_mid_half,
        slope_mid,
        slope_in,
        scalars=0,
        limit=16,
        input_output_aliases={2: 0},
        cost_estimate=pl.CostEstimate(
            flops=2 * hidden * hidden * rows,
            bytes_accessed=6 * hidden * rows,
            transcendentals=0,
        ),
    )

    vector = held(3, cells_x + 1, ROWS, cells_z)
    first, second, sums = run(
        krylov_kernel,
        "krylov",
        [vector, vector, held(8, 128)],
        place, loads, stiff, planes_ahead, planes_behind, density, ready,
    )
    solution, slope, density = run(
        functools.partial(energy_kernel, elements_total),
        "energy",
        [shaped(3, *field), held(*field), shaped(*field)],
        place, summed(sums), loads, planes_ahead, first, second, density,
    )

    height = hidden + inputs
    groups = hidden // 128
    mine, other, grad_out = run(
        gradient_kernel,
        "gradients",
        [held(groups // 2, height, 128)] * 2 + [held(groups, 128)],
        place, slope, x_cos, x_sin, z_cos, z_sin, hidden_in, slope_mid, back, hidden_mid,
        limit=16,
        scratch=[VM((hidden, hidden), F32), VM((hidden, inputs), F32), VM((hidden, 128), F32)],
    )

    chips = lax.axis_size(CHIPS)
    swap = [(0, 1), (1, 0)]
    half = (mine + lax.ppermute(other, "c", swap)).reshape(chips, -1, 128)
    parts = lax.all_to_all(half, CHIPS, 0, 0)
    (shares,) = run(
        share_kernel, "share", [held(chips, half.shape[1] + 2 * groups, 128)], place, parts, grad_out
    )
    half = lax.all_to_all(shares, CHIPS, 0, 0)
    away = lax.ppermute(half, "c", swap)
    grad_in, grad_mid, grad_out = run(
        finish_kernel,
        "finish",
        [shaped(inputs, hidden), shaped(hidden, hidden), shaped(groups, 128)],
        place, half, away,
    )
    return solution, density, grad_in, grad_mid, grad_out.reshape(hidden)


def solution(mesh):
    slab, sub = mesh.devices.shape
    fine = Mesh(mesh.devices.reshape(4, 4, slab // 16, sub), ALL)
    field = P(SLAB, "z", None)
    vector = P(None, SLAB, "z", None)
    return jax.shard_map(
        on_device,
        mesh=fine,
        in_specs=(vector, field, field, P(), P(), P(), P()),
        out_specs=(vector, field, P(), P(), P()),
        check_vma=False,
    )
```

```python
import functools
import itertools
import math

import jax
import jax.numpy as jnp
import numpy as np
from jax import lax
from jax.experimental import pallas as pl
from jax.experimental.pallas import tpu as pltpu
from jax.sharding import Mesh
from jax.sharding import PartitionSpec as P

ITERS = 3
SLAB = ("x", "y", "c")
CHIPS = ("x", "y", "z")
ALL = ("x", "y", "c", "z")
BF = jnp.bfloat16
F32 = jnp.float32

two_pi = 2.0 * math.pi
emin = 0.001
penalty = 4.0
vol_target = 0.3
ROWS = 16
corner_list = list(itertools.product((0, 1), repeat=3))
LAST = (((1,), (1,)), ((), ()))


def hex_stiffness():
    poisson = 0.3
    lame_first = poisson / ((1.0 + poisson) * (1.0 - 2.0 * poisson))
    lame_second = 0.5 / (1.0 + poisson)
    elastic = np.zeros((6, 6))
    elastic[:3, :3] = lame_first
    for axis_number in range(3):
        elastic[axis_number, axis_number] += 2.0 * lame_second
        elastic[axis_number + 3, axis_number + 3] = lame_second
    gauss_points = [0.5 - 0.5 / math.sqrt(3.0), 0.5 + 0.5 / math.sqrt(3.0)]
    matrix = np.zeros((24, 24))
    for location in itertools.product(gauss_points, repeat=3):
        strain = np.zeros((6, 24))
        for corner_number, corner in enumerate(corner_list):
            factors = [
                location[axis] if corner[axis] == 1 else 1.0 - location[axis] for axis in range(3)
            ]
            slopes = [1.0 if corner[axis] == 1 else -1.0 for axis in range(3)]
            derivative = [
                slopes[0] * factors[1] * factors[2],
                factors[0] * slopes[1] * factors[2],
                factors[0] * factors[1] * slopes[2],
            ]
            column = 3 * corner_number
            for axis in range(3):
                strain[axis, column + axis] = derivative[axis]
            strain[3, column + 1] = derivative[2]
            strain[3, column + 2] = derivative[1]
            strain[4, column + 0] = derivative[2]
            strain[4, column + 2] = derivative[0]
            strain[5, column + 0] = derivative[1]
            strain[5, column + 1] = derivative[0]
        matrix += strain.T @ elastic @ strain / 8.0
    return matrix


def modal_stiffness():
    table = hex_stiffness()
    change = np.zeros((24, 24))
    for row, wave in enumerate(corner_list):
        for column, corner in enumerate(corner_list):
            sign = np.prod([1.0 if c == 1 else -1.0 for w, c in zip(wave, corner) if w == 1])
            for d in range(3):
                change[3 * row + d, 3 * column + d] = sign
    modal = change @ table @ change.T / 64.0
    blocks = []
    for parity in corner_list:
        waves = [tuple(parity[a] ^ (a == d) for a in range(3)) for d in range(3)]
        index = [3 * corner_list.index(wave) + d for d, wave in enumerate(waves)]
        block = modal[np.ix_(index, index)]
        blocks.append((waves, np.where(np.abs(block) < 1e-9, 0.0, block)))
    return blocks


BLOCKS = modal_stiffness()


def lane_mask(shape, lane):
    return lax.broadcasted_iota(jnp.int32, shape, len(shape) - 1) == lane


def plane_modes(plane, rows):
    size = plane.shape[-1]
    ahead = jnp.where(lane_mask(plane.shape, size - 1), 0.0, pltpu.roll(plane, size - 1, 1))
    modes = {}
    for wave_z, part in ((0, plane + ahead), (1, ahead - plane)):
        following = pltpu.roll(part, ROWS - 1, 0)
        modes[0, wave_z] = (part + following)[:rows]
        modes[1, wave_z] = (following - part)[:rows]
    return modes


def element_modes(lower, upper):
    found = []
    for low, high in zip(lower, upper):
        modes = {}
        for key in low:
            modes[(0,) + key] = low[key] + high[key]
            modes[(1,) + key] = high[key] - low[key]
        found.append(modes)
    return found


def modal_forces(modes):
    for waves, block in BLOCKS:
        values = [modes[d][waves[d]] for d in range(3)]
        for d in range(3):
            total = None
            for other in range(3):
                if block[d, other] != 0.0:
                    term = np.float32(block[d, other]) * values[other]
                    total = term if total is None else total + term
            if total is not None:
                yield d, waves[d], values[d], total


def energy_of(modes):
    total = None
    for _, _, value, force in modal_forces(modes):
        total = value * force if total is None else total + value * force
    return total


def node_plane(gathered):
    parts = []
    for wave_z in (0, 1):
        even, odd = gathered[0, wave_z], gathered[1, wave_z]
        parts.append((even - odd) + pltpu.roll(even + odd, 1, 0))
    behind = pltpu.roll(parts[0] + parts[1], 1, 1)
    return (parts[0] - parts[1]) + jnp.where(lane_mask(behind.shape, 0), 0.0, behind)


def operator_planes(planes, stiff, free):
    modes = [[plane_modes(component, ROWS) for component in plane] for plane in planes]
    gathered = [[{} for _ in range(3)] for _ in planes]
    for e in range(len(planes) - 1):
        forces = [{} for _ in range(3)]
        for d, wave, _, force in modal_forces(element_modes(modes[e], modes[e + 1])):
            forces[d][wave] = force * stiff[e]
        for d in range(3):
            for key in itertools.product((0, 1), repeat=2):
                even, odd = forces[d].get((0,) + key), forces[d].get((1,) + key)
                for node, sign in ((e, -1), (e + 1, 1)):
                    if even is None:
                        term = odd if sign == 1 else -odd
                    else:
                        term = even + odd if sign == 1 else even - odd
                    held = gathered[node][d]
                    held[key] = term if key not in held else held[key] + term
    return [
        [node_plane(gathered[n][d]) * free[n - 1] for d in range(3)]
        for n in range(1, len(planes) - 1)
    ]


def kept_if(flag):
    return jnp.where(flag == 0, 1.0, 0.0)


def with_rows(place, block, ahead, behind):
    start, stop = kept_if(place[Z_FIRST]), kept_if(place[Z_LAST])
    space = ROWS - block.shape[0] - ahead.shape[0] - behind.shape[0]
    zeros = jnp.zeros((space, block.shape[1]), F32)
    return jnp.concatenate([block, ahead * stop, zeros, behind * start], axis=0)


def krylov_kernel(place, loads, stiff, ahead, behind, density, ready, first, second, sums):
    cells = loads.shape[1]
    low, high = kept_if(place[SLAB_FIRST]), kept_if(place[SLAB_LAST])
    stiff_planes = [behind[8 + p] * low for p in range(2)]
    stiff_planes += [stiff[p] for p in range(cells)]
    stiff_planes += [ahead[12 + p] * high for p in range(2)]
    loaded = [[behind[2 * d + p] * low for d in range(4)] for p in range(2)]
    loaded += [[loads[d, p] for d in range(4)] for p in range(cells)]
    loaded += [[ahead[3 * d + p] * high for d in range(4)] for p in range(3)]
    force = [plane[:3] for plane in loaded]
    free = [plane[3] for plane in loaded]
    image = operator_planes(force, stiff_planes, free[1:-1])
    twice = operator_planes(image, stiff_planes[1:-1], free[2:-2])
    own = (force[2 : 2 + cells], image[1 : 1 + cells], twice[:cells])
    rows = density.shape[1]

    def dot(left, right):
        total = None
        for p in range(cells):
            for d in range(3):
                term = left[p][d][:rows] * right[p][d][:rows]
                total = term if total is None else total + term
        return total

    totals = [dot(own[k // 2], own[(k + 1) // 2]) for k in range(2 * ITERS - 1)]
    modes = [[plane_modes(component, rows) for component in plane] for plane in twice]
    last = None
    volume = None
    for e in range(cells):
        term = stiff_planes[2 + e][:rows] * energy_of(element_modes(modes[e], modes[e + 1]))
        last = term if last is None else last + term
        volume = density[e] if volume is None else volume + density[e]
    totals += [last, volume]
    lane = lax.broadcasted_iota(jnp.int32, sums.shape, 1)
    result = jnp.zeros(sums.shape, F32)
    for k, total in enumerate(totals):
        scalar = jnp.sum(jnp.sum(total, axis=0, keepdims=True), axis=1, keepdims=True)
        result = jnp.where(lane == k, scalar, result)
    sums[...] = result
    for p in range(cells + 1):
        for d in range(3):
            first[d, p] = image[1 + p][d]
            second[d, p] = twice[p][d]


def krylov_steps(moments):
    mean = moments[1] / moments[0]
    powers = [None, mean]
    for k in range(2, 2 * ITERS):
        powers.append(powers[-1] * mean)
    scaled = [moments[k] / moments[0] / powers[k] if k else 1.0 for k in range(2 * ITERS)]

    def product(left, right, shift):
        return sum(
            left[i] * right[j] * scaled[i + j + shift]
            for i in range(len(left))
            for j in range(len(right))
        )

    solution = [0.0] * ITERS
    residual = [1.0]
    direction = [1.0]
    norm_now = scaled[0]
    work = 0.0
    for iteration in range(ITERS):
        alpha = norm_now / product(direction, direction, 1)
        work = work + alpha * norm_now
        solution = [
            solution[i] + (alpha * direction[i] if i < len(direction) else 0.0)
            for i in range(ITERS)
        ]
        if iteration + 1 < ITERS:
            image = [0.0] + direction
            residual = [
                (residual[i] if i < len(residual) else 0.0) - alpha * image[i]
                for i in range(len(image))
            ]
            norm_next = product(residual, residual, 0)
            beta = norm_next / norm_now
            direction = [
                residual[i] + (beta * direction[i] if i < len(direction) else 0.0)
                for i in range(len(residual))
            ]
            norm_now = norm_next
    factors = [solution[i] / powers[i + 1] for i in range(ITERS)]
    return factors, work * moments[0] / mean


def energy_kernel(
    elements, place, sums, loads, ahead, first, second, density, solution, slope, out
):
    total = jnp.sum(sums[...], axis=0)
    lane = lax.broadcasted_iota(jnp.int32, total.shape, 1)
    rows_of = [
        jnp.broadcast_to(
            jnp.sum(jnp.where(lane == k, total, 0.0), axis=1, keepdims=True), total.shape
        )
        for k in range(2 * ITERS + 1)
    ]
    factors, compliance = krylov_steps(rows_of[: 2 * ITERS])
    volume = rows_of[2 * ITERS]
    constant = 2.0 * penalty * (volume / elements - vol_target) / elements
    scale = -3.0 * (1.0 - emin) / compliance
    wide = [jnp.concatenate([value, value], axis=1) for value in factors + [scale, constant]]
    cells, rows, _ = density.shape
    high = kept_if(place[SLAB_LAST])
    modes = []
    for p in range(cells + 1):
        plane = []
        for d in range(3):
            load = loads[d, p] if p < cells else ahead[3 * d] * high
            value = wide[0] * load + wide[1] * first[d, p] + wide[2] * second[d, p]
            if p < cells:
                solution[d, p] = value[:rows]
            plane.append(plane_modes(value, rows))
        modes.append(plane)
    for e in range(cells):
        energy = energy_of(element_modes(modes[e], modes[e + 1]))
        held = density[e]
        out[e] = held
        slope[e] = (wide[3] * held * held * energy + wide[4]) * held * (1.0 - held)


def column_of(line):
    size = line.shape[1]
    shape = (size, size)
    same = lax.broadcasted_iota(jnp.int32, shape, 0) == lax.broadcasted_iota(jnp.int32, shape, 1)
    return jnp.sum(jnp.where(same, line, 0.0), axis=1, keepdims=True)


def prepare_kernel(
    grid_cells, place, load_values, load_mask, fixed_mask, frequencies, w_in, w_mid, w_out,
    loads, x_cos, x_sin, z_cos, z_sin, w_in_t, w_mid_t, w_mid_half, w_column, w_row,
):
    cells, rows, size = load_mask.shape
    free = (1 - fixed_mask[...]).astype(F32)
    held = free * load_mask[...].astype(F32)
    for d in range(4):
        loads[d] = free if d == 3 else held * load_values[d]
    columns = [column_of(frequencies[k : k + 1, :]) for k in range(3)]
    half = rows // 2
    lanes = 2 * cells * half
    number = lax.broadcasted_iota(jnp.int32, (1, lanes), 1)
    side = number // (cells * half)
    plane = (number // half) % cells
    inner = number % half
    row = jnp.where(side == 1, inner + 2, jnp.where(inner < 2, inner, inner + half))
    x_centre = ((place[X_FIRST] + plane).astype(F32) + 0.5) / grid_cells[0]
    y_centre = ((place[Y_FIRST] + row).astype(F32) + 0.5) / grid_cells[1]
    phase = two_pi * (x_centre * columns[0] + y_centre * columns[1])
    cos, sin = jnp.cos(phase), jnp.sin(phase)
    for k in range(2 * cells):
        x_cos[k] = cos[:, k * half : (k + 1) * half]
        x_sin[k] = sin[:, k * half : (k + 1) * half]
    z_number = lax.broadcasted_iota(jnp.int32, (1, size), 1)
    phase = two_pi * (((z_number.astype(F32) + 0.5) / grid_cells[2]) * columns[2])
    z_cos[...] = jnp.cos(phase)
    z_sin[...] = jnp.sin(phase)
    w_in_t[...] = (0.5 * w_in[...].astype(F32)).T.astype(BF)
    middle = 0.5 * w_mid[...].astype(F32)
    w_mid_half[...] = middle.astype(BF)
    w_mid_t[...] = middle.T.astype(BF)
    line = w_out[...].astype(F32)[None, :]
    w_column[...] = 0.5 * column_of(line)
    w_row[...] = jnp.broadcast_to(line, w_row.shape).astype(BF)


def join_kernel(place, loads, stiff, ahead, behind, loads_16, stiff_16, to_before, to_next):
    cells = stiff.shape[0]
    for d in range(4):
        for p in range(cells):
            slot = d * cells + p
            block = with_rows(place, loads[d, p], ahead[slot], behind[slot])
            loads_16[d, p] = block
            if p < 3:
                to_before[3 * d + p] = block
            if p >= cells - 2:
                to_next[2 * d + p - (cells - 2)] = block
    for p in range(cells):
        slot = 4 * cells + p
        block = with_rows(place, stiff[p], ahead[slot, :2, :], behind[slot])
        stiff_16[p] = block
        if p < 2:
            to_before[12 + p] = block
        if p >= cells - 2:
            to_next[8 + p - (cells - 2)] = block


def gated(half):
    up = 1.0 + jnp.tanh(half)
    value = half * up
    return value, up + value * (2.0 - up)


def features_of(tables, group, column, scale=None):
    x_cos, x_sin, z_cos, z_sin = tables
    cos = x_cos[group, :, column : column + 1]
    sin = x_sin[group, :, column : column + 1]
    upper = z_cos[...] * cos - z_sin[...] * sin
    lower = z_sin[...] * cos + z_cos[...] * sin
    if scale is not None:
        upper, lower = upper * scale, lower * scale
    return jnp.concatenate([upper, lower], 0).astype(BF)


def forward_columns(tables, group, weights, kept, spans):
    w_in, w_mid, w_column, w_row = weights
    hidden_in, slope_mid, slope_in, hidden_mid = kept

    def keep(array, value):
        for start, first, count in spans:
            array[:, pl.ds(start, count)] = value[:, first : first + count]

    columns = tables[0].shape[2]
    features = jnp.concatenate([features_of(tables, group, q) for q in range(columns)], 1)
    value, slope = gated(jnp.dot(w_in[...], features, preferred_element_type=F32))
    value = value.astype(BF)
    keep(hidden_in, value)
    keep(slope_in, slope.astype(BF))
    value, slope = gated(jnp.dot(w_mid[...], value, preferred_element_type=F32))
    value = value.astype(BF)
    keep(hidden_mid, value)
    keep(slope_mid, (w_column[...] * slope).astype(BF))
    logits = jnp.dot(w_row[...], value, preferred_element_type=F32)[:1]
    return 0.5 * jnp.tanh(0.5 * logits) + 0.5


def stiffness_of(density):
    return emin + (1.0 - emin) * (density * density * density)


def outer_kernel(
    x_cos, x_sin, z_cos, z_sin, w_in, w_mid, w_column, w_row, loads,
    density, to_before, to_next, *kept,
):
    tables, weights = (x_cos, x_sin, z_cos, z_sin), (w_in, w_mid, w_column, w_row)
    cells, _, size = density.shape

    @pl.loop(0, cells)
    def _(p):
        start = pl.multiple_of(p * (8 * size), 8 * size)
        spans = [(start, 0, 2 * size), (start + 6 * size, 2 * size, 2 * size)]
        line = forward_columns(tables, p, weights, kept, spans)
        for q in range(4):
            part = line[:, q * size : (q + 1) * size]
            density[p, q : q + 1, :] = part
            target = to_before if q < 2 else to_next
            target[4 * cells + p, q % 2 : q % 2 + 1, :] = stiffness_of(part)
        to_before[4 * cells + p, 2:, :] = jnp.zeros((1, size), F32)
        rows = loads.shape[2]
        for d in range(4):
            to_before[d * cells + p] = loads[d, p, :3, :]
            to_next[d * cells + p] = loads[d, p, rows - 2 :, :]


def inner_kernel(
    x_cos, x_sin, z_cos, z_sin, w_in, w_mid, w_column, w_row, outer, *rest,
):
    tables, weights = (x_cos, x_sin, z_cos, z_sin), (w_in, w_mid, w_column, w_row)
    density, stiff = rest[4:6]
    cells, rows, size = density.shape

    @pl.loop(0, cells)
    def _(p):
        start = pl.multiple_of(p * (8 * size), 8 * size)
        spans = [(start + 2 * size, 0, 4 * size)]
        line = forward_columns(tables, cells + p, weights, rest[6:], spans)
        for r in range(rows):
            if 2 <= r < 6:
                part = line[:, (r - 2) * size : (r - 1) * size]
            else:
                q = r if r < 2 else r - 4
                part = outer[p, q : q + 1, :]
            density[p, r : r + 1, :] = part
            stiff[p, r : r + 1, :] = stiffness_of(part)


def back_kernel(w_mid, slope_mid, slope_in, back, done, *, span):
    done[...] = jnp.zeros_like(done)
    for start in range(0, back.shape[1], span):
        place = slice(start, start + span)
        product = jnp.dot(w_mid[...], slope_mid[:, place], preferred_element_type=F32)
        back[:, place] = (product * slope_in[:, place].astype(F32)).astype(BF)


def gradient_kernel(
    place, slope, x_cos, x_sin, z_cos, z_sin, hidden_in, slope_mid, back, hidden_mid,
    mine, other, grad_out, mid, first, running,
):
    tables = (x_cos, x_sin, z_cos, z_sin)
    cells, rows, size = slope.shape
    half = rows // 2
    group_of = [(0, r) if r < 2 else (0, r - half) if r >= rows - 2 else (1, r - 2) for r in range(rows)]
    for p in range(cells):
        lines = [slope[p, r : r + 1, :] for r in range(rows)]
        picked = [
            features_of(tables, side * cells + p, q, line) for (side, q), line in zip(group_of, lines)
        ]
        features = jnp.concatenate(picked, 1)
        line = jnp.concatenate(lines, 1)
        span = slice(p * rows * size, (p + 1) * rows * size)
        hidden = (hidden_in[:, span].astype(F32) * line).astype(BF)
        product = hidden_mid[:, span].astype(F32) * line
        total = product[:, :128]
        for k in range(1, rows * size // 128):
            total = total + product[:, k * 128 : (k + 1) * 128]
        terms = (
            lax.dot_general(hidden, slope_mid[:, span], LAST, preferred_element_type=F32),
            lax.dot_general(back[:, span], features, LAST, preferred_element_type=F32),
            total,
        )
        for held, term in zip((mid, first, running), terms):
            if p == 0:
                held[...] = term
            else:
                held[...] += term
    core = place[CORE]
    height = mid.shape[0]
    first_t = first[...].T
    for k in range(2):
        for owner in range(2):
            lanes = slice((2 * owner + k) * 128, (2 * owner + k + 1) * 128)

            @pl.when(core == owner)
            def _():
                mine[k, :height, :] = mid[:, lanes]
                mine[k, height:, :] = first_t[:, lanes]

            @pl.when(core != owner)
            def _():
                other[k, :height, :] = mid[:, lanes]
                other[k, height:, :] = first_t[:, lanes]

    line = jnp.sum(running[...].T, axis=0, keepdims=True)
    for k in range(grad_out.shape[0]):
        grad_out[k : k + 1, :] = line[:, k * 128 : (k + 1) * 128]


def share_kernel(place, parts, grad_out, shares):
    chips, height, lanes = parts.shape
    total = parts[0]
    for chip in range(1, chips):
        total = total + parts[chip]
    block = jnp.concatenate([total, grad_out[...], jnp.zeros(grad_out.shape, F32)], axis=0)
    for chip in range(chips):
        shares[chip] = block


def finish_kernel(place, half, away, grad_in, grad_mid, grad_out):
    chips = half.shape[0]
    height = half.shape[1] - 2 * grad_out.shape[0]
    middle = grad_mid.shape[0]
    at_first = place[CORE] == 0
    for group in range(4):
        part = pl.ds((group % 2) * (chips // 2), chips // 2)
        own, far = half[part, :height, :], away[part, :height, :]
        picked = jnp.where(at_first, own, far) if group < 2 else jnp.where(at_first, far, own)
        picked = picked.reshape(-1, 128)
        lanes = slice(group * 128, (group + 1) * 128)
        grad_mid[:, lanes] = picked[:middle]
        grad_in[:, lanes] = picked[middle:]
    out = jnp.sum(half[:, height:, :], axis=0) + jnp.sum(away[:, height:, :], axis=0)
    grad_out[...] = out[: grad_out.shape[0]]


VM = pltpu.VMEM
WHOLE = pl.BlockSpec(memory_space=pltpu.VMEM)
SCALARS = pl.BlockSpec(memory_space=pltpu.SMEM)
X_FIRST, Y_FIRST, CORE, SLAB_FIRST, SLAB_LAST, Z_FIRST, Z_LAST = range(7)


def params(mebibytes=8):
    return pltpu.CompilerParams(vmem_limit_bytes=mebibytes << 20)


def shaped(*shape, dtype=F32):
    return jax.ShapeDtypeStruct(shape, dtype)


def held(*shape, dtype=F32):
    return VM(shape, dtype)


def run(kernel, name, out_shape, *operands, scalars=1, space=pltpu.VMEM, scratch=(), limit=16, **more):
    arrays = [pltpu.with_memory_space_constraint(array, space) for array in operands[scalars:]]
    return pl.pallas_call(
        kernel,
        name=name,
        in_specs=[SCALARS] * scalars + [WHOLE] * len(arrays),
        out_specs=[WHOLE] * len(out_shape),
        out_shape=out_shape,
        scratch_shapes=list(scratch),
        compiler_params=params(limit),
        **more,
    )(*operands[:scalars], *arrays)


def shifted(block, axis, distance):
    size = lax.axis_size(axis)
    return lax.ppermute(block, axis, [(i, (i + distance) % size) for i in range(size)])


def gathered(values):
    chip = values + lax.ppermute(values, "c", [(0, 1), (1, 0)])
    sent = jnp.broadcast_to(chip[None], (lax.axis_size(CHIPS),) + chip.shape)
    return lax.all_to_all(sent, CHIPS, 0, 0)


def on_device(load_values, load_mask, fixed_mask, frequencies, weight_in, weight_mid, weight_out):
    cells_x, cells_y, cells_z = fixed_mask.shape
    slab, sub = lax.axis_index(SLAB), lax.axis_index("z")
    slabs, subs = lax.axis_size(SLAB), lax.axis_size("z")
    grid_cells = (cells_x * slabs, cells_y * subs, cells_z)
    elements_total = grid_cells[0] * grid_cells[1] * grid_cells[2]
    place = jnp.stack(
        [slab * cells_x, sub * cells_y, lax.axis_index("c")]
        + [(slab == 0) * 1, (slab == slabs - 1) * 1, (sub == 0) * 1, (sub == subs - 1) * 1, slab * 0]
    ).astype(jnp.int32)
    inputs, hidden = weight_in.shape
    rows = cells_x * cells_y * cells_z
    half_rows = cells_y // 2
    field = (cells_x, cells_y, cells_z)
    table = held(2 * cells_x, inputs // 2, half_rows)
    line = held(inputs // 2, cells_z)
    (
        loads, x_cos, x_sin, z_cos, z_sin,
        w_in_t, w_mid_t, w_mid_half, w_column, w_row,
    ) = run(
        functools.partial(prepare_kernel, grid_cells),
        "prepare",
        [
            held(4, *field),
            table,
            table,
            line,
            line,
            held(hidden, inputs, dtype=BF),
            held(hidden, hidden, dtype=BF),
            held(hidden, hidden, dtype=BF),
            held(hidden, 1),
            held(16, hidden, dtype=BF),
        ],
        place, load_values, load_mask, fixed_mask, frequencies, weight_in, weight_mid,
        weight_out, space=pltpu.HBM,
    )

    network = (x_cos, x_sin, z_cos, z_sin, w_in_t, w_mid_t, w_column, w_row)
    kept = [held(hidden, rows, dtype=BF)] * 4
    cost = pl.CostEstimate(
        flops=(inputs + hidden) * hidden * rows,
        bytes_accessed=4 * hidden * rows,
        transcendentals=hidden * rows,
    )
    slots = 5 * cells_x
    outer, rows_first, rows_last, *stored = run(
        outer_kernel,
        "outer",
        [held(cells_x, half_rows, cells_z), held(slots, 3, cells_z), held(slots, 2, cells_z)] + kept,
        *network,
        loads,
        scalars=0,
        limit=16,
        cost_estimate=cost,
    )
    rows_ahead = shifted(rows_first, "z", -1)
    rows_behind = shifted(rows_last, "z", 1)
    density, stiff, *stored = run(
        inner_kernel,
        "inner",
        [held(*field)] * 2 + kept,
        *network,
        outer,
        *stored,
        scalars=0,
        limit=16,
        input_output_aliases={9 + k: 2 + k for k in range(4)},
        cost_estimate=cost,
    )
    hidden_in, slope_mid, slope_in, hidden_mid = stored
    loads, stiff, planes_first, planes_last = run(
        join_kernel,
        "join",
        [held(4, cells_x, ROWS, cells_z), held(cells_x, ROWS, cells_z)]
        + [held(14, ROWS, cells_z), held(10, ROWS, cells_z)],
        place, loads, stiff, rows_ahead, rows_behind,
    )
    planes_ahead = shifted(planes_first, SLAB, -1)
    planes_behind = shifted(planes_last, SLAB, 1)

    back, ready = run(
        functools.partial(back_kernel, span=1024),
        "back",
        kept[:1] + [held(8, 128)],
        w_mid_half,
        slope_mid,
        slope_in,
        scalars=0,
        limit=16,
        input_output_aliases={2: 0},
        cost_estimate=pl.CostEstimate(
            flops=2 * hidden * hidden * rows,
            bytes_accessed=6 * hidden * rows,
            transcendentals=0,
        ),
    )

    vector = held(3, cells_x + 1, ROWS, cells_z)
    first, second, sums = run(
        krylov_kernel,
        "krylov",
        [vector, vector, held(1, 128)],
        place, loads, stiff, planes_ahead, planes_behind, density, ready,
    )
    solution, slope, density = run(
        functools.partial(energy_kernel, elements_total),
        "energy",
        [shaped(3, *field), held(*field), shaped(*field)],
        place, gathered(sums), loads, planes_ahead, first, second, density,
    )

    height = hidden + inputs
    groups = hidden // 128
    mine, other, grad_out = run(
        gradient_kernel,
        "gradients",
        [held(groups // 2, height, 128)] * 2 + [held(groups, 128)],
        place, slope, x_cos, x_sin, z_cos, z_sin, hidden_in, slope_mid, back, hidden_mid,
        limit=16,
        scratch=[VM((hidden, hidden), F32), VM((hidden, inputs), F32), VM((hidden, 128), F32)],
    )

    chips = lax.axis_size(CHIPS)
    swap = [(0, 1), (1, 0)]
    half = (mine + lax.ppermute(other, "c", swap)).reshape(chips, -1, 128)
    parts = lax.all_to_all(half, CHIPS, 0, 0)
    (shares,) = run(
        share_kernel, "share", [held(chips, half.shape[1] + 2 * groups, 128)], place, parts, grad_out
    )
    half = lax.all_to_all(shares, CHIPS, 0, 0)
    away = lax.ppermute(half, "c", swap)
    grad_in, grad_mid, grad_out = run(
        finish_kernel,
        "finish",
        [shaped(inputs, hidden), shaped(hidden, hidden), shaped(groups, 128)],
        place, half, away,
    )
    return solution, density, grad_in, grad_mid, grad_out.reshape(hidden)


def solution(mesh):
    slab, sub = mesh.devices.shape
    fine = Mesh(mesh.devices.reshape(4, 4, slab // 16, sub), ALL)
    field = P(SLAB, "z", None)
    vector = P(None, SLAB, "z", None)
    return jax.shard_map(
        on_device,
        mesh=fine,
        in_specs=(vector, field, field, P(), P(), P(), P()),
        out_specs=(vector, field, P(), P(), P()),
        check_vma=False,
    )
```

```python
import functools
import itertools
import math

import jax
import jax.numpy as jnp
import numpy as np
from jax import lax
from jax.experimental import pallas as pl
from jax.experimental.pallas import tpu as pltpu
from jax.sharding import Mesh
from jax.sharding import PartitionSpec as P

ITERS = 3
SLAB = ("x", "y", "c")
CHIPS = ("x", "y", "z")
ALL = ("x", "y", "c", "z")
BF = jnp.bfloat16
F32 = jnp.float32

two_pi = 2.0 * math.pi
emin = 0.001
penalty = 4.0
vol_target = 0.3
ROWS = 16
corner_list = list(itertools.product((0, 1), repeat=3))
LAST = (((1,), (1,)), ((), ()))


def hex_stiffness():
    poisson = 0.3
    lame_first = poisson / ((1.0 + poisson) * (1.0 - 2.0 * poisson))
    lame_second = 0.5 / (1.0 + poisson)
    elastic = np.zeros((6, 6))
    elastic[:3, :3] = lame_first
    for axis_number in range(3):
        elastic[axis_number, axis_number] += 2.0 * lame_second
        elastic[axis_number + 3, axis_number + 3] = lame_second
    gauss_points = [0.5 - 0.5 / math.sqrt(3.0), 0.5 + 0.5 / math.sqrt(3.0)]
    matrix = np.zeros((24, 24))
    for location in itertools.product(gauss_points, repeat=3):
        strain = np.zeros((6, 24))
        for corner_number, corner in enumerate(corner_list):
            factors = [
                location[axis] if corner[axis] == 1 else 1.0 - location[axis] for axis in range(3)
            ]
            slopes = [1.0 if corner[axis] == 1 else -1.0 for axis in range(3)]
            derivative = [
                slopes[0] * factors[1] * factors[2],
                factors[0] * slopes[1] * factors[2],
                factors[0] * factors[1] * slopes[2],
            ]
            column = 3 * corner_number
            for axis in range(3):
                strain[axis, column + axis] = derivative[axis]
            strain[3, column + 1] = derivative[2]
            strain[3, column + 2] = derivative[1]
            strain[4, column + 0] = derivative[2]
            strain[4, column + 2] = derivative[0]
            strain[5, column + 0] = derivative[1]
            strain[5, column + 1] = derivative[0]
        matrix += strain.T @ elastic @ strain / 8.0
    return matrix


def modal_stiffness():
    table = hex_stiffness()
    change = np.zeros((24, 24))
    for row, wave in enumerate(corner_list):
        for column, corner in enumerate(corner_list):
            sign = np.prod([1.0 if c == 1 else -1.0 for w, c in zip(wave, corner) if w == 1])
            for d in range(3):
                change[3 * row + d, 3 * column + d] = sign
    modal = change @ table @ change.T / 64.0
    blocks = []
    for parity in corner_list:
        waves = [tuple(parity[a] ^ (a == d) for a in range(3)) for d in range(3)]
        index = [3 * corner_list.index(wave) + d for d, wave in enumerate(waves)]
        block = modal[np.ix_(index, index)]
        blocks.append((waves, np.where(np.abs(block) < 1e-9, 0.0, block)))
    return blocks


BLOCKS = modal_stiffness()


def lane_mask(shape, lane):
    return lax.broadcasted_iota(jnp.int32, shape, len(shape) - 1) == lane


def plane_modes(plane, rows):
    size = plane.shape[-1]
    ahead = jnp.where(lane_mask(plane.shape, size - 1), 0.0, pltpu.roll(plane, size - 1, 1))
    modes = {}
    for wave_z, part in ((0, plane + ahead), (1, ahead - plane)):
        following = pltpu.roll(part, ROWS - 1, 0)
        modes[0, wave_z] = (part + following)[:rows]
        modes[1, wave_z] = (following - part)[:rows]
    return modes


def element_modes(lower, upper):
    found = []
    for low, high in zip(lower, upper):
        modes = {}
        for key in low:
            modes[(0,) + key] = low[key] + high[key]
            modes[(1,) + key] = high[key] - low[key]
        found.append(modes)
    return found


def modal_forces(modes):
    for waves, block in BLOCKS:
        values = [modes[d][waves[d]] for d in range(3)]
        for d in range(3):
            total = None
            for other in range(3):
                if block[d, other] != 0.0:
                    term = np.float32(block[d, other]) * values[other]
                    total = term if total is None else total + term
            if total is not None:
                yield d, waves[d], values[d], total


def energy_of(modes):
    total = None
    for _, _, value, force in modal_forces(modes):
        total = value * force if total is None else total + value * force
    return total


def node_plane(gathered):
    parts = []
    for wave_z in (0, 1):
        even, odd = gathered[0, wave_z], gathered[1, wave_z]
        parts.append((even - odd) + pltpu.roll(even + odd, 1, 0))
    behind = pltpu.roll(parts[0] + parts[1], 1, 1)
    return (parts[0] - parts[1]) + jnp.where(lane_mask(behind.shape, 0), 0.0, behind)


def operator_planes(planes, stiff, free):
    modes = [[plane_modes(component, ROWS) for component in plane] for plane in planes]
    gathered = [[{} for _ in range(3)] for _ in planes]
    for e in range(len(planes) - 1):
        forces = [{} for _ in range(3)]
        for d, wave, _, force in modal_forces(element_modes(modes[e], modes[e + 1])):
            forces[d][wave] = force * stiff[e]
        for d in range(3):
            for key in itertools.product((0, 1), repeat=2):
                even, odd = forces[d].get((0,) + key), forces[d].get((1,) + key)
                for node, sign in ((e, -1), (e + 1, 1)):
                    if even is None:
                        term = odd if sign == 1 else -odd
                    else:
                        term = even + odd if sign == 1 else even - odd
                    held = gathered[node][d]
                    held[key] = term if key not in held else held[key] + term
    return [
        [node_plane(gathered[n][d]) * free[n - 1] for d in range(3)]
        for n in range(1, len(planes) - 1)
    ]


def kept_if(flag):
    return jnp.where(flag == 0, 1.0, 0.0)


def with_rows(place, block, ahead, behind):
    start, stop = kept_if(place[Z_FIRST]), kept_if(place[Z_LAST])
    space = ROWS - block.shape[0] - ahead.shape[0] - behind.shape[0]
    zeros = jnp.zeros((space, block.shape[1]), F32)
    return jnp.concatenate([block, ahead * stop, zeros, behind * start], axis=0)


def krylov_kernel(place, loads, stiff, ahead, behind, density, ready, first, second, sums):
    cells = loads.shape[1]
    low, high = kept_if(place[SLAB_FIRST]), kept_if(place[SLAB_LAST])
    stiff_planes = [behind[8 + p] * low for p in range(2)]
    stiff_planes += [stiff[p] for p in range(cells)]
    stiff_planes += [ahead[12 + p] * high for p in range(2)]
    loaded = [[behind[2 * d + p] * low for d in range(4)] for p in range(2)]
    loaded += [[loads[d, p] for d in range(4)] for p in range(cells)]
    loaded += [[ahead[3 * d + p] * high for d in range(4)] for p in range(3)]
    force = [plane[:3] for plane in loaded]
    free = [plane[3] for plane in loaded]
    image = operator_planes(force, stiff_planes, free[1:-1])
    twice = operator_planes(image, stiff_planes[1:-1], free[2:-2])
    own = (force[2 : 2 + cells], image[1 : 1 + cells], twice[:cells])
    rows = density.shape[1]

    def dot(left, right):
        total = None
        for p in range(cells):
            for d in range(3):
                term = left[p][d][:rows] * right[p][d][:rows]
                total = term if total is None else total + term
        return total

    totals = [dot(own[k // 2], own[(k + 1) // 2]) for k in range(2 * ITERS - 1)]
    modes = [[plane_modes(component, rows) for component in plane] for plane in twice]
    last = None
    volume = None
    for e in range(cells):
        term = stiff_planes[2 + e][:rows] * energy_of(element_modes(modes[e], modes[e + 1]))
        last = term if last is None else last + term
        volume = density[e] if volume is None else volume + density[e]
    totals += [last, volume]
    lane = lax.broadcasted_iota(jnp.int32, sums.shape, 1)
    result = jnp.zeros(sums.shape, F32)
    for k, total in enumerate(totals):
        scalar = jnp.sum(jnp.sum(total, axis=0, keepdims=True), axis=1, keepdims=True)
        result = jnp.where(lane == k, scalar, result)
    sums[...] = result
    for p in range(cells + 1):
        for d in range(3):
            first[d, p] = image[1 + p][d]
            second[d, p] = twice[p][d]


def krylov_steps(moments):
    mean = moments[1] / moments[0]
    powers = [None, mean]
    for k in range(2, 2 * ITERS):
        powers.append(powers[-1] * mean)
    scaled = [moments[k] / moments[0] / powers[k] if k else 1.0 for k in range(2 * ITERS)]

    def product(left, right, shift):
        return sum(
            left[i] * right[j] * scaled[i + j + shift]
            for i in range(len(left))
            for j in range(len(right))
        )

    solution = [0.0] * ITERS
    residual = [1.0]
    direction = [1.0]
    norm_now = scaled[0]
    work = 0.0
    for iteration in range(ITERS):
        alpha = norm_now / product(direction, direction, 1)
        work = work + alpha * norm_now
        solution = [
            solution[i] + (alpha * direction[i] if i < len(direction) else 0.0)
            for i in range(ITERS)
        ]
        if iteration + 1 < ITERS:
            image = [0.0] + direction
            residual = [
                (residual[i] if i < len(residual) else 0.0) - alpha * image[i]
                for i in range(len(image))
            ]
            norm_next = product(residual, residual, 0)
            beta = norm_next / norm_now
            direction = [
                residual[i] + (beta * direction[i] if i < len(direction) else 0.0)
                for i in range(len(residual))
            ]
            norm_now = norm_next
    factors = [solution[i] / powers[i + 1] for i in range(ITERS)]
    return factors, work * moments[0] / mean


def energy_kernel(
    elements, place, sums, loads, ahead, first, second, density, solution, slope, out
):
    total = jnp.sum(sums[...], axis=0)
    lane = lax.broadcasted_iota(jnp.int32, total.shape, 1)
    rows_of = [
        jnp.broadcast_to(
            jnp.sum(jnp.where(lane == k, total, 0.0), axis=1, keepdims=True), total.shape
        )
        for k in range(2 * ITERS + 1)
    ]
    factors, compliance = krylov_steps(rows_of[: 2 * ITERS])
    volume = rows_of[2 * ITERS]
    constant = 2.0 * penalty * (volume / elements - vol_target) / elements
    scale = -3.0 * (1.0 - emin) / compliance
    wide = [jnp.concatenate([value, value], axis=1) for value in factors + [scale, constant]]
    cells, rows, _ = density.shape
    high = kept_if(place[SLAB_LAST])
    modes = []
    for p in range(cells + 1):
        plane = []
        for d in range(3):
            load = loads[d, p] if p < cells else ahead[3 * d] * high
            value = wide[0] * load + wide[1] * first[d, p] + wide[2] * second[d, p]
            if p < cells:
                solution[d, p] = value[:rows]
            plane.append(plane_modes(value, rows))
        modes.append(plane)
    for e in range(cells):
        energy = energy_of(element_modes(modes[e], modes[e + 1]))
        held = density[e]
        out[e] = held
        slope[e] = (wide[3] * held * held * energy + wide[4]) * held * (1.0 - held)


def column_of(line):
    size = line.shape[1]
    shape = (size, size)
    same = lax.broadcasted_iota(jnp.int32, shape, 0) == lax.broadcasted_iota(jnp.int32, shape, 1)
    return jnp.sum(jnp.where(same, line, 0.0), axis=1, keepdims=True)


def prepare_kernel(
    grid_cells, place, load_values, load_mask, fixed_mask, frequencies, w_in, w_mid, w_out,
    loads, x_cos, x_sin, z_cos, z_sin, w_in_t, w_mid_t, w_mid_half, w_column, w_row,
):
    cells, rows, size = load_mask.shape
    free = (1 - fixed_mask[...]).astype(F32)
    held = free * load_mask[...].astype(F32)
    for d in range(4):
        loads[d] = free if d == 3 else held * load_values[d]
    columns = [column_of(frequencies[k : k + 1, :]) for k in range(3)]
    half = rows // 2
    lanes = 2 * cells * half
    number = lax.broadcasted_iota(jnp.int32, (1, lanes), 1)
    side = number // (cells * half)
    plane = (number // half) % cells
    inner = number % half
    row = jnp.where(side == 1, inner + 2, jnp.where(inner < 2, inner, inner + half))
    x_centre = ((place[X_FIRST] + plane).astype(F32) + 0.5) / grid_cells[0]
    y_centre = ((place[Y_FIRST] + row).astype(F32) + 0.5) / grid_cells[1]
    phase = two_pi * (x_centre * columns[0] + y_centre * columns[1])
    cos, sin = jnp.cos(phase), jnp.sin(phase)
    for k in range(2 * cells):
        x_cos[k] = cos[:, k * half : (k + 1) * half]
        x_sin[k] = sin[:, k * half : (k + 1) * half]
    z_number = lax.broadcasted_iota(jnp.int32, (1, size), 1)
    phase = two_pi * (((z_number.astype(F32) + 0.5) / grid_cells[2]) * columns[2])
    z_cos[...] = jnp.cos(phase)
    z_sin[...] = jnp.sin(phase)
    w_in_t[...] = (0.5 * w_in[...].astype(F32)).T.astype(BF)
    middle = 0.5 * w_mid[...].astype(F32)
    w_mid_half[...] = middle.astype(BF)
    w_mid_t[...] = middle.T.astype(BF)
    line = w_out[...].astype(F32)[None, :]
    w_column[...] = 0.5 * column_of(line)
    w_row[...] = jnp.broadcast_to(line, w_row.shape).astype(BF)


def join_kernel(place, loads, stiff, ahead, behind, loads_16, stiff_16, to_before, to_next):
    cells = stiff.shape[0]
    for d in range(4):
        for p in range(cells):
            slot = d * cells + p
            block = with_rows(place, loads[d, p], ahead[slot], behind[slot])
            loads_16[d, p] = block
            if p < 3:
                to_before[3 * d + p] = block
            if p >= cells - 2:
                to_next[2 * d + p - (cells - 2)] = block
    for p in range(cells):
        slot = 4 * cells + p
        block = with_rows(place, stiff[p], ahead[slot, :2, :], behind[slot])
        stiff_16[p] = block
        if p < 2:
            to_before[12 + p] = block
        if p >= cells - 2:
            to_next[8 + p - (cells - 2)] = block


def gated(half):
    up = 1.0 + jnp.tanh(half)
    value = half * up
    return value, up + value * (2.0 - up)


def features_of(tables, group, column, scale=None):
    x_cos, x_sin, z_cos, z_sin = tables
    cos = x_cos[group, :, column : column + 1]
    sin = x_sin[group, :, column : column + 1]
    upper = z_cos[...] * cos - z_sin[...] * sin
    lower = z_sin[...] * cos + z_cos[...] * sin
    if scale is not None:
        upper, lower = upper * scale, lower * scale
    return jnp.concatenate([upper, lower], 0).astype(BF)


def forward_columns(tables, group, weights, kept, spans):
    w_in, w_mid, w_column, w_row = weights
    hidden_in, slope_mid, slope_in, hidden_mid = kept

    def keep(array, value):
        for start, first, count in spans:
            array[:, pl.ds(start, count)] = value[:, first : first + count]

    columns = tables[0].shape[2]
    features = jnp.concatenate([features_of(tables, group, q) for q in range(columns)], 1)
    value, slope = gated(jnp.dot(w_in[...], features, preferred_element_type=F32))
    value = value.astype(BF)
    keep(hidden_in, value)
    keep(slope_in, slope.astype(BF))
    value, slope = gated(jnp.dot(w_mid[...], value, preferred_element_type=F32))
    value = value.astype(BF)
    keep(hidden_mid, value)
    keep(slope_mid, (w_column[...] * slope).astype(BF))
    logits = jnp.dot(w_row[...], value, preferred_element_type=F32)[:1]
    return 0.5 * jnp.tanh(0.5 * logits) + 0.5


def stiffness_of(density):
    return emin + (1.0 - emin) * (density * density * density)


def outer_kernel(
    x_cos, x_sin, z_cos, z_sin, w_in, w_mid, w_column, w_row, loads,
    density, to_before, to_next, *kept,
):
    tables, weights = (x_cos, x_sin, z_cos, z_sin), (w_in, w_mid, w_column, w_row)
    cells, _, size = density.shape

    @pl.loop(0, cells)
    def _(p):
        start = pl.multiple_of(p * (8 * size), 8 * size)
        spans = [(start, 0, 2 * size), (start + 6 * size, 2 * size, 2 * size)]
        line = forward_columns(tables, p, weights, kept, spans)
        for q in range(4):
            part = line[:, q * size : (q + 1) * size]
            density[p, q : q + 1, :] = part
            target = to_before if q < 2 else to_next
            target[4 * cells + p, q % 2 : q % 2 + 1, :] = stiffness_of(part)
        to_before[4 * cells + p, 2:, :] = jnp.zeros((1, size), F32)
        rows = loads.shape[2]
        for d in range(4):
            to_before[d * cells + p] = loads[d, p, :3, :]
            to_next[d * cells + p] = loads[d, p, rows - 2 :, :]


def inner_kernel(
    x_cos, x_sin, z_cos, z_sin, w_in, w_mid, w_column, w_row, outer, *rest,
):
    tables, weights = (x_cos, x_sin, z_cos, z_sin), (w_in, w_mid, w_column, w_row)
    density, stiff = rest[4:6]
    cells, rows, size = density.shape

    @pl.loop(0, cells)
    def _(p):
        start = pl.multiple_of(p * (8 * size), 8 * size)
        spans = [(start + 2 * size, 0, 4 * size)]
        line = forward_columns(tables, cells + p, weights, rest[6:], spans)
        for r in range(rows):
            if 2 <= r < 6:
                part = line[:, (r - 2) * size : (r - 1) * size]
            else:
                q = r if r < 2 else r - 4
                part = outer[p, q : q + 1, :]
            density[p, r : r + 1, :] = part
            stiff[p, r : r + 1, :] = stiffness_of(part)


def back_kernel(w_mid, slope_mid, slope_in, back, done, *, span):
    done[...] = jnp.zeros_like(done)
    for start in range(0, back.shape[1], span):
        place = slice(start, start + span)
        product = jnp.dot(w_mid[...], slope_mid[:, place], preferred_element_type=F32)
        back[:, place] = (product * slope_in[:, place].astype(F32)).astype(BF)


def gradient_kernel(
    place, slope, x_cos, x_sin, z_cos, z_sin, hidden_in, slope_mid, back, hidden_mid,
    mine, other, out_mine, mid, first, running,
):
    tables = (x_cos, x_sin, z_cos, z_sin)
    cells, rows, size = slope.shape
    half = rows // 2
    group_of = [(0, r) if r < 2 else (0, r - half) if r >= rows - 2 else (1, r - 2) for r in range(rows)]
    for p in range(cells):
        lines = [slope[p, r : r + 1, :] for r in range(rows)]
        picked = [
            features_of(tables, side * cells + p, q, line) for (side, q), line in zip(group_of, lines)
        ]
        features = jnp.concatenate(picked, 1)
        line = jnp.concatenate(lines, 1)
        span = slice(p * rows * size, (p + 1) * rows * size)
        hidden = (hidden_in[:, span].astype(F32) * line).astype(BF)
        product = hidden_mid[:, span].astype(F32) * line
        total = product[:, :128]
        for k in range(1, rows * size // 128):
            total = total + product[:, k * 128 : (k + 1) * 128]
        terms = (
            lax.dot_general(hidden, slope_mid[:, span], LAST, preferred_element_type=F32),
            lax.dot_general(back[:, span], features, LAST, preferred_element_type=F32),
            total,
        )
        for held, term in zip((mid, first, running), terms):
            if p == 0:
                held[...] = term
            else:
                held[...] += term
    core = place[CORE]
    height = mid.shape[0]
    first_t = first[...].T
    for k in range(2):
        for owner in range(2):
            lanes = slice((2 * owner + k) * 128, (2 * owner + k + 1) * 128)

            @pl.when(core == owner)
            def _():
                mine[k, :height, :] = mid[:, lanes]
                mine[k, height:, :] = first_t[:, lanes]

            @pl.when(core != owner)
            def _():
                start = k * mine.shape[1]
                other[start : start + height, :] = mid[:, lanes]
                other[start + height : start + mine.shape[1], :] = first_t[:, lanes]

    line = jnp.sum(running[...].T, axis=0, keepdims=True)
    for k in range(2):
        low = line[:, k * 128 : (k + 1) * 128]
        high = line[:, (2 + k) * 128 : (3 + k) * 128]
        out_mine[k : k + 1, :] = jnp.where(core == 0, low, high)
        at = 2 * mine.shape[1] + k
        other[at : at + 1, :] = jnp.where(core == 0, high, low)
    other[2 * mine.shape[1] + 2 :, :] = jnp.zeros((6, 128), F32)


def share_kernel(place, parts, out_mine, swapped, shares):
    chips = parts.shape[0]
    total = parts[0]
    for chip in range(1, chips):
        total = total + parts[chip]
    last = swapped.shape[0] - 8
    out = out_mine[...] + swapped[last : last + 2, :]
    block = jnp.concatenate([total, out], axis=0)
    height = block.shape[0]
    for chip in range(chips):
        shares[chip * height : (chip + 1) * height, :] = block


def finish_kernel(place, half, away, grad_in, grad_mid, grad_out):
    height = 26
    chips = half.shape[0] // height
    middle = grad_mid.shape[0]

    def put(source, owner):
        for group in range(2):
            first = group * (chips // 2)
            lanes = slice((2 * owner + group) * 128, (2 * owner + group + 1) * 128)
            for chip in range(chips // 2):
                start = (first + chip) * height
                block = source[start : start + height - 2, :]
                row = chip * (height - 2)
                if row + height - 2 <= middle:
                    grad_mid[row : row + height - 2, lanes] = block
                elif row >= middle:
                    grad_in[row - middle : row - middle + height - 2, lanes] = block
                else:
                    grad_mid[row:, lanes] = block[: middle - row]
                    grad_in[: row + height - 2 - middle, lanes] = block[middle - row :]
        total = source[height - 2 : height, :]
        for chip in range(1, chips):
            total = total + source[(chip + 1) * height - 2 : (chip + 1) * height, :]
        grad_out[2 * owner : 2 * owner + 2, :] = total

    for owner in range(2):

        @pl.when(place[CORE] == owner)
        def _():
            put(half, owner)
            put(away, 1 - owner)


VM = pltpu.VMEM
WHOLE = pl.BlockSpec(memory_space=pltpu.VMEM)
SCALARS = pl.BlockSpec(memory_space=pltpu.SMEM)
X_FIRST, Y_FIRST, CORE, SLAB_FIRST, SLAB_LAST, Z_FIRST, Z_LAST = range(7)


def params(mebibytes=8):
    return pltpu.CompilerParams(vmem_limit_bytes=mebibytes << 20)


def shaped(*shape, dtype=F32):
    return jax.ShapeDtypeStruct(shape, dtype)


def held(*shape, dtype=F32):
    return VM(shape, dtype)


def run(kernel, name, out_shape, *operands, scalars=1, space=pltpu.VMEM, scratch=(), limit=16, **more):
    arrays = [pltpu.with_memory_space_constraint(array, space) for array in operands[scalars:]]
    return pl.pallas_call(
        kernel,
        name=name,
        in_specs=[SCALARS] * scalars + [WHOLE] * len(arrays),
        out_specs=[WHOLE] * len(out_shape),
        out_shape=out_shape,
        scratch_shapes=list(scratch),
        compiler_params=params(limit),
        **more,
    )(*operands[:scalars], *arrays)


def shifted(block, axis, distance):
    size = lax.axis_size(axis)
    return lax.ppermute(block, axis, [(i, (i + distance) % size) for i in range(size)])


def gathered(values):
    chip = values + lax.ppermute(values, "c", [(0, 1), (1, 0)])
    sent = jnp.broadcast_to(chip[None], (lax.axis_size(CHIPS),) + chip.shape)
    return lax.all_to_all(sent, CHIPS, 0, 0)


def on_device(load_values, load_mask, fixed_mask, frequencies, weight_in, weight_mid, weight_out):
    cells_x, cells_y, cells_z = fixed_mask.shape
    slab, sub = lax.axis_index(SLAB), lax.axis_index("z")
    slabs, subs = lax.axis_size(SLAB), lax.axis_size("z")
    grid_cells = (cells_x * slabs, cells_y * subs, cells_z)
    elements_total = grid_cells[0] * grid_cells[1] * grid_cells[2]
    place = jnp.stack(
        [slab * cells_x, sub * cells_y, lax.axis_index("c")]
        + [(slab == 0) * 1, (slab == slabs - 1) * 1, (sub == 0) * 1, (sub == subs - 1) * 1, slab * 0]
    ).astype(jnp.int32)
    inputs, hidden = weight_in.shape
    rows = cells_x * cells_y * cells_z
    half_rows = cells_y // 2
    field = (cells_x, cells_y, cells_z)
    table = held(2 * cells_x, inputs // 2, half_rows)
    line = held(inputs // 2, cells_z)
    (
        loads, x_cos, x_sin, z_cos, z_sin,
        w_in_t, w_mid_t, w_mid_half, w_column, w_row,
    ) = run(
        functools.partial(prepare_kernel, grid_cells),
        "prepare",
        [
            held(4, *field),
            table,
            table,
            line,
            line,
            held(hidden, inputs, dtype=BF),
            held(hidden, hidden, dtype=BF),
            held(hidden, hidden, dtype=BF),
            held(hidden, 1),
            held(16, hidden, dtype=BF),
        ],
        place, load_values, load_mask, fixed_mask, frequencies, weight_in, weight_mid,
        weight_out, space=pltpu.HBM,
    )

    network = (x_cos, x_sin, z_cos, z_sin, w_in_t, w_mid_t, w_column, w_row)
    kept = [held(hidden, rows, dtype=BF)] * 4
    cost = pl.CostEstimate(
        flops=(inputs + hidden) * hidden * rows,
        bytes_accessed=4 * hidden * rows,
        transcendentals=hidden * rows,
    )
    slots = 5 * cells_x
    outer, rows_first, rows_last, *stored = run(
        outer_kernel,
        "outer",
        [held(cells_x, half_rows, cells_z), held(slots, 3, cells_z), held(slots, 2, cells_z)] + kept,
        *network,
        loads,
        scalars=0,
        limit=16,
        cost_estimate=cost,
    )
    rows_ahead = shifted(rows_first, "z", -1)
    rows_behind = shifted(rows_last, "z", 1)
    density, stiff, *stored = run(
        inner_kernel,
        "inner",
        [held(*field)] * 2 + kept,
        *network,
        outer,
        *stored,
        scalars=0,
        limit=16,
        input_output_aliases={9 + k: 2 + k for k in range(4)},
        cost_estimate=cost,
    )
    hidden_in, slope_mid, slope_in, hidden_mid = stored
    loads, stiff, planes_first, planes_last = run(
        join_kernel,
        "join",
        [held(4, cells_x, ROWS, cells_z), held(cells_x, ROWS, cells_z)]
        + [held(14, ROWS, cells_z), held(10, ROWS, cells_z)],
        place, loads, stiff, rows_ahead, rows_behind,
    )
    planes_ahead = shifted(planes_first, SLAB, -1)
    planes_behind = shifted(planes_last, SLAB, 1)

    back, ready = run(
        functools.partial(back_kernel, span=1024),
        "back",
        kept[:1] + [held(8, 128)],
        w_mid_half,
        slope_mid,
        slope_in,
        scalars=0,
        limit=16,
        input_output_aliases={2: 0},
        cost_estimate=pl.CostEstimate(
            flops=2 * hidden * hidden * rows,
            bytes_accessed=6 * hidden * rows,
            transcendentals=0,
        ),
    )

    vector = held(3, cells_x + 1, ROWS, cells_z)
    first, second, sums = run(
        krylov_kernel,
        "krylov",
        [vector, vector, held(1, 128)],
        place, loads, stiff, planes_ahead, planes_behind, density, ready,
    )
    solution, slope, density = run(
        functools.partial(energy_kernel, elements_total),
        "energy",
        [shaped(3, *field), held(*field), shaped(*field)],
        place, gathered(sums), loads, planes_ahead, first, second, density,
    )

    height = hidden + inputs
    groups = hidden // 128
    mine, other, out_mine = run(
        gradient_kernel,
        "gradients",
        [held(groups // 2, height, 128), held(groups // 2 * height + 8, 128)]
        + [held(groups // 2, 128)],
        place, slope, x_cos, x_sin, z_cos, z_sin, hidden_in, slope_mid, back, hidden_mid,
        limit=16,
        scratch=[VM((hidden, hidden), F32), VM((hidden, inputs), F32), VM((hidden, 128), F32)],
    )

    chips = lax.axis_size(CHIPS)
    swap = [(0, 1), (1, 0)]
    swapped = lax.ppermute(other, "c", swap)
    half = (mine.reshape(-1, 128) + swapped[:-8]).reshape(chips, -1, 128)
    parts = lax.all_to_all(half, CHIPS, 0, 0)
    tall = half.shape[1] + groups // 2
    (shares,) = run(
        share_kernel, "share", [held(chips * tall, 128)], place, parts, out_mine, swapped
    )
    half = lax.all_to_all(shares.reshape(chips, tall, 1, 128), CHIPS, 0, 0)
    half = half.reshape(chips * tall, 128)
    away = lax.ppermute(half, "c", swap)
    grad_in, grad_mid, grad_out = run(
        finish_kernel,
        "finish",
        [shaped(inputs, hidden), shaped(hidden, hidden), shaped(groups, 128)],
        place, half, away,
    )
    return solution, density, grad_in, grad_mid, grad_out.reshape(hidden)


def solution(mesh):
    slab, sub = mesh.devices.shape
    fine = Mesh(mesh.devices.reshape(4, 4, slab // 16, sub), ALL)
    field = P(SLAB, "z", None)
    vector = P(None, SLAB, "z", None)
    return jax.shard_map(
        on_device,
        mesh=fine,
        in_specs=(vector, field, field, P(), P(), P(), P()),
        out_specs=(vector, field, P(), P(), P()),
        check_vma=False,
    )
```

```python
import functools
import itertools
import math

import jax
import jax.numpy as jnp
import numpy as np
from jax import lax
from jax.experimental import pallas as pl
from jax.experimental.pallas import tpu as pltpu
from jax.sharding import Mesh
from jax.sharding import PartitionSpec as P

ITERS = 3
SLAB = ("x", "y", "c")
CHIPS = ("x", "y", "z")
ALL = ("x", "y", "c", "z")
BF = jnp.bfloat16
F32 = jnp.float32

two_pi = 2.0 * math.pi
emin = 0.001
penalty = 4.0
vol_target = 0.3
ROWS = 16
corner_list = list(itertools.product((0, 1), repeat=3))
LAST = (((1,), (1,)), ((), ()))


def hex_stiffness():
    poisson = 0.3
    lame_first = poisson / ((1.0 + poisson) * (1.0 - 2.0 * poisson))
    lame_second = 0.5 / (1.0 + poisson)
    elastic = np.zeros((6, 6))
    elastic[:3, :3] = lame_first
    for axis_number in range(3):
        elastic[axis_number, axis_number] += 2.0 * lame_second
        elastic[axis_number + 3, axis_number + 3] = lame_second
    gauss_points = [0.5 - 0.5 / math.sqrt(3.0), 0.5 + 0.5 / math.sqrt(3.0)]
    matrix = np.zeros((24, 24))
    for location in itertools.product(gauss_points, repeat=3):
        strain = np.zeros((6, 24))
        for corner_number, corner in enumerate(corner_list):
            factors = [
                location[axis] if corner[axis] == 1 else 1.0 - location[axis] for axis in range(3)
            ]
            slopes = [1.0 if corner[axis] == 1 else -1.0 for axis in range(3)]
            derivative = [
                slopes[0] * factors[1] * factors[2],
                factors[0] * slopes[1] * factors[2],
                factors[0] * factors[1] * slopes[2],
            ]
            column = 3 * corner_number
            for axis in range(3):
                strain[axis, column + axis] = derivative[axis]
            strain[3, column + 1] = derivative[2]
            strain[3, column + 2] = derivative[1]
            strain[4, column + 0] = derivative[2]
            strain[4, column + 2] = derivative[0]
            strain[5, column + 0] = derivative[1]
            strain[5, column + 1] = derivative[0]
        matrix += strain.T @ elastic @ strain / 8.0
    return matrix


def modal_stiffness():
    table = hex_stiffness()
    change = np.zeros((24, 24))
    for row, wave in enumerate(corner_list):
        for column, corner in enumerate(corner_list):
            sign = np.prod([1.0 if c == 1 else -1.0 for w, c in zip(wave, corner) if w == 1])
            for d in range(3):
                change[3 * row + d, 3 * column + d] = sign
    modal = change @ table @ change.T / 64.0
    blocks = []
    for parity in corner_list:
        waves = [tuple(parity[a] ^ (a == d) for a in range(3)) for d in range(3)]
        index = [3 * corner_list.index(wave) + d for d, wave in enumerate(waves)]
        block = modal[np.ix_(index, index)]
        blocks.append((waves, np.where(np.abs(block) < 1e-9, 0.0, block)))
    return blocks


def connected(block, used):
    parts = []
    for d in used:
        for part in parts:
            if block[d, part[0]] != 0.0:
                part.append(d)
                break
        else:
            parts.append([d])
    for part in parts:
        pairs = [block[i, j] for i in part for j in part if i != j]
        assert np.ptp(pairs) < 1e-9 if pairs else True
    return parts


BLOCKS = modal_stiffness()


def lane_mask(shape, lane):
    return lax.broadcasted_iota(jnp.int32, shape, len(shape) - 1) == lane


def plane_modes(plane, rows):
    size = plane.shape[-1]
    ahead = jnp.where(lane_mask(plane.shape, size - 1), 0.0, pltpu.roll(plane, size - 1, 1))
    modes = {}
    for wave_z, part in ((0, plane + ahead), (1, ahead - plane)):
        following = pltpu.roll(part, ROWS - 1, 0)
        modes[0, wave_z] = (part + following)[:rows]
        modes[1, wave_z] = (following - part)[:rows]
    return modes


def element_modes(lower, upper):
    found = []
    for low, high in zip(lower, upper):
        modes = {}
        for key in low:
            modes[(0,) + key] = low[key] + high[key]
            modes[(1,) + key] = high[key] - low[key]
        found.append(modes)
    return found


def modal_forces(modes):
    for waves, block in BLOCKS:
        used = [d for d in range(3) if np.any(block[d] != 0.0)]
        for part in connected(block, used):
            values = [modes[d][waves[d]] for d in part]
            if len(part) == 1:
                forces = [np.float32(block[part[0], part[0]]) * values[0]]
            else:
                common = block[part[0], part[1]]
                total = values[0] + values[1]
                for value in values[2:]:
                    total = total + value
                shared = np.float32(common) * total
                forces = []
                for d, value in zip(part, values):
                    extra = block[d, d] - common
                    if abs(extra) > 1e-9:
                        forces.append(shared + np.float32(extra) * value)
                    else:
                        forces.append(shared)
            for d, value, force in zip(part, values, forces):
                yield d, waves[d], value, force


def energy_of(modes):
    total = None
    for _, _, value, force in modal_forces(modes):
        total = value * force if total is None else total + value * force
    return total


def node_plane(gathered):
    parts = []
    for wave_z in (0, 1):
        even, odd = gathered[0, wave_z], gathered[1, wave_z]
        parts.append((even - odd) + pltpu.roll(even + odd, 1, 0))
    behind = pltpu.roll(parts[0] + parts[1], 1, 1)
    return (parts[0] - parts[1]) + jnp.where(lane_mask(behind.shape, 0), 0.0, behind)


def operator_planes(planes, stiff, free):
    modes = [[plane_modes(component, ROWS) for component in plane] for plane in planes]
    gathered = [[{} for _ in range(3)] for _ in planes]
    for e in range(len(planes) - 1):
        forces = [{} for _ in range(3)]
        for d, wave, _, force in modal_forces(element_modes(modes[e], modes[e + 1])):
            forces[d][wave] = force * stiff[e]
        for d in range(3):
            for key in itertools.product((0, 1), repeat=2):
                even, odd = forces[d].get((0,) + key), forces[d].get((1,) + key)
                for node, sign in ((e, -1), (e + 1, 1)):
                    if even is None:
                        term = odd if sign == 1 else -odd
                    else:
                        term = even + odd if sign == 1 else even - odd
                    held = gathered[node][d]
                    held[key] = term if key not in held else held[key] + term
    return [
        [node_plane(gathered[n][d]) * free[n - 1] for d in range(3)]
        for n in range(1, len(planes) - 1)
    ]


def kept_if(flag):
    return jnp.where(flag == 0, 1.0, 0.0)


def with_rows(place, block, ahead, behind):
    start, stop = kept_if(place[Z_FIRST]), kept_if(place[Z_LAST])
    space = ROWS - block.shape[0] - ahead.shape[0] - behind.shape[0]
    zeros = jnp.zeros((space, block.shape[1]), F32)
    return jnp.concatenate([block, ahead * stop, zeros, behind * start], axis=0)


def krylov_kernel(place, loads, stiff, ahead, behind, density, ready, first, second, sums):
    cells = loads.shape[1]
    low, high = kept_if(place[SLAB_FIRST]), kept_if(place[SLAB_LAST])
    stiff_planes = [behind[8 + p] * low for p in range(2)]
    stiff_planes += [stiff[p] for p in range(cells)]
    stiff_planes += [ahead[12 + p] * high for p in range(2)]
    loaded = [[behind[2 * d + p] * low for d in range(4)] for p in range(2)]
    loaded += [[loads[d, p] for d in range(4)] for p in range(cells)]
    loaded += [[ahead[3 * d + p] * high for d in range(4)] for p in range(3)]
    force = [plane[:3] for plane in loaded]
    free = [plane[3] for plane in loaded]
    image = operator_planes(force, stiff_planes, free[1:-1])
    twice = operator_planes(image, stiff_planes[1:-1], free[2:-2])
    own = (force[2 : 2 + cells], image[1 : 1 + cells], twice[:cells])
    rows = density.shape[1]

    def dot(left, right):
        total = None
        for p in range(cells):
            for d in range(3):
                term = left[p][d][:rows] * right[p][d][:rows]
                total = term if total is None else total + term
        return total

    totals = [dot(own[k // 2], own[(k + 1) // 2]) for k in range(2 * ITERS - 1)]
    modes = [[plane_modes(component, rows) for component in plane] for plane in twice]
    last = None
    volume = None
    for e in range(cells):
        term = stiff_planes[2 + e][:rows] * energy_of(element_modes(modes[e], modes[e + 1]))
        last = term if last is None else last + term
        volume = density[e] if volume is None else volume + density[e]
    totals += [last, volume]
    lane = lax.broadcasted_iota(jnp.int32, sums.shape, 1)
    result = jnp.zeros(sums.shape, F32)
    for k, total in enumerate(totals):
        scalar = jnp.sum(jnp.sum(total, axis=0, keepdims=True), axis=1, keepdims=True)
        result = jnp.where(lane == k, scalar, result)
    sums[...] = result
    for p in range(cells + 1):
        for d in range(3):
            first[d, p] = image[1 + p][d]
            second[d, p] = twice[p][d]


def krylov_steps(moments):
    mean = moments[1] / moments[0]
    powers = [None, mean]
    for k in range(2, 2 * ITERS):
        powers.append(powers[-1] * mean)
    scaled = [moments[k] / moments[0] / powers[k] if k else 1.0 for k in range(2 * ITERS)]

    def product(left, right, shift):
        return sum(
            left[i] * right[j] * scaled[i + j + shift]
            for i in range(len(left))
            for j in range(len(right))
        )

    solution = [0.0] * ITERS
    residual = [1.0]
    direction = [1.0]
    norm_now = scaled[0]
    work = 0.0
    for iteration in range(ITERS):
        alpha = norm_now / product(direction, direction, 1)
        work = work + alpha * norm_now
        solution = [
            solution[i] + (alpha * direction[i] if i < len(direction) else 0.0)
            for i in range(ITERS)
        ]
        if iteration + 1 < ITERS:
            image = [0.0] + direction
            residual = [
                (residual[i] if i < len(residual) else 0.0) - alpha * image[i]
                for i in range(len(image))
            ]
            norm_next = product(residual, residual, 0)
            beta = norm_next / norm_now
            direction = [
                residual[i] + (beta * direction[i] if i < len(direction) else 0.0)
                for i in range(len(residual))
            ]
            norm_now = norm_next
    factors = [solution[i] / powers[i + 1] for i in range(ITERS)]
    return factors, work * moments[0] / mean


def energy_kernel(
    elements, place, sums, loads, ahead, first, second, density, solution, slope, out
):
    total = jnp.sum(sums[...], axis=0)
    lane = lax.broadcasted_iota(jnp.int32, total.shape, 1)
    rows_of = [
        jnp.broadcast_to(
            jnp.sum(jnp.where(lane == k, total, 0.0), axis=1, keepdims=True), total.shape
        )
        for k in range(2 * ITERS + 1)
    ]
    factors, compliance = krylov_steps(rows_of[: 2 * ITERS])
    volume = rows_of[2 * ITERS]
    constant = 2.0 * penalty * (volume / elements - vol_target) / elements
    scale = -3.0 * (1.0 - emin) / compliance
    wide = [jnp.concatenate([value, value], axis=1) for value in factors + [scale, constant]]
    cells, rows, _ = density.shape
    high = kept_if(place[SLAB_LAST])
    modes = []
    for p in range(cells + 1):
        plane = []
        for d in range(3):
            load = loads[d, p] if p < cells else ahead[3 * d] * high
            value = wide[0] * load + wide[1] * first[d, p] + wide[2] * second[d, p]
            if p < cells:
                solution[d, p] = value[:rows]
            plane.append(plane_modes(value, rows))
        modes.append(plane)
    for e in range(cells):
        energy = energy_of(element_modes(modes[e], modes[e + 1]))
        held = density[e]
        out[e] = held
        slope[e] = (wide[3] * held * held * energy + wide[4]) * held * (1.0 - held)


def column_of(line):
    size = line.shape[1]
    shape = (size, size)
    same = lax.broadcasted_iota(jnp.int32, shape, 0) == lax.broadcasted_iota(jnp.int32, shape, 1)
    return jnp.sum(jnp.where(same, line, 0.0), axis=1, keepdims=True)


def prepare_kernel(
    grid_cells, place, load_values, load_mask, fixed_mask, frequencies, w_in, w_mid, w_out,
    loads, x_cos, x_sin, z_cos, z_sin, w_in_t, w_mid_t, w_mid_half, w_column, w_row,
    w_in_here, w_mid_here, arrived,
):
    copies = [
        pltpu.make_async_copy(w_in, w_in_here, arrived.at[0]),
        pltpu.make_async_copy(w_mid, w_mid_here, arrived.at[1]),
    ]
    for copy in copies:
        copy.start()
    cells, rows, size = load_mask.shape
    free = (1 - fixed_mask[...]).astype(F32)
    held = free * load_mask[...].astype(F32)
    for d in range(4):
        loads[d] = free if d == 3 else held * load_values[d]
    columns = [column_of(frequencies[k : k + 1, :]) for k in range(3)]
    half = rows // 2
    lanes = 2 * cells * half
    number = lax.broadcasted_iota(jnp.int32, (1, lanes), 1)
    side = number // (cells * half)
    plane = (number // half) % cells
    inner = number % half
    row = jnp.where(side == 1, inner + 2, jnp.where(inner < 2, inner, inner + half))
    x_centre = ((place[X_FIRST] + plane).astype(F32) + 0.5) / grid_cells[0]
    y_centre = ((place[Y_FIRST] + row).astype(F32) + 0.5) / grid_cells[1]
    phase = two_pi * (x_centre * columns[0] + y_centre * columns[1])
    cos, sin = jnp.cos(phase), jnp.sin(phase)
    for k in range(2 * cells):
        x_cos[k] = cos[:, k * half : (k + 1) * half]
        x_sin[k] = sin[:, k * half : (k + 1) * half]
    z_number = lax.broadcasted_iota(jnp.int32, (1, size), 1)
    phase = two_pi * (((z_number.astype(F32) + 0.5) / grid_cells[2]) * columns[2])
    z_cos[...] = jnp.cos(phase)
    z_sin[...] = jnp.sin(phase)
    line = w_out[...].astype(F32)[None, :]
    w_column[...] = 0.5 * column_of(line)
    w_row[...] = jnp.broadcast_to(line, w_row.shape).astype(BF)
    for copy in copies:
        copy.wait()
    w_in_t[...] = (0.5 * w_in_here[...].astype(F32)).T.astype(BF)
    middle = 0.5 * w_mid_here[...].astype(F32)
    w_mid_half[...] = middle.astype(BF)
    w_mid_t[...] = middle.T.astype(BF)


def join_kernel(place, loads, stiff, ahead, behind, loads_16, stiff_16, to_before, to_next):
    cells = stiff.shape[0]
    for d in range(4):
        for p in range(cells):
            slot = d * cells + p
            block = with_rows(place, loads[d, p], ahead[slot], behind[slot])
            loads_16[d, p] = block
            if p < 3:
                to_before[3 * d + p] = block
            if p >= cells - 2:
                to_next[2 * d + p - (cells - 2)] = block
    for p in range(cells):
        slot = 4 * cells + p
        block = with_rows(place, stiff[p], ahead[slot, :2, :], behind[slot])
        stiff_16[p] = block
        if p < 2:
            to_before[12 + p] = block
        if p >= cells - 2:
            to_next[8 + p - (cells - 2)] = block


def gated(half):
    up = 1.0 + jnp.tanh(half)
    value = half * up
    return value, up + value * (2.0 - up)


def features_of(tables, group, column, scale=None):
    x_cos, x_sin, z_cos, z_sin = tables
    cos = x_cos[group, :, column : column + 1]
    sin = x_sin[group, :, column : column + 1]
    upper = z_cos[...] * cos - z_sin[...] * sin
    lower = z_sin[...] * cos + z_cos[...] * sin
    if scale is not None:
        upper, lower = upper * scale, lower * scale
    return jnp.concatenate([upper, lower], 0).astype(BF)


def forward_columns(tables, group, weights, kept, spans):
    w_in, w_mid, w_column, w_row = weights
    hidden_in, slope_mid, slope_in, hidden_mid = kept

    def keep(array, value):
        for start, first, count in spans:
            array[:, pl.ds(start, count)] = value[:, first : first + count]

    columns = tables[0].shape[2]
    features = jnp.concatenate([features_of(tables, group, q) for q in range(columns)], 1)
    value, slope = gated(jnp.dot(w_in[...], features, preferred_element_type=F32))
    value = value.astype(BF)
    keep(hidden_in, value)
    keep(slope_in, slope.astype(BF))
    value, slope = gated(jnp.dot(w_mid[...], value, preferred_element_type=F32))
    value = value.astype(BF)
    keep(hidden_mid, value)
    keep(slope_mid, (w_column[...] * slope).astype(BF))
    logits = jnp.dot(w_row[...], value, preferred_element_type=F32)[:1]
    return 0.5 * jnp.tanh(0.5 * logits) + 0.5


def stiffness_of(density):
    return emin + (1.0 - emin) * (density * density * density)


def outer_kernel(
    x_cos, x_sin, z_cos, z_sin, w_in, w_mid, w_column, w_row, loads,
    density, to_before, to_next, *kept,
):
    tables, weights = (x_cos, x_sin, z_cos, z_sin), (w_in, w_mid, w_column, w_row)
    cells, _, size = density.shape

    @pl.loop(0, cells)
    def _(p):
        start = pl.multiple_of(p * (8 * size), 8 * size)
        spans = [(start, 0, 2 * size), (start + 6 * size, 2 * size, 2 * size)]
        line = forward_columns(tables, p, weights, kept, spans)
        for q in range(4):
            part = line[:, q * size : (q + 1) * size]
            density[p, q : q + 1, :] = part
            target = to_before if q < 2 else to_next
            target[4 * cells + p, q % 2 : q % 2 + 1, :] = stiffness_of(part)
        to_before[4 * cells + p, 2:, :] = jnp.zeros((1, size), F32)
        rows = loads.shape[2]
        for d in range(4):
            to_before[d * cells + p] = loads[d, p, :3, :]
            to_next[d * cells + p] = loads[d, p, rows - 2 :, :]


def inner_kernel(
    x_cos, x_sin, z_cos, z_sin, w_in, w_mid, w_column, w_row, outer, *rest,
):
    tables, weights = (x_cos, x_sin, z_cos, z_sin), (w_in, w_mid, w_column, w_row)
    density, stiff = rest[4:6]
    cells, rows, size = density.shape

    @pl.loop(0, cells)
    def _(p):
        start = pl.multiple_of(p * (8 * size), 8 * size)
        spans = [(start + 2 * size, 0, 4 * size)]
        line = forward_columns(tables, cells + p, weights, rest[6:], spans)
        for r in range(rows):
            if 2 <= r < 6:
                part = line[:, (r - 2) * size : (r - 1) * size]
            else:
                q = r if r < 2 else r - 4
                part = outer[p, q : q + 1, :]
            density[p, r : r + 1, :] = part
            stiff[p, r : r + 1, :] = stiffness_of(part)


def back_kernel(w_mid, slope_mid, slope_in, back, done, *, span):
    done[...] = jnp.zeros_like(done)
    for start in range(0, back.shape[1], span):
        place = slice(start, start + span)
        product = jnp.dot(w_mid[...], slope_mid[:, place], preferred_element_type=F32)
        back[:, place] = (product * slope_in[:, place].astype(F32)).astype(BF)


def gradient_kernel(
    place, slope, x_cos, x_sin, z_cos, z_sin, hidden_in, slope_mid, back, hidden_mid,
    mine, other, out_mine, mid, first, running,
):
    tables = (x_cos, x_sin, z_cos, z_sin)
    cells, rows, size = slope.shape
    half = rows // 2
    group_of = [(0, r) if r < 2 else (0, r - half) if r >= rows - 2 else (1, r - 2) for r in range(rows)]
    for p in range(cells):
        lines = [slope[p, r : r + 1, :] for r in range(rows)]
        picked = [
            features_of(tables, side * cells + p, q, line) for (side, q), line in zip(group_of, lines)
        ]
        features = jnp.concatenate(picked, 1)
        line = jnp.concatenate(lines, 1)
        span = slice(p * rows * size, (p + 1) * rows * size)
        hidden = (hidden_in[:, span].astype(F32) * line).astype(BF)
        terms = (
            lax.dot_general(hidden, slope_mid[:, span], LAST, preferred_element_type=F32),
            lax.dot_general(back[:, span], features, LAST, preferred_element_type=F32),
        )
        total = None
        for k in range(rows * size // 128):
            lanes = slice(p * rows * size + k * 128, p * rows * size + (k + 1) * 128)
            term = hidden_mid[:, lanes].astype(F32) * line[:, k * 128 : (k + 1) * 128]
            total = term if total is None else total + term
        terms = terms + (total,)
        for held, term in zip((mid, first, running), terms):
            if p == 0:
                held[...] = term
            else:
                held[...] += term
    core = place[CORE]
    height = mid.shape[0]
    first_t = first[...].T
    for k in range(2):
        for owner in range(2):
            lanes = slice((2 * owner + k) * 128, (2 * owner + k + 1) * 128)

            @pl.when(core == owner)
            def _():
                mine[k, :height, :] = mid[:, lanes]
                mine[k, height:, :] = first_t[:, lanes]

            @pl.when(core != owner)
            def _():
                start = k * mine.shape[1]
                other[start : start + height, :] = mid[:, lanes]
                other[start + height : start + mine.shape[1], :] = first_t[:, lanes]

    line = jnp.sum(running[...].T, axis=0, keepdims=True)
    for k in range(2):
        low = line[:, k * 128 : (k + 1) * 128]
        high = line[:, (2 + k) * 128 : (3 + k) * 128]
        out_mine[k : k + 1, :] = jnp.where(core == 0, low, high)
        at = 2 * mine.shape[1] + k
        other[at : at + 1, :] = jnp.where(core == 0, high, low)
    other[2 * mine.shape[1] + 2 :, :] = jnp.zeros((6, 128), F32)


def share_kernel(place, parts, out_mine, swapped, shares):
    chips = parts.shape[0]
    total = parts[0]
    for chip in range(1, chips):
        total = total + parts[chip]
    last = swapped.shape[0] - 8
    out = out_mine[...] + swapped[last : last + 2, :]
    block = jnp.concatenate([total, out], axis=0)
    height = block.shape[0]
    for chip in range(chips):
        shares[chip * height : (chip + 1) * height, :] = block


def finish_kernel(place, half, away, grad_in, grad_mid, grad_out, filled, sent):
    height = 26
    count = height - 2
    chips = half.shape[0] // height
    middle, total_rows = grad_mid.shape[0], filled.shape[0]
    some = 8

    def put(source, owner, start):
        for group in range(2):
            lanes = slice((2 * owner + group) * 128, (2 * owner + group + 1) * 128)
            for chip in range(start, start + some):
                at = (group * (chips // 2) + chip) * height
                filled[chip * count : (chip + 1) * count, lanes] = source[at : at + count, :]

    def put_out(source, owner):
        total = source[count:height, :]
        for chip in range(1, chips):
            total = total + source[chip * height + count : (chip + 1) * height, :]
        grad_out[2 * owner : 2 * owner + 2, :] = total

    copies = []
    for start in range(0, chips // 2, some):
        for owner in range(2):

            @pl.when(place[CORE] == owner)
            def _():
                put(half, owner, start)
                put(away, 1 - owner, start)

        low, high = start * count, (start + some) * count
        for target, first, last in ((grad_mid, 0, middle), (grad_in, middle, total_rows)):
            begin, end = max(low, first), min(high, last)
            if begin < end:
                copy = pltpu.make_async_copy(
                    filled.at[begin:end, :],
                    target.at[begin - first : end - first, :],
                    sent.at[len(copies)],
                )
                copy.start()
                copies.append(copy)
    for owner in range(2):

        @pl.when(place[CORE] == owner)
        def _():
            put_out(half, owner)
            put_out(away, 1 - owner)

    for copy in copies:
        copy.wait()


VM = pltpu.VMEM
WHOLE = pl.BlockSpec(memory_space=pltpu.VMEM)
SCALARS = pl.BlockSpec(memory_space=pltpu.SMEM)
FAR = pl.BlockSpec(memory_space=pltpu.HBM)
X_FIRST, Y_FIRST, CORE, SLAB_FIRST, SLAB_LAST, Z_FIRST, Z_LAST = range(7)


def params(mebibytes=8):
    return pltpu.CompilerParams(vmem_limit_bytes=mebibytes << 20)


def shaped(*shape, dtype=F32):
    return jax.ShapeDtypeStruct(shape, dtype)


def held(*shape, dtype=F32):
    return VM(shape, dtype)


def run(
    kernel, name, out_shape, *operands,
    scalars=1, space=pltpu.VMEM, scratch=(), limit=16, far_in=(), far_out=(), **more,
):
    arrays = [pltpu.with_memory_space_constraint(array, space) for array in operands[scalars:]]
    return pl.pallas_call(
        kernel,
        name=name,
        in_specs=[SCALARS] * scalars
        + [FAR if k in far_in else WHOLE for k in range(len(arrays))],
        out_specs=[FAR if k in far_out else WHOLE for k in range(len(out_shape))],
        out_shape=out_shape,
        scratch_shapes=list(scratch),
        compiler_params=params(limit),
        **more,
    )(*operands[:scalars], *arrays)


def shifted(block, axis, distance):
    size = lax.axis_size(axis)
    return lax.ppermute(block, axis, [(i, (i + distance) % size) for i in range(size)])


def gathered(values):
    chip = values + lax.ppermute(values, "c", [(0, 1), (1, 0)])
    sent = jnp.broadcast_to(chip[None], (lax.axis_size(CHIPS),) + chip.shape)
    return lax.all_to_all(sent, CHIPS, 0, 0)


def on_device(load_values, load_mask, fixed_mask, frequencies, weight_in, weight_mid, weight_out):
    cells_x, cells_y, cells_z = fixed_mask.shape
    slab, sub = lax.axis_index(SLAB), lax.axis_index("z")
    slabs, subs = lax.axis_size(SLAB), lax.axis_size("z")
    grid_cells = (cells_x * slabs, cells_y * subs, cells_z)
    elements_total = grid_cells[0] * grid_cells[1] * grid_cells[2]
    place = jnp.stack(
        [slab * cells_x, sub * cells_y, lax.axis_index("c")]
        + [(slab == 0) * 1, (slab == slabs - 1) * 1, (sub == 0) * 1, (sub == subs - 1) * 1, slab * 0]
    ).astype(jnp.int32)
    inputs, hidden = weight_in.shape
    rows = cells_x * cells_y * cells_z
    half_rows = cells_y // 2
    field = (cells_x, cells_y, cells_z)
    table = held(2 * cells_x, inputs // 2, half_rows)
    line = held(inputs // 2, cells_z)
    (
        loads, x_cos, x_sin, z_cos, z_sin,
        w_in_t, w_mid_t, w_mid_half, w_column, w_row,
    ) = run(
        functools.partial(prepare_kernel, grid_cells),
        "prepare",
        [
            held(4, *field),
            table,
            table,
            line,
            line,
            held(hidden, inputs, dtype=BF),
            held(hidden, hidden, dtype=BF),
            held(hidden, hidden, dtype=BF),
            held(hidden, 1),
            held(16, hidden, dtype=BF),
        ],
        place, load_values, load_mask, fixed_mask, frequencies, weight_in, weight_mid,
        weight_out, space=pltpu.HBM, far_in=(4, 5),
        scratch=[
            VM((inputs, hidden), BF), VM((hidden, hidden), BF), pltpu.SemaphoreType.DMA((2,)),
        ],
    )

    network = (x_cos, x_sin, z_cos, z_sin, w_in_t, w_mid_t, w_column, w_row)
    kept = [held(hidden, rows, dtype=BF)] * 4
    cost = pl.CostEstimate(
        flops=(inputs + hidden) * hidden * rows,
        bytes_accessed=4 * hidden * rows,
        transcendentals=hidden * rows,
    )
    slots = 5 * cells_x
    outer, rows_first, rows_last, *stored = run(
        outer_kernel,
        "outer",
        [held(cells_x, half_rows, cells_z), held(slots, 3, cells_z), held(slots, 2, cells_z)] + kept,
        *network,
        loads,
        scalars=0,
        limit=16,
        cost_estimate=cost,
    )
    rows_ahead = shifted(rows_first, "z", -1)
    rows_behind = shifted(rows_last, "z", 1)
    density, stiff, *stored = run(
        inner_kernel,
        "inner",
        [held(*field)] * 2 + kept,
        *network,
        outer,
        *stored,
        scalars=0,
        limit=16,
        input_output_aliases={9 + k: 2 + k for k in range(4)},
        cost_estimate=cost,
    )
    hidden_in, slope_mid, slope_in, hidden_mid = stored
    loads, stiff, planes_first, planes_last = run(
        join_kernel,
        "join",
        [held(4, cells_x, ROWS, cells_z), held(cells_x, ROWS, cells_z)]
        + [held(14, ROWS, cells_z), held(10, ROWS, cells_z)],
        place, loads, stiff, rows_ahead, rows_behind,
    )
    planes_ahead = shifted(planes_first, SLAB, -1)
    planes_behind = shifted(planes_last, SLAB, 1)

    back, ready = run(
        functools.partial(back_kernel, span=1024),
        "back",
        kept[:1] + [held(8, 128)],
        w_mid_half,
        slope_mid,
        slope_in,
        scalars=0,
        limit=16,
        input_output_aliases={2: 0},
        cost_estimate=pl.CostEstimate(
            flops=2 * hidden * hidden * rows,
            bytes_accessed=6 * hidden * rows,
            transcendentals=0,
        ),
    )

    vector = held(3, cells_x + 1, ROWS, cells_z)
    first, second, sums = run(
        krylov_kernel,
        "krylov",
        [vector, vector, held(1, 128)],
        place, loads, stiff, planes_ahead, planes_behind, density, ready,
    )
    solution, slope, density = run(
        functools.partial(energy_kernel, elements_total),
        "energy",
        [shaped(3, *field), held(*field), shaped(*field)],
        place, gathered(sums), loads, planes_ahead, first, second, density,
    )

    height = hidden + inputs
    groups = hidden // 128
    mine, other, out_mine = run(
        gradient_kernel,
        "gradients",
        [held(groups // 2, height, 128), held(groups // 2 * height + 8, 128)]
        + [held(groups // 2, 128)],
        place, slope, x_cos, x_sin, z_cos, z_sin, hidden_in, slope_mid, back, hidden_mid,
        limit=16,
        scratch=[VM((hidden, hidden), F32), VM((hidden, inputs), F32), VM((hidden, 128), F32)],
    )

    chips = lax.axis_size(CHIPS)
    swap = [(0, 1), (1, 0)]
    swapped = lax.ppermute(other, "c", swap)
    half = (mine.reshape(-1, 128) + swapped[:-8]).reshape(chips, -1, 128)
    parts = lax.all_to_all(half, CHIPS, 0, 0)
    tall = half.shape[1] + groups // 2
    (shares,) = run(
        share_kernel, "share", [held(chips * tall, 128)], place, parts, out_mine, swapped
    )
    half = lax.all_to_all(shares.reshape(chips, tall, 1, 128), CHIPS, 0, 0)
    half = half.reshape(chips * tall, 128)
    away = lax.ppermute(half, "c", swap)
    grad_in, grad_mid, grad_out = run(
        finish_kernel,
        "finish",
        [shaped(inputs, hidden), shaped(hidden, hidden), shaped(groups, 128)],
        place, half, away,
        far_out=(0, 1),
        scratch=[VM((height, hidden), F32), pltpu.SemaphoreType.DMA((5,))],
    )
    return solution, density, grad_in, grad_mid, grad_out.reshape(hidden)


def solution(mesh):
    slab, sub = mesh.devices.shape
    fine = Mesh(mesh.devices.reshape(4, 4, slab // 16, sub), ALL)
    field = P(SLAB, "z", None)
    vector = P(None, SLAB, "z", None)
    return jax.shard_map(
        on_device,
        mesh=fine,
        in_specs=(vector, field, field, P(), P(), P(), P()),
        out_specs=(vector, field, P(), P(), P()),
        check_vma=False,
    )
```

```python
import functools
import itertools
import math

import jax
import jax.numpy as jnp
import numpy as np
from jax import lax
from jax.experimental import pallas as pl
from jax.experimental.pallas import tpu as pltpu
from jax.sharding import Mesh
from jax.sharding import PartitionSpec as P

ITERS = 3
SLAB = ("x", "y", "c")
CHIPS = ("x", "y", "z")
ALL = ("x", "y", "c", "z")
BF = jnp.bfloat16
F32 = jnp.float32

two_pi = 2.0 * math.pi
emin = 0.001
penalty = 4.0
vol_target = 0.3
ROWS = 16
corner_list = list(itertools.product((0, 1), repeat=3))
LAST = (((1,), (1,)), ((), ()))


def hex_stiffness():
    poisson = 0.3
    lame_first = poisson / ((1.0 + poisson) * (1.0 - 2.0 * poisson))
    lame_second = 0.5 / (1.0 + poisson)
    elastic = np.zeros((6, 6))
    elastic[:3, :3] = lame_first
    for axis_number in range(3):
        elastic[axis_number, axis_number] += 2.0 * lame_second
        elastic[axis_number + 3, axis_number + 3] = lame_second
    gauss_points = [0.5 - 0.5 / math.sqrt(3.0), 0.5 + 0.5 / math.sqrt(3.0)]
    matrix = np.zeros((24, 24))
    for location in itertools.product(gauss_points, repeat=3):
        strain = np.zeros((6, 24))
        for corner_number, corner in enumerate(corner_list):
            factors = [
                location[axis] if corner[axis] == 1 else 1.0 - location[axis] for axis in range(3)
            ]
            slopes = [1.0 if corner[axis] == 1 else -1.0 for axis in range(3)]
            derivative = [
                slopes[0] * factors[1] * factors[2],
                factors[0] * slopes[1] * factors[2],
                factors[0] * factors[1] * slopes[2],
            ]
            column = 3 * corner_number
            for axis in range(3):
                strain[axis, column + axis] = derivative[axis]
            strain[3, column + 1] = derivative[2]
            strain[3, column + 2] = derivative[1]
            strain[4, column + 0] = derivative[2]
            strain[4, column + 2] = derivative[0]
            strain[5, column + 0] = derivative[1]
            strain[5, column + 1] = derivative[0]
        matrix += strain.T @ elastic @ strain / 8.0
    return matrix


def modal_stiffness():
    table = hex_stiffness()
    change = np.zeros((24, 24))
    for row, wave in enumerate(corner_list):
        for column, corner in enumerate(corner_list):
            sign = np.prod([1.0 if c == 1 else -1.0 for w, c in zip(wave, corner) if w == 1])
            for d in range(3):
                change[3 * row + d, 3 * column + d] = sign
    modal = change @ table @ change.T / 64.0
    blocks = []
    for parity in corner_list:
        waves = [tuple(parity[a] ^ (a == d) for a in range(3)) for d in range(3)]
        index = [3 * corner_list.index(wave) + d for d, wave in enumerate(waves)]
        block = modal[np.ix_(index, index)]
        blocks.append((waves, np.where(np.abs(block) < 1e-9, 0.0, block)))
    return blocks


def connected(block, used):
    parts = []
    for d in used:
        for part in parts:
            if block[d, part[0]] != 0.0:
                part.append(d)
                break
        else:
            parts.append([d])
    for part in parts:
        pairs = [block[i, j] for i in part for j in part if i != j]
        assert np.ptp(pairs) < 1e-9 if pairs else True
    return parts


BLOCKS = modal_stiffness()


def lane_mask(shape, lane):
    return lax.broadcasted_iota(jnp.int32, shape, len(shape) - 1) == lane


def plane_modes(plane, rows):
    size = plane.shape[-1]
    ahead = jnp.where(lane_mask(plane.shape, size - 1), 0.0, pltpu.roll(plane, size - 1, 1))
    modes = {}
    for wave_z, part in ((0, plane + ahead), (1, ahead - plane)):
        following = pltpu.roll(part, ROWS - 1, 0)
        modes[0, wave_z] = (part + following)[:rows]
        modes[1, wave_z] = (following - part)[:rows]
    return modes


def element_modes(lower, upper):
    found = []
    for low, high in zip(lower, upper):
        modes = {}
        for key in low:
            modes[(0,) + key] = low[key] + high[key]
            modes[(1,) + key] = high[key] - low[key]
        found.append(modes)
    return found


def modal_forces(modes):
    for waves, block in BLOCKS:
        used = [d for d in range(3) if np.any(block[d] != 0.0)]
        for part in connected(block, used):
            values = [modes[d][waves[d]] for d in part]
            if len(part) == 1:
                forces = [np.float32(block[part[0], part[0]]) * values[0]]
            else:
                common = block[part[0], part[1]]
                total = values[0] + values[1]
                for value in values[2:]:
                    total = total + value
                shared = np.float32(common) * total
                forces = []
                for d, value in zip(part, values):
                    extra = block[d, d] - common
                    if abs(extra) > 1e-9:
                        forces.append(shared + np.float32(extra) * value)
                    else:
                        forces.append(shared)
            for d, value, force in zip(part, values, forces):
                yield d, waves[d], value, force


def energy_of(modes):
    total = None
    for _, _, value, force in modal_forces(modes):
        total = value * force if total is None else total + value * force
    return total


def node_plane(gathered):
    parts = []
    for wave_z in (0, 1):
        even, odd = gathered[0, wave_z], gathered[1, wave_z]
        parts.append((even - odd) + pltpu.roll(even + odd, 1, 0))
    behind = pltpu.roll(parts[0] + parts[1], 1, 1)
    return (parts[0] - parts[1]) + jnp.where(lane_mask(behind.shape, 0), 0.0, behind)


def operator_planes(planes, stiff, free):
    modes = [[plane_modes(component, ROWS) for component in plane] for plane in planes]
    gathered = [[{} for _ in range(3)] for _ in planes]
    for e in range(len(planes) - 1):
        forces = [{} for _ in range(3)]
        for d, wave, _, force in modal_forces(element_modes(modes[e], modes[e + 1])):
            forces[d][wave] = force * stiff[e]
        for d in range(3):
            for key in itertools.product((0, 1), repeat=2):
                even, odd = forces[d].get((0,) + key), forces[d].get((1,) + key)
                for node, sign in ((e, -1), (e + 1, 1)):
                    if even is None:
                        term = odd if sign == 1 else -odd
                    else:
                        term = even + odd if sign == 1 else even - odd
                    held = gathered[node][d]
                    held[key] = term if key not in held else held[key] + term
    return [
        [node_plane(gathered[n][d]) * free[n - 1] for d in range(3)]
        for n in range(1, len(planes) - 1)
    ]


def kept_if(flag):
    return jnp.where(flag == 0, 1.0, 0.0)


def with_rows(place, block, ahead, behind):
    start, stop = kept_if(place[Z_FIRST]), kept_if(place[Z_LAST])
    space = ROWS - block.shape[0] - ahead.shape[0] - behind.shape[0]
    zeros = jnp.zeros((space, block.shape[1]), F32)
    return jnp.concatenate([block, ahead * stop, zeros, behind * start], axis=0)


def krylov_kernel(place, loads, stiff, ahead, behind, density, ready, first, second, sums):
    cells = loads.shape[1]
    low, high = kept_if(place[SLAB_FIRST]), kept_if(place[SLAB_LAST])
    stiff_planes = [behind[8 + p] * low for p in range(2)]
    stiff_planes += [stiff[p] for p in range(cells)]
    stiff_planes += [ahead[12 + p] * high for p in range(2)]
    loaded = [[behind[2 * d + p] * low for d in range(4)] for p in range(2)]
    loaded += [[loads[d, p] for d in range(4)] for p in range(cells)]
    loaded += [[ahead[3 * d + p] * high for d in range(4)] for p in range(3)]
    force = [plane[:3] for plane in loaded]
    free = [plane[3] for plane in loaded]
    image = operator_planes(force, stiff_planes, free[1:-1])
    twice = operator_planes(image, stiff_planes[1:-1], free[2:-2])
    own = (force[2 : 2 + cells], image[1 : 1 + cells], twice[:cells])
    rows = density.shape[1]

    def dot(left, right):
        total = None
        for p in range(cells):
            for d in range(3):
                term = left[p][d][:rows] * right[p][d][:rows]
                total = term if total is None else total + term
        return total

    totals = [dot(own[k // 2], own[(k + 1) // 2]) for k in range(2 * ITERS - 1)]
    modes = [[plane_modes(component, rows) for component in plane] for plane in twice]
    last = None
    volume = None
    for e in range(cells):
        term = stiff_planes[2 + e][:rows] * energy_of(element_modes(modes[e], modes[e + 1]))
        last = term if last is None else last + term
        volume = density[e] if volume is None else volume + density[e]
    totals += [last, volume]
    lane = lax.broadcasted_iota(jnp.int32, sums.shape, 1)
    result = jnp.zeros(sums.shape, F32)
    for k, total in enumerate(totals):
        scalar = jnp.sum(jnp.sum(total, axis=0, keepdims=True), axis=1, keepdims=True)
        result = jnp.where(lane == k, scalar, result)
    sums[...] = result
    for p in range(cells + 1):
        for d in range(3):
            first[d, p] = image[1 + p][d]
            second[d, p] = twice[p][d]


def krylov_steps(moments):
    mean = moments[1] / moments[0]
    powers = [None, mean]
    for k in range(2, 2 * ITERS):
        powers.append(powers[-1] * mean)
    scaled = [moments[k] / moments[0] / powers[k] if k else 1.0 for k in range(2 * ITERS)]

    def product(left, right, shift):
        return sum(
            left[i] * right[j] * scaled[i + j + shift]
            for i in range(len(left))
            for j in range(len(right))
        )

    solution = [0.0] * ITERS
    residual = [1.0]
    direction = [1.0]
    norm_now = scaled[0]
    work = 0.0
    for iteration in range(ITERS):
        alpha = norm_now / product(direction, direction, 1)
        work = work + alpha * norm_now
        solution = [
            solution[i] + (alpha * direction[i] if i < len(direction) else 0.0)
            for i in range(ITERS)
        ]
        if iteration + 1 < ITERS:
            image = [0.0] + direction
            residual = [
                (residual[i] if i < len(residual) else 0.0) - alpha * image[i]
                for i in range(len(image))
            ]
            norm_next = product(residual, residual, 0)
            beta = norm_next / norm_now
            direction = [
                residual[i] + (beta * direction[i] if i < len(direction) else 0.0)
                for i in range(len(residual))
            ]
            norm_now = norm_next
    factors = [solution[i] / powers[i + 1] for i in range(ITERS)]
    return factors, work * moments[0] / mean


def energy_kernel(
    elements, place, sums, loads, ahead, first, second, density, solution, slope, out
):
    total = jnp.sum(sums[...], axis=0)
    lane = lax.broadcasted_iota(jnp.int32, total.shape, 1)
    rows_of = [
        jnp.broadcast_to(
            jnp.sum(jnp.where(lane == k, total, 0.0), axis=1, keepdims=True), total.shape
        )
        for k in range(2 * ITERS + 1)
    ]
    factors, compliance = krylov_steps(rows_of[: 2 * ITERS])
    volume = rows_of[2 * ITERS]
    constant = 2.0 * penalty * (volume / elements - vol_target) / elements
    scale = -3.0 * (1.0 - emin) / compliance
    wide = [jnp.concatenate([value, value], axis=1) for value in factors + [scale, constant]]
    cells, rows, _ = density.shape
    high = kept_if(place[SLAB_LAST])
    modes = []
    for p in range(cells + 1):
        plane = []
        for d in range(3):
            load = loads[d, p] if p < cells else ahead[3 * d] * high
            value = wide[0] * load + wide[1] * first[d, p] + wide[2] * second[d, p]
            if p < cells:
                solution[d, p] = value[:rows]
            plane.append(plane_modes(value, rows))
        modes.append(plane)
    for e in range(cells):
        energy = energy_of(element_modes(modes[e], modes[e + 1]))
        held = density[e]
        out[e] = held
        slope[e] = (wide[3] * held * held * energy + wide[4]) * held * (1.0 - held)


def column_of(line):
    size = line.shape[1]
    shape = (size, size)
    same = lax.broadcasted_iota(jnp.int32, shape, 0) == lax.broadcasted_iota(jnp.int32, shape, 1)
    return jnp.sum(jnp.where(same, line, 0.0), axis=1, keepdims=True)


def prepare_kernel(
    grid_cells, place, load_values, load_mask, fixed_mask, frequencies, w_in, w_mid, w_out,
    loads, x_cos, x_sin, z_cos, z_sin, w_in_t, w_mid_t, w_mid_half, w_column, w_row,
):
    cells, rows, size = load_mask.shape
    free = (1 - fixed_mask[...]).astype(F32)
    held = free * load_mask[...].astype(F32)
    for d in range(4):
        loads[d] = free if d == 3 else held * load_values[d]
    columns = [column_of(frequencies[k : k + 1, :]) for k in range(3)]
    half = rows // 2
    lanes = 2 * cells * half
    number = lax.broadcasted_iota(jnp.int32, (1, lanes), 1)
    side = number // (cells * half)
    plane = (number // half) % cells
    inner = number % half
    row = jnp.where(side == 1, inner + 2, jnp.where(inner < 2, inner, inner + half))
    x_centre = ((place[X_FIRST] + plane).astype(F32) + 0.5) / grid_cells[0]
    y_centre = ((place[Y_FIRST] + row).astype(F32) + 0.5) / grid_cells[1]
    phase = two_pi * (x_centre * columns[0] + y_centre * columns[1])
    cos, sin = jnp.cos(phase), jnp.sin(phase)
    for k in range(2 * cells):
        x_cos[k] = cos[:, k * half : (k + 1) * half]
        x_sin[k] = sin[:, k * half : (k + 1) * half]
    z_number = lax.broadcasted_iota(jnp.int32, (1, size), 1)
    phase = two_pi * (((z_number.astype(F32) + 0.5) / grid_cells[2]) * columns[2])
    z_cos[...] = jnp.cos(phase)
    z_sin[...] = jnp.sin(phase)
    w_in_t[...] = (0.5 * w_in[...].astype(F32)).T.astype(BF)
    middle = 0.5 * w_mid[...].astype(F32)
    w_mid_half[...] = middle.astype(BF)
    w_mid_t[...] = middle.T.astype(BF)
    line = w_out[...].astype(F32)[None, :]
    w_column[...] = 0.5 * column_of(line)
    w_row[...] = jnp.broadcast_to(line, w_row.shape).astype(BF)


def join_kernel(place, loads, stiff, ahead, behind, loads_16, stiff_16, to_before, to_next):
    cells = stiff.shape[0]
    for d in range(4):
        for p in range(cells):
            slot = d * cells + p
            block = with_rows(place, loads[d, p], ahead[slot], behind[slot])
            loads_16[d, p] = block
            if p < 3:
                to_before[3 * d + p] = block
            if p >= cells - 2:
                to_next[2 * d + p - (cells - 2)] = block
    for p in range(cells):
        slot = 4 * cells + p
        block = with_rows(place, stiff[p], ahead[slot, :2, :], behind[slot])
        stiff_16[p] = block
        if p < 2:
            to_before[12 + p] = block
        if p >= cells - 2:
            to_next[8 + p - (cells - 2)] = block


def gated(half):
    up = 1.0 + jnp.tanh(half)
    value = half * up
    return value, up + value * (2.0 - up)


def features_of(tables, group, column, scale=None):
    x_cos, x_sin, z_cos, z_sin = tables
    cos = x_cos[group, :, column : column + 1]
    sin = x_sin[group, :, column : column + 1]
    upper = z_cos[...] * cos - z_sin[...] * sin
    lower = z_sin[...] * cos + z_cos[...] * sin
    if scale is not None:
        upper, lower = upper * scale, lower * scale
    return jnp.concatenate([upper, lower], 0).astype(BF)


def forward_columns(tables, group, weights, kept, spans):
    w_in, w_mid, w_column, w_row = weights
    hidden_in, slope_mid, slope_in, hidden_mid = kept

    def keep(array, value):
        for start, first, count in spans:
            array[:, pl.ds(start, count)] = value[:, first : first + count]

    columns = tables[0].shape[2]
    features = jnp.concatenate([features_of(tables, group, q) for q in range(columns)], 1)
    value, slope = gated(jnp.dot(w_in[...], features, preferred_element_type=F32))
    value = value.astype(BF)
    keep(hidden_in, value)
    keep(slope_in, slope.astype(BF))
    value, slope = gated(jnp.dot(w_mid[...], value, preferred_element_type=F32))
    value = value.astype(BF)
    keep(hidden_mid, value)
    keep(slope_mid, (w_column[...] * slope).astype(BF))
    logits = jnp.dot(w_row[...], value, preferred_element_type=F32)[:1]
    return 0.5 * jnp.tanh(0.5 * logits) + 0.5


def stiffness_of(density):
    return emin + (1.0 - emin) * (density * density * density)


def outer_kernel(
    x_cos, x_sin, z_cos, z_sin, w_in, w_mid, w_column, w_row, loads,
    density, to_before, to_next, *kept,
):
    tables, weights = (x_cos, x_sin, z_cos, z_sin), (w_in, w_mid, w_column, w_row)
    cells, _, size = density.shape

    @pl.loop(0, cells)
    def _(p):
        start = pl.multiple_of(p * (8 * size), 8 * size)
        spans = [(start, 0, 2 * size), (start + 6 * size, 2 * size, 2 * size)]
        line = forward_columns(tables, p, weights, kept, spans)
        for q in range(4):
            part = line[:, q * size : (q + 1) * size]
            density[p, q : q + 1, :] = part
            target = to_before if q < 2 else to_next
            target[4 * cells + p, q % 2 : q % 2 + 1, :] = stiffness_of(part)
        to_before[4 * cells + p, 2:, :] = jnp.zeros((1, size), F32)
        rows = loads.shape[2]
        for d in range(4):
            to_before[d * cells + p] = loads[d, p, :3, :]
            to_next[d * cells + p] = loads[d, p, rows - 2 :, :]


def inner_kernel(
    x_cos, x_sin, z_cos, z_sin, w_in, w_mid, w_column, w_row, outer, *rest,
):
    tables, weights = (x_cos, x_sin, z_cos, z_sin), (w_in, w_mid, w_column, w_row)
    density, stiff = rest[4:6]
    cells, rows, size = density.shape

    @pl.loop(0, cells)
    def _(p):
        start = pl.multiple_of(p * (8 * size), 8 * size)
        spans = [(start + 2 * size, 0, 4 * size)]
        line = forward_columns(tables, cells + p, weights, rest[6:], spans)
        for r in range(rows):
            if 2 <= r < 6:
                part = line[:, (r - 2) * size : (r - 1) * size]
            else:
                q = r if r < 2 else r - 4
                part = outer[p, q : q + 1, :]
            density[p, r : r + 1, :] = part
            stiff[p, r : r + 1, :] = stiffness_of(part)


def back_kernel(w_mid, slope_mid, slope_in, back, done, *, span):
    done[...] = jnp.zeros_like(done)
    for start in range(0, back.shape[1], span):
        place = slice(start, start + span)
        product = jnp.dot(w_mid[...], slope_mid[:, place], preferred_element_type=F32)
        back[:, place] = (product * slope_in[:, place].astype(F32)).astype(BF)


def gradient_kernel(
    place, slope, x_cos, x_sin, z_cos, z_sin, hidden_in, slope_mid, back,
    mine, other, mid, first,
):
    tables = (x_cos, x_sin, z_cos, z_sin)
    cells, rows, size = slope.shape
    half = rows // 2
    group_of = [(0, r) if r < 2 else (0, r - half) if r >= rows - 2 else (1, r - 2) for r in range(rows)]
    for p in range(cells):
        lines = [slope[p, r : r + 1, :] for r in range(rows)]
        picked = [
            features_of(tables, side * cells + p, q, line) for (side, q), line in zip(group_of, lines)
        ]
        features = jnp.concatenate(picked, 1)
        line = jnp.concatenate(lines, 1)
        span = slice(p * rows * size, (p + 1) * rows * size)
        hidden = (hidden_in[:, span].astype(F32) * line).astype(BF)
        terms = (
            lax.dot_general(hidden, slope_mid[:, span], LAST, preferred_element_type=F32),
            lax.dot_general(back[:, span], features, LAST, preferred_element_type=F32),
        )
        for held, term in zip((mid, first), terms):
            if p == 0:
                held[...] = term
            else:
                held[...] += term
    core = place[CORE]
    height = mid.shape[0]
    first_t = first[...].T
    for k in range(2):
        for owner in range(2):
            lanes = slice((2 * owner + k) * 128, (2 * owner + k + 1) * 128)

            @pl.when(core == owner)
            def _():
                mine[k, :height, :] = mid[:, lanes]
                mine[k, height:, :] = first_t[:, lanes]

            @pl.when(core != owner)
            def _():
                other[k, :height, :] = mid[:, lanes]
                other[k, height:, :] = first_t[:, lanes]


def out_kernel(slope, hidden_mid, grad_out, running):
    cells, rows, size = slope.shape
    running[...] = jnp.zeros_like(running)

    @pl.loop(0, cells)
    def _(p):
        total = None
        for r in range(rows):
            line = slope[p, r : r + 1, :]
            for k in range(size // 128):
                start = pl.multiple_of(p * (rows * size) + r * size + k * 128, 128)
                term = hidden_mid[:, pl.ds(start, 128)].astype(F32)
                term = term * line[:, k * 128 : (k + 1) * 128]
                total = term if total is None else total + term
        running[...] += total

    line = jnp.sum(running[...].T, axis=0, keepdims=True)
    for k in range(grad_out.shape[0]):
        grad_out[k : k + 1, :] = line[:, k * 128 : (k + 1) * 128]


def share_kernel(place, parts, grad_out, shares):
    chips = parts.shape[0]
    total = parts[0]
    for chip in range(1, chips):
        total = total + parts[chip]
    block = jnp.concatenate([total, grad_out[...]], axis=0)
    height = block.shape[0]
    for chip in range(chips):
        shares[chip * height : (chip + 1) * height, :] = block


def finish_kernel(place, half, away, grad_in, grad_mid, grad_out):
    extra = grad_out.shape[0]
    height = 24 + extra
    chips = half.shape[0] // height
    middle = grad_mid.shape[0]

    def put(source, owner):
        for group in range(2):
            first = group * (chips // 2)
            lanes = slice((2 * owner + group) * 128, (2 * owner + group + 1) * 128)
            for chip in range(chips // 2):
                start = (first + chip) * height
                block = source[start : start + height - extra, :]
                row = chip * (height - extra)
                if row + height - extra <= middle:
                    grad_mid[row : row + height - extra, lanes] = block
                elif row >= middle:
                    grad_in[row - middle : row - middle + height - extra, lanes] = block
                else:
                    grad_mid[row:, lanes] = block[: middle - row]
                    grad_in[: row + height - extra - middle, lanes] = block[middle - row :]
        total = source[height - extra : height, :]
        for chip in range(1, chips):
            total = total + source[(chip + 1) * height - extra : (chip + 1) * height, :]
        return total

    for owner in range(2):

        @pl.when(place[CORE] == owner)
        def _():
            own, far = put(half, owner), put(away, 1 - owner)
            grad_out[...] = own + far


VM = pltpu.VMEM
WHOLE = pl.BlockSpec(memory_space=pltpu.VMEM)
SCALARS = pl.BlockSpec(memory_space=pltpu.SMEM)
X_FIRST, Y_FIRST, CORE, SLAB_FIRST, SLAB_LAST, Z_FIRST, Z_LAST = range(7)


def params(mebibytes=8):
    return pltpu.CompilerParams(vmem_limit_bytes=mebibytes << 20)


def shaped(*shape, dtype=F32):
    return jax.ShapeDtypeStruct(shape, dtype)


def held(*shape, dtype=F32):
    return VM(shape, dtype)


def run(kernel, name, out_shape, *operands, scalars=1, space=pltpu.VMEM, scratch=(), limit=12, **more):
    arrays = [pltpu.with_memory_space_constraint(array, space) for array in operands[scalars:]]
    return pl.pallas_call(
        kernel,
        name=name,
        in_specs=[SCALARS] * scalars + [WHOLE] * len(arrays),
        out_specs=[WHOLE] * len(out_shape),
        out_shape=out_shape,
        scratch_shapes=list(scratch),
        compiler_params=params(limit),
        **more,
    )(*operands[:scalars], *arrays)


def shifted(block, axis, distance):
    size = lax.axis_size(axis)
    return lax.ppermute(block, axis, [(i, (i + distance) % size) for i in range(size)])


def gathered(values):
    chip = values + lax.ppermute(values, "c", [(0, 1), (1, 0)])
    sent = jnp.broadcast_to(chip[None], (lax.axis_size(CHIPS),) + chip.shape)
    return lax.all_to_all(sent, CHIPS, 0, 0)


def on_device(load_values, load_mask, fixed_mask, frequencies, weight_in, weight_mid, weight_out):
    cells_x, cells_y, cells_z = fixed_mask.shape
    slab, sub = lax.axis_index(SLAB), lax.axis_index("z")
    slabs, subs = lax.axis_size(SLAB), lax.axis_size("z")
    grid_cells = (cells_x * slabs, cells_y * subs, cells_z)
    elements_total = grid_cells[0] * grid_cells[1] * grid_cells[2]
    place = jnp.stack(
        [slab * cells_x, sub * cells_y, lax.axis_index("c")]
        + [(slab == 0) * 1, (slab == slabs - 1) * 1, (sub == 0) * 1, (sub == subs - 1) * 1, slab * 0]
    ).astype(jnp.int32)
    inputs, hidden = weight_in.shape
    rows = cells_x * cells_y * cells_z
    half_rows = cells_y // 2
    field = (cells_x, cells_y, cells_z)
    table = held(2 * cells_x, inputs // 2, half_rows)
    line = held(inputs // 2, cells_z)
    (
        loads, x_cos, x_sin, z_cos, z_sin,
        w_in_t, w_mid_t, w_mid_half, w_column, w_row,
    ) = run(
        functools.partial(prepare_kernel, grid_cells),
        "prepare",
        [
            held(4, *field),
            table,
            table,
            line,
            line,
            held(hidden, inputs, dtype=BF),
            held(hidden, hidden, dtype=BF),
            held(hidden, hidden, dtype=BF),
            held(hidden, 1),
            held(16, hidden, dtype=BF),
        ],
        place, load_values, load_mask, fixed_mask, frequencies, weight_in, weight_mid,
        weight_out, space=pltpu.HBM,
    )

    network = (x_cos, x_sin, z_cos, z_sin, w_in_t, w_mid_t, w_column, w_row)
    kept = [held(hidden, rows, dtype=BF)] * 4
    cost = pl.CostEstimate(
        flops=(inputs + hidden) * hidden * rows,
        bytes_accessed=4 * hidden * rows,
        transcendentals=hidden * rows,
    )
    slots = 5 * cells_x
    outer, rows_first, rows_last, *stored = run(
        outer_kernel,
        "outer",
        [held(cells_x, half_rows, cells_z), held(slots, 3, cells_z), held(slots, 2, cells_z)] + kept,
        *network,
        loads,
        scalars=0,
        limit=12,
        cost_estimate=cost,
    )
    rows_ahead = shifted(rows_first, "z", -1)
    rows_behind = shifted(rows_last, "z", 1)
    density, stiff, *stored = run(
        inner_kernel,
        "inner",
        [held(*field)] * 2 + kept,
        *network,
        outer,
        *stored,
        scalars=0,
        limit=12,
        input_output_aliases={9 + k: 2 + k for k in range(4)},
        cost_estimate=cost,
    )
    hidden_in, slope_mid, slope_in, hidden_mid = stored
    loads, stiff, planes_first, planes_last = run(
        join_kernel,
        "join",
        [held(4, cells_x, ROWS, cells_z), held(cells_x, ROWS, cells_z)]
        + [held(14, ROWS, cells_z), held(10, ROWS, cells_z)],
        place, loads, stiff, rows_ahead, rows_behind,
    )
    planes_ahead = shifted(planes_first, SLAB, -1)
    planes_behind = shifted(planes_last, SLAB, 1)

    back, ready = run(
        functools.partial(back_kernel, span=1024),
        "back",
        kept[:1] + [held(8, 128)],
        w_mid_half,
        slope_mid,
        slope_in,
        scalars=0,
        limit=12,
        input_output_aliases={2: 0},
        cost_estimate=pl.CostEstimate(
            flops=2 * hidden * hidden * rows,
            bytes_accessed=6 * hidden * rows,
            transcendentals=0,
        ),
    )

    vector = held(3, cells_x + 1, ROWS, cells_z)
    first, second, sums = run(
        krylov_kernel,
        "krylov",
        [vector, vector, held(1, 128)],
        place, loads, stiff, planes_ahead, planes_behind, density, ready,
    )
    solution, slope, density = run(
        functools.partial(energy_kernel, elements_total),
        "energy",
        [shaped(3, *field), held(*field), shaped(*field)],
        place, gathered(sums), loads, planes_ahead, first, second, density,
    )

    height = hidden + inputs
    groups = hidden // 128
    mine, other = run(
        gradient_kernel,
        "gradients",
        [held(groups // 2, height, 128)] * 2,
        place, slope, x_cos, x_sin, z_cos, z_sin, hidden_in, slope_mid, back,
        limit=12,
        scratch=[VM((hidden, hidden), F32), VM((hidden, inputs), F32)],
    )

    chips = lax.axis_size(CHIPS)
    swap = [(0, 1), (1, 0)]
    swapped = lax.ppermute(other, "c", swap)
    (grad_out,) = run(
        out_kernel,
        "grad_out",
        [held(groups, 128)],
        lax.optimization_barrier((slope, other))[0],
        hidden_mid,
        scalars=0,
        scratch=[VM((hidden, 128), F32)],
        cost_estimate=pl.CostEstimate(
            flops=2 * hidden * rows, bytes_accessed=2 * hidden * rows, transcendentals=0
        ),
    )
    half = (mine + swapped).reshape(chips, -1, 128)
    half, grad_out = lax.optimization_barrier((half, grad_out))
    parts = lax.all_to_all(half, CHIPS, 0, 0)
    tall = half.shape[1] + groups
    (shares,) = run(share_kernel, "share", [held(chips * tall, 128)], place, parts, grad_out)
    half = lax.all_to_all(shares.reshape(chips, tall, 1, 128), CHIPS, 0, 0)
    half = half.reshape(chips * tall, 128)
    away = lax.ppermute(half, "c", swap)
    grad_in, grad_mid, grad_out = run(
        finish_kernel,
        "finish",
        [shaped(inputs, hidden), shaped(hidden, hidden), shaped(groups, 128)],
        place, half, away,
    )
    return solution, density, grad_in, grad_mid, grad_out.reshape(hidden)


def solution(mesh):
    slab, sub = mesh.devices.shape
    fine = Mesh(mesh.devices.reshape(4, 4, slab // 16, sub), ALL)
    field = P(SLAB, "z", None)
    vector = P(None, SLAB, "z", None)
    return jax.shard_map(
        on_device,
        mesh=fine,
        in_specs=(vector, field, field, P(), P(), P(), P()),
        out_specs=(vector, field, P(), P(), P()),
        check_vma=False,
    )
```

```python
import functools
import itertools
import math

import jax
import jax.numpy as jnp
import numpy as np
from jax import lax
from jax.experimental import pallas as pl
from jax.experimental.pallas import tpu as pltpu
from jax.sharding import Mesh
from jax.sharding import PartitionSpec as P

ITERS = 3
SLAB = ("x", "y", "c")
CHIPS = ("x", "y", "z")
ALL = ("x", "y", "c", "z")
BF = jnp.bfloat16
F32 = jnp.float32

two_pi = 2.0 * math.pi
emin = 0.001
penalty = 4.0
vol_target = 0.3
ROWS = 16
corner_list = list(itertools.product((0, 1), repeat=3))
LAST = (((1,), (1,)), ((), ()))


def hex_stiffness():
    poisson = 0.3
    lame_first = poisson / ((1.0 + poisson) * (1.0 - 2.0 * poisson))
    lame_second = 0.5 / (1.0 + poisson)
    elastic = np.zeros((6, 6))
    elastic[:3, :3] = lame_first
    for axis_number in range(3):
        elastic[axis_number, axis_number] += 2.0 * lame_second
        elastic[axis_number + 3, axis_number + 3] = lame_second
    gauss_points = [0.5 - 0.5 / math.sqrt(3.0), 0.5 + 0.5 / math.sqrt(3.0)]
    matrix = np.zeros((24, 24))
    for location in itertools.product(gauss_points, repeat=3):
        strain = np.zeros((6, 24))
        for corner_number, corner in enumerate(corner_list):
            factors = [
                location[axis] if corner[axis] == 1 else 1.0 - location[axis] for axis in range(3)
            ]
            slopes = [1.0 if corner[axis] == 1 else -1.0 for axis in range(3)]
            derivative = [
                slopes[0] * factors[1] * factors[2],
                factors[0] * slopes[1] * factors[2],
                factors[0] * factors[1] * slopes[2],
            ]
            column = 3 * corner_number
            for axis in range(3):
                strain[axis, column + axis] = derivative[axis]
            strain[3, column + 1] = derivative[2]
            strain[3, column + 2] = derivative[1]
            strain[4, column + 0] = derivative[2]
            strain[4, column + 2] = derivative[0]
            strain[5, column + 0] = derivative[1]
            strain[5, column + 1] = derivative[0]
        matrix += strain.T @ elastic @ strain / 8.0
    return matrix


def modal_stiffness():
    table = hex_stiffness()
    change = np.zeros((24, 24))
    for row, wave in enumerate(corner_list):
        for column, corner in enumerate(corner_list):
            sign = np.prod([1.0 if c == 1 else -1.0 for w, c in zip(wave, corner) if w == 1])
            for d in range(3):
                change[3 * row + d, 3 * column + d] = sign
    modal = change @ table @ change.T / 64.0
    blocks = []
    for parity in corner_list:
        waves = [tuple(parity[a] ^ (a == d) for a in range(3)) for d in range(3)]
        index = [3 * corner_list.index(wave) + d for d, wave in enumerate(waves)]
        block = modal[np.ix_(index, index)]
        blocks.append((waves, np.where(np.abs(block) < 1e-9, 0.0, block)))
    return blocks


def connected(block, used):
    parts = []
    for d in used:
        for part in parts:
            if block[d, part[0]] != 0.0:
                part.append(d)
                break
        else:
            parts.append([d])
    for part in parts:
        pairs = [block[i, j] for i in part for j in part if i != j]
        assert np.ptp(pairs) < 1e-9 if pairs else True
    return parts


BLOCKS = modal_stiffness()


def lane_mask(shape, lane):
    return lax.broadcasted_iota(jnp.int32, shape, len(shape) - 1) == lane


def plane_modes(plane, rows):
    size = plane.shape[-1]
    ahead = jnp.where(lane_mask(plane.shape, size - 1), 0.0, pltpu.roll(plane, size - 1, 1))
    modes = {}
    for wave_z, part in ((0, plane + ahead), (1, ahead - plane)):
        following = pltpu.roll(part, ROWS - 1, 0)
        modes[0, wave_z] = (part + following)[:rows]
        modes[1, wave_z] = (following - part)[:rows]
    return modes


def element_modes(lower, upper):
    found = []
    for low, high in zip(lower, upper):
        modes = {}
        for key in low:
            modes[(0,) + key] = low[key] + high[key]
            modes[(1,) + key] = high[key] - low[key]
        found.append(modes)
    return found


def modal_forces(modes):
    for waves, block in BLOCKS:
        used = [d for d in range(3) if np.any(block[d] != 0.0)]
        for part in connected(block, used):
            values = [modes[d][waves[d]] for d in part]
            if len(part) == 1:
                forces = [np.float32(block[part[0], part[0]]) * values[0]]
            else:
                common = block[part[0], part[1]]
                total = values[0] + values[1]
                for value in values[2:]:
                    total = total + value
                shared = np.float32(common) * total
                forces = []
                for d, value in zip(part, values):
                    extra = block[d, d] - common
                    if abs(extra) > 1e-9:
                        forces.append(shared + np.float32(extra) * value)
                    else:
                        forces.append(shared)
            for d, value, force in zip(part, values, forces):
                yield d, waves[d], value, force


def energy_of(modes):
    total = None
    for _, _, value, force in modal_forces(modes):
        total = value * force if total is None else total + value * force
    return total


def node_plane(gathered):
    parts = []
    for wave_z in (0, 1):
        even, odd = gathered[0, wave_z], gathered[1, wave_z]
        parts.append((even - odd) + pltpu.roll(even + odd, 1, 0))
    behind = pltpu.roll(parts[0] + parts[1], 1, 1)
    return (parts[0] - parts[1]) + jnp.where(lane_mask(behind.shape, 0), 0.0, behind)


def operator_planes(planes, stiff, free):
    modes = [[plane_modes(component, ROWS) for component in plane] for plane in planes]
    gathered = [[{} for _ in range(3)] for _ in planes]
    for e in range(len(planes) - 1):
        forces = [{} for _ in range(3)]
        for d, wave, _, force in modal_forces(element_modes(modes[e], modes[e + 1])):
            forces[d][wave] = force * stiff[e]
        for d in range(3):
            for key in itertools.product((0, 1), repeat=2):
                even, odd = forces[d].get((0,) + key), forces[d].get((1,) + key)
                for node, sign in ((e, -1), (e + 1, 1)):
                    if even is None:
                        term = odd if sign == 1 else -odd
                    else:
                        term = even + odd if sign == 1 else even - odd
                    held = gathered[node][d]
                    held[key] = term if key not in held else held[key] + term
    return [
        [node_plane(gathered[n][d]) * free[n - 1] for d in range(3)]
        for n in range(1, len(planes) - 1)
    ]


def kept_if(flag):
    return jnp.where(flag == 0, 1.0, 0.0)


def with_rows(place, block, ahead, behind):
    start, stop = kept_if(place[Z_FIRST]), kept_if(place[Z_LAST])
    space = ROWS - block.shape[0] - ahead.shape[0] - behind.shape[0]
    zeros = jnp.zeros((space, block.shape[1]), F32)
    return jnp.concatenate([block, ahead * stop, zeros, behind * start], axis=0)


def krylov_kernel(place, loads, stiff, ahead, behind, density, ready, first, second, sums):
    cells = loads.shape[1]
    low, high = kept_if(place[SLAB_FIRST]), kept_if(place[SLAB_LAST])
    stiff_planes = [behind[8 + p] * low for p in range(2)]
    stiff_planes += [stiff[p] for p in range(cells)]
    stiff_planes += [ahead[12 + p] * high for p in range(2)]
    loaded = [[behind[2 * d + p] * low for d in range(4)] for p in range(2)]
    loaded += [[loads[d, p] for d in range(4)] for p in range(cells)]
    loaded += [[ahead[3 * d + p] * high for d in range(4)] for p in range(3)]
    force = [plane[:3] for plane in loaded]
    free = [plane[3] for plane in loaded]
    image = operator_planes(force, stiff_planes, free[1:-1])
    twice = operator_planes(image, stiff_planes[1:-1], free[2:-2])
    own = (force[2 : 2 + cells], image[1 : 1 + cells], twice[:cells])
    rows = density.shape[1]

    def dot(left, right):
        total = None
        for p in range(cells):
            for d in range(3):
                term = left[p][d][:rows] * right[p][d][:rows]
                total = term if total is None else total + term
        return total

    totals = [dot(own[k // 2], own[(k + 1) // 2]) for k in range(2 * ITERS - 1)]
    modes = [[plane_modes(component, rows) for component in plane] for plane in twice]
    last = None
    volume = None
    for e in range(cells):
        term = stiff_planes[2 + e][:rows] * energy_of(element_modes(modes[e], modes[e + 1]))
        last = term if last is None else last + term
        volume = density[e] if volume is None else volume + density[e]
    totals += [last, volume]
    lane = lax.broadcasted_iota(jnp.int32, sums.shape, 1)
    result = jnp.zeros(sums.shape, F32)
    for k, total in enumerate(totals):
        scalar = jnp.sum(jnp.sum(total, axis=0, keepdims=True), axis=1, keepdims=True)
        result = jnp.where(lane == k, scalar, result)
    sums[...] = result
    for p in range(cells + 1):
        for d in range(3):
            first[d, p] = image[1 + p][d]
            second[d, p] = twice[p][d]


def krylov_steps(moments):
    mean = moments[1] / moments[0]
    powers = [None, mean]
    for k in range(2, 2 * ITERS):
        powers.append(powers[-1] * mean)
    scaled = [moments[k] / moments[0] / powers[k] if k else 1.0 for k in range(2 * ITERS)]

    def product(left, right, shift):
        return sum(
            left[i] * right[j] * scaled[i + j + shift]
            for i in range(len(left))
            for j in range(len(right))
        )

    solution = [0.0] * ITERS
    residual = [1.0]
    direction = [1.0]
    norm_now = scaled[0]
    work = 0.0
    for iteration in range(ITERS):
        alpha = norm_now / product(direction, direction, 1)
        work = work + alpha * norm_now
        solution = [
            solution[i] + (alpha * direction[i] if i < len(direction) else 0.0)
            for i in range(ITERS)
        ]
        if iteration + 1 < ITERS:
            image = [0.0] + direction
            residual = [
                (residual[i] if i < len(residual) else 0.0) - alpha * image[i]
                for i in range(len(image))
            ]
            norm_next = product(residual, residual, 0)
            beta = norm_next / norm_now
            direction = [
                residual[i] + (beta * direction[i] if i < len(direction) else 0.0)
                for i in range(len(residual))
            ]
            norm_now = norm_next
    factors = [solution[i] / powers[i + 1] for i in range(ITERS)]
    return factors, work * moments[0] / mean


def energy_kernel(
    elements, place, sums, loads, ahead, first, second, density, solution, slope, out
):
    total = jnp.sum(sums[...], axis=0)
    lane = lax.broadcasted_iota(jnp.int32, total.shape, 1)
    rows_of = [
        jnp.broadcast_to(
            jnp.sum(jnp.where(lane == k, total, 0.0), axis=1, keepdims=True), total.shape
        )
        for k in range(2 * ITERS + 1)
    ]
    factors, compliance = krylov_steps(rows_of[: 2 * ITERS])
    volume = rows_of[2 * ITERS]
    constant = 2.0 * penalty * (volume / elements - vol_target) / elements
    scale = -3.0 * (1.0 - emin) / compliance
    wide = [jnp.concatenate([value, value], axis=1) for value in factors + [scale, constant]]
    cells, rows, _ = density.shape
    high = kept_if(place[SLAB_LAST])
    modes = []
    for p in range(cells + 1):
        plane = []
        for d in range(3):
            load = loads[d, p] if p < cells else ahead[3 * d] * high
            value = wide[0] * load + wide[1] * first[d, p] + wide[2] * second[d, p]
            if p < cells:
                solution[d, p] = value[:rows]
            plane.append(plane_modes(value, rows))
        modes.append(plane)
    for e in range(cells):
        energy = energy_of(element_modes(modes[e], modes[e + 1]))
        held = density[e]
        out[e] = held
        slope[e] = (wide[3] * held * held * energy + wide[4]) * held * (1.0 - held)


def column_of(line):
    size = line.shape[1]
    shape = (size, size)
    same = lax.broadcasted_iota(jnp.int32, shape, 0) == lax.broadcasted_iota(jnp.int32, shape, 1)
    return jnp.sum(jnp.where(same, line, 0.0), axis=1, keepdims=True)


def prepare_kernel(
    grid_cells, place, load_values, load_mask, fixed_mask, frequencies, w_in, w_mid, w_out,
    loads, x_cos, x_sin, z_cos, z_sin, w_in_t, w_mid_t, w_mid_half, w_column, w_row,
):
    cells, rows, size = load_mask.shape
    free = (1 - fixed_mask[...]).astype(F32)
    held = free * load_mask[...].astype(F32)
    for d in range(4):
        loads[d] = free if d == 3 else held * load_values[d]
    columns = [column_of(frequencies[k : k + 1, :]) for k in range(3)]
    half = rows // 2
    lanes = 2 * cells * half
    number = lax.broadcasted_iota(jnp.int32, (1, lanes), 1)
    side = number // (cells * half)
    plane = (number // half) % cells
    inner = number % half
    row = jnp.where(side == 1, inner + 2, jnp.where(inner < 2, inner, inner + half))
    x_centre = ((place[X_FIRST] + plane).astype(F32) + 0.5) / grid_cells[0]
    y_centre = ((place[Y_FIRST] + row).astype(F32) + 0.5) / grid_cells[1]
    phase = two_pi * (x_centre * columns[0] + y_centre * columns[1])
    cos, sin = jnp.cos(phase), jnp.sin(phase)
    for k in range(2 * cells):
        x_cos[k] = cos[:, k * half : (k + 1) * half]
        x_sin[k] = sin[:, k * half : (k + 1) * half]
    z_number = lax.broadcasted_iota(jnp.int32, (1, size), 1)
    phase = two_pi * (((z_number.astype(F32) + 0.5) / grid_cells[2]) * columns[2])
    z_cos[...] = jnp.cos(phase)
    z_sin[...] = jnp.sin(phase)
    w_in_t[...] = (0.5 * w_in[...].astype(F32)).T.astype(BF)
    middle = 0.5 * w_mid[...].astype(F32)
    w_mid_half[...] = middle.astype(BF)
    w_mid_t[...] = middle.T.astype(BF)
    line = w_out[...].astype(F32)[None, :]
    w_column[...] = 0.5 * column_of(line)
    w_row[...] = jnp.broadcast_to(line, w_row.shape).astype(BF)


def join_kernel(place, loads, stiff, ahead, behind, loads_16, stiff_16, to_before, to_next):
    cells = stiff.shape[0]
    for d in range(4):
        for p in range(cells):
            slot = d * cells + p
            block = with_rows(place, loads[d, p], ahead[slot], behind[slot])
            loads_16[d, p] = block
            if p < 3:
                to_before[3 * d + p] = block
            if p >= cells - 2:
                to_next[2 * d + p - (cells - 2)] = block
    for p in range(cells):
        slot = 4 * cells + p
        block = with_rows(place, stiff[p], ahead[slot, :2, :], behind[slot])
        stiff_16[p] = block
        if p < 2:
            to_before[12 + p] = block
        if p >= cells - 2:
            to_next[8 + p - (cells - 2)] = block


def gated(half):
    up = 1.0 + jnp.tanh(half)
    value = half * up
    return value, up + value * (2.0 - up)


def features_of(tables, group, column, scale=None):
    x_cos, x_sin, z_cos, z_sin = tables
    cos = x_cos[group, :, column : column + 1]
    sin = x_sin[group, :, column : column + 1]
    upper = z_cos[...] * cos - z_sin[...] * sin
    lower = z_sin[...] * cos + z_cos[...] * sin
    if scale is not None:
        upper, lower = upper * scale, lower * scale
    return jnp.concatenate([upper, lower], 0).astype(BF)


def forward_columns(tables, group, weights, kept, spans):
    w_in, w_mid, w_column, w_row = weights
    hidden_in, slope_mid, slope_in, hidden_mid = kept

    def keep(array, value):
        for start, first, count in spans:
            array[:, pl.ds(start, count)] = value[:, first : first + count]

    columns = tables[0].shape[2]
    features = jnp.concatenate([features_of(tables, group, q) for q in range(columns)], 1)
    value, slope = gated(jnp.dot(w_in[...], features, preferred_element_type=F32))
    value = value.astype(BF)
    keep(hidden_in, value)
    keep(slope_in, slope.astype(BF))
    value, slope = gated(jnp.dot(w_mid[...], value, preferred_element_type=F32))
    value = value.astype(BF)
    keep(hidden_mid, value)
    keep(slope_mid, (w_column[...] * slope).astype(BF))
    logits = jnp.dot(w_row[...], value, preferred_element_type=F32)[:1]
    return 0.5 * jnp.tanh(0.5 * logits) + 0.5


def stiffness_of(density):
    return emin + (1.0 - emin) * (density * density * density)


def outer_kernel(
    x_cos, x_sin, z_cos, z_sin, w_in, w_mid, w_column, w_row, loads,
    density, to_before, to_next, *kept,
):
    tables, weights = (x_cos, x_sin, z_cos, z_sin), (w_in, w_mid, w_column, w_row)
    cells, _, size = density.shape

    for p in range(cells):
        start = p * (8 * size)
        spans = [(start, 0, 2 * size), (start + 6 * size, 2 * size, 2 * size)]
        line = forward_columns(tables, p, weights, kept, spans)
        for q in range(4):
            part = line[:, q * size : (q + 1) * size]
            density[p, q : q + 1, :] = part
            target = to_before if q < 2 else to_next
            target[4 * cells + p, q % 2 : q % 2 + 1, :] = stiffness_of(part)
        to_before[4 * cells + p, 2:, :] = jnp.zeros((1, size), F32)
        rows = loads.shape[2]
        for d in range(4):
            to_before[d * cells + p] = loads[d, p, :3, :]
            to_next[d * cells + p] = loads[d, p, rows - 2 :, :]


def inner_kernel(
    x_cos, x_sin, z_cos, z_sin, w_in, w_mid, w_column, w_row, outer, *rest,
):
    tables, weights = (x_cos, x_sin, z_cos, z_sin), (w_in, w_mid, w_column, w_row)
    density, stiff = rest[4:6]
    cells, rows, size = density.shape

    @pl.loop(0, cells)
    def _(p):
        start = pl.multiple_of(p * (8 * size), 8 * size)
        spans = [(start + 2 * size, 0, 4 * size)]
        line = forward_columns(tables, cells + p, weights, rest[6:], spans)
        for r in range(rows):
            if 2 <= r < 6:
                part = line[:, (r - 2) * size : (r - 1) * size]
            else:
                q = r if r < 2 else r - 4
                part = outer[p, q : q + 1, :]
            density[p, r : r + 1, :] = part
            stiff[p, r : r + 1, :] = stiffness_of(part)


def back_kernel(w_mid, slope_mid, slope_in, back, done, *, span):
    done[...] = jnp.zeros_like(done)
    for start in range(0, back.shape[1], span):
        place = slice(start, start + span)
        product = jnp.dot(w_mid[...], slope_mid[:, place], preferred_element_type=F32)
        back[:, place] = (product * slope_in[:, place].astype(F32)).astype(BF)


def gradient_kernel(
    place, slope, x_cos, x_sin, z_cos, z_sin, hidden_in, slope_mid, back,
    mine, other, mid, first,
):
    tables = (x_cos, x_sin, z_cos, z_sin)
    cells, rows, size = slope.shape
    half = rows // 2
    group_of = [(0, r) if r < 2 else (0, r - half) if r >= rows - 2 else (1, r - 2) for r in range(rows)]
    for p in range(cells):
        lines = [slope[p, r : r + 1, :] for r in range(rows)]
        picked = [
            features_of(tables, side * cells + p, q, line) for (side, q), line in zip(group_of, lines)
        ]
        features = jnp.concatenate(picked, 1)
        line = jnp.concatenate(lines, 1)
        span = slice(p * rows * size, (p + 1) * rows * size)
        hidden = (hidden_in[:, span].astype(F32) * line).astype(BF)
        terms = (
            lax.dot_general(hidden, slope_mid[:, span], LAST, preferred_element_type=F32),
            lax.dot_general(back[:, span], features, LAST, preferred_element_type=F32),
        )
        for held, term in zip((mid, first), terms):
            if p == 0:
                held[...] = term
            else:
                held[...] += term
    core = place[CORE]
    height = mid.shape[0]
    first_t = first[...].T
    for k in range(2):
        for owner in range(2):
            lanes = slice((2 * owner + k) * 128, (2 * owner + k + 1) * 128)

            @pl.when(core == owner)
            def _():
                mine[k, :height, :] = mid[:, lanes]
                mine[k, height:, :] = first_t[:, lanes]

            @pl.when(core != owner)
            def _():
                other[k, :height, :] = mid[:, lanes]
                other[k, height:, :] = first_t[:, lanes]


def out_kernel(slope, hidden_mid, grad_out, running):
    cells, rows, size = slope.shape
    running[...] = jnp.zeros_like(running)

    @pl.loop(0, cells)
    def _(p):
        total = None
        for r in range(rows):
            line = slope[p, r : r + 1, :]
            for k in range(size // 128):
                start = pl.multiple_of(p * (rows * size) + r * size + k * 128, 128)
                term = hidden_mid[:, pl.ds(start, 128)].astype(F32)
                term = term * line[:, k * 128 : (k + 1) * 128]
                total = term if total is None else total + term
        running[...] += total

    line = jnp.sum(running[...].T, axis=0, keepdims=True)
    for k in range(grad_out.shape[0]):
        grad_out[k : k + 1, :] = line[:, k * 128 : (k + 1) * 128]


def share_kernel(place, parts, grad_out, shares):
    chips = parts.shape[0]
    total = parts[0]
    for chip in range(1, chips):
        total = total + parts[chip]
    block = jnp.concatenate([total, grad_out[...]], axis=0)
    height = block.shape[0]
    for chip in range(chips):
        shares[chip * height : (chip + 1) * height, :] = block


def finish_kernel(place, half, away, grad_in, grad_mid, grad_out):
    extra = grad_out.shape[0]
    height = 24 + extra
    chips = half.shape[0] // height
    middle = grad_mid.shape[0]

    def put(source, owner):
        for group in range(2):
            first = group * (chips // 2)
            lanes = slice((2 * owner + group) * 128, (2 * owner + group + 1) * 128)
            for chip in range(chips // 2):
                start = (first + chip) * height
                block = source[start : start + height - extra, :]
                row = chip * (height - extra)
                if row + height - extra <= middle:
                    grad_mid[row : row + height - extra, lanes] = block
                elif row >= middle:
                    grad_in[row - middle : row - middle + height - extra, lanes] = block
                else:
                    grad_mid[row:, lanes] = block[: middle - row]
                    grad_in[: row + height - extra - middle, lanes] = block[middle - row :]
        total = source[height - extra : height, :]
        for chip in range(1, chips):
            total = total + source[(chip + 1) * height - extra : (chip + 1) * height, :]
        return total

    for owner in range(2):

        @pl.when(place[CORE] == owner)
        def _():
            own, far = put(half, owner), put(away, 1 - owner)
            grad_out[...] = own + far


VM = pltpu.VMEM
WHOLE = pl.BlockSpec(memory_space=pltpu.VMEM)
SCALARS = pl.BlockSpec(memory_space=pltpu.SMEM)
X_FIRST, Y_FIRST, CORE, SLAB_FIRST, SLAB_LAST, Z_FIRST, Z_LAST = range(7)


def params(mebibytes=8):
    return pltpu.CompilerParams(vmem_limit_bytes=mebibytes << 20)


def shaped(*shape, dtype=F32):
    return jax.ShapeDtypeStruct(shape, dtype)


def held(*shape, dtype=F32):
    return VM(shape, dtype)


def run(kernel, name, out_shape, *operands, scalars=1, space=pltpu.VMEM, scratch=(), limit=12, **more):
    arrays = [pltpu.with_memory_space_constraint(array, space) for array in operands[scalars:]]
    return pl.pallas_call(
        kernel,
        name=name,
        in_specs=[SCALARS] * scalars + [WHOLE] * len(arrays),
        out_specs=[WHOLE] * len(out_shape),
        out_shape=out_shape,
        scratch_shapes=list(scratch),
        compiler_params=params(limit),
        **more,
    )(*operands[:scalars], *arrays)


def shifted(block, axis, distance):
    size = lax.axis_size(axis)
    return lax.ppermute(block, axis, [(i, (i + distance) % size) for i in range(size)])


def gathered(values):
    chip = values + lax.ppermute(values, "c", [(0, 1), (1, 0)])
    sent = jnp.broadcast_to(chip[None], (lax.axis_size(CHIPS),) + chip.shape)
    return lax.all_to_all(sent, CHIPS, 0, 0)


def on_device(load_values, load_mask, fixed_mask, frequencies, weight_in, weight_mid, weight_out):
    cells_x, cells_y, cells_z = fixed_mask.shape
    slab, sub = lax.axis_index(SLAB), lax.axis_index("z")
    slabs, subs = lax.axis_size(SLAB), lax.axis_size("z")
    grid_cells = (cells_x * slabs, cells_y * subs, cells_z)
    elements_total = grid_cells[0] * grid_cells[1] * grid_cells[2]
    place = jnp.stack(
        [slab * cells_x, sub * cells_y, lax.axis_index("c")]
        + [(slab == 0) * 1, (slab == slabs - 1) * 1, (sub == 0) * 1, (sub == subs - 1) * 1, slab * 0]
    ).astype(jnp.int32)
    inputs, hidden = weight_in.shape
    rows = cells_x * cells_y * cells_z
    half_rows = cells_y // 2
    field = (cells_x, cells_y, cells_z)
    table = held(2 * cells_x, inputs // 2, half_rows)
    line = held(inputs // 2, cells_z)
    (
        loads, x_cos, x_sin, z_cos, z_sin,
        w_in_t, w_mid_t, w_mid_half, w_column, w_row,
    ) = run(
        functools.partial(prepare_kernel, grid_cells),
        "prepare",
        [
            held(4, *field),
            table,
            table,
            line,
            line,
            held(hidden, inputs, dtype=BF),
            held(hidden, hidden, dtype=BF),
            held(hidden, hidden, dtype=BF),
            held(hidden, 1),
            held(16, hidden, dtype=BF),
        ],
        place, load_values, load_mask, fixed_mask, frequencies, weight_in, weight_mid,
        weight_out, space=pltpu.HBM,
    )

    network = (x_cos, x_sin, z_cos, z_sin, w_in_t, w_mid_t, w_column, w_row)
    kept = [held(hidden, rows, dtype=BF)] * 4
    cost = pl.CostEstimate(
        flops=(inputs + hidden) * hidden * rows,
        bytes_accessed=4 * hidden * rows,
        transcendentals=hidden * rows,
    )
    slots = 5 * cells_x
    outer, rows_first, rows_last, *stored = run(
        outer_kernel,
        "outer",
        [held(cells_x, half_rows, cells_z), held(slots, 3, cells_z), held(slots, 2, cells_z)] + kept,
        *network,
        loads,
        scalars=0,
        limit=12,
        cost_estimate=cost,
    )
    rows_ahead = shifted(rows_first, "z", -1)
    rows_behind = shifted(rows_last, "z", 1)
    density, stiff, *stored = run(
        inner_kernel,
        "inner",
        [held(*field)] * 2 + kept,
        *network,
        outer,
        *stored,
        scalars=0,
        limit=12,
        input_output_aliases={9 + k: 2 + k for k in range(4)},
        cost_estimate=cost,
    )
    hidden_in, slope_mid, slope_in, hidden_mid = stored
    loads, stiff, planes_first, planes_last = run(
        join_kernel,
        "join",
        [held(4, cells_x, ROWS, cells_z), held(cells_x, ROWS, cells_z)]
        + [held(14, ROWS, cells_z), held(10, ROWS, cells_z)],
        place, loads, stiff, rows_ahead, rows_behind,
    )
    planes_ahead = shifted(planes_first, SLAB, -1)
    planes_behind = shifted(planes_last, SLAB, 1)

    back, ready = run(
        functools.partial(back_kernel, span=1024),
        "back",
        kept[:1] + [held(8, 128)],
        w_mid_half,
        slope_mid,
        slope_in,
        scalars=0,
        limit=12,
        input_output_aliases={2: 0},
        cost_estimate=pl.CostEstimate(
            flops=2 * hidden * hidden * rows,
            bytes_accessed=6 * hidden * rows,
            transcendentals=0,
        ),
    )

    vector = held(3, cells_x + 1, ROWS, cells_z)
    first, second, sums = run(
        krylov_kernel,
        "krylov",
        [vector, vector, held(1, 128)],
        place, loads, stiff, planes_ahead, planes_behind, density, ready,
    )
    solution, slope, density = run(
        functools.partial(energy_kernel, elements_total),
        "energy",
        [shaped(3, *field), held(*field), shaped(*field)],
        place, gathered(sums), loads, planes_ahead, first, second, density,
    )

    height = hidden + inputs
    groups = hidden // 128
    mine, other = run(
        gradient_kernel,
        "gradients",
        [held(groups // 2, height, 128)] * 2,
        place, slope, x_cos, x_sin, z_cos, z_sin, hidden_in, slope_mid, back,
        limit=12,
        scratch=[VM((hidden, hidden), F32), VM((hidden, inputs), F32)],
    )

    chips = lax.axis_size(CHIPS)
    swap = [(0, 1), (1, 0)]
    swapped = lax.ppermute(other, "c", swap)
    (grad_out,) = run(
        out_kernel,
        "grad_out",
        [held(groups, 128)],
        lax.optimization_barrier((slope, other))[0],
        hidden_mid,
        scalars=0,
        scratch=[VM((hidden, 128), F32)],
        cost_estimate=pl.CostEstimate(
            flops=2 * hidden * rows, bytes_accessed=2 * hidden * rows, transcendentals=0
        ),
    )
    half = (mine + swapped).reshape(chips, -1, 128)
    half, grad_out = lax.optimization_barrier((half, grad_out))
    parts = lax.all_to_all(half, CHIPS, 0, 0)
    tall = half.shape[1] + groups
    (shares,) = run(share_kernel, "share", [held(chips * tall, 128)], place, parts, grad_out)
    half = lax.all_to_all(shares.reshape(chips, tall, 1, 128), CHIPS, 0, 0)
    half = half.reshape(chips * tall, 128)
    away = lax.ppermute(half, "c", swap)
    grad_in, grad_mid, grad_out = run(
        finish_kernel,
        "finish",
        [shaped(inputs, hidden), shaped(hidden, hidden), shaped(groups, 128)],
        place, half, away,
    )
    return solution, density, grad_in, grad_mid, grad_out.reshape(hidden)


def solution(mesh):
    slab, sub = mesh.devices.shape
    fine = Mesh(mesh.devices.reshape(4, 4, slab // 16, sub), ALL)
    field = P(SLAB, "z", None)
    vector = P(None, SLAB, "z", None)
    return jax.shard_map(
        on_device,
        mesh=fine,
        in_specs=(vector, field, field, P(), P(), P(), P()),
        out_specs=(vector, field, P(), P(), P()),
        check_vma=False,
    )
```
